32 devices in a mesh: chan: 32 (over z, y, x, core).
Axes of the slice: x: 2, y: 2, z: 4, core: 2. Of those that a mesh axis runs over, the one named last changes fastest.
Arguments:
- tokens: bfloat16 [11328, 768], P('chan'), may hold values from -6 to 6
- row_pixel: int32 [11328], replicated, may hold values from 0 to 11327, each once
- coef_height: float32 [768, 64], P('chan'), may hold values from -0.75 to 0.75
- rate_height: float32 [768, 64], P('chan'), may hold values from -1 to 2.5
- coef_width: float32 [768, 64], P('chan'), may hold values from -0.75 to 0.75
- rate_width: float32 [768, 64], P('chan'), may hold values from -1 to 2.5
- skip_weight: float32 [768], P('chan'), may hold values from 0.5 to 1.5
- norm_gain: float32 [768], replicated, may hold values from 0.5 to 1.5
- norm_bias: float32 [768], replicated, may hold values from -4 to 4
- weight_in: bfloat16 [768, 3072], replicated, may hold values from -0.21875 to 0.21875
- bias_in: float32 [3072], replicated, may hold values from -4 to 4
- weight_out: bfloat16 [3072, 768], replicated, may hold values from -0.109375 to 0.109375
- bias_out: float32 [768], replicated, may hold values from -4 to 4
- layer_scale: float32 [768], replicated, may hold values from 0.5 to 1.5
- out_grad: bfloat16 [11328, 768], P('chan'), may hold values from -6 to 6
Outputs:
- block_out: bfloat16 [11328, 768], P('chan')
- grad_tokens: float32 [11328, 768], P('chan')
- grad_coef_height: float32 [768, 64], P('chan')
- grad_rate_height: float32 [768, 64], P('chan')
- grad_coef_width: float32 [768, 64], P('chan')
- grad_rate_width: float32 [768, 64], P('chan')
- grad_skip_weight: float32 [768], P('chan')
- grad_norm_gain: float32 [768], P('chan')
- grad_norm_bias: float32 [768], P('chan')
- grad_weight_in: float32 [768, 3072], P('chan')
- grad_bias_in: float32 [3072], P('chan')
- grad_weight_out: float32 [3072, 768], P('chan')
- grad_bias_out: float32 [768], P('chan')
- grad_layer_scale: float32 [768], P('chan')
The draws below stay inside these ranges and needn't reach their ends.
Inputs may be any that keep to these rules, and one draw needn't show every extreme that they name: Row r of the block holds pixel row_pixel[r] of the image order; every pixel is held by exactly one row.
All inputs are finite; a program needn't handle non-finite values.
Results may differ from the reference program's by a relative error of at most 0.0073.
Values may be sent and summed in bfloat16 or wider, within the bound.
No kernel may reach another device: no remote copies, remote signals or barrier semaphores. Data moves between devices by JAX's collectives and lax.ppermute only.
A program may use at most 320 MiB of HBM per device.

```python
import math
import jax
import jax.numpy as jnp
from jax import lax

D = 768
FF = 3072
NS = 64
GRID_A = 10
GRID_B = 14
GRID_C = 18
ROWS_DEV = 354
IMAGES_A = 12
IMAGES_B = 12
IMAGES_C = 24
PIXELS = 11328


def raised(values, stream_key, source, target, shards_of, factor):
    def block_of(axis_at):
        return (jnp.arange(values.shape[axis_at]) // (values.shape[axis_at] // shards_of)).reshape((-1,) + (1,) * (values.ndim - 1 - axis_at))

    one_side = jax.random.permutation(stream_key, shards_of)[block_of(target)]
    other_side = (block_of(target) + shards_of // 2) % shards_of
    return jnp.where((block_of(source) == one_side) | (block_of(source) == other_side), factor * values, values)


def levels(key, extent, shards, smallest, high):
    level = 1.0
    for dim, shards_of in shards:
        heights = jax.random.uniform(jax.random.fold_in(jax.random.fold_in(key, 6), dim), (shards_of,), jnp.float32, smallest / len(shards), high / len(shards))
        level = level * jnp.repeat(jnp.exp(heights), extent[dim] // shards_of).reshape((-1,) + (1,) * (len(extent) - 1 - dim))
    return level


def bell_draw(key, shape, deviation, bound, cuts=(), kind=jnp.bfloat16):
    values = deviation * jax.random.normal(key, shape, jnp.float32)
    if cuts:
        values = values * levels(key, shape, cuts, -0.22, 0.18)
    return jnp.clip(values, -bound, bound).astype(kind)


def noise_with(rng, shape, scale, limit, cuts, heavy, held_as=jnp.bfloat16):
    values = scale * jax.random.normal(rng, shape, jnp.float32)
    if cuts:
        values = values * levels(rng, shape, cuts, -0.22, 0.18)
    return jnp.clip(raised(values, jax.random.fold_in(rng, 3), *heavy), -limit, limit).astype(held_as)


def setup_inputs(seed: int = 0) -> dict:
    splits = jax.random.split(jax.random.key(seed), 16)
    return {
        "tokens": bell_draw(splits[0], (PIXELS, D), 1.0, 6.0, ((0, 32),)),
        "row_pixel": jax.random.permutation(splits[1], PIXELS).astype(jnp.int32),
        "coef_height": bell_draw(splits[2], (D, NS), NS ** -0.5, 0.75, ((0, 32),), jnp.float32),
        "rate_height": jnp.clip(-1.0 + 3.5 * jax.random.uniform(splits[3], (D, NS), jnp.float32) ** levels(splits[3], (D, NS), ((0, 32),), -0.2, 0.2), -1.0, 2.5),
        "coef_width": bell_draw(splits[4], (D, NS), NS ** -0.5, 0.75, ((0, 32),), jnp.float32),
        "rate_width": jnp.clip(-1.0 + 3.5 * jax.random.uniform(splits[5], (D, NS), jnp.float32) ** levels(splits[5], (D, NS), ((0, 32),), -0.2, 0.2), -1.0, 2.5),
        "skip_weight": jnp.clip(0.5 + 1.0 * jax.random.uniform(splits[6], (D,), jnp.float32) ** levels(splits[6], (D,), ((0, 32),), -0.2, 0.2), 0.5, 1.5),
        "norm_gain": jnp.clip(1.0 + 0.1 * jax.random.normal(splits[7], (D,), jnp.float32), 0.5, 1.5),
        "norm_bias": bell_draw(splits[8], (D,), 0.3, 4.0, (), jnp.float32),
        "weight_in": bell_draw(splits[9], (D, FF), D ** -0.5, 0.21875),
        "bias_in": bell_draw(splits[10], (FF,), 0.3, 4.0, (), jnp.float32),
        "weight_out": bell_draw(splits[11], (FF, D), FF ** -0.5, 0.109375),
        "bias_out": bell_draw(splits[12], (D,), 0.3, 4.0, (), jnp.float32),
        "layer_scale": jnp.clip(jax.random.uniform(splits[13], (D,), jnp.float32, 0.5, 1.5), 0.5, 1.5),
        "out_grad": noise_with(splits[14], (PIXELS, D), 1.0, 6.0, ((0, 32),), (0, 1, 32, 2.75)),
    }


@jax.custom_vjp
def low(v):
    return lax.optimization_barrier(v.astype(jnp.bfloat16)).astype(jnp.float32)

@jax.custom_vjp
def low_back(v):
    return v

def low_keep(v):
    return (low(v), None)

def low_pass(kept, grad):
    return (grad,)

def back_keep(v):
    return (v, None)

def back_low(kept, grad):
    return (low(grad),)
low.defvjp(low_keep, low_pass)
low_back.defvjp(back_keep, back_low)

def kernel_matrix(coefficient, log_rate, grid_size):
    places = jnp.arange(grid_size).astype(jnp.float32)
    decayed = jnp.exp(-jnp.exp(log_rate)[:, :, None] * places[None, None, :] / grid_size)
    profile = lax.optimization_barrier(jnp.sum(coefficient[:, :, None] * decayed, axis=1)) / math.sqrt(grid_size)
    indices = jnp.arange(grid_size).astype(jnp.int32)
    offsets = indices[:, None] - indices[None, :]
    picked = jnp.take(profile, jnp.maximum(offsets, 0).astype(jnp.int32), axis=1)
    return jnp.where(offsets[None, :, :] >= 0, picked, jnp.zeros_like(picked))

def mix_images(pixels, coef_height, rate_height, coef_width, rate_width, skip_weight):
    channel_first = pixels.T
    pieces = []
    offset_pixels = 0
    for grid_size, images in ((GRID_A, IMAGES_A), (GRID_B, IMAGES_B), (GRID_C, IMAGES_C)):
        grid_area = grid_size * grid_size
        pixel_block = channel_first[:, offset_pixels:offset_pixels + images * grid_area]
        pixel_block = pixel_block.reshape(D, images, grid_size, grid_size)
        height_matrix = kernel_matrix(coef_height, rate_height, grid_size)
        width_matrix = kernel_matrix(coef_width, rate_width, grid_size)
        mixed = jnp.einsum('cik,cnkl,cjl->cnij', height_matrix, pixel_block, width_matrix, precision=lax.Precision.HIGHEST)
        pieces.append(mixed.reshape(D, images * grid_area))
        offset_pixels = offset_pixels + images * grid_area
    joined = jnp.concatenate(pieces, axis=1) + skip_weight[:, None] * channel_first
    return joined.T

def forward(row_pixel, tokens, coef_height, rate_height, coef_width, rate_width, skip_weight, norm_gain, norm_bias, weight_in, bias_in, weight_out, bias_out, layer_scale):
    branch_input = low_back(tokens)
    pixels = jnp.zeros_like(branch_input).at[row_pixel].set(branch_input)
    mixed = mix_images(pixels, coef_height, rate_height, coef_width, rate_width, skip_weight)
    normin = low(low_back(mixed[row_pixel]))
    block_rows = 4 * ROWS_DEV
    normin_blocks = normin.reshape(PIXELS // block_rows, block_rows, D)
    token_blocks = tokens.reshape(PIXELS // block_rows, block_rows, D)

    def one_block(pair):
        rows_in, rows_res = pair
        row_mean = lax.optimization_barrier(jnp.mean(rows_in, axis=1, keepdims=True))
        centred = rows_in - row_mean
        inv_std = lax.rsqrt(lax.optimization_barrier(jnp.mean(centred * centred, axis=1, keepdims=True)) + 1e-06)
        normed = low(centred * inv_std * norm_gain + norm_bias)
        pre = low_back(jnp.dot(normed, weight_in, precision=lax.Precision.HIGHEST, preferred_element_type=jnp.float32)) + bias_in
        activated = low(jax.nn.gelu(pre, approximate=False))
        branch = low_back(jnp.dot(activated, weight_out, precision=lax.Precision.HIGHEST, preferred_element_type=jnp.float32)) + bias_out
        return rows_res + layer_scale * branch
    outputs = lax.map(jax.checkpoint(one_block), (normin_blocks, token_blocks))
    return outputs.reshape(PIXELS, D)

def reference(tokens, row_pixel, coef_height, rate_height, coef_width, rate_width, skip_weight, norm_gain, norm_bias, weight_in, bias_in, weight_out, bias_out, layer_scale, out_grad):
    floats = (tokens.astype(jnp.float32), coef_height, rate_height, coef_width, rate_width, skip_weight, norm_gain, norm_bias, weight_in.astype(jnp.float32), bias_in, weight_out.astype(jnp.float32), bias_out, layer_scale)
    result, pullback = jax.vjp(partial_forward(row_pixel), *floats)
    grads = pullback(out_grad.astype(jnp.float32))
    return (result.astype(jnp.bfloat16), grads[0], grads[1], grads[2], grads[3], grads[4], grads[5], grads[6], grads[7], grads[8], grads[9], grads[10], grads[11], grads[12])

def partial_forward(row_pixel):

    def inner(*values):
        return forward(row_pixel, *values)
    return inner
```

```python
import functools
import math

import jax
import jax.numpy as jnp
import numpy as np
from jax import lax
from jax.experimental import pallas as pl
from jax.experimental.pallas import tpu as pltpu
from jax.sharding import PartitionSpec as P

SIDES = (10, 14, 18)
SHARES = (1, 1, 2)
UNIT = sum(m * s * s for s, m in zip(SIDES, SHARES))
TAPS = sum(SIDES)
EPSILON = 1e-06
LANES = 128
SUB = 8
MARGIN = 32
UNROLL = 64
VMEM = 56 * 2**20
F32 = jnp.float32
BF16 = jnp.bfloat16


class Plan:
    def __init__(self, devices, rows, channels):
        self.devices, self.rows, self.channels = devices, rows, channels
        self.pixels = devices * rows
        self.units = self.pixels // UNIT
        self.slots = LANES // channels
        self.row_pad = -(-rows // SUB) * SUB
        self.sections = []
        image_row, packed_row, tap, mask_row, pixel = 0, 0, 0, 0, 0
        for side, share in zip(SIDES, SHARES):
            images = share * self.units
            pitch = -(-side // SUB) * SUB
            groups = -(-images // self.slots)
            self.sections.append(
                dict(side=side, images=images, pitch=pitch, groups=groups, image_row=image_row, packed_row=packed_row, tap=tap, mask_row=mask_row, pixel=pixel)
            )
            image_row += groups * self.slots * side * pitch
            packed_row += groups * side * pitch
            tap += side
            mask_row += side * pitch
            pixel += images * side * side
        self.dump = image_row
        self.image_rows = image_row + SUB
        self.packed_rows = packed_row
        self.mask_rows = mask_row
        self.source_rows = -(-devices * self.row_pad // UNROLL) * UNROLL

    def fits(self):
        return 4 * LANES * (self.image_rows + self.source_rows + 5 * self.packed_rows) < 40 * 2**20

    def address(self, row_pixel):
        where = jnp.zeros_like(row_pixel)
        for part in self.sections:
            local = row_pixel - part["pixel"]
            line = local // part["side"]
            spot = part["image_row"] + line * part["pitch"] + local - line * part["side"]
            where = jnp.where(local >= 0, spot, where)
        table = where.reshape(self.devices, self.rows)
        table = jnp.pad(table, ((0, 0), (0, self.row_pad - self.rows)), constant_values=self.dump)
        table = table.reshape(-1)
        return jnp.pad(table, (0, self.source_rows - table.shape[0]), constant_values=self.dump)

    def spread(self):
        lane = np.arange(LANES)
        held = (lane[None, :] % self.channels == np.arange(self.channels)[:, None]) & (lane[None, :] < self.slots * self.channels)
        return jnp.asarray(held.astype(np.float32), BF16)

    def tile_taps(self, taps):
        tiled = jnp.tile(taps, (1, self.slots))
        return jnp.pad(tiled, ((0, 0), (0, LANES - tiled.shape[1])))

    def fold_taps(self, sums):
        held = sums.reshape(-1, SUB, LANES)[:, :, : self.slots * self.channels]
        return held.reshape(-1, SUB, self.slots, self.channels).sum(axis=(1, 2))


def slot_masks(plan):
    lane = lax.broadcasted_iota(jnp.int32, (SUB, LANES), 1)
    return [(lane >= q * plan.channels) & (lane < (q + 1) * plan.channels) for q in range(plan.slots)]


def scatter_rows(plan, where, block, spread, source, image):
    def turn(s, carry):
        rows = lax.dot_general(block[s], spread[...], (((0,), (0,)), ((), ())), preferred_element_type=F32)
        source[pl.ds(pl.multiple_of(s * plan.row_pad, SUB), plan.rows), :] = rows
        return carry

    lax.fori_loop(0, plan.devices, turn, 0)

    def place(b, carry):
        base = pl.multiple_of(b * UNROLL, UNROLL)
        for u in range(UNROLL):
            image[pl.ds(where[base + u], 1), :] = source[pl.ds(base + u, 1), :]
        return carry

    lax.fori_loop(0, plan.source_rows // UNROLL, place, 0)


def gather_rows(plan, where, spread, source, image, out):
    def fetch(b, carry):
        base = pl.multiple_of(b * UNROLL, UNROLL)
        for u in range(UNROLL):
            source[pl.ds(base + u, 1), :] = image[pl.ds(where[base + u], 1), :]
        return carry

    lax.fori_loop(0, plan.source_rows // UNROLL, fetch, 0)

    def turn(s, carry):
        rows = source[pl.ds(pl.multiple_of(s * plan.row_pad, SUB), plan.rows), :].astype(BF16)
        folded = lax.dot_general(spread[...], rows, (((1,), (1,)), ((), ())), preferred_element_type=F32)
        out[s] = folded.astype(BF16)
        return carry

    lax.fori_loop(0, plan.devices, turn, 0)


def pack_images(plan, masks, image, packed):
    place = lax.broadcasted_iota(jnp.int32, (SUB, LANES), 0)
    for part in plan.sections:
        side, pitch = part["side"], part["pitch"]
        area = side * pitch

        def group(t, carry, part=part, side=side, pitch=pitch, area=area):
            start = part["image_row"] + t * (plan.slots * area)
            target = MARGIN + part["packed_row"] + t * area

            def line(i, inner):
                for j in range(0, pitch, SUB):
                    value = jnp.zeros((SUB, LANES), F32)
                    for q in range(plan.slots):
                        row = pl.multiple_of(start + q * area + i * pitch + j, SUB)
                        here = masks[q] & (t * plan.slots + q < part["images"])
                        if j + SUB > side:
                            here = here & (place + j < side)
                        value = jnp.where(here, image[pl.ds(row, SUB), :], value)
                    packed[pl.ds(pl.multiple_of(target + i * pitch + j, SUB), SUB), :] = value
                return inner

            return lax.fori_loop(0, side, line, carry, unroll=2)

        lax.fori_loop(0, part["groups"], group, 0)


def unpack_line(plan, masks, part, t, offset, value, image):
    area = part["side"] * part["pitch"]
    for q in range(plan.slots):
        row = pl.multiple_of(part["image_row"] + (t * plan.slots + q) * area + offset, SUB)
        image[pl.ds(row, SUB), :] = jnp.where(masks[q], value, 0.0)


def wide_taps(plan, taps, table):
    for tap in range(TAPS):
        table[pl.ds(tap * SUB, SUB), :] = jnp.broadcast_to(taps[pl.ds(tap, 1), :], (SUB, LANES))


def masked_taps(plan, taps, table):
    for part in plan.sections:
        side, pitch = part["side"], part["pitch"]
        place = lax.broadcasted_iota(jnp.int32, (pitch, LANES), 0)
        for tap in range(side):
            row = taps[pl.ds(part["tap"] + tap, 1), :]
            table[pl.ds(part["mask_row"] + tap * pitch, pitch), :] = jnp.where(place >= tap, row, 0.0)


def forward_kernel(plan, where, block, spread, height, width, skip, out, packed, across, source, image, px, pu, height_wide, width_masked):
    masks = slot_masks(plan)
    px[pl.ds(0, MARGIN), :] = jnp.zeros((MARGIN, LANES), F32)
    wide_taps(plan, height, height_wide)
    masked_taps(plan, width, width_masked)
    scatter_rows(plan, where, block, spread, source, image)
    pack_images(plan, masks, image, px)
    skips = jnp.broadcast_to(skip[...], (SUB, LANES))
    for part in plan.sections:
        side, pitch = part["side"], part["pitch"]
        area = side * pitch

        def group(t, carry, part=part, side=side, pitch=pitch, area=area):
            start = MARGIN + part["packed_row"] + t * area

            def line(i, inner):
                base = start + i * pitch
                for j in range(0, pitch, SUB):
                    total = jnp.zeros((SUB, LANES), F32)
                    for tap in range(min(side, j + SUB)):
                        weight = width_masked[pl.ds(part["mask_row"] + tap * pitch + j, SUB), :]
                        total = total + weight * px[pl.ds(base + j - tap, SUB), :]
                    pu[pl.ds(pl.multiple_of(base + j, SUB), SUB), :] = total
                return inner

            lax.fori_loop(0, side, line, 0)

            def column(c, inner):
                first = pl.multiple_of(start + c * SUB, SUB)
                held = [pu[pl.ds(pl.multiple_of(first + k * pitch, SUB), SUB), :] for k in range(side)]
                for i in range(side):
                    total = skips * px[pl.ds(pl.multiple_of(first + i * pitch, SUB), SUB), :]
                    for k in range(i + 1):
                        total = total + height_wide[pl.ds((part["tap"] + i - k) * SUB, SUB), :] * held[k]
                    unpack_line(plan, masks, part, t, i * pitch + c * SUB, total, image)
                return inner

            lax.fori_loop(0, pitch // SUB, column, 0)
            return carry

        lax.fori_loop(0, part["groups"], group, 0)
    packed[...] = px[pl.ds(MARGIN, plan.packed_rows), :]
    across[...] = pu[pl.ds(MARGIN, plan.packed_rows), :]
    gather_rows(plan, where, spread, source, image, out)


def backward_kernel(plan, where, block, spread, height, width, skip, packed, across, out, height_sums, width_sums, skip_sums, source, image, pg, pd, height_wide, width_wide):
    masks = slot_masks(plan)
    place = lax.broadcasted_iota(jnp.int32, (SUB, LANES), 0)
    pd[pl.ds(MARGIN + plan.packed_rows, MARGIN), :] = jnp.zeros((MARGIN, LANES), F32)
    wide_taps(plan, height, height_wide)
    wide_taps(plan, width, width_wide)
    scatter_rows(plan, where, block, spread, source, image)
    pack_images(plan, masks, image, pg)
    skips = jnp.broadcast_to(skip[...], (SUB, LANES))
    skip_sums[...] = jnp.zeros((SUB, LANES), F32)
    height_sums[...] = jnp.zeros((TAPS * SUB, LANES), F32)
    width_sums[...] = jnp.zeros((TAPS * SUB, LANES), F32)
    for part in plan.sections:
        side, pitch = part["side"], part["pitch"]
        area = side * pitch

        def group(t, carry, part=part, side=side, pitch=pitch, area=area):
            start = part["packed_row"] + t * area

            def column(c, inner):
                first = pl.multiple_of(start + c * SUB, SUB)
                held = [pg[pl.ds(pl.multiple_of(MARGIN + first + k * pitch, SUB), SUB), :] for k in range(side)]
                for k in range(side):
                    total = jnp.zeros((SUB, LANES), F32)
                    for i in range(k, side):
                        total = total + height_wide[pl.ds((part["tap"] + i - k) * SUB, SUB), :] * held[i]
                    pd[pl.ds(pl.multiple_of(MARGIN + first + k * pitch, SUB), SUB), :] = total
                ways = [across[pl.ds(pl.multiple_of(first + k * pitch, SUB), SUB), :] for k in range(side)]
                for tap in range(side):
                    total = held[tap] * ways[0]
                    for k in range(1, side - tap):
                        total = total + held[k + tap] * ways[k]
                    at = pl.ds((part["tap"] + tap) * SUB, SUB)
                    height_sums[at, :] += total
                return inner

            lax.fori_loop(0, pitch // SUB, column, 0)
            return carry

        lax.fori_loop(0, part["groups"], group, 0)
    for part in plan.sections:
        side, pitch = part["side"], part["pitch"]
        area = side * pitch

        def group(t, carry, part=part, side=side, pitch=pitch, area=area):
            start = part["packed_row"] + t * area

            def line(i, sums):
                sums = list(sums)
                base = start + i * pitch
                aligned = pl.multiple_of(base, SUB)
                for j in range(0, pitch, SUB):
                    mine = packed[pl.ds(pl.multiple_of(aligned + j, SUB), SUB), :]
                    grad = pg[pl.ds(pl.multiple_of(MARGIN + aligned + j, SUB), SUB), :]
                    total = skips * grad
                    sums[side] = sums[side] + mine * grad
                    for tap in range(min(side, side - j)):
                        moved = pd[pl.ds(MARGIN + base + j + tap, SUB), :]
                        if j + SUB - 1 + tap >= pitch:
                            moved = jnp.where(place + (j + tap) < side, moved, 0.0)
                        total = total + width_wide[pl.ds((part["tap"] + tap) * SUB, SUB), :] * moved
                        sums[tap] = sums[tap] + mine * moved
                    unpack_line(plan, masks, part, t, i * pitch + j, total, image)
                return tuple(sums)

            return lax.fori_loop(0, side, line, carry)

        zero = jnp.zeros((SUB, LANES), F32)
        sums = lax.fori_loop(0, part["groups"], group, (zero,) * (side + 1))
        for tap in range(side):
            width_sums[pl.ds((part["tap"] + tap) * SUB, SUB), :] = sums[tap]
        skip_sums[...] += sums[side]
    gather_rows(plan, where, spread, source, image, out)


def whole(memory):
    return pl.BlockSpec(memory_space=memory)


def mixer_forward(plan, where, block, spread, height, width, skip):
    rows = plan.packed_rows
    return pl.pallas_call(
        functools.partial(forward_kernel, plan),
        out_shape=(
            jax.ShapeDtypeStruct(block.shape, BF16),
            jax.ShapeDtypeStruct((rows, LANES), F32),
            jax.ShapeDtypeStruct((rows, LANES), F32),
        ),
        in_specs=[whole(pltpu.SMEM)] + [whole(pltpu.VMEM)] * 5,
        out_specs=(whole(pltpu.VMEM),) * 3,
        scratch_shapes=[
            pltpu.VMEM((plan.source_rows, LANES), F32),
            pltpu.VMEM((plan.image_rows, LANES), F32),
            pltpu.VMEM((rows + 2 * MARGIN, LANES), F32),
            pltpu.VMEM((rows + 2 * MARGIN, LANES), F32),
            pltpu.VMEM((TAPS * SUB, LANES), F32),
            pltpu.VMEM((plan.mask_rows, LANES), F32),
        ],
        compiler_params=pltpu.CompilerParams(vmem_limit_bytes=VMEM),
        cost_estimate=pl.CostEstimate(flops=30_000_000, bytes_accessed=90_000_000, transcendentals=0),
        name="mixer_forward",
    )(where, block, spread, height, width, skip)


def mixer_backward(plan, where, block, spread, height, width, skip, packed, across):
    rows = plan.packed_rows
    return pl.pallas_call(
        functools.partial(backward_kernel, plan),
        out_shape=(
            jax.ShapeDtypeStruct(block.shape, BF16),
            jax.ShapeDtypeStruct((TAPS * SUB, LANES), F32),
            jax.ShapeDtypeStruct((TAPS * SUB, LANES), F32),
            jax.ShapeDtypeStruct((SUB, LANES), F32),
        ),
        in_specs=[whole(pltpu.SMEM)] + [whole(pltpu.VMEM)] * 7,
        out_specs=(whole(pltpu.VMEM),) * 4,
        scratch_shapes=[
            pltpu.VMEM((plan.source_rows, LANES), F32),
            pltpu.VMEM((plan.image_rows, LANES), F32),
            pltpu.VMEM((rows + 2 * MARGIN, LANES), F32),
            pltpu.VMEM((rows + 2 * MARGIN, LANES), F32),
            pltpu.VMEM((TAPS * SUB, LANES), F32),
            pltpu.VMEM((TAPS * SUB, LANES), F32),
        ],
        compiler_params=pltpu.CompilerParams(vmem_limit_bytes=VMEM),
        cost_estimate=pl.CostEstimate(flops=60_000_000, bytes_accessed=110_000_000, transcendentals=0),
        name="mixer_backward",
    )(where, block, spread, height, width, skip, packed, across)


def tap_places():
    reach = np.concatenate([np.arange(s) / s for s in SIDES]).astype(np.float32)
    scale = np.concatenate([np.full(s, 1.0 / math.sqrt(s)) for s in SIDES]).astype(np.float32)
    return jnp.asarray(reach), jnp.asarray(scale)


def profiles(coefficient, log_rate):
    reach, scale = tap_places()
    decayed = jnp.exp(-jnp.exp(log_rate)[None] * reach[:, None, None])
    return jnp.sum(coefficient[None] * decayed, axis=2) * scale[:, None]


def profile_grads(coefficient, log_rate, grads):
    reach, scale = tap_places()
    rate = jnp.exp(log_rate)
    decayed = jnp.exp(-rate[None] * reach[:, None, None])
    weighted = (grads * scale[:, None])[:, :, None] * decayed
    return jnp.sum(weighted, axis=0), -coefficient * rate * jnp.sum(weighted * reach[:, None, None], axis=0)


def kernel_matrix(profile, part):
    side = part["side"]
    offsets = np.arange(side)[:, None] - np.arange(side)[None, :]
    picked = profile[part["tap"] + np.maximum(offsets, 0)]
    return jnp.where((offsets >= 0)[:, :, None], picked, 0.0)


def mix_plain(plan, row_pixel, channel_rows, height, width, skip):
    def one_channel(given):
        values, high, wide, weight = given
        image_order = jnp.zeros_like(values).at[row_pixel].set(values)
        pieces = []
        for part in plan.sections:
            side, count = part["side"], part["images"] * part["side"] ** 2
            block = image_order[part["pixel"] : part["pixel"] + count].reshape(-1, side, side)
            left = kernel_matrix(high[:, None], part)[:, :, 0]
            right = kernel_matrix(wide[:, None], part)[:, :, 0]
            mixed = jnp.einsum("ik,nkl,jl->nij", left, block, right, precision=lax.Precision.HIGHEST)
            pieces.append(mixed.reshape(-1))
        joined = jnp.concatenate(pieces) + weight * image_order
        return joined[row_pixel]

    return lax.map(jax.checkpoint(one_channel), (channel_rows, height.T, width.T, skip))


def exchange(blocks):
    return lax.all_to_all(blocks, "chan", 0, 0, tiled=True)


def to_blocks(rows, devices):
    return rows.T.reshape(devices, rows.shape[1] // devices, rows.shape[0])


def to_rows(blocks):
    return blocks.reshape(-1, blocks.shape[2]).T


def halve(blocks, bits):
    myself = lax.axis_index("chan")
    size = lax.axis_size("chan")
    pairs = lambda bit: [(i, i ^ 1 << bit) for i in range(size)]
    left = list(range(size.bit_length() - 1))
    for bit in bits:
        at = left.index(bit)
        viewed = blocks.reshape((-1, 2, 1 << at) + blocks.shape[1:])
        own = myself >> bit & 1
        keep = lax.dynamic_index_in_dim(viewed, own, 1, keepdims=False)
        send = lax.dynamic_index_in_dim(viewed, 1 - own, 1, keepdims=False)
        got = lax.ppermute(send, "chan", pairs(bit))
        total = keep.astype(F32) + got.astype(F32)
        left.remove(bit)
        blocks = (total if not left else total.astype(BF16)).reshape((-1,) + blocks.shape[1:])
    return blocks[0]


def body(
    tokens,
    row_pixel,
    coef_height,
    rate_height,
    coef_width,
    rate_width,
    skip_weight,
    norm_gain,
    norm_bias,
    weight_in,
    bias_in,
    weight_out,
    bias_out,
    layer_scale,
    out_grad,
):
    devices = lax.axis_size("chan")
    rows, width_all = tokens.shape
    plan = Plan(devices, rows, width_all // devices)
    token_blocks = exchange(to_blocks(tokens, devices))

    height = profiles(coef_height, rate_height)
    width = profiles(coef_width, rate_width)
    if plan.fits():
        where = plan.address(row_pixel)
        spread = plan.spread()
        fixed = (plan.tile_taps(height), plan.tile_taps(width), plan.tile_taps(skip_weight[None]))
        mixed_blocks, packed, across = mixer_forward(plan, where, token_blocks, spread, *fixed)
    else:
        lines = lambda blocks: blocks.transpose(1, 0, 2).reshape(blocks.shape[1], -1)
        blocks_of = lambda values: values.astype(BF16).reshape(-1, devices, rows).transpose(1, 0, 2)
        mixed, mixer_back = jax.vjp(
            functools.partial(mix_plain, plan, row_pixel), lines(token_blocks).astype(F32), height, width, skip_weight
        )
        mixed_blocks = blocks_of(mixed)
    normin = to_rows(exchange(mixed_blocks)).astype(F32)

    upstream = out_grad.astype(F32)
    scaled = upstream * layer_scale
    scaled_low = scaled.astype(BF16)
    grad_act = lax.dot_general(scaled_low, weight_out, (((1,), (1,)), ((), ())), preferred_element_type=F32)

    row_mean = jnp.mean(normin, axis=1, keepdims=True)
    centred = normin - row_mean
    inv_std = lax.rsqrt(jnp.mean(centred * centred, axis=1, keepdims=True) + EPSILON)
    unit_rows = centred * inv_std
    normed = (unit_rows * norm_gain + norm_bias).astype(BF16)
    hidden_pre = jnp.dot(normed, weight_in, preferred_element_type=F32) + bias_in
    cdf = 0.5 * (1.0 + lax.erf(hidden_pre * math.sqrt(0.5)))
    act_low = (hidden_pre * cdf).astype(BF16)
    slope = cdf + hidden_pre * jnp.exp(-0.5 * hidden_pre * hidden_pre) * (1.0 / math.sqrt(2.0 * math.pi))
    grad_pre = grad_act * slope
    grad_pre_low = grad_pre.astype(BF16)
    grad_normed = lax.dot_general(grad_pre_low, weight_in, (((1,), (1,)), ((), ())), preferred_element_type=F32)
    grad_unit = grad_normed * norm_gain
    grad_normin = inv_std * (
        grad_unit
        - jnp.mean(grad_unit, axis=1, keepdims=True)
        - unit_rows * jnp.mean(grad_unit * unit_rows, axis=1, keepdims=True)
    )
    grad_blocks = exchange(to_blocks(grad_normin.astype(BF16), devices))

    branch = jnp.dot(act_low, weight_out, preferred_element_type=F32) + bias_out
    block_out = (tokens.astype(F32) + layer_scale * branch).astype(BF16)
    small = (
        jnp.sum(grad_normed * unit_rows, axis=0),
        jnp.sum(grad_normed, axis=0),
        jnp.sum(grad_pre, axis=0),
        jnp.sum(scaled, axis=0),
        jnp.sum(upstream * branch, axis=0),
    )
    weight_in_part = lax.dot_general(normed, grad_pre_low, (((0,), (0,)), ((), ())), preferred_element_type=F32)
    weight_out_part = lax.dot_general(act_low, scaled_low, (((0,), (0,)), ((), ())), preferred_element_type=F32)

    if plan.fits():
        grad_rows, height_sums, width_sums, skip_sums = mixer_backward(plan, where, grad_blocks, spread, *fixed, packed, across)
        grad_height, grad_width = plan.fold_taps(height_sums), plan.fold_taps(width_sums)
        grad_skip = plan.fold_taps(skip_sums)[0]
    else:
        grad_mixed, grad_height, grad_width, grad_skip = mixer_back(lines(grad_blocks).astype(F32))
        grad_rows = blocks_of(grad_mixed)
    coef_height_grad, rate_height_grad = profile_grads(coef_height, rate_height, grad_height)
    coef_width_grad, rate_width_grad = profile_grads(coef_width, rate_width, grad_width)
    grad_tokens = upstream + to_rows(exchange(grad_rows)).astype(F32)

    levels = list(range(devices.bit_length() - 1))
    other = levels[:1] + levels[1:3][::-1] + levels[3:]
    in_sum = halve(weight_in_part.astype(BF16).reshape(devices, -1, weight_in.shape[1]), levels)
    out_sum = halve(weight_out_part.astype(BF16).reshape(devices, -1, weight_out.shape[1]), other)
    shares = jnp.concatenate([s.reshape(devices, -1) for s in small], axis=1)
    shares = exchange(shares).sum(axis=0)
    cuts = np.cumsum([s.shape[0] // devices for s in small])[:-1]
    gain_grad, norm_bias_grad, bias_in_grad, bias_out_grad, scale_grad = jnp.split(shares, cuts)
    return (
        block_out,
        grad_tokens,
        coef_height_grad,
        rate_height_grad,
        coef_width_grad,
        rate_width_grad,
        grad_skip,
        gain_grad,
        norm_bias_grad,
        in_sum,
        bias_in_grad,
        out_sum,
        bias_out_grad,
        scale_grad,
    )


def solution(mesh):
    split, copied = P("chan"), P()
    in_specs = (split, copied) + (split,) * 5 + (copied,) * 7 + (split,)
    return jax.shard_map(body, mesh=mesh, in_specs=in_specs, out_specs=(split,) * 14, check_vma=False)
```

```python
import functools
import math

import jax
import jax.numpy as jnp
import numpy as np
from jax import lax
from jax.experimental import pallas as pl
from jax.experimental.pallas import tpu as pltpu
from jax.sharding import PartitionSpec as P

SIDES = (10, 14, 18)
SHARES = (1, 1, 2)
UNIT = sum(m * s * s for s, m in zip(SIDES, SHARES))
TAPS = sum(SIDES)
EPSILON = 1e-06
LANES = 128
SUB = 8
MARGIN = 32
VMEM = 56 * 2**20
F32 = jnp.float32
BF16 = jnp.bfloat16


class Plan:
    def __init__(self, devices, rows, channels):
        self.devices, self.rows, self.channels = devices, rows, channels
        self.pixels = devices * rows
        self.units = self.pixels // UNIT
        self.slots = LANES // channels
        self.row_pad = -(-rows // LANES) * LANES
        self.extra_row = -(-rows // SUB) * SUB
        self.sections = []
        image_row, packed_row, tap, mask_row, pixel = 0, 0, 0, 0, 0
        for side, share in zip(SIDES, SHARES):
            images = share * self.units
            pitch = -(-side // SUB) * SUB
            groups = -(-images // self.slots)
            self.sections.append(
                dict(side=side, images=images, pitch=pitch, groups=groups, image_row=image_row, packed_row=packed_row, tap=tap, mask_row=mask_row, pixel=pixel)
            )
            image_row += groups * self.slots * side * pitch
            packed_row += groups * side * pitch
            tap += side
            mask_row += side * pitch
            pixel += images * side * side
        self.image_rows = image_row
        self.packed_rows = packed_row
        self.mask_rows = mask_row

    def fits(self):
        room = self.row_pad - self.extra_row >= 2 * SUB
        return room and self.channels % SUB == 0 and 4 * LANES * (self.image_rows + 2 * self.row_pad + 5 * self.packed_rows) < 40 * 2**20

    def address(self, row_pixel):
        where = jnp.zeros_like(row_pixel)
        for part in self.sections:
            local = row_pixel - part["pixel"]
            line = local // part["side"]
            spot = part["image_row"] + line * part["pitch"] + local - line * part["side"]
            where = jnp.where(local >= 0, spot, where)
        return where

    def spread(self):
        lane = np.arange(LANES)
        held = (lane[None, :] % self.channels == np.arange(self.channels)[:, None]) & (lane[None, :] < self.slots * self.channels)
        return jnp.asarray(held.astype(np.float32), BF16)

    def tile_taps(self, taps):
        tiled = jnp.tile(taps, (1, self.slots))
        return jnp.pad(tiled, ((0, 0), (0, LANES - tiled.shape[1])))


def slot_masks(plan):
    lane = lax.broadcasted_iota(jnp.int32, (SUB, LANES), 1)
    return [(lane >= q * plan.channels) & (lane < (q + 1) * plan.channels) for q in range(plan.slots)]


def in_turn(plan, first, second):
    first(0, 0)

    def pair(k, carry):
        first(2 * k + 1, 1)
        second(2 * k, 0)
        first(2 * k + 2, 0)
        second(2 * k + 1, 1)
        return carry

    lax.fori_loop(0, plan.devices // 2 - 1, pair, 0)
    first(plan.devices - 1, 1)
    second(plan.devices - 2, 0)
    second(plan.devices - 1, 1)


def scatter_rows(plan, where, block, spread, buffers, image):
    def turn(s, held):
        rows = lax.dot_general(block[s], spread[...], (((0,), (0,)), ((), ())), preferred_element_type=F32)
        buffers[held][pl.ds(0, plan.rows), :] = rows

    def place(s, held):
        base = s * plan.rows
        for u in range(plan.rows):
            image[pl.ds(where[base + u], 1), :] = buffers[held][pl.ds(u, 1), :]

    in_turn(plan, turn, place)


def gather_rows(plan, where, spread, buffers, image, out, extra=None):
    used = plan.rows if extra is None else plan.row_pad

    def fetch(s, held):
        base = s * plan.rows
        for u in range(plan.rows):
            buffers[held][pl.ds(u, 1), :] = image[pl.ds(where[base + u], 1), :]

    def fold(s, held):
        if extra is not None:
            high = extra[s].astype(BF16).astype(F32)
            buffers[held][pl.ds(plan.extra_row, SUB), :] = high
            buffers[held][pl.ds(plan.extra_row + SUB, SUB), :] = extra[s] - high
        rows = buffers[held][pl.ds(0, used), :].astype(BF16)
        folded = lax.dot_general(spread[...], rows, (((1,), (1,)), ((), ())), preferred_element_type=F32)
        out[s] = folded.astype(BF16)

    in_turn(plan, fetch, fold)


def pack_images(plan, masks, image, packed, margin):
    place = lax.broadcasted_iota(jnp.int32, (SUB, LANES), 0)
    for part in plan.sections:
        side, pitch = part["side"], part["pitch"]
        area = side * pitch

        def group(t, carry, part=part, side=side, pitch=pitch, area=area):
            start = part["image_row"] + t * (plan.slots * area)
            target = margin + part["packed_row"] + t * area

            def line(i, inner):
                for j in range(0, pitch, SUB):
                    value = jnp.zeros((SUB, LANES), F32)
                    for q in range(plan.slots):
                        row = pl.multiple_of(start + q * area + i * pitch + j, SUB)
                        here = masks[q] & (t * plan.slots + q < part["images"])
                        if j + SUB > side:
                            here = here & (place + j < side)
                        value = jnp.where(here, image[pl.ds(row, SUB), :], value)
                    packed[pl.ds(pl.multiple_of(target + i * pitch + j, SUB), SUB), :] = value
                return inner

            return lax.fori_loop(0, side, line, carry, unroll=2)

        lax.fori_loop(0, part["groups"], group, 0)


def unpack_line(plan, masks, part, t, offset, value, image):
    area = part["side"] * part["pitch"]
    for q in range(plan.slots):
        row = pl.multiple_of(part["image_row"] + (t * plan.slots + q) * area + offset, SUB)
        image[pl.ds(row, SUB), :] = jnp.where(masks[q], value, 0.0)


def wide_taps(plan, taps, table):
    for tap in range(TAPS):
        table[pl.ds(tap * SUB, SUB), :] = jnp.broadcast_to(taps[pl.ds(tap, 1), :], (SUB, LANES))


def masked_taps(plan, taps, table):
    for part in plan.sections:
        side, pitch = part["side"], part["pitch"]
        place = lax.broadcasted_iota(jnp.int32, (pitch, LANES), 0)
        for tap in range(side):
            row = taps[pl.ds(part["tap"] + tap, 1), :]
            table[pl.ds(part["mask_row"] + tap * pitch, pitch), :] = jnp.where(place >= tap, row, 0.0)


def forward_kernel(plan, where, block, spread, height, width, skip, out, packed, across, near, far, image, px, pu, height_wide, width_masked):
    masks = slot_masks(plan)
    px[pl.ds(0, MARGIN), :] = jnp.zeros((MARGIN, LANES), F32)
    wide_taps(plan, height, height_wide)
    masked_taps(plan, width, width_masked)
    scatter_rows(plan, where, block, spread, (near, far), image)
    pack_images(plan, masks, image, px, MARGIN)
    skips = jnp.broadcast_to(skip[...], (SUB, LANES))
    for part in plan.sections:
        side, pitch = part["side"], part["pitch"]
        area = side * pitch

        def group(t, carry, part=part, side=side, pitch=pitch, area=area):
            start = MARGIN + part["packed_row"] + t * area

            def line(i, inner):
                base = start + i * pitch
                for j in range(0, pitch, SUB):
                    total = jnp.zeros((SUB, LANES), F32)
                    for tap in range(min(side, j + SUB)):
                        weight = width_masked[pl.ds(part["mask_row"] + tap * pitch + j, SUB), :]
                        total = total + weight * px[pl.ds(base + j - tap, SUB), :]
                    pu[pl.ds(pl.multiple_of(base + j, SUB), SUB), :] = total
                return inner

            lax.fori_loop(0, side, line, 0)

            def column(c, inner):
                first = pl.multiple_of(start + c * SUB, SUB)
                held = [pu[pl.ds(pl.multiple_of(first + k * pitch, SUB), SUB), :] for k in range(side)]
                for i in range(side):
                    total = skips * px[pl.ds(pl.multiple_of(first + i * pitch, SUB), SUB), :]
                    for k in range(i + 1):
                        total = total + height_wide[pl.ds((part["tap"] + i - k) * SUB, SUB), :] * held[k]
                    unpack_line(plan, masks, part, t, i * pitch + c * SUB, total, image)
                return inner

            lax.fori_loop(0, pitch // SUB, column, 0)
            return carry

        lax.fori_loop(0, part["groups"], group, 0)
    packed[...] = px[pl.ds(MARGIN, plan.packed_rows), :]
    across[...] = pu[pl.ds(MARGIN, plan.packed_rows), :]
    gather_rows(plan, where, spread, (near, far), image, out)


def arrive_kernel(plan, where, block, spread, *rest):
    grads, near, far, image = rest[-4:]
    scatter_rows(plan, where, block, spread, (near, far), image)
    pack_images(plan, slot_masks(plan), image, grads, 0)


def leave_kernel(plan, where, grads, spread, extra, *rest):
    out, near, far, image = rest[-4:]
    masks = slot_masks(plan)
    for part in plan.sections:
        area = part["side"] * part["pitch"]

        def group(t, carry, part=part, area=area):
            for offset in range(0, area, SUB):
                row = pl.multiple_of(part["packed_row"] + t * area + offset, SUB)
                unpack_line(plan, masks, part, t, offset, grads[pl.ds(row, SUB), :], image)
            return carry

        lax.fori_loop(0, part["groups"], group, 0)
    gather_rows(plan, where, spread, (near, far), image, out, extra)


def backward_kernel(plan, pg, height, width, skip, packed, across, *rest):
    out, height_sums, width_sums, skip_sums, pd, height_wide, width_wide = rest[-7:]
    place = lax.broadcasted_iota(jnp.int32, (SUB, LANES), 0)
    pd[pl.ds(plan.packed_rows, MARGIN), :] = jnp.zeros((MARGIN, LANES), F32)
    wide_taps(plan, height, height_wide)
    wide_taps(plan, width, width_wide)
    skips = jnp.broadcast_to(skip[...], (SUB, LANES))
    skip_sums[...] = jnp.zeros((SUB, LANES), F32)
    height_sums[...] = jnp.zeros((TAPS * SUB, LANES), F32)
    for part in plan.sections:
        side, pitch = part["side"], part["pitch"]
        area = side * pitch

        def group(t, carry, part=part, side=side, pitch=pitch, area=area):
            start = part["packed_row"] + t * area

            def column(c, inner):
                first = pl.multiple_of(start + c * SUB, SUB)
                rows = [pl.ds(pl.multiple_of(first + k * pitch, SUB), SUB) for k in range(side)]
                held = [pg[row, :] for row in rows]
                for k in range(side):
                    total = jnp.zeros((SUB, LANES), F32)
                    for i in range(k, side):
                        total = total + height_wide[pl.ds((part["tap"] + i - k) * SUB, SUB), :] * held[i]
                    pd[rows[k], :] = total
                ways = [across[row, :] for row in rows]
                for tap in range(side):
                    total = held[tap] * ways[0]
                    for k in range(1, side - tap):
                        total = total + held[k + tap] * ways[k]
                    height_sums[pl.ds((part["tap"] + tap) * SUB, SUB), :] += total
                return inner

            lax.fori_loop(0, pitch // SUB, column, 0)
            return carry

        lax.fori_loop(0, part["groups"], group, 0)
    for part in plan.sections:
        side, pitch = part["side"], part["pitch"]
        area = side * pitch

        def group(t, carry, part=part, side=side, pitch=pitch, area=area):
            start = part["packed_row"] + t * area

            def line(i, sums):
                sums = list(sums)
                base = start + i * pitch
                aligned = pl.multiple_of(base, SUB)
                for j in range(0, pitch, SUB):
                    here = pl.ds(pl.multiple_of(aligned + j, SUB), SUB)
                    mine, grad = packed[here, :], pg[here, :]
                    total = skips * grad
                    sums[side] = sums[side] + mine * grad
                    for tap in range(min(side, side - j)):
                        moved = pd[pl.ds(base + j + tap, SUB), :]
                        if j + SUB - 1 + tap >= pitch:
                            moved = jnp.where(place + (j + tap) < side, moved, 0.0)
                        total = total + width_wide[pl.ds((part["tap"] + tap) * SUB, SUB), :] * moved
                        sums[tap] = sums[tap] + mine * moved
                    out[here, :] = total
                return tuple(sums)

            return lax.fori_loop(0, side, line, carry)

        zero = jnp.zeros((SUB, LANES), F32)
        sums = lax.fori_loop(0, part["groups"], group, (zero,) * (side + 1))
        for tap in range(side):
            width_sums[pl.ds((part["tap"] + tap) * SUB, SUB), :] = sums[tap]
        skip_sums[...] += sums[side]


def whole(memory):
    return pl.BlockSpec(memory_space=memory)


def lanes_of(rows):
    return jax.ShapeDtypeStruct((rows, LANES), F32)


def row_buffers(plan):
    return [pltpu.VMEM((plan.row_pad, LANES), F32)] * 2 + [pltpu.VMEM((plan.image_rows, LANES), F32)]


def kernel_call(kernel, name, micros, memories, out_shape, scratch, args, after=()):
    outs = jax.tree.map(lambda _: whole(pltpu.VMEM), out_shape)
    return pl.pallas_call(
        kernel,
        out_shape=out_shape,
        in_specs=[whole(m) for m in memories] + [whole(pl.ANY)] * len(after),
        out_specs=outs,
        scratch_shapes=scratch,
        compiler_params=pltpu.CompilerParams(vmem_limit_bytes=VMEM),
        cost_estimate=pl.CostEstimate(flops=1_000_000, bytes_accessed=int(3_690_000 * micros), transcendentals=0),
        name=name,
    )(*args, *after)


def mixer_forward(plan, where, block, spread, height, width, skip):
    rows = plan.packed_rows
    scratch = row_buffers(plan) + [
        pltpu.VMEM((rows + MARGIN, LANES), F32),
        pltpu.VMEM((rows + MARGIN, LANES), F32),
        pltpu.VMEM((TAPS * SUB, LANES), F32),
        pltpu.VMEM((plan.mask_rows, LANES), F32),
    ]
    outs = (jax.ShapeDtypeStruct(block.shape, BF16), lanes_of(rows), lanes_of(rows))
    memories = [pltpu.SMEM] + [pltpu.VMEM] * 5
    args = (where, block, spread, height, width, skip)
    return kernel_call(functools.partial(forward_kernel, plan), "mixer_forward", 33, memories, outs, scratch, args)


def mixer_arrive(plan, where, block, spread, after):
    return kernel_call(
        functools.partial(arrive_kernel, plan), "mixer_arrive", 15, [pltpu.SMEM] + [pltpu.VMEM] * 2, lanes_of(plan.packed_rows), row_buffers(plan), (where, block, spread), after
    )


def mixer_backward(plan, grads, height, width, skip, packed, across, after):
    scratch = [
        pltpu.VMEM((plan.packed_rows + MARGIN, LANES), F32),
        pltpu.VMEM((TAPS * SUB, LANES), F32),
        pltpu.VMEM((TAPS * SUB, LANES), F32),
    ]
    outs = (lanes_of(plan.packed_rows), lanes_of(TAPS * SUB), lanes_of(TAPS * SUB), lanes_of(SUB))
    args = (grads, height, width, skip, packed, across)
    return kernel_call(functools.partial(backward_kernel, plan), "mixer_backward", 8, [pltpu.VMEM] * 6, outs, scratch, args, after)


def mixer_leave(plan, where, grads, spread, extra, after):
    out = jax.ShapeDtypeStruct((plan.devices, plan.channels, plan.row_pad), BF16)
    return kernel_call(
        functools.partial(leave_kernel, plan), "mixer_leave", 13, [pltpu.SMEM] + [pltpu.VMEM] * 3, out, row_buffers(plan), (where, grads, spread, extra), after
    )


def taps_kernel(plan, coef_height, rate_height, coef_width, rate_width, spread, height_sums, width_sums, skip_sums, *outs):
    reach, scale = tap_places()
    fold = lambda sums: lax.dot_general(spread[...], sums, (((1,), (1,)), ((), ())), precision=lax.Precision.HIGHEST, preferred_element_type=F32)
    for coef, log_rate, sums, coef_out, rate_out in (
        (coef_height, rate_height, height_sums, outs[0], outs[1]),
        (coef_width, rate_width, width_sums, outs[2], outs[3]),
    ):
        grads = fold(sums[...].reshape(TAPS, SUB, LANES).sum(axis=1))
        rate = jnp.exp(log_rate[...])
        plain, moved = jnp.zeros_like(rate), jnp.zeros_like(rate)
        for tap in range(TAPS):
            weighted = (grads[:, tap : tap + 1] * float(scale[tap])) * jnp.exp(rate * float(-reach[tap]))
            plain = plain + weighted
            moved = moved + weighted * float(reach[tap])
        coef_out[...] = plain
        rate_out[...] = -coef[...] * rate * moved
    outs[4][...] = fold(skip_sums[...])


def tap_grads(plan, coefs, spread, sums, after):
    shape = jax.ShapeDtypeStruct(coefs[0].shape, F32)
    outs = (shape,) * 4 + (jax.ShapeDtypeStruct((plan.channels, SUB), F32),)
    *grads, skips = kernel_call(functools.partial(taps_kernel, plan), "tap_grads", 1, [pltpu.VMEM] * 8, outs, [], (*coefs, spread, *sums), after)
    return *grads, skips.sum(axis=1)


def tokens_kernel(plan, blocks, out_grad, out, shares, flipped):
    total = jnp.zeros(shares.shape, F32)
    for s in range(plan.devices):
        block = blocks[s].astype(F32)
        flipped[pl.ds(s * plan.channels, plan.channels), :] = block[:, : plan.rows]
        total = total + block[:, plan.row_pad - LANES :]
    shares[...] = total
    out[...] = out_grad[...].astype(F32) + flipped[...].T


def token_grads(plan, blocks, out_grad):
    outs = (jax.ShapeDtypeStruct(out_grad.shape, F32), jax.ShapeDtypeStruct((plan.channels, LANES), F32))
    grads, shares = kernel_call(
        functools.partial(tokens_kernel, plan), "token_grads", 3, [pltpu.VMEM] * 2, outs, [pltpu.VMEM(out_grad.shape[::-1], F32)], (blocks, out_grad)
    )
    first = plan.extra_row - (plan.row_pad - LANES)
    return grads, (shares[:, first : first + SUB] + shares[:, first + SUB : first + 2 * SUB]).T


def out_kernel(plan, own, act, scaled, keep, send):
    height = keep.shape[1]
    total = lax.dot_general(act[...], scaled[...], (((0,), (0,)), ((), ())), preferred_element_type=F32).astype(BF16)
    for chip in range(keep.shape[0]):
        first = total[2 * chip * height : (2 * chip + 1) * height]
        second = total[(2 * chip + 1) * height : (2 * chip + 2) * height]
        keep[chip] = jnp.where(own[0] == 0, first, second)
        send[chip] = jnp.where(own[0] == 0, second, first)


def in_kernel(plan, own, flipped, grad_pre, keep, send):
    height = keep.shape[1]
    total = jnp.dot(flipped[...], grad_pre[...], preferred_element_type=F32)
    for chip in range(keep.shape[0]):
        first = total[2 * chip * height : (2 * chip + 1) * height]
        second = total[(2 * chip + 1) * height : (2 * chip + 2) * height]
        keep[chip] = jnp.where(own[0] == 0, first, second).astype(BF16)
        send[chip] = jnp.where(own[0] == 0, second, first).astype(BF16)


def small_call(kernel, name, grid, in_specs, out_specs, out_shape, args, scalars):
    return pl.pallas_call(
        kernel,
        grid_spec=pltpu.PrefetchScalarGridSpec(num_scalar_prefetch=1, grid=grid, in_specs=in_specs, out_specs=out_specs),
        out_shape=out_shape,
        compiler_params=pltpu.CompilerParams(vmem_limit_bytes=VMEM),
        cost_estimate=pl.CostEstimate(flops=1000, bytes_accessed=1000, transcendentals=0),
        name=name,
    )(scalars, *args)


def weight_out_halves(plan, own, act, scaled):
    rows, hidden = act.shape
    width, chips = scaled.shape[1], plan.devices // 2
    height = hidden // plan.devices
    group = 2
    tile = 2 * group * height
    half = jax.ShapeDtypeStruct((chips, height, width), BF16)
    out = pl.BlockSpec((group, height, width), lambda i, own: (i, 0, 0))
    return small_call(
        functools.partial(out_kernel, plan), "weight_out_halves", (hidden // tile,),
        [pl.BlockSpec((rows, tile), lambda i, own: (0, i)), pl.BlockSpec((rows, width), lambda i, own: (0, 0))],
        (out, out), (half, half), (act, scaled), own,
    )


def weight_in_halves(plan, own, flipped, grad_pre):
    width, rows = flipped.shape
    hidden, chips = grad_pre.shape[1], plan.devices // 2
    tile = 3 * LANES
    half = jax.ShapeDtypeStruct((chips, plan.channels, hidden), BF16)
    out = pl.BlockSpec((chips, plan.channels, tile), lambda i, own: (0, 0, i))
    return small_call(
        functools.partial(in_kernel, plan), "weight_in_halves", (hidden // tile,),
        [pl.BlockSpec((width, rows), lambda i, own: (0, 0)), pl.BlockSpec((rows, tile), lambda i, own: (0, i))],
        (out, out), (half, half), (flipped, grad_pre), own,
    )


def merge_kernel(own, keep_mine, got_mine, keep_other, got_other, keep, send):
    keep[...] = (keep_mine[...].astype(F32) + got_mine[...].astype(F32)).astype(BF16)
    send[...] = (keep_other[...].astype(F32) + got_other[...].astype(F32)).astype(BF16)


def merge(keep, got, at, own):
    count = keep.shape[0] // 2
    low = (1 << at) - 1
    entry = lambda e, bit: ((e >> at) << at + 1) + (bit << at) + (e & low)
    shape = (1,) + keep.shape[1:]
    mine = pl.BlockSpec(shape, lambda e, own: (entry(e, own[0]), 0, 0))
    other = pl.BlockSpec(shape, lambda e, own: (entry(e, 1 - own[0]), 0, 0))
    out = pl.BlockSpec(shape, lambda e, own: (e, 0, 0))
    half = jax.ShapeDtypeStruct((count,) + keep.shape[1:], BF16)
    return small_call(merge_kernel, "merge_halves", (count,), [mine, mine, other, other], (out, out), (half, half), (keep, got, keep, got), own)


def tap_places():
    reach = np.concatenate([np.arange(s) / s for s in SIDES]).astype(np.float32)
    scale = np.concatenate([np.full(s, 1.0 / math.sqrt(s)) for s in SIDES]).astype(np.float32)
    return reach, scale


def profiles(coefficient, log_rate):
    reach, scale = tap_places()
    decayed = jnp.exp(-jnp.exp(log_rate)[None] * reach[:, None, None])
    return jnp.sum(coefficient[None] * decayed, axis=2) * scale[:, None]


def profile_grads(coefficient, log_rate, grads):
    reach, scale = tap_places()
    rate = jnp.exp(log_rate)
    decayed = jnp.exp(-rate[None] * reach[:, None, None])
    weighted = (grads * scale[:, None])[:, :, None] * decayed
    return jnp.sum(weighted, axis=0), -coefficient * rate * jnp.sum(weighted * reach[:, None, None], axis=0)


def kernel_matrix(profile, part):
    side = part["side"]
    offsets = np.arange(side)[:, None] - np.arange(side)[None, :]
    picked = profile[part["tap"] + np.maximum(offsets, 0)]
    return jnp.where((offsets >= 0)[:, :, None], picked, 0.0)


def mix_plain(plan, row_pixel, channel_rows, height, width, skip):
    def one_channel(given):
        values, high, wide, weight = given
        image_order = jnp.zeros_like(values).at[row_pixel].set(values)
        pieces = []
        for part in plan.sections:
            side, count = part["side"], part["images"] * part["side"] ** 2
            block = image_order[part["pixel"] : part["pixel"] + count].reshape(-1, side, side)
            left = kernel_matrix(high[:, None], part)[:, :, 0]
            right = kernel_matrix(wide[:, None], part)[:, :, 0]
            mixed = jnp.einsum("ik,nkl,jl->nij", left, block, right, precision=lax.Precision.HIGHEST)
            pieces.append(mixed.reshape(-1))
        joined = jnp.concatenate(pieces) + weight * image_order
        return joined[row_pixel]

    return lax.map(jax.checkpoint(one_channel), (channel_rows, height.T, width.T, skip))


def exchange(blocks):
    return lax.all_to_all(blocks, "chan", 0, 0, tiled=True)


def to_blocks(rows, devices):
    return rows.T.reshape(devices, rows.shape[1] // devices, rows.shape[0])


def to_rows(blocks):
    return blocks.reshape(-1, blocks.shape[2]).T


def feed_kernel(plan, blocks, gain, bias, weight_in, bias_in, grad_act, grads, flipped, act, grad_pre, gain_sum, bias_sum, pre_sum, normed, unit, inverse, total):
    step, channels, count = pl.program_id(0), plan.channels, plan.devices
    width = channels * count

    @pl.when(step == 0)
    def _():
        for s in range(count):
            unit[pl.ds(s * channels, channels), :] = blocks[s].astype(F32)
        mean = jnp.sum(unit[...], axis=0, keepdims=True) * (1.0 / width)
        centred = unit[...] - mean
        scale = lax.rsqrt(jnp.sum(centred * centred, axis=0, keepdims=True) * (1.0 / width) + EPSILON)
        inverse[...] = scale
        unit[...] = centred * scale
        scaled = unit[...] * gain[...] + bias[...]
        flipped[...] = scaled.astype(BF16)
        normed[...] = scaled.T.astype(BF16)
        total[...] = jnp.zeros_like(total)

    tile = 256
    for c in range(0, weight_in.shape[1], tile):
        at = pl.ds(c, tile)
        pre = jnp.dot(normed[...], weight_in[:, at], preferred_element_type=F32) + bias_in[:, at]
        cdf = 0.5 * (1.0 + lax.erf(pre * math.sqrt(0.5)))
        act[:, at] = (pre * cdf).astype(BF16)
        slope = cdf + pre * jnp.exp(-0.5 * pre * pre) * (1.0 / math.sqrt(2.0 * math.pi))
        grad = grad_act[:, at] * slope
        pre_sum[:, at] = jnp.sum(grad, axis=0, keepdims=True)
        low = grad.astype(BF16)
        grad_pre[:, at] = low
        total[...] += lax.dot_general(low, weight_in[:, at], (((1,), (1,)), ((), ())), preferred_element_type=F32)

    @pl.when(step == pl.num_programs(0) - 1)
    def _():
        turned = total[...].T
        gain_sum[...] = jnp.sum(turned * unit[...], axis=1, keepdims=True)
        bias_sum[...] = jnp.sum(turned, axis=1, keepdims=True)
        grad = turned * gain[...]
        level = jnp.sum(grad, axis=0, keepdims=True) * (1.0 / width)
        tilt = jnp.sum(grad * unit[...], axis=0, keepdims=True) * (1.0 / width)
        total_low = (inverse[...] * (grad - level - unit[...] * tilt)).astype(BF16)
        for s in range(count):
            grads[s] = total_low[s * channels : (s + 1) * channels]


def feed(plan, blocks, gain, bias, weight_in, bias_in, grad_act):
    rows, width, hidden = plan.rows, plan.devices * plan.channels, weight_in.shape[1]
    steps = 4
    part = hidden // steps
    same = lambda *shape: pl.BlockSpec(shape, lambda i: (0,) * len(shape))
    across = lambda height: pl.BlockSpec((height, part), lambda i: (0, i))
    shape = jax.ShapeDtypeStruct
    return pl.pallas_call(
        functools.partial(feed_kernel, plan),
        grid=(steps,),
        out_shape=(
            shape(blocks.shape, BF16),
            shape((width, rows), BF16),
            shape((rows, hidden), BF16),
            shape((rows, hidden), BF16),
            shape((width, 1), F32),
            shape((width, 1), F32),
            shape((1, hidden), F32),
        ),
        in_specs=[same(*blocks.shape), same(width, 1), same(width, 1), across(width), across(1), across(rows)],
        out_specs=(same(*blocks.shape), same(width, rows), across(rows), across(rows), same(width, 1), same(width, 1), across(1)),
        scratch_shapes=[pltpu.VMEM((rows, width), BF16), pltpu.VMEM((width, rows), F32), pltpu.VMEM((1, rows), F32), pltpu.VMEM((rows, width), F32)],
        compiler_params=pltpu.CompilerParams(vmem_limit_bytes=VMEM),
        cost_estimate=pl.CostEstimate(flops=1_000_000, bytes_accessed=40_000_000, transcendentals=0),
        name="feed_forward",
    )(blocks, gain[:, None], bias[:, None], weight_in, bias_in[None], grad_act)


def halve(blocks, bits):
    myself = lax.axis_index("chan")
    size = lax.axis_size("chan")
    pairs = lambda bit: [(i, i ^ 1 << bit) for i in range(size)]
    left = list(range(size.bit_length() - 1))
    for bit in bits:
        at = left.index(bit)
        viewed = blocks.reshape((-1, 2, 1 << at) + blocks.shape[1:])
        own = myself >> bit & 1
        keep = lax.dynamic_index_in_dim(viewed, own, 1, keepdims=False)
        send = lax.dynamic_index_in_dim(viewed, 1 - own, 1, keepdims=False)
        got = lax.ppermute(send, "chan", pairs(bit))
        total = keep.astype(F32) + got.astype(F32)
        left.remove(bit)
        blocks = (total if not left else total.astype(BF16)).reshape((-1,) + blocks.shape[1:])
    return blocks[0]


def swapped(x, bit):
    return lax.ppermute(x, "chan", [(i, i ^ 1 << bit) for i in range(lax.axis_size("chan"))])


def body_fast(
    tokens,
    row_pixel,
    coef_height,
    rate_height,
    coef_width,
    rate_width,
    skip_weight,
    norm_gain,
    norm_bias,
    weight_in,
    bias_in,
    weight_out,
    bias_out,
    layer_scale,
    out_grad,
):
    devices = lax.axis_size("chan")
    rows, width_all = tokens.shape
    plan = Plan(devices, rows, width_all // devices)
    token_blocks = exchange(to_blocks(tokens, devices))
    here = lax.axis_index("chan")
    own = [(here >> bit & 1).reshape(1) for bit in range(devices.bit_length() - 1)]

    where = plan.address(row_pixel)
    spread = plan.spread()
    taps = (plan.tile_taps(profiles(coef_height, rate_height)), plan.tile_taps(profiles(coef_width, rate_width)), plan.tile_taps(skip_weight[None]))
    mixed_blocks, packed, across = mixer_forward(plan, where, token_blocks, spread, *taps)

    upstream = out_grad.astype(F32)
    scaled = upstream * layer_scale
    scaled_low = scaled.astype(BF16)
    grad_act = lax.dot_general(scaled_low, weight_out, (((1,), (1,)), ((), ())), preferred_element_type=F32)
    grad_normin, flipped, act_low, grad_pre_low, gain_sum, norm_bias_sum, bias_in_sum = feed(
        plan, exchange(mixed_blocks), norm_gain, norm_bias, weight_in, bias_in, grad_act
    )
    grad_blocks = exchange(grad_normin)

    out_keep, out_send = weight_out_halves(plan, own[0], act_low, scaled_low)
    out_got = swapped(out_send, 0)
    in_keep, in_send = weight_in_halves(plan, own[0], flipped, grad_pre_low)
    in_got = swapped(in_send, 0)
    branch = jnp.dot(act_low, weight_out, preferred_element_type=F32) + bias_out
    block_out = (tokens.astype(F32) + layer_scale * branch).astype(BF16)
    small = (gain_sum, norm_bias_sum, bias_in_sum, jnp.sum(scaled, axis=0), jnp.sum(upstream * branch, axis=0))
    shares = jnp.concatenate([part.reshape(devices, -1, plan.channels) for part in small], axis=1)
    shares = jnp.pad(shares, ((0, 0), (0, 0), (0, LANES - plan.channels)))

    left = list(range(1, devices.bit_length() - 1))
    in_order = left
    out_order = left[:2][::-1] + left[2:]

    def halve(keep, got, order, step):
        bit = order[step]
        at = sorted(order[step:]).index(bit)
        keep, send = merge(keep, got, at, own[bit])
        return keep, send, swapped(send, bit)

    out_keep, out_send, out_got = halve(out_keep, out_got, out_order, 0)
    in_keep, in_send, in_got = halve(in_keep, in_got, in_order, 0)
    grads = mixer_arrive(plan, where, grad_blocks, spread, (out_send, in_send, shares))
    grads, *sums = mixer_backward(plan, grads, *taps, packed, across, ())
    out_keep, out_send, out_got = halve(out_keep, out_got, out_order, 1)
    in_keep, in_send, in_got = halve(in_keep, in_got, in_order, 1)
    leaving = exchange(mixer_leave(plan, where, grads, spread, shares, (out_send, in_send)))
    coefs = (coef_height, rate_height, coef_width, rate_width)
    coef_grads = tap_grads(plan, coefs, spread.astype(F32), sums, ())
    for step in range(2, len(left)):
        out_keep, out_send, out_got = halve(out_keep, out_got, out_order, step)
        in_keep, in_send, in_got = halve(in_keep, in_got, in_order, step)
    out_sum = out_keep[0].astype(F32) + out_got[0].astype(F32)
    in_sum = in_keep[0].astype(F32) + in_got[0].astype(F32)
    grad_tokens, shares = token_grads(plan, leaving, out_grad)
    shares = shares.reshape(-1)
    cuts = np.cumsum([part.size // devices for part in small])[:-1]
    gain_grad, norm_bias_grad, bias_in_grad, bias_out_grad, scale_grad = jnp.split(shares, cuts)
    return (block_out, grad_tokens, *coef_grads, gain_grad, norm_bias_grad, in_sum, bias_in_grad, out_sum, bias_out_grad, scale_grad)


def body_plain(
    tokens,
    row_pixel,
    coef_height,
    rate_height,
    coef_width,
    rate_width,
    skip_weight,
    norm_gain,
    norm_bias,
    weight_in,
    bias_in,
    weight_out,
    bias_out,
    layer_scale,
    out_grad,
):
    devices = lax.axis_size("chan")
    rows, width_all = tokens.shape
    plan = Plan(devices, rows, width_all // devices)
    token_blocks = exchange(to_blocks(tokens, devices))

    height = profiles(coef_height, rate_height)
    width = profiles(coef_width, rate_width)
    lines = lambda blocks: blocks.transpose(1, 0, 2).reshape(blocks.shape[1], -1)
    blocks_of = lambda values: values.astype(BF16).reshape(-1, devices, rows).transpose(1, 0, 2)
    mixed, mixer_back = jax.vjp(
        functools.partial(mix_plain, plan, row_pixel), lines(token_blocks).astype(F32), height, width, skip_weight
    )
    mixed_blocks = blocks_of(mixed)
    normin = to_rows(exchange(mixed_blocks)).astype(F32)

    upstream = out_grad.astype(F32)
    scaled = upstream * layer_scale
    scaled_low = scaled.astype(BF16)
    grad_act = lax.dot_general(scaled_low, weight_out, (((1,), (1,)), ((), ())), preferred_element_type=F32)

    row_mean = jnp.mean(normin, axis=1, keepdims=True)
    centred = normin - row_mean
    inv_std = lax.rsqrt(jnp.mean(centred * centred, axis=1, keepdims=True) + EPSILON)
    unit_rows = centred * inv_std
    normed = (unit_rows * norm_gain + norm_bias).astype(BF16)
    hidden_pre = jnp.dot(normed, weight_in, preferred_element_type=F32) + bias_in
    cdf = 0.5 * (1.0 + lax.erf(hidden_pre * math.sqrt(0.5)))
    act_low = (hidden_pre * cdf).astype(BF16)
    slope = cdf + hidden_pre * jnp.exp(-0.5 * hidden_pre * hidden_pre) * (1.0 / math.sqrt(2.0 * math.pi))
    grad_pre = grad_act * slope
    grad_pre_low = grad_pre.astype(BF16)
    grad_normed = lax.dot_general(grad_pre_low, weight_in, (((1,), (1,)), ((), ())), preferred_element_type=F32)
    grad_unit = grad_normed * norm_gain
    grad_normin = inv_std * (
        grad_unit
        - jnp.mean(grad_unit, axis=1, keepdims=True)
        - unit_rows * jnp.mean(grad_unit * unit_rows, axis=1, keepdims=True)
    )
    grad_blocks = exchange(to_blocks(grad_normin.astype(BF16), devices))

    branch = jnp.dot(act_low, weight_out, preferred_element_type=F32) + bias_out
    block_out = (tokens.astype(F32) + layer_scale * branch).astype(BF16)
    small = (
        jnp.sum(grad_normed * unit_rows, axis=0),
        jnp.sum(grad_normed, axis=0),
        jnp.sum(grad_pre, axis=0),
        jnp.sum(scaled, axis=0),
        jnp.sum(upstream * branch, axis=0),
    )
    weight_in_part = lax.dot_general(normed, grad_pre_low, (((0,), (0,)), ((), ())), preferred_element_type=F32)
    weight_out_part = lax.dot_general(act_low, scaled_low, (((0,), (0,)), ((), ())), preferred_element_type=F32)

    grad_mixed, grad_height, grad_width, grad_skip = mixer_back(lines(grad_blocks).astype(F32))
    grad_rows = blocks_of(grad_mixed)
    coef_height_grad, rate_height_grad = profile_grads(coef_height, rate_height, grad_height)
    coef_width_grad, rate_width_grad = profile_grads(coef_width, rate_width, grad_width)
    grad_tokens = upstream + to_rows(exchange(grad_rows)).astype(F32)

    levels = list(range(devices.bit_length() - 1))
    other = levels[:1] + levels[1:3][::-1] + levels[3:]
    in_sum = halve(weight_in_part.astype(BF16).reshape(devices, -1, weight_in.shape[1]), levels)
    out_sum = halve(weight_out_part.astype(BF16).reshape(devices, -1, weight_out.shape[1]), other)
    shares = jnp.concatenate([s.reshape(devices, -1) for s in small], axis=1)
    shares = exchange(shares).sum(axis=0)
    cuts = np.cumsum([s.shape[0] // devices for s in small])[:-1]
    gain_grad, norm_bias_grad, bias_in_grad, bias_out_grad, scale_grad = jnp.split(shares, cuts)
    return (
        block_out,
        grad_tokens,
        coef_height_grad,
        rate_height_grad,
        coef_width_grad,
        rate_width_grad,
        grad_skip,
        gain_grad,
        norm_bias_grad,
        in_sum,
        bias_in_grad,
        out_sum,
        bias_out_grad,
        scale_grad,
    )


def solution(mesh):
    split, copied = P("chan"), P()

    def body(tokens, *rest):
        devices = lax.axis_size("chan")
        fast = Plan(devices, tokens.shape[0], tokens.shape[1] // devices).fits() and devices >= 16
        return (body_fast if fast else body_plain)(tokens, *rest)

    in_specs = (split, copied) + (split,) * 5 + (copied,) * 7 + (split,)
    return jax.shard_map(body, mesh=mesh, in_specs=in_specs, out_specs=(split,) * 14, check_vma=False)
```

```python
import functools
import math

import jax
import jax.numpy as jnp
import numpy as np
from jax import lax
from jax.experimental import pallas as pl
from jax.experimental.pallas import tpu as pltpu
from jax.sharding import PartitionSpec as P

SIDES = (10, 14, 18)
SHARES = (1, 1, 2)
UNIT = sum(m * s * s for s, m in zip(SIDES, SHARES))
TAPS = sum(SIDES)
EPSILON = 1e-06
LANES = 128
SUB = 8
MARGIN = 32
VMEM = 56 * 2**20
LESS = 36 * 2**20
F32 = jnp.float32
BF16 = jnp.bfloat16


class Plan:
    def __init__(self, devices, rows, channels):
        self.devices, self.rows, self.channels = devices, rows, channels
        self.pixels = devices * rows
        self.units = self.pixels // UNIT
        self.slots = LANES // channels
        self.row_pad = -(-rows // LANES) * LANES
        self.extra_row = -(-rows // SUB) * SUB
        self.sections = []
        image_row, packed_row, tap, mask_row, pixel = 0, 0, 0, 0, 0
        for side, share in zip(SIDES, SHARES):
            images = share * self.units
            pitch = -(-side // SUB) * SUB
            groups = -(-images // self.slots)
            self.sections.append(
                dict(side=side, images=images, pitch=pitch, groups=groups, image_row=image_row, packed_row=packed_row, tap=tap, mask_row=mask_row, pixel=pixel)
            )
            image_row += groups * self.slots * side * pitch
            packed_row += groups * side * pitch
            tap += side
            mask_row += side * pitch
            pixel += images * side * side
        self.image_rows = image_row
        self.packed_rows = packed_row
        self.mask_rows = mask_row

    def fits(self):
        room = self.row_pad - self.extra_row >= 2 * SUB
        return room and self.channels % SUB == 0 and 4 * LANES * (self.image_rows + 2 * self.row_pad + 5 * self.packed_rows) < 40 * 2**20

    def address(self, row_pixel):
        where = jnp.zeros_like(row_pixel)
        for part in self.sections:
            local = row_pixel - part["pixel"]
            line = local // part["side"]
            spot = part["image_row"] + line * part["pitch"] + local - line * part["side"]
            where = jnp.where(local >= 0, spot, where)
        return where

    def spread(self):
        lane = np.arange(LANES)
        held = (lane[None, :] % self.channels == np.arange(self.channels)[:, None]) & (lane[None, :] < self.slots * self.channels)
        return jnp.asarray(held.astype(np.float32), BF16)

    def tile_taps(self, taps):
        tiled = jnp.tile(taps, (1, self.slots))
        return jnp.pad(tiled, ((0, 0), (0, LANES - tiled.shape[1])))


def slot_masks(plan):
    lane = lax.broadcasted_iota(jnp.int32, (SUB, LANES), 1)
    return [(lane >= q * plan.channels) & (lane < (q + 1) * plan.channels) for q in range(plan.slots)]


def in_turn(plan, first, second):
    first(0, 0)

    def pair(k, carry):
        first(2 * k + 1, 1)
        second(2 * k, 0)
        first(2 * k + 2, 0)
        second(2 * k + 1, 1)
        return carry

    lax.fori_loop(0, plan.devices // 2 - 1, pair, 0)
    first(plan.devices - 1, 1)
    second(plan.devices - 2, 0)
    second(plan.devices - 1, 1)


def scatter_rows(plan, where, block, spread, buffers, image):
    def turn(s, held):
        rows = lax.dot_general(block[s], spread[...], (((0,), (0,)), ((), ())), preferred_element_type=F32)
        buffers[held][pl.ds(0, plan.rows), :] = rows

    def place(s, held):
        base = s * plan.rows
        for u in range(plan.rows):
            image[pl.ds(where[base + u], 1), :] = buffers[held][pl.ds(u, 1), :]

    in_turn(plan, turn, place)


def gather_rows(plan, where, spread, buffers, image, out, extra=None):
    used = plan.rows if extra is None else plan.row_pad

    def fetch(s, held):
        base = s * plan.rows
        for u in range(plan.rows):
            buffers[held][pl.ds(u, 1), :] = image[pl.ds(where[base + u], 1), :]

    def fold(s, held):
        if extra is not None:
            high = extra[s].astype(BF16).astype(F32)
            buffers[held][pl.ds(plan.extra_row, SUB), :] = high
            buffers[held][pl.ds(plan.extra_row + SUB, SUB), :] = extra[s] - high
        rows = buffers[held][pl.ds(0, used), :].astype(BF16)
        folded = lax.dot_general(spread[...], rows, (((1,), (1,)), ((), ())), preferred_element_type=F32)
        out[s] = folded.astype(BF16)

    in_turn(plan, fetch, fold)


def pack_images(plan, masks, image, packed, margin):
    place = lax.broadcasted_iota(jnp.int32, (SUB, LANES), 0)
    for part in plan.sections:
        side, pitch = part["side"], part["pitch"]
        area = side * pitch

        def group(t, carry, part=part, side=side, pitch=pitch, area=area):
            start = part["image_row"] + t * (plan.slots * area)
            target = margin + part["packed_row"] + t * area

            def line(i, inner):
                for j in range(0, pitch, SUB):
                    value = jnp.zeros((SUB, LANES), F32)
                    for q in range(plan.slots):
                        row = pl.multiple_of(start + q * area + i * pitch + j, SUB)
                        here = masks[q] & (t * plan.slots + q < part["images"])
                        if j + SUB > side:
                            here = here & (place + j < side)
                        value = jnp.where(here, image[pl.ds(row, SUB), :], value)
                    packed[pl.ds(pl.multiple_of(target + i * pitch + j, SUB), SUB), :] = value
                return inner

            return lax.fori_loop(0, side, line, carry, unroll=2)

        lax.fori_loop(0, part["groups"], group, 0)


def unpack_line(plan, masks, part, t, offset, value, image):
    area = part["side"] * part["pitch"]
    for q in range(plan.slots):
        row = pl.multiple_of(part["image_row"] + (t * plan.slots + q) * area + offset, SUB)
        image[pl.ds(row, SUB), :] = jnp.where(masks[q], value, 0.0)


def wide_taps(plan, taps, table):
    for tap in range(TAPS):
        table[pl.ds(tap * SUB, SUB), :] = jnp.broadcast_to(taps[pl.ds(tap, 1), :], (SUB, LANES))


def masked_taps(plan, taps, table):
    for part in plan.sections:
        side, pitch = part["side"], part["pitch"]
        place = lax.broadcasted_iota(jnp.int32, (pitch, LANES), 0)
        for tap in range(side):
            row = taps[pl.ds(part["tap"] + tap, 1), :]
            table[pl.ds(part["mask_row"] + tap * pitch, pitch), :] = jnp.where(place >= tap, row, 0.0)


def forward_kernel(plan, where, block, spread, height, width, skip, out, packed, across, near, far, image, px, pu, height_wide, width_masked):
    masks = slot_masks(plan)
    px[pl.ds(0, MARGIN), :] = jnp.zeros((MARGIN, LANES), F32)
    wide_taps(plan, height, height_wide)
    masked_taps(plan, width, width_masked)
    scatter_rows(plan, where, block, spread, (near, far), image)
    pack_images(plan, masks, image, px, MARGIN)
    skips = jnp.broadcast_to(skip[...], (SUB, LANES))
    for part in plan.sections:
        side, pitch = part["side"], part["pitch"]
        area = side * pitch

        def group(t, carry, part=part, side=side, pitch=pitch, area=area):
            start = MARGIN + part["packed_row"] + t * area

            def line(i, inner):
                base = start + i * pitch
                for j in range(0, pitch, SUB):
                    total = jnp.zeros((SUB, LANES), F32)
                    for tap in range(min(side, j + SUB)):
                        weight = width_masked[pl.ds(part["mask_row"] + tap * pitch + j, SUB), :]
                        total = total + weight * px[pl.ds(base + j - tap, SUB), :]
                    pu[pl.ds(pl.multiple_of(base + j, SUB), SUB), :] = total
                return inner

            lax.fori_loop(0, side, line, 0)

            def column(c, inner):
                first = pl.multiple_of(start + c * SUB, SUB)
                held = [pu[pl.ds(pl.multiple_of(first + k * pitch, SUB), SUB), :] for k in range(side)]
                for i in range(side):
                    total = skips * px[pl.ds(pl.multiple_of(first + i * pitch, SUB), SUB), :]
                    for k in range(i + 1):
                        total = total + height_wide[pl.ds((part["tap"] + i - k) * SUB, SUB), :] * held[k]
                    unpack_line(plan, masks, part, t, i * pitch + c * SUB, total, image)
                return inner

            lax.fori_loop(0, pitch // SUB, column, 0)
            return carry

        lax.fori_loop(0, part["groups"], group, 0)
    packed[...] = px[pl.ds(MARGIN, plan.packed_rows), :]
    across[...] = pu[pl.ds(MARGIN, plan.packed_rows), :]
    gather_rows(plan, where, spread, (near, far), image, out)


def arrive_kernel(plan, where, block, spread, *rest):
    grads, near, far, image = rest[-4:]
    scatter_rows(plan, where, block, spread, (near, far), image)
    pack_images(plan, slot_masks(plan), image, grads, 0)


def leave_kernel(plan, where, grads, spread, extra, *rest):
    out, near, far, image = rest[-4:]
    masks = slot_masks(plan)
    for part in plan.sections:
        area = part["side"] * part["pitch"]

        def group(t, carry, part=part, area=area):
            for offset in range(0, area, SUB):
                row = pl.multiple_of(part["packed_row"] + t * area + offset, SUB)
                unpack_line(plan, masks, part, t, offset, grads[pl.ds(row, SUB), :], image)
            return carry

        lax.fori_loop(0, part["groups"], group, 0)
    gather_rows(plan, where, spread, (near, far), image, out, extra)


def backward_kernel(plan, pg, height, width, skip, packed, across, *rest):
    out, height_sums, width_sums, skip_sums, pd, height_wide, width_wide = rest[-7:]
    place = lax.broadcasted_iota(jnp.int32, (SUB, LANES), 0)
    pd[pl.ds(plan.packed_rows, MARGIN), :] = jnp.zeros((MARGIN, LANES), F32)
    wide_taps(plan, height, height_wide)
    wide_taps(plan, width, width_wide)
    skips = jnp.broadcast_to(skip[...], (SUB, LANES))
    skip_sums[...] = jnp.zeros((SUB, LANES), F32)
    height_sums[...] = jnp.zeros((TAPS * SUB, LANES), F32)
    for part in plan.sections:
        side, pitch = part["side"], part["pitch"]
        area = side * pitch

        def group(t, carry, part=part, side=side, pitch=pitch, area=area):
            start = part["packed_row"] + t * area

            def column(c, inner):
                first = pl.multiple_of(start + c * SUB, SUB)
                rows = [pl.ds(pl.multiple_of(first + k * pitch, SUB), SUB) for k in range(side)]
                held = [pg[row, :] for row in rows]
                for k in range(side):
                    total = jnp.zeros((SUB, LANES), F32)
                    for i in range(k, side):
                        total = total + height_wide[pl.ds((part["tap"] + i - k) * SUB, SUB), :] * held[i]
                    pd[rows[k], :] = total
                ways = [across[row, :] for row in rows]
                for tap in range(side):
                    total = held[tap] * ways[0]
                    for k in range(1, side - tap):
                        total = total + held[k + tap] * ways[k]
                    height_sums[pl.ds((part["tap"] + tap) * SUB, SUB), :] += total
                return inner

            lax.fori_loop(0, pitch // SUB, column, 0)
            return carry

        lax.fori_loop(0, part["groups"], group, 0)
    for part in plan.sections:
        side, pitch = part["side"], part["pitch"]
        area = side * pitch

        def group(t, carry, part=part, side=side, pitch=pitch, area=area):
            start = part["packed_row"] + t * area

            def line(i, sums):
                sums = list(sums)
                base = start + i * pitch
                aligned = pl.multiple_of(base, SUB)
                for j in range(0, pitch, SUB):
                    here = pl.ds(pl.multiple_of(aligned + j, SUB), SUB)
                    mine, grad = packed[here, :], pg[here, :]
                    total = skips * grad
                    sums[side] = sums[side] + mine * grad
                    for tap in range(min(side, side - j)):
                        moved = pd[pl.ds(base + j + tap, SUB), :]
                        if j + SUB - 1 + tap >= pitch:
                            moved = jnp.where(place + (j + tap) < side, moved, 0.0)
                        total = total + width_wide[pl.ds((part["tap"] + tap) * SUB, SUB), :] * moved
                        sums[tap] = sums[tap] + mine * moved
                    out[here, :] = total
                return tuple(sums)

            return lax.fori_loop(0, side, line, carry)

        zero = jnp.zeros((SUB, LANES), F32)
        sums = lax.fori_loop(0, part["groups"], group, (zero,) * (side + 1))
        for tap in range(side):
            width_sums[pl.ds((part["tap"] + tap) * SUB, SUB), :] = sums[tap]
        skip_sums[...] += sums[side]


def whole(memory):
    return pl.BlockSpec(memory_space=memory)


def lanes_of(rows):
    return jax.ShapeDtypeStruct((rows, LANES), F32)


def row_buffers(plan):
    return [pltpu.VMEM((plan.row_pad, LANES), F32)] * 2 + [pltpu.VMEM((plan.image_rows, LANES), F32)]


def near(values):
    return pltpu.with_memory_space_constraint(values, pltpu.VMEM)


def kernel_call(kernel, name, micros, memories, out_shape, scratch, args, after=(), stays=(), held=()):
    outs = jax.tree.map(lambda _: whole(pltpu.VMEM), out_shape)
    if stays:
        out_shape = tuple(pltpu.VMEM(o.shape, o.dtype) if i in stays else o for i, o in enumerate(out_shape))
    args = [near(value) if i in held else value for i, value in enumerate(args)]
    return pl.pallas_call(
        kernel,
        out_shape=out_shape,
        in_specs=[whole(m) for m in memories] + [whole(pl.ANY)] * len(after),
        out_specs=outs,
        scratch_shapes=scratch,
        compiler_params=pltpu.CompilerParams(vmem_limit_bytes=LESS if stays or held else VMEM),
        cost_estimate=pl.CostEstimate(flops=1_000_000, bytes_accessed=int(3_690_000 * micros), transcendentals=0),
        name=name,
    )(*args, *after)


def mixer_forward(plan, where, block, spread, height, width, skip):
    rows = plan.packed_rows
    scratch = row_buffers(plan) + [
        pltpu.VMEM((rows + MARGIN, LANES), F32),
        pltpu.VMEM((rows + MARGIN, LANES), F32),
        pltpu.VMEM((TAPS * SUB, LANES), F32),
        pltpu.VMEM((plan.mask_rows, LANES), F32),
    ]
    outs = (jax.ShapeDtypeStruct(block.shape, BF16), lanes_of(rows), lanes_of(rows))
    memories = [pltpu.SMEM] + [pltpu.VMEM] * 5
    args = (where, block, spread, height, width, skip)
    return kernel_call(functools.partial(forward_kernel, plan), "mixer_forward", 33, memories, outs, scratch, args)


def mixer_arrive(plan, where, block, spread, after):
    return kernel_call(
        functools.partial(arrive_kernel, plan), "mixer_arrive", 15, [pltpu.SMEM] + [pltpu.VMEM] * 2, (lanes_of(plan.packed_rows),), row_buffers(plan), (where, block, spread), after, (0,)
    )[0]


def mixer_backward(plan, grads, height, width, skip, packed, across, after):
    scratch = [
        pltpu.VMEM((plan.packed_rows + MARGIN, LANES), F32),
        pltpu.VMEM((TAPS * SUB, LANES), F32),
        pltpu.VMEM((TAPS * SUB, LANES), F32),
    ]
    outs = (lanes_of(plan.packed_rows), lanes_of(TAPS * SUB), lanes_of(TAPS * SUB), lanes_of(SUB))
    args = (grads, height, width, skip, packed, across)
    return kernel_call(functools.partial(backward_kernel, plan), "mixer_backward", 8, [pltpu.VMEM] * 6, outs, scratch, args, after, (0,), (0,))


def mixer_leave(plan, where, grads, spread, extra, after):
    out = jax.ShapeDtypeStruct((plan.devices, plan.channels, plan.row_pad), BF16)
    return kernel_call(
        functools.partial(leave_kernel, plan), "mixer_leave", 13, [pltpu.SMEM] + [pltpu.VMEM] * 3, out, row_buffers(plan), (where, grads, spread, extra), after, (), (1,)
    )


def taps_kernel(plan, coef_height, rate_height, coef_width, rate_width, spread, height_sums, width_sums, skip_sums, *rest):
    outs = rest[-5:]
    reach, scale = tap_places()
    fold = lambda sums: lax.dot_general(spread[...], sums, (((1,), (1,)), ((), ())), precision=lax.Precision.HIGHEST, preferred_element_type=F32)
    for coef, log_rate, sums, coef_out, rate_out in (
        (coef_height, rate_height, height_sums, outs[0], outs[1]),
        (coef_width, rate_width, width_sums, outs[2], outs[3]),
    ):
        grads = fold(sums[...].reshape(TAPS, SUB, LANES).sum(axis=1))
        rate = jnp.exp(log_rate[...])
        plain, moved = jnp.zeros_like(rate), jnp.zeros_like(rate)
        for tap in range(TAPS):
            weighted = (grads[:, tap : tap + 1] * float(scale[tap])) * jnp.exp(rate * float(-reach[tap]))
            plain = plain + weighted
            moved = moved + weighted * float(reach[tap])
        coef_out[...] = plain
        rate_out[...] = -coef[...] * rate * moved
    outs[4][...] = fold(skip_sums[...])


def tap_grads(plan, coefs, spread, sums, after):
    shape = jax.ShapeDtypeStruct(coefs[0].shape, F32)
    outs = (shape,) * 4 + (jax.ShapeDtypeStruct((plan.channels, SUB), F32),)
    *grads, skips = kernel_call(functools.partial(taps_kernel, plan), "tap_grads", 0.01, [pltpu.VMEM] * 8, outs, [], (*coefs, spread, *sums), after)
    return *grads, skips.sum(axis=1)


def tokens_kernel(plan, blocks, out_grad, out, shares, flipped):
    total = jnp.zeros(shares.shape, F32)
    for s in range(plan.devices):
        block = blocks[s].astype(F32)
        flipped[pl.ds(s * plan.channels, plan.channels), :] = block[:, : plan.rows]
        total = total + block[:, plan.row_pad - LANES :]
    shares[...] = total
    out[...] = out_grad[...].astype(F32) + flipped[...].T


def token_grads(plan, blocks, out_grad):
    outs = (jax.ShapeDtypeStruct(out_grad.shape, F32), jax.ShapeDtypeStruct((plan.channels, LANES), F32))
    grads, shares = kernel_call(
        functools.partial(tokens_kernel, plan), "token_grads", 3, [pltpu.VMEM] * 2, outs, [pltpu.VMEM(out_grad.shape[::-1], F32)], (blocks, out_grad)
    )
    first = plan.extra_row - (plan.row_pad - LANES)
    return grads, (shares[:, first : first + SUB] + shares[:, first + SUB : first + 2 * SUB]).T


def branch_kernel(act, weight_out, bias_out, scale, tokens, out_grad, *rest):
    out, scale_sum = rest[-2:]
    branch = jnp.dot(act[...], weight_out[...], preferred_element_type=F32) + bias_out[...]
    out[...] = (tokens[...].astype(F32) + scale[...] * branch).astype(BF16)
    scale_sum[...] = jnp.sum(out_grad[...].astype(F32) * branch, axis=0, keepdims=True)


def branch_out(act, weight_out, bias_out, scale, tokens, out_grad, after):
    outs = (jax.ShapeDtypeStruct(tokens.shape, BF16), jax.ShapeDtypeStruct((1, tokens.shape[1]), F32))
    return kernel_call(branch_kernel, "branch_out", 0.01, [pltpu.VMEM] * 6, outs, [], (act, weight_out, bias_out[None], scale[None], tokens, out_grad), after)


PIECES = 8


def merge_entries(cut_at, bit, keep, got, mine, other):
    low = (1 << cut_at) - 1
    for e in range(mine.shape[0]):
        at = (e >> cut_at << cut_at + 1) + (e & low)
        pair = [keep[entry] + got[entry] for entry in (at, at + low + 1)]
        mine[e] = jnp.where(bit == 1, pair[1], pair[0])
        other[e] = jnp.where(bit == 1, pair[0], pair[1])


def merge_kernel(cut_at, bits, keep, got, *rest):
    merge_entries(cut_at, bits[1], keep, got, *rest[-2:])


def merge(keep, got, cut_at, bits, after):
    half = jax.ShapeDtypeStruct((keep.shape[0] // 2,) + keep.shape[1:], BF16)
    memories = [pltpu.SMEM] + [pltpu.VMEM] * 2
    return kernel_call(functools.partial(merge_kernel, cut_at), "merge_halves", 0.01, memories, (half, half), [], (bits, keep, got), after, (0, 1), (1,))


def first_merge_kernel(cut_at, pieces, bits, pairs, *rest):
    got, (mine, other, held, came, sems) = rest[:pieces], rest[-5:]
    copies = [pltpu.make_async_copy(pairs.at[:, bits[0]], held, sems.at[pieces])]
    first = 0
    for i, part in enumerate(got):
        copies.append(pltpu.make_async_copy(part, came.at[pl.ds(first, part.shape[0])], sems.at[i]))
        first += part.shape[0]
    for copy in copies:
        copy.start()
    for copy in copies:
        copy.wait()
    merge_entries(cut_at, bits[1], held, came, mine, other)


def first_merge(pairs, got, cut_at, bits, after):
    shape = (pairs.shape[0],) + pairs.shape[2:]
    half = pltpu.VMEM((shape[0] // 2,) + shape[1:], BF16)
    far = [pltpu.with_memory_space_constraint(part, pltpu.HBM) for part in (pairs, *got)]
    return pl.pallas_call(
        functools.partial(first_merge_kernel, cut_at, len(got)),
        out_shape=(half, half),
        in_specs=[whole(pltpu.SMEM)] + [whole(pltpu.HBM)] * len(far) + [whole(pl.ANY)] * len(after),
        out_specs=(whole(pltpu.VMEM),) * 2,
        scratch_shapes=[pltpu.VMEM(shape, BF16), pltpu.VMEM(shape, BF16), pltpu.SemaphoreType.DMA((len(far),))],
        compiler_params=pltpu.CompilerParams(vmem_limit_bytes=LESS),
        cost_estimate=pl.CostEstimate(flops=1000, bytes_accessed=1000, transcendentals=0),
        name="first_merge",
    )(bits, *far, *after)


def tap_places():
    reach = np.concatenate([np.arange(s) / s for s in SIDES]).astype(np.float32)
    scale = np.concatenate([np.full(s, 1.0 / math.sqrt(s)) for s in SIDES]).astype(np.float32)
    return reach, scale


def profiles(coefficient, log_rate):
    reach, scale = tap_places()
    decayed = jnp.exp(-jnp.exp(log_rate)[None] * reach[:, None, None])
    return jnp.sum(coefficient[None] * decayed, axis=2) * scale[:, None]


def profile_grads(coefficient, log_rate, grads):
    reach, scale = tap_places()
    rate = jnp.exp(log_rate)
    decayed = jnp.exp(-rate[None] * reach[:, None, None])
    weighted = (grads * scale[:, None])[:, :, None] * decayed
    return jnp.sum(weighted, axis=0), -coefficient * rate * jnp.sum(weighted * reach[:, None, None], axis=0)


def kernel_matrix(profile, part):
    side = part["side"]
    offsets = np.arange(side)[:, None] - np.arange(side)[None, :]
    picked = profile[part["tap"] + np.maximum(offsets, 0)]
    return jnp.where((offsets >= 0)[:, :, None], picked, 0.0)


def mix_plain(plan, row_pixel, channel_rows, height, width, skip):
    def one_channel(given):
        values, high, wide, weight = given
        image_order = jnp.zeros_like(values).at[row_pixel].set(values)
        pieces = []
        for part in plan.sections:
            side, count = part["side"], part["images"] * part["side"] ** 2
            block = image_order[part["pixel"] : part["pixel"] + count].reshape(-1, side, side)
            left = kernel_matrix(high[:, None], part)[:, :, 0]
            right = kernel_matrix(wide[:, None], part)[:, :, 0]
            mixed = jnp.einsum("ik,nkl,jl->nij", left, block, right, precision=lax.Precision.HIGHEST)
            pieces.append(mixed.reshape(-1))
        joined = jnp.concatenate(pieces) + weight * image_order
        return joined[row_pixel]

    return lax.map(jax.checkpoint(one_channel), (channel_rows, height.T, width.T, skip))


def exchange(blocks):
    return lax.all_to_all(blocks, "chan", 0, 0, tiled=True)


def to_blocks(rows, devices):
    return rows.T.reshape(devices, rows.shape[1] // devices, rows.shape[0])


def to_rows(blocks):
    return blocks.reshape(-1, blocks.shape[2]).T


def feed_kernel(plan, blocks, gain, bias, weight_in, bias_in, grad_act, grads, flipped, act, grad_pre, gain_sum, bias_sum, pre_sum, normed, unit, inverse, total):
    step, channels, count = pl.program_id(0), plan.channels, plan.devices
    width = channels * count

    @pl.when(step == 0)
    def _():
        for s in range(count):
            unit[pl.ds(s * channels, channels), :] = blocks[s].astype(F32)
        mean = jnp.sum(unit[...], axis=0, keepdims=True) * (1.0 / width)
        centred = unit[...] - mean
        scale = lax.rsqrt(jnp.sum(centred * centred, axis=0, keepdims=True) * (1.0 / width) + EPSILON)
        inverse[...] = scale
        unit[...] = centred * scale
        scaled = unit[...] * gain[...] + bias[...]
        flipped[...] = scaled.astype(BF16)
        normed[...] = scaled.T.astype(BF16)
        total[...] = jnp.zeros_like(total)

    tile = 256
    for c in range(0, weight_in.shape[1], tile):
        at = pl.ds(c, tile)
        pre = jnp.dot(normed[...], weight_in[:, at], preferred_element_type=F32) + bias_in[:, at]
        cdf = 0.5 * (1.0 + lax.erf(pre * math.sqrt(0.5)))
        act[:, at] = (pre * cdf).astype(BF16)
        slope = cdf + pre * jnp.exp(-0.5 * pre * pre) * (1.0 / math.sqrt(2.0 * math.pi))
        grad = grad_act[:, at] * slope
        pre_sum[:, at] = jnp.sum(grad, axis=0, keepdims=True)
        low = grad.astype(BF16)
        grad_pre[:, at] = low
        total[...] += lax.dot_general(low, weight_in[:, at], (((1,), (1,)), ((), ())), preferred_element_type=F32)

    @pl.when(step == pl.num_programs(0) - 1)
    def _():
        turned = total[...].T
        gain_sum[...] = jnp.sum(turned * unit[...], axis=1, keepdims=True)
        bias_sum[...] = jnp.sum(turned, axis=1, keepdims=True)
        grad = turned * gain[...]
        level = jnp.sum(grad, axis=0, keepdims=True) * (1.0 / width)
        tilt = jnp.sum(grad * unit[...], axis=0, keepdims=True) * (1.0 / width)
        total_low = (inverse[...] * (grad - level - unit[...] * tilt)).astype(BF16)
        for s in range(count):
            grads[s] = total_low[s * channels : (s + 1) * channels]


def feed(plan, blocks, gain, bias, weight_in, bias_in, grad_act):
    rows, width, hidden = plan.rows, plan.devices * plan.channels, weight_in.shape[1]
    steps = 4
    part = hidden // steps
    same = lambda *shape: pl.BlockSpec(shape, lambda i: (0,) * len(shape))
    across = lambda height: pl.BlockSpec((height, part), lambda i: (0, i))
    shape = jax.ShapeDtypeStruct
    return pl.pallas_call(
        functools.partial(feed_kernel, plan),
        grid=(steps,),
        out_shape=(
            shape(blocks.shape, BF16),
            shape((width, rows), BF16),
            shape((rows, hidden), BF16),
            shape((rows, hidden), BF16),
            shape((width, 1), F32),
            shape((width, 1), F32),
            shape((1, hidden), F32),
        ),
        in_specs=[same(*blocks.shape), same(width, 1), same(width, 1), across(width), across(1), across(rows)],
        out_specs=(same(*blocks.shape), same(width, rows), across(rows), across(rows), same(width, 1), same(width, 1), across(1)),
        scratch_shapes=[pltpu.VMEM((rows, width), BF16), pltpu.VMEM((width, rows), F32), pltpu.VMEM((1, rows), F32), pltpu.VMEM((rows, width), F32)],
        compiler_params=pltpu.CompilerParams(vmem_limit_bytes=VMEM),
        cost_estimate=pl.CostEstimate(flops=1_000_000, bytes_accessed=40_000_000, transcendentals=0),
        name="feed_forward",
    )(blocks, gain[:, None], bias[:, None], weight_in, bias_in[None], grad_act)


def halve(blocks, bits):
    myself = lax.axis_index("chan")
    size = lax.axis_size("chan")
    pairs = lambda bit: [(i, i ^ 1 << bit) for i in range(size)]
    left = list(range(size.bit_length() - 1))
    for bit in bits:
        at = left.index(bit)
        viewed = blocks.reshape((-1, 2, 1 << at) + blocks.shape[1:])
        own = myself >> bit & 1
        keep = lax.dynamic_index_in_dim(viewed, own, 1, keepdims=False)
        send = lax.dynamic_index_in_dim(viewed, 1 - own, 1, keepdims=False)
        got = lax.ppermute(send, "chan", pairs(bit))
        total = keep.astype(F32) + got.astype(F32)
        left.remove(bit)
        blocks = (total if not left else total.astype(BF16)).reshape((-1,) + blocks.shape[1:])
    return blocks[0]


def swapped(x, bit):
    return lax.ppermute(x, "chan", [(i, i ^ 1 << bit) for i in range(lax.axis_size("chan"))])


def body_fast(
    tokens,
    row_pixel,
    coef_height,
    rate_height,
    coef_width,
    rate_width,
    skip_weight,
    norm_gain,
    norm_bias,
    weight_in,
    bias_in,
    weight_out,
    bias_out,
    layer_scale,
    out_grad,
):
    devices = lax.axis_size("chan")
    rows, width_all = tokens.shape
    plan = Plan(devices, rows, width_all // devices)
    token_blocks = exchange(to_blocks(tokens, devices))
    here = lax.axis_index("chan")
    own = [here >> bit & 1 for bit in range(devices.bit_length() - 1)]

    where = plan.address(row_pixel)
    spread = plan.spread()
    taps = (plan.tile_taps(profiles(coef_height, rate_height)), plan.tile_taps(profiles(coef_width, rate_width)), plan.tile_taps(skip_weight[None]))
    mixed_blocks, packed, across = mixer_forward(plan, where, token_blocks, spread, *taps)

    upstream = out_grad.astype(F32)
    scaled = upstream * layer_scale
    scaled_low = scaled.astype(BF16)
    grad_act = lax.dot_general(scaled_low, weight_out, (((1,), (1,)), ((), ())), preferred_element_type=F32)
    grad_normin, flipped, act_low, grad_pre_low, gain_sum, norm_bias_sum, bias_in_sum = feed(
        plan, exchange(mixed_blocks), norm_gain, norm_bias, weight_in, bias_in, grad_act
    )
    grad_blocks = exchange(grad_normin)

    def across_cores(whole):
        pairs = whole.astype(BF16).reshape((devices // 2, 2, -1, whole.shape[1]))
        other = lax.dynamic_index_in_dim(pairs, 1 - own[0], 1, keepdims=False)
        size = pairs.shape[0] // PIECES
        return pairs, [swapped(other[i : i + size], 0) for i in range(0, pairs.shape[0], size)]

    out_part = lax.dot_general(act_low, scaled_low, (((0,), (0,)), ((), ())), preferred_element_type=F32)
    out_keep, out_got = across_cores(out_part)
    in_part = jnp.dot(flipped, grad_pre_low, preferred_element_type=F32)
    in_keep, in_got = across_cores(in_part)
    block_out, scale_sum = branch_out(act_low, weight_out, bias_out, layer_scale, tokens, out_grad, (out_keep, in_keep))
    small = (gain_sum, norm_bias_sum, bias_in_sum, jnp.sum(scaled, axis=0), scale_sum)
    shares = jnp.concatenate([part.reshape(devices, -1, plan.channels) for part in small], axis=1)
    shares = jnp.pad(shares, ((0, 0), (0, 0), (0, LANES - plan.channels)))

    left = list(range(1, devices.bit_length() - 1))
    in_order = left
    out_order = left[:2][::-1] + left[2:]

    def halve(keep, got, order, step, after):
        bit = order[step]
        at = sorted(order[step:]).index(bit)
        bits = jnp.stack([own[0], own[bit]])
        keep, send = (merge if step else first_merge)(keep, got, at, bits, after)
        return keep, send, swapped(send, bit)

    out_keep, out_send, out_got = halve(out_keep, out_got, out_order, 0, (grad_blocks, shares))
    in_keep, in_send, in_got = halve(in_keep, in_got, in_order, 0, (grad_blocks, shares))
    grads = mixer_arrive(plan, where, grad_blocks, spread, (out_send, in_send, shares))
    grads, *sums = mixer_backward(plan, grads, *taps, packed, across, ())
    out_keep, out_send, out_got = halve(out_keep, out_got, out_order, 1, (grads,))
    in_keep, in_send, in_got = halve(in_keep, in_got, in_order, 1, (grads,))
    leaving = mixer_leave(plan, where, grads, spread, shares, (out_send, in_send))
    coefs = (coef_height, rate_height, coef_width, rate_width)
    coef_grads = tap_grads(plan, coefs, spread.astype(F32), sums, (leaving,))
    for step in range(2, len(left)):
        out_keep, out_send, out_got = halve(out_keep, out_got, out_order, step, (leaving,))
        in_keep, in_send, in_got = halve(in_keep, in_got, in_order, step, (leaving,))
    leaving = exchange(leaving)
    out_sum = out_keep[0].astype(F32) + out_got[0].astype(F32)
    in_sum = in_keep[0].astype(F32) + in_got[0].astype(F32)
    grad_tokens, shares = token_grads(plan, leaving, out_grad)
    shares = shares.reshape(-1)
    cuts = np.cumsum([part.size // devices for part in small])[:-1]
    gain_grad, norm_bias_grad, bias_in_grad, bias_out_grad, scale_grad = jnp.split(shares, cuts)
    return (block_out, grad_tokens, *coef_grads, gain_grad, norm_bias_grad, in_sum, bias_in_grad, out_sum, bias_out_grad, scale_grad)


def body_plain(
    tokens,
    row_pixel,
    coef_height,
    rate_height,
    coef_width,
    rate_width,
    skip_weight,
    norm_gain,
    norm_bias,
    weight_in,
    bias_in,
    weight_out,
    bias_out,
    layer_scale,
    out_grad,
):
    devices = lax.axis_size("chan")
    rows, width_all = tokens.shape
    plan = Plan(devices, rows, width_all // devices)
    token_blocks = exchange(to_blocks(tokens, devices))

    height = profiles(coef_height, rate_height)
    width = profiles(coef_width, rate_width)
    lines = lambda blocks: blocks.transpose(1, 0, 2).reshape(blocks.shape[1], -1)
    blocks_of = lambda values: values.astype(BF16).reshape(-1, devices, rows).transpose(1, 0, 2)
    mixed, mixer_back = jax.vjp(
        functools.partial(mix_plain, plan, row_pixel), lines(token_blocks).astype(F32), height, width, skip_weight
    )
    mixed_blocks = blocks_of(mixed)
    normin = to_rows(exchange(mixed_blocks)).astype(F32)

    upstream = out_grad.astype(F32)
    scaled = upstream * layer_scale
    scaled_low = scaled.astype(BF16)
    grad_act = lax.dot_general(scaled_low, weight_out, (((1,), (1,)), ((), ())), preferred_element_type=F32)

    row_mean = jnp.mean(normin, axis=1, keepdims=True)
    centred = normin - row_mean
    inv_std = lax.rsqrt(jnp.mean(centred * centred, axis=1, keepdims=True) + EPSILON)
    unit_rows = centred * inv_std
    normed = (unit_rows * norm_gain + norm_bias).astype(BF16)
    hidden_pre = jnp.dot(normed, weight_in, preferred_element_type=F32) + bias_in
    cdf = 0.5 * (1.0 + lax.erf(hidden_pre * math.sqrt(0.5)))
    act_low = (hidden_pre * cdf).astype(BF16)
    slope = cdf + hidden_pre * jnp.exp(-0.5 * hidden_pre * hidden_pre) * (1.0 / math.sqrt(2.0 * math.pi))
    grad_pre = grad_act * slope
    grad_pre_low = grad_pre.astype(BF16)
    grad_normed = lax.dot_general(grad_pre_low, weight_in, (((1,), (1,)), ((), ())), preferred_element_type=F32)
    grad_unit = grad_normed * norm_gain
    grad_normin = inv_std * (
        grad_unit
        - jnp.mean(grad_unit, axis=1, keepdims=True)
        - unit_rows * jnp.mean(grad_unit * unit_rows, axis=1, keepdims=True)
    )
    grad_blocks = exchange(to_blocks(grad_normin.astype(BF16), devices))

    branch = jnp.dot(act_low, weight_out, preferred_element_type=F32) + bias_out
    block_out = (tokens.astype(F32) + layer_scale * branch).astype(BF16)
    small = (
        jnp.sum(grad_normed * unit_rows, axis=0),
        jnp.sum(grad_normed, axis=0),
        jnp.sum(grad_pre, axis=0),
        jnp.sum(scaled, axis=0),
        jnp.sum(upstream * branch, axis=0),
    )
    weight_in_part = lax.dot_general(normed, grad_pre_low, (((0,), (0,)), ((), ())), preferred_element_type=F32)
    weight_out_part = lax.dot_general(act_low, scaled_low, (((0,), (0,)), ((), ())), preferred_element_type=F32)

    grad_mixed, grad_height, grad_width, grad_skip = mixer_back(lines(grad_blocks).astype(F32))
    grad_rows = blocks_of(grad_mixed)
    coef_height_grad, rate_height_grad = profile_grads(coef_height, rate_height, grad_height)
    coef_width_grad, rate_width_grad = profile_grads(coef_width, rate_width, grad_width)
    grad_tokens = upstream + to_rows(exchange(grad_rows)).astype(F32)

    levels = list(range(devices.bit_length() - 1))
    other = levels[:1] + levels[1:3][::-1] + levels[3:]
    in_sum = halve(weight_in_part.astype(BF16).reshape(devices, -1, weight_in.shape[1]), levels)
    out_sum = halve(weight_out_part.astype(BF16).reshape(devices, -1, weight_out.shape[1]), other)
    shares = jnp.concatenate([s.reshape(devices, -1) for s in small], axis=1)
    shares = exchange(shares).sum(axis=0)
    cuts = np.cumsum([s.shape[0] // devices for s in small])[:-1]
    gain_grad, norm_bias_grad, bias_in_grad, bias_out_grad, scale_grad = jnp.split(shares, cuts)
    return (
        block_out,
        grad_tokens,
        coef_height_grad,
        rate_height_grad,
        coef_width_grad,
        rate_width_grad,
        grad_skip,
        gain_grad,
        norm_bias_grad,
        in_sum,
        bias_in_grad,
        out_sum,
        bias_out_grad,
        scale_grad,
    )


def solution(mesh):
    split, copied = P("chan"), P()

    def body(tokens, *rest):
        devices = lax.axis_size("chan")
        fast = Plan(devices, tokens.shape[0], tokens.shape[1] // devices).fits() and devices >= 16
        return (body_fast if fast else body_plain)(tokens, *rest)

    in_specs = (split, copied) + (split,) * 5 + (copied,) * 7 + (split,)
    return jax.shard_map(body, mesh=mesh, in_specs=in_specs, out_specs=(split,) * 14, check_vma=False)
```

```python
import functools
import math

import jax
import jax.numpy as jnp
import numpy as np
from jax import lax
from jax.experimental import pallas as pl
from jax.experimental.pallas import tpu as pltpu
from jax.sharding import PartitionSpec as P

SIDES = (10, 14, 18)
SHARES = (1, 1, 2)
UNIT = sum(m * s * s for s, m in zip(SIDES, SHARES))
TAPS = sum(SIDES)
EPSILON = 1e-06
LANES = 128
SUB = 8
MARGIN = 32
VMEM = 56 * 2**20
LESS = 36 * 2**20
SMALL = 20 * 2**20
CHUNKS = 3
F32 = jnp.float32
BF16 = jnp.bfloat16


class Plan:
    def __init__(self, devices, rows, channels):
        self.devices, self.rows, self.channels = devices, rows, channels
        self.pixels = devices * rows
        self.units = self.pixels // UNIT
        self.slots = LANES // channels
        self.row_pad = -(-rows // LANES) * LANES
        self.extra_row = -(-rows // SUB) * SUB
        self.sections = []
        image_row, packed_row, tap, mask_row, pixel = 0, 0, 0, 0, 0
        for side, share in zip(SIDES, SHARES):
            images = share * self.units
            pitch = -(-side // SUB) * SUB
            groups = -(-images // self.slots)
            self.sections.append(
                dict(side=side, images=images, pitch=pitch, groups=groups, image_row=image_row, packed_row=packed_row, tap=tap, mask_row=mask_row, pixel=pixel)
            )
            image_row += groups * self.slots * side * pitch
            packed_row += groups * side * pitch
            tap += side
            mask_row += side * pitch
            pixel += images * side * side
        self.image_rows = image_row
        self.packed_rows = packed_row
        self.mask_rows = mask_row

    @property
    def extra_lane(self):
        return self.extra_row - (self.row_pad - LANES)

    def kind(self, lane, which):
        return (lane == self.extra_lane + which) | (lane == self.extra_lane + SUB + which)

    def fits(self):
        room = self.row_pad - self.extra_row >= 2 * SUB
        return room and self.channels % SUB == 0 and 4 * LANES * (self.image_rows + 2 * self.row_pad + 5 * self.packed_rows) < 40 * 2**20

    def address(self, row_pixel):
        where = jnp.zeros_like(row_pixel)
        for part in self.sections:
            local = row_pixel - part["pixel"]
            line = local // part["side"]
            spot = part["image_row"] + line * part["pitch"] + local - line * part["side"]
            where = jnp.where(local >= 0, spot, where)
        return where

    def spread(self):
        lane = np.arange(LANES)
        held = (lane[None, :] % self.channels == np.arange(self.channels)[:, None]) & (lane[None, :] < self.slots * self.channels)
        return jnp.asarray(held.astype(np.float32), BF16)

    def tile_taps(self, taps):
        tiled = jnp.tile(taps, (1, self.slots))
        return jnp.pad(tiled, ((0, 0), (0, LANES - tiled.shape[1])))


def slot_masks(plan):
    lane = lax.broadcasted_iota(jnp.int32, (SUB, LANES), 1)
    return [(lane >= q * plan.channels) & (lane < (q + 1) * plan.channels) for q in range(plan.slots)]


def in_turn(plan, first, second):
    first(0, 0)

    def pair(k, carry):
        first(2 * k + 1, 1)
        second(2 * k, 0)
        first(2 * k + 2, 0)
        second(2 * k + 1, 1)
        return carry

    lax.fori_loop(0, plan.devices // 2 - 1, pair, 0)
    first(plan.devices - 1, 1)
    second(plan.devices - 2, 0)
    second(plan.devices - 1, 1)


def scatter_rows(plan, where, block, spread, buffers, image):
    def turn(s, held):
        rows = lax.dot_general(block[s], spread[...], (((0,), (0,)), ((), ())), preferred_element_type=F32)
        buffers[held][pl.ds(0, plan.rows), :] = rows

    def place(s, held):
        base = s * plan.rows
        for u in range(plan.rows):
            image[pl.ds(where[base + u], 1), :] = buffers[held][pl.ds(u, 1), :]

    in_turn(plan, turn, place)


def gather_rows(plan, where, spread, buffers, image, out, extra=None):
    used = plan.rows if extra is None else plan.row_pad

    def fetch(s, held):
        base = s * plan.rows
        for u in range(plan.rows):
            buffers[held][pl.ds(u, 1), :] = image[pl.ds(where[base + u], 1), :]

    def fold(s, held):
        rows = buffers[held][pl.ds(0, used), :].astype(BF16)
        folded = lax.dot_general(spread[...], rows, (((1,), (1,)), ((), ())), preferred_element_type=F32)
        out[s] = folded.astype(BF16)
        if extra is not None:
            exact = extra[pl.ds(pl.multiple_of(s * plan.channels, SUB), plan.channels), :]
            high = exact.astype(BF16).astype(F32)
            lane = lax.broadcasted_iota(jnp.int32, exact.shape, 1) + (plan.row_pad - LANES)
            sums = jnp.where(lane < plan.extra_row + SUB, high, exact - high)
            out[s, :, pl.ds(plan.row_pad - LANES, LANES)] = jnp.where(lane < plan.extra_row, folded[:, plan.row_pad - LANES :], sums).astype(BF16)

    in_turn(plan, fetch, fold)


def pack_images(plan, masks, image, packed, margin):
    place = lax.broadcasted_iota(jnp.int32, (SUB, LANES), 0)
    for part in plan.sections:
        side, pitch = part["side"], part["pitch"]
        area = side * pitch

        def group(t, carry, part=part, side=side, pitch=pitch, area=area):
            start = part["image_row"] + t * (plan.slots * area)
            target = margin + part["packed_row"] + t * area

            def line(i, inner):
                for j in range(0, pitch, SUB):
                    value = jnp.zeros((SUB, LANES), F32)
                    for q in range(plan.slots):
                        row = pl.multiple_of(start + q * area + i * pitch + j, SUB)
                        here = masks[q] & (t * plan.slots + q < part["images"])
                        if j + SUB > side:
                            here = here & (place + j < side)
                        value = jnp.where(here, image[pl.ds(row, SUB), :], value)
                    packed[pl.ds(pl.multiple_of(target + i * pitch + j, SUB), SUB), :] = value
                return inner

            return lax.fori_loop(0, side, line, carry, unroll=2)

        lax.fori_loop(0, part["groups"], group, 0)


def unpack_line(plan, masks, part, t, offset, value, image):
    area = part["side"] * part["pitch"]
    for q in range(plan.slots):
        row = pl.multiple_of(part["image_row"] + (t * plan.slots + q) * area + offset, SUB)
        image[pl.ds(row, SUB), :] = jnp.where(masks[q], value, 0.0)


def wide_taps(plan, taps, table):
    for tap in range(TAPS):
        table[pl.ds(tap * SUB, SUB), :] = jnp.broadcast_to(taps[pl.ds(tap, 1), :], (SUB, LANES))


def masked_taps(plan, taps, table):
    for part in plan.sections:
        side, pitch = part["side"], part["pitch"]
        place = lax.broadcasted_iota(jnp.int32, (pitch, LANES), 0)
        for tap in range(side):
            row = taps[pl.ds(part["tap"] + tap, 1), :]
            table[pl.ds(part["mask_row"] + tap * pitch, pitch), :] = jnp.where(place >= tap, row, 0.0)


def forward_kernel(plan, where, block, spread, height, width, skip, out, packed, across, near, far, image, px, pu, height_wide, width_masked):
    masks = slot_masks(plan)
    px[pl.ds(0, MARGIN), :] = jnp.zeros((MARGIN, LANES), F32)
    wide_taps(plan, height, height_wide)
    masked_taps(plan, width, width_masked)
    scatter_rows(plan, where, block, spread, (near, far), image)
    pack_images(plan, masks, image, px, MARGIN)
    skips = jnp.broadcast_to(skip[...], (SUB, LANES))
    for part in plan.sections:
        side, pitch = part["side"], part["pitch"]
        area = side * pitch

        def group(t, carry, part=part, side=side, pitch=pitch, area=area):
            start = MARGIN + part["packed_row"] + t * area

            def line(i, inner):
                base = start + i * pitch
                for j in range(0, pitch, SUB):
                    total = jnp.zeros((SUB, LANES), F32)
                    for tap in range(min(side, j + SUB)):
                        weight = width_masked[pl.ds(part["mask_row"] + tap * pitch + j, SUB), :]
                        total = total + weight * px[pl.ds(base + j - tap, SUB), :]
                    pu[pl.ds(pl.multiple_of(base + j, SUB), SUB), :] = total
                return inner

            lax.fori_loop(0, side, line, 0)

            def column(c, inner):
                first = pl.multiple_of(start + c * SUB, SUB)
                held = [pu[pl.ds(pl.multiple_of(first + k * pitch, SUB), SUB), :] for k in range(side)]
                for i in range(side):
                    total = skips * px[pl.ds(pl.multiple_of(first + i * pitch, SUB), SUB), :]
                    for k in range(i + 1):
                        total = total + height_wide[pl.ds((part["tap"] + i - k) * SUB, SUB), :] * held[k]
                    unpack_line(plan, masks, part, t, i * pitch + c * SUB, total, image)
                return inner

            lax.fori_loop(0, pitch // SUB, column, 0)
            return carry

        lax.fori_loop(0, part["groups"], group, 0)
    packed[...] = px[pl.ds(MARGIN, plan.packed_rows), :]
    across[...] = pu[pl.ds(MARGIN, plan.packed_rows), :]
    gather_rows(plan, where, spread, (near, far), image, out)


def arrive_kernel(plan, where, block, spread, *rest):
    grads, mark, near, far, image = rest[-5:]
    mark[...] = jnp.zeros_like(mark)
    scatter_rows(plan, where, block, spread, (near, far), image)
    pack_images(plan, slot_masks(plan), image, grads, 0)


def leave_kernel(plan, where, grads, spread, extra, *rest):
    out, mark, near, far, image = rest[-5:]
    mark[...] = jnp.zeros_like(mark)
    masks = slot_masks(plan)
    for part in plan.sections:
        area = part["side"] * part["pitch"]

        def group(t, carry, part=part, area=area):
            for offset in range(0, area, SUB):
                row = pl.multiple_of(part["packed_row"] + t * area + offset, SUB)
                unpack_line(plan, masks, part, t, offset, grads[pl.ds(row, SUB), :], image)
            return carry

        lax.fori_loop(0, part["groups"], group, 0)
    gather_rows(plan, where, spread, (near, far), image, out, extra)


def backward_kernel(plan, pg, height, width, skip, packed, across, *rest):
    out, height_sums, width_sums, skip_sums, pd, height_wide, width_wide = rest[-7:]
    place = lax.broadcasted_iota(jnp.int32, (SUB, LANES), 0)
    pd[pl.ds(plan.packed_rows, MARGIN), :] = jnp.zeros((MARGIN, LANES), F32)
    wide_taps(plan, height, height_wide)
    wide_taps(plan, width, width_wide)
    skips = jnp.broadcast_to(skip[...], (SUB, LANES))
    skip_sums[...] = jnp.zeros((SUB, LANES), F32)
    height_sums[...] = jnp.zeros((TAPS * SUB, LANES), F32)
    for part in plan.sections:
        side, pitch = part["side"], part["pitch"]
        area = side * pitch

        def group(t, carry, part=part, side=side, pitch=pitch, area=area):
            start = part["packed_row"] + t * area

            def column(c, inner):
                first = pl.multiple_of(start + c * SUB, SUB)
                rows = [pl.ds(pl.multiple_of(first + k * pitch, SUB), SUB) for k in range(side)]
                held = [pg[row, :] for row in rows]
                for k in range(side):
                    total = jnp.zeros((SUB, LANES), F32)
                    for i in range(k, side):
                        total = total + height_wide[pl.ds((part["tap"] + i - k) * SUB, SUB), :] * held[i]
                    pd[rows[k], :] = total
                ways = [across[row, :] for row in rows]
                for tap in range(side):
                    total = held[tap] * ways[0]
                    for k in range(1, side - tap):
                        total = total + held[k + tap] * ways[k]
                    height_sums[pl.ds((part["tap"] + tap) * SUB, SUB), :] += total
                return inner

            lax.fori_loop(0, pitch // SUB, column, 0)
            return carry

        lax.fori_loop(0, part["groups"], group, 0)
    for part in plan.sections:
        side, pitch = part["side"], part["pitch"]
        area = side * pitch

        def group(t, carry, part=part, side=side, pitch=pitch, area=area):
            start = part["packed_row"] + t * area

            def line(i, sums):
                sums = list(sums)
                base = start + i * pitch
                aligned = pl.multiple_of(base, SUB)
                for j in range(0, pitch, SUB):
                    here = pl.ds(pl.multiple_of(aligned + j, SUB), SUB)
                    mine, grad = packed[here, :], pg[here, :]
                    total = skips * grad
                    sums[side] = sums[side] + mine * grad
                    for tap in range(min(side, side - j)):
                        moved = pd[pl.ds(base + j + tap, SUB), :]
                        if j + SUB - 1 + tap >= pitch:
                            moved = jnp.where(place + (j + tap) < side, moved, 0.0)
                        total = total + width_wide[pl.ds((part["tap"] + tap) * SUB, SUB), :] * moved
                        sums[tap] = sums[tap] + mine * moved
                    out[here, :] = total
                return tuple(sums)

            return lax.fori_loop(0, side, line, carry)

        zero = jnp.zeros((SUB, LANES), F32)
        sums = lax.fori_loop(0, part["groups"], group, (zero,) * (side + 1))
        for tap in range(side):
            width_sums[pl.ds((part["tap"] + tap) * SUB, SUB), :] = sums[tap]
        skip_sums[...] += sums[side]


def whole(memory):
    return pl.BlockSpec(memory_space=memory)


def lanes_of(rows):
    return jax.ShapeDtypeStruct((rows, LANES), F32)


def row_buffers(plan):
    return [pltpu.VMEM((plan.row_pad, LANES), F32)] * 2 + [pltpu.VMEM((plan.image_rows, LANES), F32)]


def near(values):
    return pltpu.with_memory_space_constraint(values, pltpu.VMEM)


def distant(values):
    return pltpu.with_memory_space_constraint(values, pltpu.HBM)


def kernel_call(kernel, name, micros, memories, out_shape, scratch, args, after=(), stays=(), held=(), left=()):
    single = not isinstance(out_shape, tuple)
    shapes = (out_shape,) if single else out_shape
    shapes = tuple((pltpu.VMEM if i in stays else pltpu.HBM)(o.shape, o.dtype) for i, o in enumerate(shapes))
    outs = tuple(whole(pltpu.VMEM) for _ in shapes)
    place = lambda i, value: near(value) if i in held else value if memories[i] is pltpu.SMEM or i in left else distant(value)
    out = pl.pallas_call(
        kernel,
        out_shape=shapes,
        in_specs=[whole(m) for m in memories] + [whole(pltpu.HBM)] * len(after),
        out_specs=outs,
        scratch_shapes=scratch,
        compiler_params=pltpu.CompilerParams(vmem_limit_bytes=LESS if stays or held else VMEM),
        cost_estimate=pl.CostEstimate(flops=1_000_000, bytes_accessed=int(3_690_000 * micros), transcendentals=0),
        name=name,
    )(*[place(i, value) for i, value in enumerate(args)], *map(distant, after))
    return out[0] if single else out


def mixer_forward(plan, where, block, spread, height, width, skip):
    rows = plan.packed_rows
    scratch = row_buffers(plan) + [
        pltpu.VMEM((rows + MARGIN, LANES), F32),
        pltpu.VMEM((rows + MARGIN, LANES), F32),
        pltpu.VMEM((TAPS * SUB, LANES), F32),
        pltpu.VMEM((plan.mask_rows, LANES), F32),
    ]
    outs = (jax.ShapeDtypeStruct(block.shape, BF16), lanes_of(rows), lanes_of(rows))
    memories = [pltpu.SMEM] + [pltpu.VMEM] * 5
    args = (where, block, spread, height, width, skip)
    return kernel_call(functools.partial(forward_kernel, plan), "mixer_forward", 33, memories, outs, scratch, args, held=(1,))


def mixer_arrive(plan, where, block, spread, after):
    return kernel_call(
        functools.partial(arrive_kernel, plan), "mixer_arrive", 15, [pltpu.SMEM] + [pltpu.VMEM] * 2, (lanes_of(plan.packed_rows), lanes_of(SUB)), row_buffers(plan), (where, block, spread), after, (0,), (1,)
    )


def mixer_backward(plan, grads, height, width, skip, packed, across, after):
    scratch = [
        pltpu.VMEM((plan.packed_rows + MARGIN, LANES), F32),
        pltpu.VMEM((TAPS * SUB, LANES), F32),
        pltpu.VMEM((TAPS * SUB, LANES), F32),
    ]
    outs = (lanes_of(plan.packed_rows), lanes_of(TAPS * SUB), lanes_of(TAPS * SUB), lanes_of(SUB))
    args = (grads, height, width, skip, packed, across)
    return kernel_call(functools.partial(backward_kernel, plan), "mixer_backward", 8, [pltpu.VMEM] * 6, outs, scratch, args, after, (0,), (0,), (4, 5))


def mixer_leave(plan, where, grads, spread, extra, after):
    out = (jax.ShapeDtypeStruct((plan.devices, plan.channels, plan.row_pad), BF16), lanes_of(SUB))
    return kernel_call(
        functools.partial(leave_kernel, plan), "mixer_leave", 13, [pltpu.SMEM] + [pltpu.VMEM] * 3, out, row_buffers(plan), (where, grads, spread, extra), after, (), (1,)
    )


def taps_kernel(plan, coef_height, rate_height, coef_width, rate_width, spread, height_sums, width_sums, skip_sums, *rest):
    outs = rest[-5:]
    reach, scale = tap_places()
    fold = lambda sums: lax.dot_general(spread[...], sums, (((1,), (1,)), ((), ())), precision=lax.Precision.HIGHEST, preferred_element_type=F32)
    for coef, log_rate, sums, coef_out, rate_out in (
        (coef_height, rate_height, height_sums, outs[0], outs[1]),
        (coef_width, rate_width, width_sums, outs[2], outs[3]),
    ):
        grads = fold(sums[...].reshape(TAPS, SUB, LANES).sum(axis=1))
        rate = jnp.exp(log_rate[...])
        plain, moved = jnp.zeros_like(rate), jnp.zeros_like(rate)
        for tap in range(TAPS):
            weighted = (grads[:, tap : tap + 1] * float(scale[tap])) * jnp.exp(rate * float(-reach[tap]))
            plain = plain + weighted
            moved = moved + weighted * float(reach[tap])
        coef_out[...] = plain
        rate_out[...] = -coef[...] * rate * moved
    outs[4][...] = fold(skip_sums[...])


def tap_grads(plan, coefs, spread, sums, after):
    shape = jax.ShapeDtypeStruct(coefs[0].shape, F32)
    outs = (shape,) * 4 + (jax.ShapeDtypeStruct((plan.channels, SUB), F32),)
    *grads, skips = kernel_call(functools.partial(taps_kernel, plan), "tap_grads", 0.01, [pltpu.VMEM] * 8, outs, [], (*coefs, spread, *sums), after)
    return *grads, skips.sum(axis=1)


def tokens_kernel(plan, blocks, out_grad, out, shares, flipped):
    total = jnp.zeros(shares.shape, F32)
    for s in range(plan.devices):
        block = blocks[s].astype(F32)
        flipped[pl.ds(s * plan.channels, plan.channels), :] = block[:, : plan.rows]
        total = total + block[:, plan.row_pad - LANES :]
    shares[...] = total
    out[...] = out_grad[...].astype(F32) + flipped[...].T


def token_grads(plan, blocks, out_grad):
    outs = (jax.ShapeDtypeStruct(out_grad.shape, F32), jax.ShapeDtypeStruct((plan.channels, LANES), F32))
    grads, shares = kernel_call(
        functools.partial(tokens_kernel, plan), "token_grads", 3, [pltpu.VMEM] * 2, outs, [pltpu.VMEM(out_grad.shape[::-1], F32)], (blocks, out_grad), held=(0,)
    )
    first = plan.extra_row - (plan.row_pad - LANES)
    return grads, (shares[:, first : first + SUB] + shares[:, first + SUB : first + 2 * SUB]).T


def started(pairs, sems):
    copies = [pltpu.make_async_copy(source, target, sems.at[i]) for i, (source, target) in enumerate(pairs)]
    for copy in copies:
        copy.start()
    return copies


NEAR, FAR, AUTO, OPEN, SCALAR = "near", "far", "auto", "open", "scalar"


def run(kernel, name, ins, outs, scratch, after=(), micros=0.01, limit=VMEM):
    same = lambda value: value
    memory = {NEAR: pltpu.VMEM, FAR: pltpu.HBM, AUTO: pltpu.VMEM, OPEN: pltpu.VMEM, SCALAR: pltpu.SMEM}
    hold = {NEAR: near, FAR: distant, AUTO: distant, OPEN: same, SCALAR: same}
    make = {NEAR: pltpu.VMEM, FAR: pltpu.HBM, AUTO: pltpu.HBM, OPEN: jax.ShapeDtypeStruct}
    return pl.pallas_call(
        kernel,
        out_shape=tuple(make[place](shape, dtype) for shape, dtype, place in outs),
        in_specs=[whole(memory[place]) for _, place in ins] + [whole(pltpu.HBM)] * len(after),
        out_specs=tuple(whole(memory[place]) for _, _, place in outs),
        scratch_shapes=scratch,
        compiler_params=pltpu.CompilerParams(vmem_limit_bytes=limit),
        cost_estimate=pl.CostEstimate(flops=1000, bytes_accessed=int(3_690_000 * micros), transcendentals=0),
        name=name,
    )(*[hold[place](value) for value, place in ins], *map(distant, after))


def feed_kernel(plan, blocks, gain, bias, weight_far, bias_in, grad_act_far, grads, flipped, act_far, grad_pre_far, sums, pre_sum, *scratch):
    normed, unit, total, weight_in, grad_act, act, grad_pre, came, left = scratch
    channels, count = plan.channels, plan.devices
    width, hidden = weight_in.shape
    tile, group = 256, 3
    steps = hidden // (tile * group)
    chunk = lambda step: pl.ds(pl.multiple_of(step * (tile * group), tile * group), tile * group)

    def arriving(step):
        return [
            pltpu.make_async_copy(weight_far.at[:, chunk(step)], weight_in.at[:, chunk(step)], came.at[0, step]),
            pltpu.make_async_copy(grad_act_far.at[:, chunk(step)], grad_act.at[:, chunk(step)], came.at[1, step]),
        ]

    def leaving(step):
        return [
            pltpu.make_async_copy(act.at[:, chunk(step)], act_far.at[:, chunk(step)], left.at[0, step]),
            pltpu.make_async_copy(grad_pre.at[:, chunk(step)], grad_pre_far.at[:, chunk(step)], left.at[1, step]),
        ]

    for step in range(steps):
        for copy in arriving(step):
            copy.start()
    for s in range(count):
        unit[pl.ds(s * channels, channels), :] = blocks[s].astype(F32)
    mean = jnp.sum(unit[...], axis=0, keepdims=True) * (1.0 / width)
    centred = unit[...] - mean
    inverse = lax.rsqrt(jnp.sum(centred * centred, axis=0, keepdims=True) * (1.0 / width) + EPSILON)
    unit[...] = centred * inverse
    scaled = unit[...] * gain[...] + bias[...]
    flipped[...] = scaled.astype(BF16)
    normed[...] = scaled.T.astype(BF16)
    total[...] = jnp.zeros_like(total)

    def tiles(step, carry):
        for copy in arriving(step):
            copy.wait()
        for c in range(group):
            at = pl.ds(pl.multiple_of((step * group + c) * tile, tile), tile)
            pre = jnp.dot(normed[...], weight_in[:, at], preferred_element_type=F32) + bias_in[:, at]
            cdf = 0.5 * (1.0 + lax.erf(pre * math.sqrt(0.5)))
            act[:, at] = (pre * cdf).astype(BF16)
            slope = cdf + pre * jnp.exp(-0.5 * pre * pre) * (1.0 / math.sqrt(2.0 * math.pi))
            grad = grad_act[:, at] * slope
            pre_sum[:, at] = jnp.sum(grad, axis=0, keepdims=True)
            low = grad.astype(BF16)
            grad_pre[:, at] = low
            total[...] += lax.dot_general(low, weight_in[:, at], (((1,), (1,)), ((), ())), preferred_element_type=F32)
        for copy in leaving(step):
            copy.start()
        return carry

    lax.fori_loop(0, steps, tiles, 0)
    turned = total[...].T
    lane = lax.broadcasted_iota(jnp.int32, sums.shape, 1)
    sums[...] = jnp.where(
        plan.kind(lane, 0),
        jnp.sum(turned * unit[...], axis=1, keepdims=True),
        jnp.where(plan.kind(lane, 1), jnp.sum(turned, axis=1, keepdims=True), 0.0),
    )
    grad = turned * gain[...]
    level = jnp.sum(grad, axis=0, keepdims=True) * (1.0 / width)
    tilt = jnp.sum(grad * unit[...], axis=0, keepdims=True) * (1.0 / width)
    total_low = (inverse * (grad - level - unit[...] * tilt)).astype(BF16)
    for s in range(count):
        grads[s] = total_low[s * channels : (s + 1) * channels]
    for step in range(steps):
        for copy in leaving(step):
            copy.wait()


def feed(plan, blocks, gain, bias, weight_in, bias_in, grad_act):
    rows, width, hidden = plan.rows, plan.devices * plan.channels, weight_in.shape[1]
    steps = hidden // 768
    ins = [(blocks, NEAR), (gain[:, None], AUTO), (bias[:, None], AUTO), (weight_in, FAR), (bias_in[None], AUTO), (grad_act, FAR)]
    outs = [
        (blocks.shape, BF16, AUTO),
        ((width, rows), BF16, AUTO),
        ((rows, hidden), BF16, FAR),
        ((rows, hidden), BF16, FAR),
        ((width, LANES), F32, AUTO),
        ((1, hidden), F32, AUTO),
    ]
    room = [
        pltpu.VMEM((rows, width), BF16),
        pltpu.VMEM((width, rows), F32),
        pltpu.VMEM((rows, width), F32),
        pltpu.VMEM((width, hidden), BF16),
        pltpu.VMEM((rows, hidden), F32),
        pltpu.VMEM((rows, hidden), BF16),
        pltpu.VMEM((rows, hidden), BF16),
        pltpu.SemaphoreType.DMA((2, steps)),
        pltpu.SemaphoreType.DMA((2, steps)),
    ]
    return run(functools.partial(feed_kernel, plan), "feed_forward", ins, outs, room, micros=10, limit=LESS)


def out_grad_kernel(own, act_far, scaled_far, weight_far, given, keep_far, *rest):
    sent, (scale_sum, act, scaled, weight_out, keep, other, came, left) = rest[:-8], rest[-8:]
    chunks, chips, high, width = keep.shape
    height, steps = chunks * high, weight_out.shape[0] // 768
    tile, each, part = act.shape[1] // steps, chips // steps, chips // len(sent)
    parts = [pl.ds(i * tile, tile) for i in range(steps)]
    there = [(scaled_far, scaled)]
    for at in parts:
        there += [(act_far.at[:, at], act.at[:, at]), (weight_far.at[at, :], weight_out.at[at, :])]
    arriving, leaving = started(there, came), []
    arriving[0].wait()
    product = jnp.zeros((1, width), F32)
    for i, at in enumerate(parts):
        arriving[1 + 2 * i].wait()
        total = lax.dot_general(act[:, at], scaled[...], (((0,), (0,)), ((), ())), preferred_element_type=F32)
        low = total.astype(BF16)
        for c in range(each):
            first = low[2 * c * height : (2 * c + 1) * height]
            second = low[(2 * c + 1) * height : (2 * c + 2) * height]
            mine, yours = jnp.where(own[0] == 0, first, second), jnp.where(own[0] == 0, second, first)
            for chunk in range(chunks):
                keep[chunk, i * each + c] = mine[chunk * high : (chunk + 1) * high]
                other[chunk, i * each + c] = yours[chunk * high : (chunk + 1) * high]
        some = pl.ds(i * each, each)
        there = [(other.at[:, pl.ds(p * part, part)], sent[p]) for p in range(i * each // part, (i + 1) * each // part)]
        there += [(keep.at[:, some], keep_far.at[:, some])]
        leaving += started(there, left.at[pl.ds(len(leaving), len(there))])
        arriving[2 + 2 * i].wait()
        product = product + jnp.sum(total * weight_out[at, :].astype(F32), axis=0, keepdims=True)
    scale, bias_out, bias_row = (given[pl.ds(i, 1), :] for i in range(3))
    scale_sum[...] = (product + bias_out * bias_row) / scale
    for copy in leaving:
        copy.wait()


def out_grad_halves(plan, own, act, scaled, weight_out, given):
    (rows, hidden), width, chips = act.shape, scaled.shape[1], plan.devices // 2
    high, steps, pieces = hidden // plan.devices // CHUNKS, hidden // 768, 8
    ins = [(own, SCALAR), (act, FAR), (scaled, FAR), (weight_out, FAR), (given, AUTO)]
    outs = [((CHUNKS, chips, high, width), BF16, FAR)]
    outs += [((CHUNKS, chips // pieces, high, width), BF16, FAR)] * pieces + [((1, width), F32, AUTO)]
    room = [pltpu.VMEM(value.shape, BF16) for value in (act, scaled, weight_out)] + [pltpu.VMEM(outs[0][0], BF16)] * 2
    room += [pltpu.SemaphoreType.DMA((1 + 2 * steps,)), pltpu.SemaphoreType.DMA((pieces + steps,))]
    keep, *sent, scale_sum = run(out_grad_kernel, "out_grad_halves", ins, outs, room)
    return keep, sent, scale_sum


def retiled(values, width):
    tiles = [values[r : r + SUB, c : c + LANES] for r in range(0, values.shape[0], SUB) for c in range(0, values.shape[1], LANES)]
    each = width // LANES
    return jnp.concatenate([jnp.concatenate(tiles[i : i + each], axis=1) for i in range(0, len(tiles), each)], axis=0)


def in_grad_kernel(own, flipped_far, grad_pre_far, keep_far, *rest):
    sent, (flipped, grad_pre, keep, other, came, left) = rest[:-6], rest[-6:]
    chunks, chips, _, width = keep.shape
    height, tile, each = flipped.shape[0] // chips // 2, grad_pre.shape[1] // chunks, len(sent) // chunks
    parts = [pl.ds(i * tile, tile) for i in range(chunks)]
    arriving = started([(flipped_far, flipped)] + [(grad_pre_far.at[:, at], grad_pre.at[:, at]) for at in parts], came)
    arriving[0].wait()
    leaving = []
    for i, at in enumerate(parts):
        arriving[1 + i].wait()
        total = jnp.dot(flipped[...], grad_pre[:, at], preferred_element_type=F32)
        for c in range(chips):
            first = total[2 * c * height : (2 * c + 1) * height]
            second = total[(2 * c + 1) * height : (2 * c + 2) * height]
            keep[i, c] = retiled(jnp.where(own[0] == 0, first, second), width).astype(BF16)
            other[i, c] = retiled(jnp.where(own[0] == 0, second, first), width).astype(BF16)
        some = chips // each
        there = [(other.at[i, pl.ds(p * some, some)], sent[i * each + p]) for p in range(each)] + [(keep.at[i], keep_far.at[i])]
        leaving += started(there, left.at[pl.ds(len(leaving), len(there))])
    for copy in leaving:
        copy.wait()


def in_grad_halves(plan, own, flipped, grad_pre):
    width, hidden, chips = flipped.shape[0], grad_pre.shape[1], plan.devices // 2
    high, each = plan.channels * hidden // CHUNKS // width, 4
    outs = [((CHUNKS, chips, high, width), BF16, FAR)] + [((chips // each, high, width), BF16, FAR)] * (CHUNKS * each)
    room = [pltpu.VMEM(value.shape, BF16) for value in (flipped, grad_pre)] + [pltpu.VMEM(outs[0][0], BF16)] * 2
    room += [pltpu.SemaphoreType.DMA((1 + CHUNKS,)), pltpu.SemaphoreType.DMA((CHUNKS * (each + 1),))]
    keep, *sent = run(in_grad_kernel, "in_grad_halves", [(own, SCALAR), (flipped, FAR), (grad_pre, FAR)], outs, room)
    return keep, sent


def shares_kernel(plan, sums, pre_sum, given, scale_sum, shares, rows):
    channels, count = plan.channels, plan.devices
    width = channels * count
    kinds = pre_sum.shape[1] // width
    lane = lax.broadcasted_iota(jnp.int32, shares.shape, 1)
    rows[...] = jnp.zeros_like(rows)
    for kind, row in ((2 + kinds, given[pl.ds(2, 1), :]), (3 + kinds, scale_sum[...])):
        for again in (0, SUB):
            rows[pl.ds(plan.extra_lane + kind + again, 1), :] = row
    total = sums[...] + rows[...].T
    columns = jnp.broadcast_to(pre_sum[...], (SUB, pre_sum.shape[1])).T.reshape(count, kinds, channels, SUB)
    for kind in range(kinds):
        column = columns[:, kind].reshape(width, SUB)[:, :1]
        total = total + jnp.where(plan.kind(lane, 2 + kind), column, 0.0)
    shares[...] = total


def small_shares(plan, sums, pre_sum, given, scale_sum, after):
    ins = [(value, AUTO) for value in (sums, pre_sum, given, scale_sum)]
    room = [pltpu.VMEM((LANES, sums.shape[0]), F32)]
    return run(functools.partial(shares_kernel, plan), "small_shares", ins, [(sums.shape, F32, AUTO)], room, after)[0]


def branch_kernel(act_far, weight_far, given, tokens, *rest):
    out, act, weight_out, sems = rest[-4:]
    steps = sems.shape[0] // 2
    tile = act.shape[1] // steps
    parts = [pl.ds(i * tile, tile) for i in range(steps)]
    copies = []
    for part in parts:
        copies += [(act_far.at[:, part], act.at[:, part]), (weight_far.at[part, :], weight_out.at[part, :])]
    copies = started(copies, sems)
    branch = given[pl.ds(1, 1), :]
    for i, part in enumerate(parts):
        copies[2 * i].wait()
        copies[2 * i + 1].wait()
        branch = branch + jnp.dot(act[:, part], weight_out[part, :], preferred_element_type=F32)
    out[...] = (tokens[...].astype(F32) + given[pl.ds(0, 1), :] * branch).astype(BF16)


def branch_out(act, weight_out, given, tokens, after):
    ins = [(act, FAR), (weight_out, FAR), (given, AUTO), (tokens, AUTO)]
    room = [pltpu.VMEM(act.shape, BF16), pltpu.VMEM(weight_out.shape, BF16), pltpu.SemaphoreType.DMA((4,))]
    return run(branch_kernel, "branch_out", ins, [(tokens.shape, BF16, AUTO)], room, after)[0]


def held_back(arrays, after):
    kept = len(arrays)
    return pl.pallas_call(
        lambda *refs: None,
        out_shape=tuple(pltpu.HBM(a.shape, a.dtype) for a in arrays),
        in_specs=[whole(pltpu.HBM)] * kept + [whole(pl.ANY)] * len(after),
        out_specs=(whole(pltpu.HBM),) * kept,
        input_output_aliases={i: i for i in range(kept)},
        cost_estimate=pl.CostEstimate(flops=0, bytes_accessed=0, transcendentals=0),
        name="held_back",
    )(*map(distant, arrays), *after)


def act_grads_kernel(scaled, weight_out, out):
    tile = 768
    for c in range(0, out.shape[1], tile):
        out[:, pl.ds(c, tile)] = lax.dot_general(scaled[...], weight_out[pl.ds(c, tile), :], (((1,), (1,)), ((), ())), preferred_element_type=F32)


def act_grads(scaled, weight_out):
    outs = [((scaled.shape[0], weight_out.shape[0]), F32, AUTO)]
    return run(act_grads_kernel, "act_grads", [(scaled, AUTO), (weight_out, AUTO)], outs, [], micros=6)[0]


def merge_entries(at, bit, keep, got, mine, other):
    low = (1 << at) - 1
    for e in range(mine.shape[0]):
        first = (e >> at << at + 1) + (e & low)
        here, there = first + bit * (low + 1), first + (1 - bit) * (low + 1)
        other[e] = keep(here) + got(there if False else here) if False else keep(there) + got(there)
        mine[e] = keep(here) + got(here)


def first_merge_kernel(cuts, pieces, bits, keep_far, *rest):
    got, (main_mine, main_other, less_mine, less_other, mark, keep, came, sems) = rest[:pieces], rest[-8:]
    chunks, chips, high, _ = keep.shape
    mark[...] = jnp.zeros_like(mark)
    groups = []
    for i in range(chunks):
        there = [(keep_far.at[i], keep.at[i])]
        if len(got[0].shape) == 4:
            part = got[0].shape[1]
            there += [(piece.at[i], came.at[i, pl.ds(p * part, part)]) for p, piece in enumerate(got)]
        else:
            each = pieces // chunks
            part = chips // each
            there += [(got[i * each + p], came.at[i, pl.ds(p * part, part)]) for p in range(each)]
        groups.append(started(there, sems.at[pl.ds(i * len(there), len(there))]))
    for i in range(chunks):
        for copy in groups[i]:
            copy.wait()
        if i < chunks - 1:
            rows = pl.ds(i * high, high)
            mine, other, (at, bit) = main_mine.at[:, rows], main_other.at[:, rows], cuts[0]
        else:
            mine, other, (at, bit) = less_mine, less_other, cuts[1]
        merge_entries(at, bits[bit], lambda e: keep[i, e], lambda e: came[i, e], mine, other)


def first_merge(keep, got, cuts, bits, after):
    chunks, chips, high, width = keep.shape
    ins = [(bits, SCALAR), (keep, FAR)] + [(part, FAR) for part in got]
    outs = [((chips // 2, rows, width), BF16, NEAR) for rows in ((chunks - 1) * high, high) for _ in range(2)]
    room = [pltpu.VMEM(keep.shape, BF16)] * 2 + [pltpu.SemaphoreType.DMA((chunks + len(got) * (chunks if got[0].ndim == 4 else 1),))]
    return run(functools.partial(first_merge_kernel, cuts, len(got)), "first_merge", ins, outs + [((SUB, LANES), F32, AUTO)], room, after, limit=LESS)


def merge_kernel(jobs, bits, *refs):
    count, pairs = sum(len(job) for job in jobs), 2 * len(jobs)
    outs, mark = refs[-1 - pairs : -1], refs[-1]
    mark[...] = jnp.zeros_like(mark)
    i = 0
    for j, job in enumerate(jobs):
        row = 0
        for at, bit in job:
            keep, got = refs[i], refs[count + i]
            rows = pl.ds(row, keep.shape[1])
            merge_entries(at, bits[bit], lambda e: keep[e], lambda e: got[e], outs[2 * j].at[:, rows], outs[2 * j + 1].at[:, rows])
            row += keep.shape[1]
            i += 1


def merge(keeps, gots, jobs, bits, after=()):
    ins = [(bits, SCALAR)] + [(value, NEAR) for value in keeps] + [(value, OPEN) for value in gots]
    outs, i = [], 0
    for job in jobs:
        parts = keeps[i : i + len(job)]
        i += len(job)
        outs += [((parts[0].shape[0] // 2, sum(part.shape[1] for part in parts), parts[0].shape[2]), BF16, NEAR)] * 2
    *halves, mark = run(functools.partial(merge_kernel, jobs), "merge_halves", ins, outs + [((SUB, LANES), F32, AUTO)], [], after, limit=LESS)
    return halves[0::2], halves[1::2], mark


def last_kernel(keep, got, less_keep, less_got, in_sum, out_sum):
    total = keep[0].astype(F32) + got[0].astype(F32)
    less = less_keep[0].astype(F32) + less_got[0].astype(F32)
    high = less.shape[0] // 2
    tile = in_sum.shape[1] // CHUNKS
    for i, part in enumerate((total[:high], total[high : 2 * high], less[:high])):
        in_sum[:, pl.ds(i * tile, tile)] = retiled(part, tile)
    out_sum[pl.ds(0, 2 * high), :] = total[2 * high :]
    out_sum[pl.ds(2 * high, high), :] = less[high:]


def last_sums(parts, channels, hidden, after):
    ins = [(parts[0], NEAR), (parts[1], OPEN), (parts[2], NEAR), (parts[3], OPEN)]
    high, width = parts[2].shape[1] // 2, parts[2].shape[2]
    outs = [((channels, hidden), F32, AUTO), ((CHUNKS * high, width), F32, AUTO)]

    def kernel(*refs):
        last_kernel(*refs[:4], *refs[-2:])

    return run(kernel, "last_sums", ins, outs, [], after)


def tap_places():
    reach = np.concatenate([np.arange(s) / s for s in SIDES]).astype(np.float32)
    scale = np.concatenate([np.full(s, 1.0 / math.sqrt(s)) for s in SIDES]).astype(np.float32)
    return reach, scale


def profiles(coefficient, log_rate):
    reach, scale = tap_places()
    decayed = jnp.exp(-jnp.exp(log_rate)[None] * reach[:, None, None])
    return jnp.sum(coefficient[None] * decayed, axis=2) * scale[:, None]


def profile_grads(coefficient, log_rate, grads):
    reach, scale = tap_places()
    rate = jnp.exp(log_rate)
    decayed = jnp.exp(-rate[None] * reach[:, None, None])
    weighted = (grads * scale[:, None])[:, :, None] * decayed
    return jnp.sum(weighted, axis=0), -coefficient * rate * jnp.sum(weighted * reach[:, None, None], axis=0)


def kernel_matrix(profile, part):
    side = part["side"]
    offsets = np.arange(side)[:, None] - np.arange(side)[None, :]
    picked = profile[part["tap"] + np.maximum(offsets, 0)]
    return jnp.where((offsets >= 0)[:, :, None], picked, 0.0)


def mix_plain(plan, row_pixel, channel_rows, height, width, skip):
    def one_channel(given):
        values, high, wide, weight = given
        image_order = jnp.zeros_like(values).at[row_pixel].set(values)
        pieces = []
        for part in plan.sections:
            side, count = part["side"], part["images"] * part["side"] ** 2
            block = image_order[part["pixel"] : part["pixel"] + count].reshape(-1, side, side)
            left = kernel_matrix(high[:, None], part)[:, :, 0]
            right = kernel_matrix(wide[:, None], part)[:, :, 0]
            mixed = jnp.einsum("ik,nkl,jl->nij", left, block, right, precision=lax.Precision.HIGHEST)
            pieces.append(mixed.reshape(-1))
        joined = jnp.concatenate(pieces) + weight * image_order
        return joined[row_pixel]

    return lax.map(jax.checkpoint(one_channel), (channel_rows, height.T, width.T, skip))


def exchange(blocks):
    return lax.all_to_all(blocks, "chan", 0, 0, tiled=True)


def to_blocks(rows, devices):
    return rows.T.reshape(devices, rows.shape[1] // devices, rows.shape[0])


def to_rows(blocks):
    return blocks.reshape(-1, blocks.shape[2]).T


def halve(blocks, bits):
    myself = lax.axis_index("chan")
    size = lax.axis_size("chan")
    pairs = lambda bit: [(i, i ^ 1 << bit) for i in range(size)]
    left = list(range(size.bit_length() - 1))
    for bit in bits:
        at = left.index(bit)
        viewed = blocks.reshape((-1, 2, 1 << at) + blocks.shape[1:])
        own = myself >> bit & 1
        keep = lax.dynamic_index_in_dim(viewed, own, 1, keepdims=False)
        send = lax.dynamic_index_in_dim(viewed, 1 - own, 1, keepdims=False)
        got = lax.ppermute(send, "chan", pairs(bit))
        total = keep.astype(F32) + got.astype(F32)
        left.remove(bit)
        blocks = (total if not left else total.astype(BF16)).reshape((-1,) + blocks.shape[1:])
    return blocks[0]


def swapped(x, bit):
    return lax.ppermute(x, "chan", [(i, i ^ 1 << bit) for i in range(lax.axis_size("chan"))])


def body_fast(
    tokens,
    row_pixel,
    coef_height,
    rate_height,
    coef_width,
    rate_width,
    skip_weight,
    norm_gain,
    norm_bias,
    weight_in,
    bias_in,
    weight_out,
    bias_out,
    layer_scale,
    out_grad,
):
    devices = lax.axis_size("chan")
    rows, width_all = tokens.shape
    plan = Plan(devices, rows, width_all // devices)
    token_blocks = exchange(to_blocks(tokens, devices))
    here = lax.axis_index("chan")
    bits = here >> jnp.arange(devices.bit_length() - 1) & 1

    where = plan.address(row_pixel)
    spread = plan.spread()
    taps = (plan.tile_taps(profiles(coef_height, rate_height)), plan.tile_taps(profiles(coef_width, rate_width)), plan.tile_taps(skip_weight[None]))
    mixed_blocks, packed, across = mixer_forward(plan, where, token_blocks, spread, *taps)

    scaled = out_grad.astype(F32) * layer_scale
    scaled_low = scaled.astype(BF16)
    rows_given = jnp.stack([layer_scale, bias_out, jnp.sum(scaled, axis=0)])
    grad_act = act_grads(scaled_low, weight_out)
    grad_normin, flipped, act, grad_pre, sums, pre_sum = feed(plan, exchange(mixed_blocks), norm_gain, norm_bias, weight_in, bias_in, grad_act)
    grad_blocks = exchange(grad_normin)
    out_keep, out_sent, scale_sum = out_grad_halves(plan, bits, act, scaled_low, weight_out, rows_given)
    out_got = [swapped(piece, 0) for piece in out_sent]
    in_keep, in_sent = in_grad_halves(plan, bits, flipped, grad_pre)
    in_got = [swapped(piece, 0) for piece in in_sent]
    shares = small_shares(plan, sums, pre_sum, rows_given, scale_sum, ())

    x, y, near_z, far_z = range(1, 5)
    in_keep, in_send, in_less, in_less_send, in_mark = first_merge(in_keep, in_got, ((0, x), (2, near_z)), bits, (grad_blocks,))
    out_keep, out_send, out_less, out_less_send, out_mark = first_merge(out_keep, out_got, ((1, y), (2, near_z)), bits, (grad_blocks,))
    gots = [swapped(in_send, x), swapped(out_send, y), swapped(in_less_send, near_z), swapped(out_less_send, near_z)]
    grads, mark = mixer_arrive(plan, where, grad_blocks, spread, (in_mark, out_mark, shares))
    keeps, sends, mark = merge((in_keep, out_keep, in_less, out_less), gots, (((0, y),), ((0, x),), ((2, far_z), (2, far_z))), bits, (mark,))
    gots = [swapped(send, bit) for send, bit in zip(sends, (y, x, far_z))]
    grads, *tap_sums = mixer_backward(plan, grads, *taps, packed, across, (mark,))
    leaving, left = mixer_leave(plan, where, grads, spread, shares, ())
    block_out = branch_out(act, weight_out, rows_given, tokens, (left,))
    (moved,) = held_back((leaving,), gots)
    grad_tokens, shares = token_grads(plan, exchange(moved), out_grad)
    keeps, sends, mark = merge(keeps, gots, (((0, near_z), (0, near_z)), ((0, x),)), bits)
    gots = [swapped(send, bit) for send, bit in zip(sends, (near_z, x))]
    coef_grads = tap_grads(plan, (coef_height, rate_height, coef_width, rate_width), spread.astype(F32), tap_sums, (mark,))
    keeps, sends, _ = merge(keeps, gots, (((0, far_z),), ((0, y),)), bits)
    gots = [swapped(send, bit) for send, bit in zip(sends, (far_z, y))]
    in_sum, out_sum = last_sums(
        (keeps[0], gots[0], keeps[1], gots[1]), plan.channels, weight_in.shape[1], (grad_tokens, shares, block_out, *coef_grads)
    )
    kinds = pre_sum.shape[1] // width_all
    gain_grad, norm_bias_grad, bias_out_grad, scale_grad = (shares[kind] for kind in (0, 1, 2 + kinds, 3 + kinds))
    bias_in_grad = shares[2 : 2 + kinds].reshape(-1)
    return (block_out, grad_tokens, *coef_grads, gain_grad, norm_bias_grad, in_sum, bias_in_grad, out_sum, bias_out_grad, scale_grad)


def body_plain(
    tokens,
    row_pixel,
    coef_height,
    rate_height,
    coef_width,
    rate_width,
    skip_weight,
    norm_gain,
    norm_bias,
    weight_in,
    bias_in,
    weight_out,
    bias_out,
    layer_scale,
    out_grad,
):
    devices = lax.axis_size("chan")
    rows, width_all = tokens.shape
    plan = Plan(devices, rows, width_all // devices)
    token_blocks = exchange(to_blocks(tokens, devices))

    height = profiles(coef_height, rate_height)
    width = profiles(coef_width, rate_width)
    lines = lambda blocks: blocks.transpose(1, 0, 2).reshape(blocks.shape[1], -1)
    blocks_of = lambda values: values.astype(BF16).reshape(-1, devices, rows).transpose(1, 0, 2)
    mixed, mixer_back = jax.vjp(
        functools.partial(mix_plain, plan, row_pixel), lines(token_blocks).astype(F32), height, width, skip_weight
    )
    mixed_blocks = blocks_of(mixed)
    normin = to_rows(exchange(mixed_blocks)).astype(F32)

    upstream = out_grad.astype(F32)
    scaled = upstream * layer_scale
    scaled_low = scaled.astype(BF16)
    grad_act = lax.dot_general(scaled_low, weight_out, (((1,), (1,)), ((), ())), preferred_element_type=F32)

    row_mean = jnp.mean(normin, axis=1, keepdims=True)
    centred = normin - row_mean
    inv_std = lax.rsqrt(jnp.mean(centred * centred, axis=1, keepdims=True) + EPSILON)
    unit_rows = centred * inv_std
    normed = (unit_rows * norm_gain + norm_bias).astype(BF16)
    hidden_pre = jnp.dot(normed, weight_in, preferred_element_type=F32) + bias_in
    cdf = 0.5 * (1.0 + lax.erf(hidden_pre * math.sqrt(0.5)))
    act_low = (hidden_pre * cdf).astype(BF16)
    slope = cdf + hidden_pre * jnp.exp(-0.5 * hidden_pre * hidden_pre) * (1.0 / math.sqrt(2.0 * math.pi))
    grad_pre = grad_act * slope
    grad_pre_low = grad_pre.astype(BF16)
    grad_normed = lax.dot_general(grad_pre_low, weight_in, (((1,), (1,)), ((), ())), preferred_element_type=F32)
    grad_unit = grad_normed * norm_gain
    grad_normin = inv_std * (
        grad_unit
        - jnp.mean(grad_unit, axis=1, keepdims=True)
        - unit_rows * jnp.mean(grad_unit * unit_rows, axis=1, keepdims=True)
    )
    grad_blocks = exchange(to_blocks(grad_normin.astype(BF16), devices))

    branch = jnp.dot(act_low, weight_out, preferred_element_type=F32) + bias_out
    block_out = (tokens.astype(F32) + layer_scale * branch).astype(BF16)
    small = (
        jnp.sum(grad_normed * unit_rows, axis=0),
        jnp.sum(grad_normed, axis=0),
        jnp.sum(grad_pre, axis=0),
        jnp.sum(scaled, axis=0),
        jnp.sum(upstream * branch, axis=0),
    )
    weight_in_part = lax.dot_general(normed, grad_pre_low, (((0,), (0,)), ((), ())), preferred_element_type=F32)
    weight_out_part = lax.dot_general(act_low, scaled_low, (((0,), (0,)), ((), ())), preferred_element_type=F32)

    grad_mixed, grad_height, grad_width, grad_skip = mixer_back(lines(grad_blocks).astype(F32))
    grad_rows = blocks_of(grad_mixed)
    coef_height_grad, rate_height_grad = profile_grads(coef_height, rate_height, grad_height)
    coef_width_grad, rate_width_grad = profile_grads(coef_width, rate_width, grad_width)
    grad_tokens = upstream + to_rows(exchange(grad_rows)).astype(F32)

    levels = list(range(devices.bit_length() - 1))
    other = levels[:1] + levels[1:3][::-1] + levels[3:]
    in_sum = halve(weight_in_part.astype(BF16).reshape(devices, -1, weight_in.shape[1]), levels)
    out_sum = halve(weight_out_part.astype(BF16).reshape(devices, -1, weight_out.shape[1]), other)
    shares = jnp.concatenate([s.reshape(devices, -1) for s in small], axis=1)
    shares = exchange(shares).sum(axis=0)
    cuts = np.cumsum([s.shape[0] // devices for s in small])[:-1]
    gain_grad, norm_bias_grad, bias_in_grad, bias_out_grad, scale_grad = jnp.split(shares, cuts)
    return (
        block_out,
        grad_tokens,
        coef_height_grad,
        rate_height_grad,
        coef_width_grad,
        rate_width_grad,
        grad_skip,
        gain_grad,
        norm_bias_grad,
        in_sum,
        bias_in_grad,
        out_sum,
        bias_out_grad,
        scale_grad,
    )


def solution(mesh):
    split, copied = P("chan"), P()

    def body(tokens, *rest):
        devices = lax.axis_size("chan")
        fast = Plan(devices, tokens.shape[0], tokens.shape[1] // devices).fits() and devices == 32
        return (body_fast if fast else body_plain)(tokens, *rest)

    in_specs = (split, copied) + (split,) * 5 + (copied,) * 7 + (split,)
    return jax.shard_map(body, mesh=mesh, in_specs=in_specs, out_specs=(split,) * 14, check_vma=False)
```

```python
import functools
import math

import jax
import jax.numpy as jnp
import numpy as np
from jax import lax
from jax.experimental import pallas as pl
from jax.experimental.pallas import tpu as pltpu
from jax.sharding import PartitionSpec as P

SIDES = (10, 14, 18)
SHARES = (1, 1, 2)
UNIT = sum(m * s * s for s, m in zip(SIDES, SHARES))
TAPS = sum(SIDES)
EPSILON = 1e-06
LANES = 128
SUB = 8
MARGIN = 32
VMEM = 63 * 2**20
LESS = 36 * 2**20
SMALL = 20 * 2**20
CHUNKS = 3
F32 = jnp.float32
BF16 = jnp.bfloat16


class Plan:
    def __init__(self, devices, rows, channels):
        self.devices, self.rows, self.channels = devices, rows, channels
        self.pixels = devices * rows
        self.units = self.pixels // UNIT
        self.slots = LANES // channels
        self.row_pad = -(-rows // LANES) * LANES
        self.extra_row = -(-rows // SUB) * SUB
        self.sections = []
        image_row, packed_row, tap, mask_row, pixel = 0, 0, 0, 0, 0
        for side, share in zip(SIDES, SHARES):
            images = share * self.units
            pitch = -(-side // SUB) * SUB
            groups = -(-images // self.slots)
            self.sections.append(
                dict(side=side, images=images, pitch=pitch, groups=groups, image_row=image_row, packed_row=packed_row, tap=tap, mask_row=mask_row, pixel=pixel)
            )
            image_row += groups * self.slots * side * pitch
            packed_row += groups * side * pitch
            tap += side
            mask_row += side * pitch
            pixel += images * side * side
        self.image_rows = image_row
        self.packed_rows = packed_row
        self.mask_rows = mask_row

    @property
    def extra_lane(self):
        return self.extra_row - (self.row_pad - LANES)

    def kind(self, lane, which):
        return (lane == self.extra_lane + which) | (lane == self.extra_lane + SUB + which)

    def fits(self):
        room = self.row_pad - self.extra_row >= 2 * SUB
        return room and self.channels % SUB == 0 and 4 * LANES * (self.image_rows + 2 * self.row_pad + 5 * self.packed_rows) < 40 * 2**20

    def address(self, row_pixel):
        where = jnp.zeros_like(row_pixel)
        for part in self.sections:
            local = row_pixel - part["pixel"]
            line = local // part["side"]
            spot = part["image_row"] + line * part["pitch"] + local - line * part["side"]
            where = jnp.where(local >= 0, spot, where)
        return where

    def spread(self):
        lane = np.arange(LANES)
        held = (lane[None, :] % self.channels == np.arange(self.channels)[:, None]) & (lane[None, :] < self.slots * self.channels)
        return jnp.asarray(held.astype(np.float32), BF16)

    def tile_taps(self, taps):
        tiled = jnp.tile(taps, (1, self.slots))
        return jnp.pad(tiled, ((0, 0), (0, LANES - tiled.shape[1])))


def slot_masks(plan):
    lane = lax.broadcasted_iota(jnp.int32, (SUB, LANES), 1)
    return [(lane >= q * plan.channels) & (lane < (q + 1) * plan.channels) for q in range(plan.slots)]


def in_turn(plan, first, second, beside=None, steps=0, ready=None):
    first(0, 0)

    def pair(k):
        first(2 * k + 1, 1)
        second(2 * k, 0)
        first(2 * k + 2, 0)
        second(2 * k + 1, 1)

    def plain(k, carry):
        pair(k)
        return carry

    def more(k, carry):
        beside(k - begin)
        pair(k)
        return carry

    pairs = plan.devices // 2 - 1
    begin = pairs - steps
    lax.fori_loop(0, begin, plain, 0)
    if steps:
        ready()
        lax.fori_loop(begin, pairs, more, 0)
    first(plan.devices - 1, 1)
    second(plan.devices - 2, 0)
    second(plan.devices - 1, 1)


def scatter_rows(plan, where, block, buffers, image, beside=None, steps=0, ready=None):
    def turn(s, held):
        rows = block[s].astype(F32)
        full = [rows] * plan.slots
        if LANES > plan.slots * plan.channels:
            full.append(rows[: LANES - plan.slots * plan.channels])
        buffers[held][pl.ds(0, plan.rows), :] = jnp.concatenate(full, axis=0).T

    def place(s, held):
        base = s * plan.rows
        for u in range(plan.rows):
            image[pl.ds(where[base + u], 1), :] = buffers[held][pl.ds(u, 1), :]

    in_turn(plan, turn, place, beside, steps, ready)


def gather_rows(plan, where, buffers, image, out, extra=None):
    def fetch(s, held):
        base = s * plan.rows
        for u in range(plan.rows):
            buffers[held][pl.ds(u, 1), :] = image[pl.ds(where[base + u], 1), :]

    def fold(s, held):
        turned = buffers[held][...].T
        folded = turned[: plan.channels]
        for q in range(1, plan.slots):
            folded = folded + turned[q * plan.channels : (q + 1) * plan.channels]
        if extra is None:
            out[s] = folded[:, : plan.rows].astype(BF16)
            return
        last = plan.row_pad - LANES
        exact = extra[pl.ds(pl.multiple_of(s * plan.channels, SUB), plan.channels), :]
        high = exact.astype(BF16).astype(F32)
        lane = lax.broadcasted_iota(jnp.int32, exact.shape, 1) + last
        sums = jnp.where(lane < plan.extra_row + SUB, high, exact - high)
        out[s, :, pl.ds(0, last)] = folded[:, :last].astype(BF16)
        out[s, :, pl.ds(last, LANES)] = jnp.where(lane < plan.extra_row, folded[:, last:], sums).astype(BF16)

    in_turn(plan, fetch, fold)


def pack_images(plan, masks, image, packed, margin):
    place = lax.broadcasted_iota(jnp.int32, (SUB, LANES), 0)
    for part in plan.sections:
        side, pitch = part["side"], part["pitch"]
        area = side * pitch
        ragged = part["images"] < part["groups"] * plan.slots

        def group(t, carry, part=part, side=side, pitch=pitch, area=area, ragged=ragged):
            start = part["image_row"] + t * (plan.slots * area)
            target = margin + part["packed_row"] + t * area
            used = masks
            if ragged:
                used = [mask & (t * plan.slots + q < part["images"]) for q, mask in enumerate(masks)]
            ends = [mask & (place < side % SUB) for mask in used]
            for i in range(side):
                for j in range(0, pitch, SUB):
                    value = jnp.zeros((SUB, LANES), F32)
                    for q in range(plan.slots):
                        row = pl.multiple_of(start + (q * area + i * pitch + j), SUB)
                        value = jnp.where((ends if j + SUB > side else used)[q], image[pl.ds(row, SUB), :], value)
                    packed[pl.ds(pl.multiple_of(target + (i * pitch + j), SUB), SUB), :] = value
            return carry

        lax.fori_loop(0, part["groups"], group, 0)


def unpack_line(plan, masks, part, t, offset, value, image):
    area = part["side"] * part["pitch"]
    for q in range(plan.slots):
        row = pl.multiple_of(part["image_row"] + (t * plan.slots + q) * area + offset, SUB)
        image[pl.ds(row, SUB), :] = jnp.where(masks[q], value, 0.0)


def wide_taps(plan, taps, table):
    for tap in range(TAPS):
        table[pl.ds(tap * SUB, SUB), :] = jnp.broadcast_to(taps[pl.ds(tap, 1), :], (SUB, LANES))


def masked_taps(plan, taps, table):
    for part in plan.sections:
        side, pitch = part["side"], part["pitch"]
        place = lax.broadcasted_iota(jnp.int32, (pitch, LANES), 0)
        for tap in range(side):
            row = taps[pl.ds(part["tap"] + tap, 1), :]
            table[pl.ds(part["mask_row"] + tap * pitch, pitch), :] = jnp.where(place >= tap, row, 0.0)


def forward_kernel(plan, where_far, block, height, width, skip, out, packed, across, first, second, image, where, px, pu, height_wide, width_masked, sems):
    masks = slot_masks(plan)
    indices = pltpu.make_async_copy(where_far, where, sems.at[0])
    indices.start()
    px[pl.ds(0, MARGIN), :] = jnp.zeros((MARGIN, LANES), F32)
    wide_taps(plan, height, height_wide)
    masked_taps(plan, width, width_masked)
    indices.wait()
    scatter_rows(plan, where, block, (first, second), image)
    pack_images(plan, masks, image, px, MARGIN)
    skips = jnp.broadcast_to(skip[...], (SUB, LANES))
    for part in plan.sections:
        side, pitch = part["side"], part["pitch"]
        area = side * pitch

        def group(t, carry, part=part, side=side, pitch=pitch, area=area):
            start = MARGIN + part["packed_row"] + t * area

            def line(i, inner):
                base = start + i * pitch
                for j in range(0, pitch, SUB):
                    total = jnp.zeros((SUB, LANES), F32)
                    for tap in range(min(side, j + SUB)):
                        weight = width_masked[pl.ds(part["mask_row"] + tap * pitch + j, SUB), :]
                        total = total + weight * px[pl.ds(base + j - tap, SUB), :]
                    pu[pl.ds(pl.multiple_of(base + j, SUB), SUB), :] = total
                return inner

            lax.fori_loop(0, side, line, 0)

            def column(c, inner):
                first = pl.multiple_of(start + c * SUB, SUB)
                held = [pu[pl.ds(pl.multiple_of(first + k * pitch, SUB), SUB), :] for k in range(side)]
                for i in range(side):
                    total = skips * px[pl.ds(pl.multiple_of(first + i * pitch, SUB), SUB), :]
                    for k in range(i + 1):
                        total = total + height_wide[pl.ds((part["tap"] + i - k) * SUB, SUB), :] * held[k]
                    unpack_line(plan, masks, part, t, i * pitch + c * SUB, total, image)
                return inner

            lax.fori_loop(0, pitch // SUB, column, 0)
            return carry

        lax.fori_loop(0, part["groups"], group, 0)
    kept = [(px.at[pl.ds(MARGIN, plan.packed_rows)], packed), (pu.at[pl.ds(MARGIN, plan.packed_rows)], across)]
    kept = started(kept, sems.at[pl.ds(1, 2)])
    gather_rows(plan, where, (first, second), image, out)
    for copy in kept:
        copy.wait()


def arrive_kernel(plan, where_far, block_far, act_far, weight_far, given_far, tokens_far, out_grad_far, sums_far, pre_sum_far, *rest):
    grads, block_out, shares, mark, *rest = rest[-20:]
    where, block, first, second, image, act, weight_out, given, tokens, out_grad, sums, pre_sum, branch, rows, came, sems = rest
    mark[...] = jnp.zeros_like(mark)
    soon = started([(block_far, block), (where_far, where)], came.at[pl.ds(2, 2)])
    arriving = started([(act_far, act), (weight_far, weight_out)], came.at[pl.ds(0, 2)])
    there = [(given_far, given), (tokens_far, tokens), (out_grad_far, out_grad), (sums_far, sums), (pre_sum_far, pre_sum)]
    later = started(there, sems)

    def ready():
        for copy in arriving:
            copy.wait()

    def product(k):
        lanes = pl.ds(pl.multiple_of(k * LANES, LANES), LANES)
        branch[:, lanes] = jnp.dot(act[...], weight_out[:, lanes], preferred_element_type=F32)

    for copy in soon:
        copy.wait()
    scatter_rows(plan, where, block, (first, second), image, product, tokens.shape[1] // LANES, ready)
    for copy in later:
        copy.wait()
    scale, bias_out, bias_row = (given[pl.ds(i, 1), :] for i in range(3))
    total = branch[...] + bias_out
    block_out[...] = (tokens[...].astype(F32) + scale * total).astype(BF16)
    scale_row = jnp.sum(out_grad[...].astype(F32) * total, axis=0, keepdims=True)
    shares[...] = small_shares(plan, sums[...], pre_sum[...], bias_row, scale_row, rows)
    pack_images(plan, slot_masks(plan), image, grads, 0)


def leave_kernel(plan, where_far, grads, extra, *rest):
    out, mark, near, far, image, where, sem = rest[-7:]
    indices = pltpu.make_async_copy(where_far, where, sem)
    indices.start()
    mark[...] = jnp.zeros_like(mark)
    masks = slot_masks(plan)
    for part in plan.sections:
        area = part["side"] * part["pitch"]

        def group(t, carry, part=part, area=area):
            for offset in range(0, area, SUB):
                row = pl.multiple_of(part["packed_row"] + t * area + offset, SUB)
                unpack_line(plan, masks, part, t, offset, grads[pl.ds(row, SUB), :], image)
            return carry

        lax.fori_loop(0, part["groups"], group, 0)
    indices.wait()
    gather_rows(plan, where, (near, far), image, out, extra)


def backward_kernel(plan, pg, height, width, skip, packed_far, across_far, *rest):
    out, height_sums, width_sums, skip_sums, mark, pd, height_wide, width_wide, packed, across, sems = rest[-11:]
    mark[...] = jnp.zeros_like(mark)
    arriving = started([(across_far, across), (packed_far, packed)], sems)
    place = lax.broadcasted_iota(jnp.int32, (SUB, LANES), 0)
    pd[pl.ds(plan.packed_rows, MARGIN), :] = jnp.zeros((MARGIN, LANES), F32)
    wide_taps(plan, height, height_wide)
    wide_taps(plan, width, width_wide)
    skips = jnp.broadcast_to(skip[...], (SUB, LANES))
    skip_sums[...] = jnp.zeros((SUB, LANES), F32)
    height_sums[...] = jnp.zeros((TAPS * SUB, LANES), F32)
    for part in plan.sections:
        side, pitch = part["side"], part["pitch"]
        area = side * pitch

        def group(t, carry, part=part, side=side, pitch=pitch, area=area):
            start = part["packed_row"] + t * area

            def column(c, inner):
                first = pl.multiple_of(start + c * SUB, SUB)
                rows = [pl.ds(pl.multiple_of(first + k * pitch, SUB), SUB) for k in range(side)]
                held = [pg[row, :] for row in rows]
                for k in range(side):
                    total = jnp.zeros((SUB, LANES), F32)
                    for i in range(k, side):
                        total = total + height_wide[pl.ds((part["tap"] + i - k) * SUB, SUB), :] * held[i]
                    pd[rows[k], :] = total
                return inner

            lax.fori_loop(0, pitch // SUB, column, 0)
            return carry

        lax.fori_loop(0, part["groups"], group, 0)
    arriving[0].wait()
    for part in plan.sections:
        side, pitch = part["side"], part["pitch"]
        area = side * pitch

        def group(t, carry, part=part, side=side, pitch=pitch, area=area):
            start = part["packed_row"] + t * area

            def column(c, inner):
                first = pl.multiple_of(start + c * SUB, SUB)
                rows = [pl.ds(pl.multiple_of(first + k * pitch, SUB), SUB) for k in range(side)]
                held = [pg[row, :] for row in rows]
                ways = [across[row, :] for row in rows]
                for tap in range(side):
                    total = held[tap] * ways[0]
                    for k in range(1, side - tap):
                        total = total + held[k + tap] * ways[k]
                    height_sums[pl.ds((part["tap"] + tap) * SUB, SUB), :] += total
                return inner

            lax.fori_loop(0, pitch // SUB, column, 0)
            return carry

        lax.fori_loop(0, part["groups"], group, 0)
    arriving[1].wait()
    for part in plan.sections:
        side, pitch = part["side"], part["pitch"]
        area = side * pitch

        def group(t, carry, part=part, side=side, pitch=pitch, area=area):
            start = part["packed_row"] + t * area

            def line(i, sums):
                sums = list(sums)
                base = start + i * pitch
                aligned = pl.multiple_of(base, SUB)
                for j in range(0, pitch, SUB):
                    here = pl.ds(pl.multiple_of(aligned + j, SUB), SUB)
                    mine, grad = packed[here, :], pg[here, :]
                    total = skips * grad
                    sums[side] = sums[side] + mine * grad
                    for tap in range(min(side, side - j)):
                        moved = pd[pl.ds(base + j + tap, SUB), :]
                        if j + SUB - 1 + tap >= pitch:
                            moved = jnp.where(place + (j + tap) < side, moved, 0.0)
                        total = total + width_wide[pl.ds((part["tap"] + tap) * SUB, SUB), :] * moved
                        sums[tap] = sums[tap] + mine * moved
                    out[here, :] = total
                return tuple(sums)

            return lax.fori_loop(0, side, line, carry)

        zero = jnp.zeros((SUB, LANES), F32)
        sums = lax.fori_loop(0, part["groups"], group, (zero,) * (side + 1))
        for tap in range(side):
            width_sums[pl.ds((part["tap"] + tap) * SUB, SUB), :] = sums[tap]
        skip_sums[...] += sums[side]


def whole(memory):
    return pl.BlockSpec(memory_space=memory)


def lanes_of(rows):
    return jax.ShapeDtypeStruct((rows, LANES), F32)


def row_buffers(plan):
    return [pltpu.VMEM((plan.row_pad, LANES), F32)] * 2 + [pltpu.VMEM((plan.image_rows, LANES), F32)]


def near(values):
    return pltpu.with_memory_space_constraint(values, pltpu.VMEM)


def distant(values):
    return pltpu.with_memory_space_constraint(values, pltpu.HBM)


def kernel_call(kernel, name, micros, memories, out_shape, scratch, args, after=(), stays=(), held=(), left=()):
    single = not isinstance(out_shape, tuple)
    shapes = (out_shape,) if single else out_shape
    shapes = tuple((pltpu.VMEM if i in stays else pltpu.HBM)(o.shape, o.dtype) for i, o in enumerate(shapes))
    outs = tuple(whole(pltpu.VMEM) for _ in shapes)
    place = lambda i, value: near(value) if i in held else value if memories[i] is pltpu.SMEM or i in left else distant(value)
    out = pl.pallas_call(
        kernel,
        out_shape=shapes,
        in_specs=[whole(m) for m in memories] + [whole(pltpu.HBM)] * len(after),
        out_specs=outs,
        scratch_shapes=scratch,
        compiler_params=pltpu.CompilerParams(vmem_limit_bytes=LESS if stays or held else VMEM),
        cost_estimate=pl.CostEstimate(flops=1_000_000, bytes_accessed=int(3_690_000 * micros), transcendentals=0),
        name=name,
    )(*[place(i, value) for i, value in enumerate(args)], *map(distant, after))
    return out[0] if single else out


def mixer_forward(plan, where, block, height, width, skip):
    rows = plan.packed_rows
    ins = [(where, FAR), (block, NEAR), (height, AUTO), (width, AUTO), (skip, AUTO)]
    outs = [(block.shape, BF16, AUTO), ((rows, LANES), F32, FAR), ((rows, LANES), F32, FAR)]
    room = row_buffers(plan) + [
        pltpu.SMEM(where.shape, jnp.int32),
        pltpu.VMEM((rows + MARGIN, LANES), F32),
        pltpu.VMEM((rows + MARGIN, LANES), F32),
        pltpu.VMEM((TAPS * SUB, LANES), F32),
        pltpu.VMEM((plan.mask_rows, LANES), F32),
        pltpu.SemaphoreType.DMA((3,)),
    ]
    return run(functools.partial(forward_kernel, plan), "mixer_forward", ins, outs, room, micros=30, limit=LESS)


def mixer_arrive(plan, where, block, act, weight_out, given, tokens, out_grad, sums, pre_sum, after):
    ins = [(value, FAR) for value in (where, block, act, weight_out, given, tokens, out_grad, sums, pre_sum)]
    width = tokens.shape[1]
    outs = [((plan.packed_rows, LANES), F32, NEAR), (tokens.shape, BF16, AUTO), ((width, LANES), F32, AUTO), ((SUB, LANES), F32, AUTO)]
    room = [pltpu.SMEM(where.shape, jnp.int32), pltpu.VMEM(block.shape, BF16)] + row_buffers(plan) + [pltpu.VMEM(value.shape, value.dtype) for value in (act, weight_out, given, tokens, out_grad, sums, pre_sum)]
    room += [pltpu.VMEM(tokens.shape, F32), pltpu.VMEM((LANES, width), F32), pltpu.SemaphoreType.DMA((4,)), pltpu.SemaphoreType.DMA((5,))]
    return run(functools.partial(arrive_kernel, plan), "mixer_arrive", ins, outs, room, after, limit=LESS)


def mixer_backward(plan, grads, height, width, skip, packed, across, after):
    rows = plan.packed_rows
    ins = [(grads, NEAR), (height, AUTO), (width, AUTO), (skip, AUTO), (packed, FAR), (across, FAR)]
    outs = [((rows, LANES), F32, NEAR)] + [((size, LANES), F32, AUTO) for size in (TAPS * SUB, TAPS * SUB, SUB, SUB)]
    room = [pltpu.VMEM((size, LANES), F32) for size in (rows + MARGIN, TAPS * SUB, TAPS * SUB, rows, rows)]
    room += [pltpu.SemaphoreType.DMA((2,))]
    return run(functools.partial(backward_kernel, plan), "mixer_backward", ins, outs, room, after, limit=LESS)


def mixer_leave(plan, where, grads, extra, after):
    ins = [(where, FAR), (grads, NEAR), (extra, AUTO)]
    outs = [((plan.devices, plan.channels, plan.row_pad), BF16, AUTO), ((SUB, LANES), F32, AUTO)]
    room = row_buffers(plan) + [pltpu.SMEM(where.shape, jnp.int32), pltpu.SemaphoreType.DMA]
    return run(functools.partial(leave_kernel, plan), "mixer_leave", ins, outs, room, after, limit=LESS)


def taps_kernel(plan, coef_height, rate_height, coef_width, rate_width, spread, height_sums, width_sums, skip_sums, *rest):
    outs = rest[-5:]
    reach, scale = tap_places()
    fold = lambda sums: lax.dot_general(spread[...], sums, (((1,), (1,)), ((), ())), precision=lax.Precision.HIGHEST, preferred_element_type=F32)
    for coef, log_rate, sums, coef_out, rate_out in (
        (coef_height, rate_height, height_sums, outs[0], outs[1]),
        (coef_width, rate_width, width_sums, outs[2], outs[3]),
    ):
        grads = fold(sums[...].reshape(TAPS, SUB, LANES).sum(axis=1))
        rate = jnp.exp(log_rate[...])
        plain, moved = jnp.zeros_like(rate), jnp.zeros_like(rate)
        for tap in range(TAPS):
            weighted = (grads[:, tap : tap + 1] * float(scale[tap])) * jnp.exp(rate * float(-reach[tap]))
            plain = plain + weighted
            moved = moved + weighted * float(reach[tap])
        coef_out[...] = plain
        rate_out[...] = -coef[...] * rate * moved
    total = jnp.sum(skip_sums[...], axis=0, keepdims=True)
    outs[4][...] = lax.dot_general(total, spread[...], (((1,), (1,)), ((), ())), precision=lax.Precision.HIGHEST, preferred_element_type=F32)


def tap_grads(plan, coefs, spread, sums, after):
    shape = jax.ShapeDtypeStruct(coefs[0].shape, F32)
    outs = (shape,) * 4 + (jax.ShapeDtypeStruct((1, plan.channels), F32),)
    *grads, skips = kernel_call(functools.partial(taps_kernel, plan), "tap_grads", 0.01, [pltpu.VMEM] * 8, outs, [], (*coefs, spread, *sums), after)
    return *grads, skips[0]


def tokens_kernel(plan, blocks, out_grad, out, *rest):
    smalls, flipped = rest[:-1], rest[-1]
    total = jnp.zeros((plan.channels, LANES), F32)
    for s in range(plan.devices):
        block = blocks[s].astype(F32)
        flipped[pl.ds(s * plan.channels, plan.channels), :] = block[:, : plan.rows]
        total = total + block[:, plan.row_pad - LANES :]
    first = plan.extra_lane
    rows = total.T
    rows = rows[first : first + SUB] + rows[first + SUB : first + 2 * SUB]
    kind = 0
    for small in smalls:
        for i in range(small.shape[1] // plan.channels):
            small[:, pl.ds(i * plan.channels, plan.channels)] = rows[kind : kind + 1]
            kind += 1
    out[...] = out_grad[...].astype(F32) + flipped[...].T


def token_grads(plan, blocks, out_grad, kinds):
    outs = [(out_grad.shape, F32, AUTO)] + [((1, count * plan.channels), F32, AUTO) for count in (1, 1, kinds, 1, 1)]
    room = [pltpu.VMEM(out_grad.shape[::-1], F32)]
    return run(functools.partial(tokens_kernel, plan), "token_grads", [(blocks, NEAR), (out_grad, AUTO)], outs, room)


def started(pairs, sems):
    copies = [pltpu.make_async_copy(source, target, sems.at[i]) for i, (source, target) in enumerate(pairs)]
    for copy in copies:
        copy.start()
    return copies


NEAR, FAR, AUTO, OPEN, SCALAR = "near", "far", "auto", "open", "scalar"


def run(kernel, name, ins, outs, scratch, after=(), micros=0.01, limit=VMEM):
    same = lambda value: value
    memory = {NEAR: pltpu.VMEM, FAR: pltpu.HBM, AUTO: pltpu.VMEM, OPEN: pltpu.VMEM, SCALAR: pltpu.SMEM}
    hold = {NEAR: near, FAR: distant, AUTO: distant, OPEN: same, SCALAR: same}
    make = {NEAR: pltpu.VMEM, FAR: pltpu.HBM, AUTO: pltpu.HBM, OPEN: jax.ShapeDtypeStruct}
    return pl.pallas_call(
        kernel,
        out_shape=tuple(make[place](shape, dtype) for shape, dtype, place in outs),
        in_specs=[whole(memory[place]) for _, place in ins] + [whole(pltpu.HBM)] * len(after),
        out_specs=tuple(whole(memory[place]) for _, _, place in outs),
        scratch_shapes=scratch,
        compiler_params=pltpu.CompilerParams(vmem_limit_bytes=limit),
        cost_estimate=pl.CostEstimate(flops=1000, bytes_accessed=int(3_690_000 * micros), transcendentals=0),
        name=name,
    )(*[hold[place](value) for value, place in ins], *map(distant, after))


def feed_kernel(plan, blocks, gain, bias, weight_far, bias_in, grad_act_far, grads, flipped, act_far, grad_pre_far, sums, pre_sum, *scratch):
    normed, unit, total, weight_in, grad_act, act, grad_pre, came, left = scratch
    channels, count = plan.channels, plan.devices
    width, hidden = weight_in.shape
    tile, group = 256, 3
    steps = hidden // (tile * group)
    chunk = lambda step: pl.ds(pl.multiple_of(step * (tile * group), tile * group), tile * group)

    def arriving(step):
        return [
            pltpu.make_async_copy(weight_far.at[:, chunk(step)], weight_in.at[:, chunk(step)], came.at[0, step]),
            pltpu.make_async_copy(grad_act_far.at[:, chunk(step)], grad_act.at[:, chunk(step)], came.at[1, step]),
        ]

    def leaving(step):
        return [
            pltpu.make_async_copy(act.at[:, chunk(step)], act_far.at[:, chunk(step)], left.at[0, step]),
            pltpu.make_async_copy(grad_pre.at[:, chunk(step)], grad_pre_far.at[:, chunk(step)], left.at[1, step]),
        ]

    for step in range(steps):
        for copy in arriving(step):
            copy.start()
    for s in range(count):
        unit[pl.ds(s * channels, channels), :] = blocks[s].astype(F32)
    mean = jnp.sum(unit[...], axis=0, keepdims=True) * (1.0 / width)
    centred = unit[...] - mean
    inverse = lax.rsqrt(jnp.sum(centred * centred, axis=0, keepdims=True) * (1.0 / width) + EPSILON)
    unit[...] = centred * inverse
    scaled = unit[...] * gain[...] + bias[...]
    flipped[...] = scaled.astype(BF16)
    normed[...] = scaled.T.astype(BF16)
    total[...] = jnp.zeros_like(total)

    def tiles(step, carry):
        for copy in arriving(step):
            copy.wait()
        for c in range(group):
            at = pl.ds(pl.multiple_of((step * group + c) * tile, tile), tile)
            pre = jnp.dot(normed[...], weight_in[:, at], preferred_element_type=F32) + bias_in[:, at]
            cdf = 0.5 * (1.0 + lax.erf(pre * math.sqrt(0.5)))
            act[:, at] = (pre * cdf).astype(BF16)
            slope = cdf + pre * jnp.exp(-0.5 * pre * pre) * (1.0 / math.sqrt(2.0 * math.pi))
            grad = grad_act[:, at] * slope
            pre_sum[:, at] = jnp.sum(grad, axis=0, keepdims=True)
            low = grad.astype(BF16)
            grad_pre[:, at] = low
            total[...] += lax.dot_general(low, weight_in[:, at], (((1,), (1,)), ((), ())), preferred_element_type=F32)
        for copy in leaving(step):
            copy.start()
        return carry

    lax.fori_loop(0, steps, tiles, 0)
    turned = total[...].T
    lane = lax.broadcasted_iota(jnp.int32, sums.shape, 1)
    sums[...] = jnp.where(
        plan.kind(lane, 0),
        jnp.sum(turned * unit[...], axis=1, keepdims=True),
        jnp.where(plan.kind(lane, 1), jnp.sum(turned, axis=1, keepdims=True), 0.0),
    )
    grad = turned * gain[...]
    level = jnp.sum(grad, axis=0, keepdims=True) * (1.0 / width)
    tilt = jnp.sum(grad * unit[...], axis=0, keepdims=True) * (1.0 / width)
    total_low = (inverse * (grad - level - unit[...] * tilt)).astype(BF16)
    for s in range(count):
        grads[s] = total_low[s * channels : (s + 1) * channels]
    for step in range(steps):
        for copy in leaving(step):
            copy.wait()


def feed(plan, blocks, gain, bias, weight_in, bias_in, grad_act):
    rows, width, hidden = plan.rows, plan.devices * plan.channels, weight_in.shape[1]
    steps = hidden // 768
    ins = [(blocks, NEAR), (gain[:, None], AUTO), (bias[:, None], AUTO), (weight_in, FAR), (bias_in[None], AUTO), (grad_act, FAR)]
    outs = [
        (blocks.shape, BF16, AUTO),
        ((width, rows), BF16, AUTO),
        ((rows, hidden), BF16, FAR),
        ((rows, hidden), BF16, FAR),
        ((width, LANES), F32, AUTO),
        ((1, hidden), F32, AUTO),
    ]
    room = [
        pltpu.VMEM((rows, width), BF16),
        pltpu.VMEM((width, rows), F32),
        pltpu.VMEM((rows, width), F32),
        pltpu.VMEM((width, hidden), BF16),
        pltpu.VMEM((rows, hidden), F32),
        pltpu.VMEM((rows, hidden), BF16),
        pltpu.VMEM((rows, hidden), BF16),
        pltpu.SemaphoreType.DMA((2, steps)),
        pltpu.SemaphoreType.DMA((2, steps)),
    ]
    return run(functools.partial(feed_kernel, plan), "feed_forward", ins, outs, room, micros=10, limit=LESS)


def out_grad_kernel(act_far, scaled_far, keep_far, *rest):
    sent, (act, scaled, keep, other, came, left) = rest[:-6], rest[-6:]
    core = own_bit(0)
    chunks, chips, high, width = keep.shape
    height, steps = chunks * high, came.shape[0] - 1
    tile, each, part = act.shape[1] // steps, chips // steps, chips // len(sent)
    parts = [pl.ds(i * tile, tile) for i in range(steps)]
    arriving, leaving = started([(scaled_far, scaled)] + [(act_far.at[:, at], act.at[:, at]) for at in parts], came), []
    arriving[0].wait()
    for i, at in enumerate(parts):
        arriving[1 + i].wait()
        low = lax.dot_general(act[:, at], scaled[...], (((0,), (0,)), ((), ())), preferred_element_type=F32).astype(BF16)
        for c in range(each):
            first = low[2 * c * height : (2 * c + 1) * height]
            second = low[(2 * c + 1) * height : (2 * c + 2) * height]
            mine, yours = jnp.where(core == 0, first, second), jnp.where(core == 0, second, first)
            for chunk in range(chunks):
                keep[chunk, i * each + c] = mine[chunk * high : (chunk + 1) * high]
                other[chunk, i * each + c] = yours[chunk * high : (chunk + 1) * high]
        some = pl.ds(i * each, each)
        there = [(other.at[:, pl.ds(p * part, part)], sent[p]) for p in range(i * each // part, (i + 1) * each // part)]
        there += [(keep.at[:, some], keep_far.at[:, some])]
        leaving += started(there, left.at[pl.ds(len(leaving), len(there))])
    for copy in leaving:
        copy.wait()


def out_grad_halves(plan, act, scaled):
    hidden, width, chips = act.shape[1], scaled.shape[1], plan.devices // 2
    high, steps, pieces = hidden // plan.devices // CHUNKS, hidden // 768, 4
    ins = [(act, FAR), (scaled, FAR)]
    outs = [((CHUNKS, chips, high, width), BF16, FAR)] + [((CHUNKS, chips // pieces, high, width), BF16, FAR)] * pieces
    room = [pltpu.VMEM(value.shape, BF16) for value in (act, scaled)] + [pltpu.VMEM(outs[0][0], BF16)] * 2
    room += [pltpu.SemaphoreType.DMA((1 + steps,)), pltpu.SemaphoreType.DMA((pieces + steps,))]
    keep, *sent = run(out_grad_kernel, "out_grad_halves", ins, outs, room)
    return keep, sent


def own_bit(bit):
    return lax.axis_index("chan") >> bit & 1


def lane_parts(width, count):
    return [pl.ds(p * (width // count), width // count) for p in range(count)]


def retiled(values, width):
    tiles = [values[r : r + SUB, c : c + LANES] for r in range(0, values.shape[0], SUB) for c in range(0, values.shape[1], LANES)]
    each = width // LANES
    return jnp.concatenate([jnp.concatenate(tiles[i : i + each], axis=1) for i in range(0, len(tiles), each)], axis=0)


def in_grad_kernel(flipped_far, grad_pre_far, keep_far, *rest):
    sent, (flipped, grad_pre, keep, other, came, left) = rest[:-6], rest[-6:]
    chunks, chips, _, width = keep.shape
    height, tile, each = flipped.shape[0] // chips // 2, grad_pre.shape[1] // chunks, len(sent) // chunks
    core = own_bit(0)
    parts = [pl.ds(i * tile, tile) for i in range(chunks)]
    arriving = started([(flipped_far, flipped)] + [(grad_pre_far.at[:, at], grad_pre.at[:, at]) for at in parts], came)
    arriving[0].wait()
    leaving = []
    for i, at in enumerate(parts):
        arriving[1 + i].wait()
        total = jnp.dot(flipped[...], grad_pre[:, at], preferred_element_type=F32)
        for c in range(chips):
            first = total[2 * c * height : (2 * c + 1) * height]
            second = total[(2 * c + 1) * height : (2 * c + 2) * height]
            keep[i, c] = retiled(jnp.where(core == 0, first, second), width).astype(BF16)
            other[i, c] = retiled(jnp.where(core == 0, second, first), width).astype(BF16)
        there = [(other.at[i, :, :, lanes], sent[i * each + p]) for p, lanes in enumerate(lane_parts(width, each))]
        leaving += started(there + [(keep.at[i], keep_far.at[i])], left.at[pl.ds(len(leaving), len(there) + 1)])
    for copy in leaving:
        copy.wait()


def in_grad_halves(plan, flipped, grad_pre):
    width, hidden, chips = flipped.shape[0], grad_pre.shape[1], plan.devices // 2
    high, each = plan.channels * hidden // CHUNKS // width, 2
    outs = [((CHUNKS, chips, high, width), BF16, FAR)] + [((chips, high, width // each), BF16, FAR)] * (CHUNKS * each)
    room = [pltpu.VMEM(value.shape, BF16) for value in (flipped, grad_pre)] + [pltpu.VMEM(outs[0][0], BF16)] * 2
    room += [pltpu.SemaphoreType.DMA((1 + CHUNKS,)), pltpu.SemaphoreType.DMA((CHUNKS * (each + 1),))]
    keep, *sent = run(in_grad_kernel, "in_grad_halves", [(flipped, FAR), (grad_pre, FAR)], outs, room)
    return keep, sent


def small_shares(plan, sums, pre_sum, bias_row, scale_row, rows):
    channels, count = plan.channels, plan.devices
    width = channels * count
    kinds = pre_sum.shape[1] // width
    lane = lax.broadcasted_iota(jnp.int32, sums.shape, 1)
    rows[...] = jnp.zeros_like(rows)
    for kind, row in ((2 + kinds, bias_row), (3 + kinds, scale_row)):
        for again in (0, SUB):
            rows[pl.ds(plan.extra_lane + kind + again, 1), :] = row
    total = sums + rows[...].T
    columns = jnp.broadcast_to(pre_sum, (SUB, pre_sum.shape[1])).T.reshape(count, kinds, channels, SUB)
    for kind in range(kinds):
        column = columns[:, kind].reshape(width, SUB)[:, :1]
        total = total + jnp.where(plan.kind(lane, 2 + kind), column, 0.0)
    return total


def held_back(arrays, after):
    kept = len(arrays)
    return pl.pallas_call(
        lambda *refs: None,
        out_shape=tuple(pltpu.HBM(a.shape, a.dtype) for a in arrays),
        in_specs=[whole(pltpu.HBM)] * kept + [whole(pl.ANY)] * len(after),
        out_specs=(whole(pltpu.HBM),) * kept,
        input_output_aliases={i: i for i in range(kept)},
        cost_estimate=pl.CostEstimate(flops=0, bytes_accessed=0, transcendentals=0),
        name="held_back",
    )(*map(distant, arrays), *after)


def act_grads_kernel(scaled, weight_out, *rest):
    out = rest[-1]
    tile = 768
    for c in range(0, out.shape[1], tile):
        out[:, pl.ds(c, tile)] = lax.dot_general(scaled[...], weight_out[pl.ds(c, tile), :], (((1,), (1,)), ((), ())), preferred_element_type=F32)


def act_grads(scaled, weight_out, after):
    outs = [((scaled.shape[0], weight_out.shape[0]), F32, AUTO)]
    return run(act_grads_kernel, "act_grads", [(scaled, AUTO), (weight_out, AUTO)], outs, [], after, micros=6)[0]


def merge_entries(at, bit, keep, got, mine, other):
    low = (1 << at) - 1
    for e in range(mine.shape[0]):
        first = (e >> at << at + 1) + (e & low)
        here, there = first + bit * (low + 1), first + (1 - bit) * (low + 1)
        other[e] = keep(here) + got(there if False else here) if False else keep(there) + got(there)
        mine[e] = keep(here) + got(here)


def first_merge_kernel(cuts, counts, *refs):
    outs, mark, scratch = refs[-12:-6], refs[-6], refs[-5:]
    mark[...] = jnp.zeros_like(mark)
    sems, groups, used, at = scratch[-1], [], 0, 0
    for which, count in enumerate(counts):
        keep, came, got = scratch[2 * which], scratch[2 * which + 1], refs[at + 1 : at + 1 + count]
        chunks, chips, high, width = keep.shape
        for i in range(chunks):
            there = [(refs[at].at[i], keep.at[i])]
            if len(got[0].shape) == 4:
                part = chips // count
                there += [(piece.at[i], came.at[i, pl.ds(p * part, part)]) for p, piece in enumerate(got)]
            else:
                each = count // chunks
                there += [(got[i * each + p], came.at[i, :, :, lanes]) for p, lanes in enumerate(lane_parts(width, each))]
            groups.append(started(there, sems.at[pl.ds(used, len(there))]))
            used += len(there)
        at += 1 + count
    for which in range(2):
        keep, came = scratch[2 * which], scratch[2 * which + 1]
        chunks, _, high, _ = keep.shape
        for i in range(chunks):
            for copy in groups[which * chunks + i]:
                copy.wait()
            pair, row = (which, i * high) if i < chunks - 1 else (2, which * high)
            cut, bit = cuts[pair]
            mine, other = (out.at[:, pl.ds(row, high)] for out in outs[2 * pair : 2 * pair + 2])
            merge_entries(cut, own_bit(bit), lambda e: keep[i, e], lambda e: came[i, e], mine, other)


def first_merge(parts, cuts, after):
    chunks, chips, high, width = parts[0][0].shape
    ins = [(value, place) for (keep, got), near_by in zip(parts, (FAR, NEAR)) for value, place in ((keep, FAR), *((piece, near_by) for piece in got))]
    outs = [((chips // 2, rows, width), BF16, NEAR) for rows in ((chunks - 1) * high, (chunks - 1) * high, 2 * high) for _ in range(2)]
    room = [pltpu.VMEM(keep.shape, BF16) for keep, _ in parts for _ in range(2)] + [pltpu.SemaphoreType.DMA((64,))]
    kernel = functools.partial(first_merge_kernel, cuts, [len(got) for _, got in parts])
    *halves, mark = run(kernel, "first_merge", ins, outs + [((SUB, LANES), F32, AUTO)], room, after, limit=LESS)
    return halves[0::2], halves[1::2], mark


def merge_kernel(jobs, *refs):
    count, pairs = sum(len(job) for job in jobs), 2 * len(jobs)
    outs, mark = refs[-1 - pairs : -1], refs[-1]
    mark[...] = jnp.zeros_like(mark)
    i = 0
    for j, job in enumerate(jobs):
        row = 0
        for at, bit in job:
            keep, got = refs[i], refs[count + i]
            rows = pl.ds(row, keep.shape[1])
            merge_entries(at, own_bit(bit), lambda e: keep[e], lambda e: got[e], outs[2 * j].at[:, rows], outs[2 * j + 1].at[:, rows])
            row += keep.shape[1]
            i += 1


def merge(keeps, gots, jobs, after=()):
    ins = [(value, NEAR) for value in keeps] + [(value, OPEN) for value in gots]
    outs, i = [], 0
    for job in jobs:
        parts = keeps[i : i + len(job)]
        i += len(job)
        outs += [((parts[0].shape[0] // 2, sum(part.shape[1] for part in parts), parts[0].shape[2]), BF16, NEAR)] * 2
    *halves, mark = run(functools.partial(merge_kernel, jobs), "merge_halves", ins, outs + [((SUB, LANES), F32, AUTO)], [], after, limit=LESS)
    return halves[0::2], halves[1::2], mark


def last_kernel(keep, got, less_keep, less_got, in_sum, out_sum):
    total = keep[0].astype(F32) + got[0].astype(F32)
    less = less_keep[0].astype(F32) + less_got[0].astype(F32)
    high = less.shape[0] // 2
    tile = in_sum.shape[1] // CHUNKS
    for i, part in enumerate((total[:high], total[high : 2 * high], less[:high])):
        in_sum[:, pl.ds(i * tile, tile)] = retiled(part, tile)
    out_sum[pl.ds(0, 2 * high), :] = total[2 * high :]
    out_sum[pl.ds(2 * high, high), :] = less[high:]


def last_sums(parts, channels, hidden, after):
    ins = [(parts[0], NEAR), (parts[1], OPEN), (parts[2], NEAR), (parts[3], OPEN)]
    high, width = parts[2].shape[1] // 2, parts[2].shape[2]
    outs = [((channels, hidden), F32, AUTO), ((CHUNKS * high, width), F32, AUTO)]

    def kernel(*refs):
        last_kernel(*refs[:4], *refs[-2:])

    return run(kernel, "last_sums", ins, outs, [], after)


def tap_places():
    reach = np.concatenate([np.arange(s) / s for s in SIDES]).astype(np.float32)
    scale = np.concatenate([np.full(s, 1.0 / math.sqrt(s)) for s in SIDES]).astype(np.float32)
    return reach, scale


def profiles(coefficient, log_rate):
    reach, scale = tap_places()
    decayed = jnp.exp(-jnp.exp(log_rate)[None] * reach[:, None, None])
    return jnp.sum(coefficient[None] * decayed, axis=2) * scale[:, None]


def profile_grads(coefficient, log_rate, grads):
    reach, scale = tap_places()
    rate = jnp.exp(log_rate)
    decayed = jnp.exp(-rate[None] * reach[:, None, None])
    weighted = (grads * scale[:, None])[:, :, None] * decayed
    return jnp.sum(weighted, axis=0), -coefficient * rate * jnp.sum(weighted * reach[:, None, None], axis=0)


def kernel_matrix(profile, part):
    side = part["side"]
    offsets = np.arange(side)[:, None] - np.arange(side)[None, :]
    picked = profile[part["tap"] + np.maximum(offsets, 0)]
    return jnp.where((offsets >= 0)[:, :, None], picked, 0.0)


def mix_plain(plan, row_pixel, channel_rows, height, width, skip):
    def one_channel(given):
        values, high, wide, weight = given
        image_order = jnp.zeros_like(values).at[row_pixel].set(values)
        pieces = []
        for part in plan.sections:
            side, count = part["side"], part["images"] * part["side"] ** 2
            block = image_order[part["pixel"] : part["pixel"] + count].reshape(-1, side, side)
            left = kernel_matrix(high[:, None], part)[:, :, 0]
            right = kernel_matrix(wide[:, None], part)[:, :, 0]
            mixed = jnp.einsum("ik,nkl,jl->nij", left, block, right, precision=lax.Precision.HIGHEST)
            pieces.append(mixed.reshape(-1))
        joined = jnp.concatenate(pieces) + weight * image_order
        return joined[row_pixel]

    return lax.map(jax.checkpoint(one_channel), (channel_rows, height.T, width.T, skip))


def exchange(blocks):
    return lax.all_to_all(blocks, "chan", 0, 0, tiled=True)


def to_blocks(rows, devices):
    return rows.T.reshape(devices, rows.shape[1] // devices, rows.shape[0])


def to_rows(blocks):
    return blocks.reshape(-1, blocks.shape[2]).T


def halve(blocks, bits):
    myself = lax.axis_index("chan")
    size = lax.axis_size("chan")
    pairs = lambda bit: [(i, i ^ 1 << bit) for i in range(size)]
    left = list(range(size.bit_length() - 1))
    for bit in bits:
        at = left.index(bit)
        viewed = blocks.reshape((-1, 2, 1 << at) + blocks.shape[1:])
        own = myself >> bit & 1
        keep = lax.dynamic_index_in_dim(viewed, own, 1, keepdims=False)
        send = lax.dynamic_index_in_dim(viewed, 1 - own, 1, keepdims=False)
        got = lax.ppermute(send, "chan", pairs(bit))
        total = keep.astype(F32) + got.astype(F32)
        left.remove(bit)
        blocks = (total if not left else total.astype(BF16)).reshape((-1,) + blocks.shape[1:])
    return blocks[0]


def swapped(x, bit):
    return lax.ppermute(x, "chan", [(i, i ^ 1 << bit) for i in range(lax.axis_size("chan"))])


def body_fast(
    tokens,
    row_pixel,
    coef_height,
    rate_height,
    coef_width,
    rate_width,
    skip_weight,
    norm_gain,
    norm_bias,
    weight_in,
    bias_in,
    weight_out,
    bias_out,
    layer_scale,
    out_grad,
):
    devices = lax.axis_size("chan")
    rows, width_all = tokens.shape
    plan = Plan(devices, rows, width_all // devices)
    token_blocks = exchange(to_blocks(tokens, devices))
    where = plan.address(row_pixel)
    spread = plan.spread()
    taps = (plan.tile_taps(profiles(coef_height, rate_height)), plan.tile_taps(profiles(coef_width, rate_width)), plan.tile_taps(skip_weight[None]))
    mixed_blocks, packed, across = mixer_forward(plan, where, token_blocks, *taps)

    scaled = out_grad.astype(F32) * layer_scale
    scaled_low = scaled.astype(BF16)
    rows_given = jnp.stack([layer_scale, bias_out, jnp.sum(scaled, axis=0)])
    grad_act = act_grads(scaled_low, weight_out, (rows_given,))
    grad_normin, flipped, act, grad_pre, sums, pre_sum = feed(plan, exchange(mixed_blocks), norm_gain, norm_bias, weight_in, bias_in, grad_act)
    grad_blocks = exchange(grad_normin)
    out_keep, out_sent = out_grad_halves(plan, act, scaled_low)
    out_got = [swapped(piece, 0) for piece in out_sent]
    in_keep, in_sent = in_grad_halves(plan, flipped, grad_pre)
    in_got = [swapped(piece, 0) for piece in in_sent]

    x, y, near_z, far_z = range(1, 5)
    swap = lambda parts, bits: [swapped(part, bit) for part, bit in zip(parts, bits)]
    keeps, sends, mark = first_merge(((in_keep, in_got), (out_keep, out_got)), ((0, x), (1, y), (2, near_z)), (grad_blocks,))
    gots = swap(sends, (x, y, near_z))
    grads, block_out, shares, mark = mixer_arrive(plan, where, grad_blocks, act, weight_out, rows_given, tokens, out_grad, sums, pre_sum, (mark,))
    keeps, sends, mark = merge(keeps, gots, (((0, y),), ((0, x),), ((2, far_z),)), (mark,))
    gots = swap(sends, (y, x, far_z))
    grads, *tap_sums, mark = mixer_backward(plan, grads, *taps, packed, across, (mark,))
    both_keeps, both_sends, mark = merge(keeps[:2], gots[:2], (((0, near_z), (0, near_z)),), (mark,))
    both_gots = swap(both_sends, (near_z,))
    leaving, left = mixer_leave(plan, where, grads, shares, (mark,))
    keeps, sends, mark = merge((both_keeps[0], keeps[2]), (both_gots[0], gots[2]), (((0, far_z),), ((0, x),)), (left,))
    (moved,) = held_back((leaving,), (mark,))
    grad_tokens, *smalls = token_grads(plan, exchange(moved), out_grad, pre_sum.shape[1] // width_all)
    both_got, less_got = swap(sends, (far_z, x))
    less_keeps, less_sends, mark = merge(keeps[1:], (less_got,), (((0, y),),))
    (less_got,) = swap(less_sends, (y,))
    coef_grads = tap_grads(plan, (coef_height, rate_height, coef_width, rate_width), spread.astype(F32), tap_sums, (mark,))
    in_sum, out_sum = last_sums(
        (keeps[0], both_got, less_keeps[0], less_got), plan.channels, weight_in.shape[1], (grad_tokens, *coef_grads)
    )
    gain_grad, norm_bias_grad, bias_in_grad, bias_out_grad, scale_grad = (small[0] for small in smalls)
    return (block_out, grad_tokens, *coef_grads, gain_grad, norm_bias_grad, in_sum, bias_in_grad, out_sum, bias_out_grad, scale_grad)


def body_plain(
    tokens,
    row_pixel,
    coef_height,
    rate_height,
    coef_width,
    rate_width,
    skip_weight,
    norm_gain,
    norm_bias,
    weight_in,
    bias_in,
    weight_out,
    bias_out,
    layer_scale,
    out_grad,
):
    devices = lax.axis_size("chan")
    rows, width_all = tokens.shape
    plan = Plan(devices, rows, width_all // devices)
    token_blocks = exchange(to_blocks(tokens, devices))

    height = profiles(coef_height, rate_height)
    width = profiles(coef_width, rate_width)
    lines = lambda blocks: blocks.transpose(1, 0, 2).reshape(blocks.shape[1], -1)
    blocks_of = lambda values: values.astype(BF16).reshape(-1, devices, rows).transpose(1, 0, 2)
    mixed, mixer_back = jax.vjp(
        functools.partial(mix_plain, plan, row_pixel), lines(token_blocks).astype(F32), height, width, skip_weight
    )
    mixed_blocks = blocks_of(mixed)
    normin = to_rows(exchange(mixed_blocks)).astype(F32)

    upstream = out_grad.astype(F32)
    scaled = upstream * layer_scale
    scaled_low = scaled.astype(BF16)
    grad_act = lax.dot_general(scaled_low, weight_out, (((1,), (1,)), ((), ())), preferred_element_type=F32)

    row_mean = jnp.mean(normin, axis=1, keepdims=True)
    centred = normin - row_mean
    inv_std = lax.rsqrt(jnp.mean(centred * centred, axis=1, keepdims=True) + EPSILON)
    unit_rows = centred * inv_std
    normed = (unit_rows * norm_gain + norm_bias).astype(BF16)
    hidden_pre = jnp.dot(normed, weight_in, preferred_element_type=F32) + bias_in
    cdf = 0.5 * (1.0 + lax.erf(hidden_pre * math.sqrt(0.5)))
    act_low = (hidden_pre * cdf).astype(BF16)
    slope = cdf + hidden_pre * jnp.exp(-0.5 * hidden_pre * hidden_pre) * (1.0 / math.sqrt(2.0 * math.pi))
    grad_pre = grad_act * slope
    grad_pre_low = grad_pre.astype(BF16)
    grad_normed = lax.dot_general(grad_pre_low, weight_in, (((1,), (1,)), ((), ())), preferred_element_type=F32)
    grad_unit = grad_normed * norm_gain
    grad_normin = inv_std * (
        grad_unit
        - jnp.mean(grad_unit, axis=1, keepdims=True)
        - unit_rows * jnp.mean(grad_unit * unit_rows, axis=1, keepdims=True)
    )
    grad_blocks = exchange(to_blocks(grad_normin.astype(BF16), devices))

    branch = jnp.dot(act_low, weight_out, preferred_element_type=F32) + bias_out
    block_out = (tokens.astype(F32) + layer_scale * branch).astype(BF16)
    small = (
        jnp.sum(grad_normed * unit_rows, axis=0),
        jnp.sum(grad_normed, axis=0),
        jnp.sum(grad_pre, axis=0),
        jnp.sum(scaled, axis=0),
        jnp.sum(upstream * branch, axis=0),
    )
    weight_in_part = lax.dot_general(normed, grad_pre_low, (((0,), (0,)), ((), ())), preferred_element_type=F32)
    weight_out_part = lax.dot_general(act_low, scaled_low, (((0,), (0,)), ((), ())), preferred_element_type=F32)

    grad_mixed, grad_height, grad_width, grad_skip = mixer_back(lines(grad_blocks).astype(F32))
    grad_rows = blocks_of(grad_mixed)
    coef_height_grad, rate_height_grad = profile_grads(coef_height, rate_height, grad_height)
    coef_width_grad, rate_width_grad = profile_grads(coef_width, rate_width, grad_width)
    grad_tokens = upstream + to_rows(exchange(grad_rows)).astype(F32)

    levels = list(range(devices.bit_length() - 1))
    other = levels[:1] + levels[1:3][::-1] + levels[3:]
    in_sum = halve(weight_in_part.astype(BF16).reshape(devices, -1, weight_in.shape[1]), levels)
    out_sum = halve(weight_out_part.astype(BF16).reshape(devices, -1, weight_out.shape[1]), other)
    shares = jnp.concatenate([s.reshape(devices, -1) for s in small], axis=1)
    shares = exchange(shares).sum(axis=0)
    cuts = np.cumsum([s.shape[0] // devices for s in small])[:-1]
    gain_grad, norm_bias_grad, bias_in_grad, bias_out_grad, scale_grad = jnp.split(shares, cuts)
    return (
        block_out,
        grad_tokens,
        coef_height_grad,
        rate_height_grad,
        coef_width_grad,
        rate_width_grad,
        grad_skip,
        gain_grad,
        norm_bias_grad,
        in_sum,
        bias_in_grad,
        out_sum,
        bias_out_grad,
        scale_grad,
    )


def solution(mesh):
    split, copied = P("chan"), P()

    def body(tokens, *rest):
        devices = lax.axis_size("chan")
        fast = Plan(devices, tokens.shape[0], tokens.shape[1] // devices).fits() and devices == 32
        return (body_fast if fast else body_plain)(tokens, *rest)

    in_specs = (split, copied) + (split,) * 5 + (copied,) * 7 + (split,)
    return jax.shard_map(body, mesh=mesh, in_specs=in_specs, out_specs=(split,) * 14, check_vma=False)
```

```python
import functools
import math

import jax
import jax.numpy as jnp
import numpy as np
from jax import lax
from jax.experimental import pallas as pl
from jax.experimental.pallas import tpu as pltpu
from jax.sharding import PartitionSpec as P

SIDES = (10, 14, 18)
SHARES = (1, 1, 2)
UNIT = sum(m * s * s for s, m in zip(SIDES, SHARES))
TAPS = sum(SIDES)
EPSILON = 1e-06
LANES = 128
SUB = 8
MARGIN = 32
VMEM = 63 * 2**20
LESS = 36 * 2**20
SMALL = 20 * 2**20
CHUNKS = 3
F32 = jnp.float32
BF16 = jnp.bfloat16


class Plan:
    def __init__(self, devices, rows, channels):
        self.devices, self.rows, self.channels = devices, rows, channels
        self.pixels = devices * rows
        self.units = self.pixels // UNIT
        self.slots = LANES // channels
        self.row_pad = -(-rows // LANES) * LANES
        self.extra_row = -(-rows // SUB) * SUB
        self.sections = []
        image_row, packed_row, tap, mask_row, pixel = 0, 0, 0, 0, 0
        for side, share in zip(SIDES, SHARES):
            images = share * self.units
            pitch = -(-side // SUB) * SUB
            groups = -(-images // self.slots)
            self.sections.append(
                dict(side=side, images=images, pitch=pitch, groups=groups, image_row=image_row, packed_row=packed_row, tap=tap, mask_row=mask_row, pixel=pixel)
            )
            image_row += groups * self.slots * side * pitch
            packed_row += groups * side * pitch
            tap += side
            mask_row += side * pitch
            pixel += images * side * side
        self.image_rows = image_row
        self.packed_rows = packed_row
        self.mask_rows = mask_row

    @property
    def extra_lane(self):
        return self.extra_row - (self.row_pad - LANES)

    def kind(self, lane, which):
        return (lane == self.extra_lane + which) | (lane == self.extra_lane + SUB + which)

    def fits(self):
        room = self.row_pad - self.extra_row >= 2 * SUB
        return room and self.channels % SUB == 0 and 4 * LANES * (self.image_rows + 2 * self.row_pad + 5 * self.packed_rows) < 40 * 2**20

    def address(self, row_pixel):
        where = jnp.zeros_like(row_pixel)
        for part in self.sections:
            local = row_pixel - part["pixel"]
            line = local // part["side"]
            spot = part["image_row"] + line * part["pitch"] + local - line * part["side"]
            where = jnp.where(local >= 0, spot, where)
        return where

    def spread(self):
        lane = np.arange(LANES)
        held = (lane[None, :] % self.channels == np.arange(self.channels)[:, None]) & (lane[None, :] < self.slots * self.channels)
        return jnp.asarray(held.astype(np.float32), BF16)

    def tile_taps(self, taps):
        tiled = jnp.tile(taps, (1, self.slots))
        return jnp.pad(tiled, ((0, 0), (0, LANES - tiled.shape[1])))


def slot_masks(plan):
    lane = lax.broadcasted_iota(jnp.int32, (SUB, LANES), 1)
    return [(lane >= q * plan.channels) & (lane < (q + 1) * plan.channels) for q in range(plan.slots)]


def in_turn(plan, first, second, beside=None, steps=0, ready=None):
    first(0, 0)

    def pair(k):
        first(2 * k + 1, 1)
        second(2 * k, 0)
        first(2 * k + 2, 0)
        second(2 * k + 1, 1)

    def plain(k, carry):
        pair(k)
        return carry

    def more(k, carry):
        beside(k - begin)
        pair(k)
        return carry

    pairs = plan.devices // 2 - 1
    begin = pairs - steps
    lax.fori_loop(0, begin, plain, 0)
    if steps:
        ready()
        lax.fori_loop(begin, pairs, more, 0)
    first(plan.devices - 1, 1)
    second(plan.devices - 2, 0)
    second(plan.devices - 1, 1)


def scatter_rows(plan, where, block, buffers, image, beside=None, steps=0, ready=None):
    def turn(s, held):
        rows = block[s].astype(F32)
        full = [rows] * plan.slots
        if LANES > plan.slots * plan.channels:
            full.append(rows[: LANES - plan.slots * plan.channels])
        buffers[held][pl.ds(0, plan.rows), :] = jnp.concatenate(full, axis=0).T

    def place(s, held):
        base = s * plan.rows
        for u in range(plan.rows):
            image[pl.ds(where[base + u], 1), :] = buffers[held][pl.ds(u, 1), :]

    in_turn(plan, turn, place, beside, steps, ready)


def gather_rows(plan, where, buffers, image, out, extra=None):
    def fetch(s, held):
        base = s * plan.rows
        for u in range(plan.rows):
            buffers[held][pl.ds(u, 1), :] = image[pl.ds(where[base + u], 1), :]

    def fold(s, held):
        turned = buffers[held][...].T
        folded = turned[: plan.channels]
        for q in range(1, plan.slots):
            folded = folded + turned[q * plan.channels : (q + 1) * plan.channels]
        if extra is None:
            out[s] = folded[:, : plan.rows].astype(BF16)
            return
        last = plan.row_pad - LANES
        exact = extra[pl.ds(pl.multiple_of(s * plan.channels, SUB), plan.channels), :]
        high = exact.astype(BF16).astype(F32)
        lane = lax.broadcasted_iota(jnp.int32, exact.shape, 1) + last
        sums = jnp.where(lane < plan.extra_row + SUB, high, exact - high)
        out[s, :, pl.ds(0, last)] = folded[:, :last].astype(BF16)
        out[s, :, pl.ds(last, LANES)] = jnp.where(lane < plan.extra_row, folded[:, last:], sums).astype(BF16)

    in_turn(plan, fetch, fold)


def pack_images(plan, masks, image, packed, margin):
    place = lax.broadcasted_iota(jnp.int32, (SUB, LANES), 0)
    for part in plan.sections:
        side, pitch = part["side"], part["pitch"]
        area = side * pitch
        ragged = part["images"] < part["groups"] * plan.slots

        def group(t, carry, part=part, side=side, pitch=pitch, area=area, ragged=ragged):
            start = part["image_row"] + t * (plan.slots * area)
            target = margin + part["packed_row"] + t * area
            used = masks
            if ragged:
                used = [mask & (t * plan.slots + q < part["images"]) for q, mask in enumerate(masks)]
            ends = [mask & (place < side % SUB) for mask in used]
            for i in range(side):
                for j in range(0, pitch, SUB):
                    value = jnp.zeros((SUB, LANES), F32)
                    for q in range(plan.slots):
                        row = pl.multiple_of(start + (q * area + i * pitch + j), SUB)
                        value = jnp.where((ends if j + SUB > side else used)[q], image[pl.ds(row, SUB), :], value)
                    packed[pl.ds(pl.multiple_of(target + (i * pitch + j), SUB), SUB), :] = value
            return carry

        lax.fori_loop(0, part["groups"], group, 0)


def unpack_line(plan, masks, part, t, offset, value, image):
    area = part["side"] * part["pitch"]
    for q in range(plan.slots):
        row = pl.multiple_of(part["image_row"] + (t * plan.slots + q) * area + offset, SUB)
        image[pl.ds(row, SUB), :] = jnp.where(masks[q], value, 0.0)


def wide_taps(plan, taps, table):
    for tap in range(TAPS):
        table[pl.ds(tap * SUB, SUB), :] = jnp.broadcast_to(taps[pl.ds(tap, 1), :], (SUB, LANES))


def masked_taps(plan, taps, table):
    for part in plan.sections:
        side, pitch = part["side"], part["pitch"]
        place = lax.broadcasted_iota(jnp.int32, (pitch, LANES), 0)
        for tap in range(side):
            row = taps[pl.ds(part["tap"] + tap, 1), :]
            table[pl.ds(part["mask_row"] + tap * pitch, pitch), :] = jnp.where(place >= tap, row, 0.0)


def forward_kernel(plan, where_far, block, height, width, skip, out, packed, across, first, second, image, where, px, pu, height_wide, width_masked, sems):
    masks = slot_masks(plan)
    indices = pltpu.make_async_copy(where_far, where, sems.at[0])
    indices.start()
    px[pl.ds(0, MARGIN), :] = jnp.zeros((MARGIN, LANES), F32)
    wide_taps(plan, height, height_wide)
    masked_taps(plan, width, width_masked)
    indices.wait()
    scatter_rows(plan, where, block, (first, second), image)
    pack_images(plan, masks, image, px, MARGIN)
    skips = jnp.broadcast_to(skip[...], (SUB, LANES))
    for part in plan.sections:
        side, pitch = part["side"], part["pitch"]
        area = side * pitch

        def group(t, carry, part=part, side=side, pitch=pitch, area=area):
            start = MARGIN + part["packed_row"] + t * area

            for j in range(0, pitch, SUB):
                reach = range(min(side, j + SUB))
                weights = [width_masked[pl.ds(part["mask_row"] + tap * pitch + j, SUB), :] for tap in reach]

                def line(i, inner, j=j, weights=weights):
                    base = start + i * pitch + j
                    total = weights[0] * px[pl.ds(pl.multiple_of(base, SUB), SUB), :]
                    for tap in range(1, len(weights)):
                        total = total + weights[tap] * px[pl.ds(base - tap, SUB), :]
                    pu[pl.ds(pl.multiple_of(base, SUB), SUB), :] = total
                    return inner

                lax.fori_loop(0, side, line, 0, unroll=2)

            def column(c, inner):
                first = pl.multiple_of(start + c * SUB, SUB)
                held = [pu[pl.ds(pl.multiple_of(first + k * pitch, SUB), SUB), :] for k in range(side)]
                for i in range(side):
                    total = skips * px[pl.ds(pl.multiple_of(first + i * pitch, SUB), SUB), :]
                    for k in range(i + 1):
                        total = total + height_wide[pl.ds((part["tap"] + i - k) * SUB, SUB), :] * held[k]
                    unpack_line(plan, masks, part, t, i * pitch + c * SUB, total, image)
                return inner

            lax.fori_loop(0, pitch // SUB, column, 0)
            return carry

        lax.fori_loop(0, part["groups"], group, 0)
    kept = [(px.at[pl.ds(MARGIN, plan.packed_rows)], packed), (pu.at[pl.ds(MARGIN, plan.packed_rows)], across)]
    kept = started(kept, sems.at[pl.ds(1, 2)])
    gather_rows(plan, where, (first, second), image, out)
    for copy in kept:
        copy.wait()


def arrive_kernel(plan, where_far, block_far, act_far, weight_far, given_far, tokens_far, out_grad_far, sums_far, pre_sum_far, *rest):
    grads, block_out, shares, mark, *rest = rest[-20:]
    where, block, first, second, image, act, weight_out, given, tokens, out_grad, sums, pre_sum, branch, rows, came, sems = rest
    mark[...] = jnp.zeros_like(mark)
    soon = started([(block_far, block), (where_far, where)], came.at[pl.ds(2, 2)])
    arriving = started([(act_far, act), (weight_far, weight_out)], came.at[pl.ds(0, 2)])
    there = [(given_far, given), (tokens_far, tokens), (out_grad_far, out_grad), (sums_far, sums), (pre_sum_far, pre_sum)]
    later = started(there, sems)

    def ready():
        for copy in arriving:
            copy.wait()

    def product(k):
        lanes = pl.ds(pl.multiple_of(k * LANES, LANES), LANES)
        branch[:, lanes] = jnp.dot(act[...], weight_out[:, lanes], preferred_element_type=F32)

    for copy in soon:
        copy.wait()
    scatter_rows(plan, where, block, (first, second), image, product, tokens.shape[1] // LANES, ready)
    for copy in later:
        copy.wait()
    scale, bias_out, bias_row = (given[pl.ds(i, 1), :] for i in range(3))
    total = branch[...] + bias_out
    block_out[...] = (tokens[...].astype(F32) + scale * total).astype(BF16)
    scale_row = jnp.sum(out_grad[...].astype(F32) * total, axis=0, keepdims=True)
    shares[...] = small_shares(plan, sums[...], pre_sum[...], bias_row, scale_row, rows)
    pack_images(plan, slot_masks(plan), image, grads, 0)


def leave_kernel(plan, where_far, grads, extra, *rest):
    out, mark, near, far, image, where, sem = rest[-7:]
    indices = pltpu.make_async_copy(where_far, where, sem)
    indices.start()
    mark[...] = jnp.zeros_like(mark)
    masks = slot_masks(plan)
    for part in plan.sections:
        area = part["side"] * part["pitch"]

        def group(t, carry, part=part, area=area):
            for offset in range(0, area, SUB):
                row = pl.multiple_of(part["packed_row"] + t * area + offset, SUB)
                unpack_line(plan, masks, part, t, offset, grads[pl.ds(row, SUB), :], image)
            return carry

        lax.fori_loop(0, part["groups"], group, 0)
    indices.wait()
    gather_rows(plan, where, (near, far), image, out, extra)


def backward_kernel(plan, pg, height, width, skip, packed_far, across_far, *rest):
    out, height_sums, width_sums, skip_sums, mark, pd, height_wide, width_wide, packed, across, sems = rest[-11:]
    mark[...] = jnp.zeros_like(mark)
    arriving = started([(across_far, across), (packed_far, packed)], sems)
    place = lax.broadcasted_iota(jnp.int32, (SUB, LANES), 0)
    pd[pl.ds(plan.packed_rows, MARGIN), :] = jnp.zeros((MARGIN, LANES), F32)
    wide_taps(plan, height, height_wide)
    wide_taps(plan, width, width_wide)
    skips = jnp.broadcast_to(skip[...], (SUB, LANES))
    skip_sums[...] = jnp.zeros((SUB, LANES), F32)
    height_sums[...] = jnp.zeros((TAPS * SUB, LANES), F32)
    for part in plan.sections:
        side, pitch = part["side"], part["pitch"]
        area = side * pitch

        def group(t, carry, part=part, side=side, pitch=pitch, area=area):
            start = part["packed_row"] + t * area

            def column(c, inner):
                first = pl.multiple_of(start + c * SUB, SUB)
                rows = [pl.ds(pl.multiple_of(first + k * pitch, SUB), SUB) for k in range(side)]
                held = [pg[row, :] for row in rows]
                for k in range(side):
                    total = jnp.zeros((SUB, LANES), F32)
                    for i in range(k, side):
                        total = total + height_wide[pl.ds((part["tap"] + i - k) * SUB, SUB), :] * held[i]
                    pd[rows[k], :] = total
                return inner

            lax.fori_loop(0, pitch // SUB, column, 0)
            return carry

        lax.fori_loop(0, part["groups"], group, 0)
    arriving[0].wait()
    for part in plan.sections:
        side, pitch = part["side"], part["pitch"]
        area = side * pitch

        def group(t, carry, part=part, side=side, pitch=pitch, area=area):
            start = part["packed_row"] + t * area

            def column(c, inner):
                first = pl.multiple_of(start + c * SUB, SUB)
                rows = [pl.ds(pl.multiple_of(first + k * pitch, SUB), SUB) for k in range(side)]
                held = [pg[row, :] for row in rows]
                ways = [across[row, :] for row in rows]
                for tap in range(side):
                    total = held[tap] * ways[0]
                    for k in range(1, side - tap):
                        total = total + held[k + tap] * ways[k]
                    height_sums[pl.ds((part["tap"] + tap) * SUB, SUB), :] += total
                return inner

            lax.fori_loop(0, pitch // SUB, column, 0)
            return carry

        lax.fori_loop(0, part["groups"], group, 0)
    arriving[1].wait()
    for part in plan.sections:
        side, pitch = part["side"], part["pitch"]
        area = side * pitch

        def group(t, carry, part=part, side=side, pitch=pitch, area=area):
            start = part["packed_row"] + t * area

            def line(i, sums):
                sums = list(sums)
                base = start + i * pitch
                aligned = pl.multiple_of(base, SUB)
                for j in range(0, pitch, SUB):
                    here = pl.ds(pl.multiple_of(aligned + j, SUB), SUB)
                    mine, grad = packed[here, :], pg[here, :]
                    total = skips * grad
                    sums[side] = sums[side] + mine * grad
                    for tap in range(min(side, side - j)):
                        moved = pd[pl.ds(base + j + tap, SUB), :]
                        if j + SUB - 1 + tap >= pitch:
                            moved = jnp.where(place + (j + tap) < side, moved, 0.0)
                        total = total + width_wide[pl.ds((part["tap"] + tap) * SUB, SUB), :] * moved
                        sums[tap] = sums[tap] + mine * moved
                    out[here, :] = total
                return tuple(sums)

            return lax.fori_loop(0, side, line, carry)

        zero = jnp.zeros((SUB, LANES), F32)
        sums = lax.fori_loop(0, part["groups"], group, (zero,) * (side + 1))
        for tap in range(side):
            width_sums[pl.ds((part["tap"] + tap) * SUB, SUB), :] = sums[tap]
        skip_sums[...] += sums[side]


def whole(memory):
    return pl.BlockSpec(memory_space=memory)


def lanes_of(rows):
    return jax.ShapeDtypeStruct((rows, LANES), F32)


def row_buffers(plan):
    return [pltpu.VMEM((plan.row_pad, LANES), F32)] * 2 + [pltpu.VMEM((plan.image_rows, LANES), F32)]


def near(values):
    return pltpu.with_memory_space_constraint(values, pltpu.VMEM)


def distant(values):
    return pltpu.with_memory_space_constraint(values, pltpu.HBM)


def kernel_call(kernel, name, micros, memories, out_shape, scratch, args, after=(), stays=(), held=(), left=()):
    single = not isinstance(out_shape, tuple)
    shapes = (out_shape,) if single else out_shape
    shapes = tuple((pltpu.VMEM if i in stays else pltpu.HBM)(o.shape, o.dtype) for i, o in enumerate(shapes))
    outs = tuple(whole(pltpu.VMEM) for _ in shapes)
    place = lambda i, value: near(value) if i in held else value if memories[i] is pltpu.SMEM or i in left else distant(value)
    out = pl.pallas_call(
        kernel,
        out_shape=shapes,
        in_specs=[whole(m) for m in memories] + [whole(pltpu.HBM)] * len(after),
        out_specs=outs,
        scratch_shapes=scratch,
        compiler_params=pltpu.CompilerParams(vmem_limit_bytes=LESS if stays or held else VMEM),
        cost_estimate=pl.CostEstimate(flops=1_000_000, bytes_accessed=int(3_690_000 * micros), transcendentals=0),
        name=name,
    )(*[place(i, value) for i, value in enumerate(args)], *map(distant, after))
    return out[0] if single else out


def mixer_forward(plan, where, block, height, width, skip):
    rows = plan.packed_rows
    ins = [(where, FAR), (block, NEAR), (height, AUTO), (width, AUTO), (skip, AUTO)]
    outs = [(block.shape, BF16, AUTO), ((rows, LANES), F32, FAR), ((rows, LANES), F32, FAR)]
    room = row_buffers(plan) + [
        pltpu.SMEM(where.shape, jnp.int32),
        pltpu.VMEM((rows + MARGIN, LANES), F32),
        pltpu.VMEM((rows + MARGIN, LANES), F32),
        pltpu.VMEM((TAPS * SUB, LANES), F32),
        pltpu.VMEM((plan.mask_rows, LANES), F32),
        pltpu.SemaphoreType.DMA((3,)),
    ]
    return run(functools.partial(forward_kernel, plan), "mixer_forward", ins, outs, room, micros=30, limit=LESS)


def mixer_arrive(plan, where, block, act, weight_out, given, tokens, out_grad, sums, pre_sum, after):
    ins = [(value, FAR) for value in (where, block, act, weight_out, given, tokens, out_grad, sums, pre_sum)]
    width = tokens.shape[1]
    outs = [((plan.packed_rows, LANES), F32, NEAR), (tokens.shape, BF16, AUTO), ((width, LANES), F32, AUTO), ((SUB, LANES), F32, AUTO)]
    room = [pltpu.SMEM(where.shape, jnp.int32), pltpu.VMEM(block.shape, BF16)] + row_buffers(plan) + [pltpu.VMEM(value.shape, value.dtype) for value in (act, weight_out, given, tokens, out_grad, sums, pre_sum)]
    room += [pltpu.VMEM(tokens.shape, F32), pltpu.VMEM((LANES, width), F32), pltpu.SemaphoreType.DMA((4,)), pltpu.SemaphoreType.DMA((5,))]
    return run(functools.partial(arrive_kernel, plan), "mixer_arrive", ins, outs, room, after, limit=LESS)


def mixer_backward(plan, grads, height, width, skip, packed, across, after):
    rows = plan.packed_rows
    ins = [(grads, NEAR), (height, AUTO), (width, AUTO), (skip, AUTO), (packed, FAR), (across, FAR)]
    outs = [((rows, LANES), F32, NEAR)] + [((size, LANES), F32, AUTO) for size in (TAPS * SUB, TAPS * SUB, SUB, SUB)]
    room = [pltpu.VMEM((size, LANES), F32) for size in (rows + MARGIN, TAPS * SUB, TAPS * SUB, rows, rows)]
    room += [pltpu.SemaphoreType.DMA((2,))]
    return run(functools.partial(backward_kernel, plan), "mixer_backward", ins, outs, room, after, limit=LESS)


def mixer_leave(plan, where, grads, extra, after):
    ins = [(where, FAR), (grads, NEAR), (extra, AUTO)]
    outs = [((plan.devices, plan.channels, plan.row_pad), BF16, AUTO), ((SUB, LANES), F32, AUTO)]
    room = row_buffers(plan) + [pltpu.SMEM(where.shape, jnp.int32), pltpu.SemaphoreType.DMA]
    return run(functools.partial(leave_kernel, plan), "mixer_leave", ins, outs, room, after, limit=LESS)


def taps_kernel(plan, coef_height, rate_height, coef_width, rate_width, spread, height_sums, width_sums, skip_sums, *rest):
    outs = rest[-5:]
    reach, scale = tap_places()
    fold = lambda sums: lax.dot_general(spread[...], sums, (((1,), (1,)), ((), ())), precision=lax.Precision.HIGHEST, preferred_element_type=F32)
    for coef, log_rate, sums, coef_out, rate_out in (
        (coef_height, rate_height, height_sums, outs[0], outs[1]),
        (coef_width, rate_width, width_sums, outs[2], outs[3]),
    ):
        grads = fold(sums[...].reshape(TAPS, SUB, LANES).sum(axis=1))
        rate = jnp.exp(log_rate[...])
        plain, moved = jnp.zeros_like(rate), jnp.zeros_like(rate)
        for tap in range(TAPS):
            weighted = (grads[:, tap : tap + 1] * float(scale[tap])) * jnp.exp(rate * float(-reach[tap]))
            plain = plain + weighted
            moved = moved + weighted * float(reach[tap])
        coef_out[...] = plain
        rate_out[...] = -coef[...] * rate * moved
    total = jnp.sum(skip_sums[...], axis=0, keepdims=True)
    outs[4][...] = lax.dot_general(total, spread[...], (((1,), (1,)), ((), ())), precision=lax.Precision.HIGHEST, preferred_element_type=F32)


def tap_grads(plan, coefs, spread, sums, after):
    shape = jax.ShapeDtypeStruct(coefs[0].shape, F32)
    outs = (shape,) * 4 + (jax.ShapeDtypeStruct((1, plan.channels), F32),)
    *grads, skips = kernel_call(functools.partial(taps_kernel, plan), "tap_grads", 0.01, [pltpu.VMEM] * 8, outs, [], (*coefs, spread, *sums), after)
    return *grads, skips[0]


def tokens_kernel(plan, blocks, out_grad, out, *rest):
    smalls, flipped = rest[:-1], rest[-1]
    total = jnp.zeros((plan.channels, LANES), F32)
    for s in range(plan.devices):
        block = blocks[s].astype(F32)
        flipped[pl.ds(s * plan.channels, plan.channels), :] = block[:, : plan.rows]
        total = total + block[:, plan.row_pad - LANES :]
    first = plan.extra_lane
    rows = total.T
    rows = rows[first : first + SUB] + rows[first + SUB : first + 2 * SUB]
    kind = 0
    for small in smalls:
        for i in range(small.shape[1] // plan.channels):
            small[:, pl.ds(i * plan.channels, plan.channels)] = rows[kind : kind + 1]
            kind += 1
    out[...] = out_grad[...].astype(F32) + flipped[...].T


def token_grads(plan, blocks, out_grad, kinds):
    outs = [(out_grad.shape, F32, AUTO)] + [((1, count * plan.channels), F32, AUTO) for count in (1, 1, kinds, 1, 1)]
    room = [pltpu.VMEM(out_grad.shape[::-1], F32)]
    return run(functools.partial(tokens_kernel, plan), "token_grads", [(blocks, NEAR), (out_grad, AUTO)], outs, room)


def started(pairs, sems):
    copies = [pltpu.make_async_copy(source, target, sems.at[i]) for i, (source, target) in enumerate(pairs)]
    for copy in copies:
        copy.start()
    return copies


NEAR, FAR, AUTO, OPEN, SCALAR = "near", "far", "auto", "open", "scalar"


def run(kernel, name, ins, outs, scratch, after=(), micros=0.01, limit=VMEM):
    same = lambda value: value
    memory = {NEAR: pltpu.VMEM, FAR: pltpu.HBM, AUTO: pltpu.VMEM, OPEN: pltpu.VMEM, SCALAR: pltpu.SMEM}
    hold = {NEAR: near, FAR: distant, AUTO: distant, OPEN: same, SCALAR: same}
    make = {NEAR: pltpu.VMEM, FAR: pltpu.HBM, AUTO: pltpu.HBM, OPEN: jax.ShapeDtypeStruct}
    return pl.pallas_call(
        kernel,
        out_shape=tuple(make[place](shape, dtype) for shape, dtype, place in outs),
        in_specs=[whole(memory[place]) for _, place in ins] + [whole(pltpu.HBM)] * len(after),
        out_specs=tuple(whole(memory[place]) for _, _, place in outs),
        scratch_shapes=scratch,
        compiler_params=pltpu.CompilerParams(vmem_limit_bytes=limit),
        cost_estimate=pl.CostEstimate(flops=1000, bytes_accessed=int(3_690_000 * micros), transcendentals=0),
        name=name,
    )(*[hold[place](value) for value, place in ins], *map(distant, after))


def feed_kernel(plan, blocks, gain, bias, weight_far, bias_in, grad_act_far, grads, act_far, sums, pre_sum, keep_far, *rest):
    sent, scratch = rest[:-12], rest[-12:]
    normed, flipped, unit, total, weight_in, grad_act, act, grad_pre, keep, other, came, left = scratch
    channels, count = plan.channels, plan.devices
    width, hidden = weight_in.shape
    chunks, chips, _, _ = keep.shape
    tile, each = hidden // chunks, len(sent) // chunks
    core = own_bit(0)
    parts = [pl.ds(i * tile, tile) for i in range(chunks)]
    arriving = []
    for i, at in enumerate(parts):
        there = [(weight_far.at[:, at], weight_in.at[:, at]), (grad_act_far.at[:, at], grad_act.at[:, at])]
        arriving.append(started(there, came.at[pl.ds(2 * i, 2)]))
    for s in range(count):
        unit[pl.ds(s * channels, channels), :] = blocks[s].astype(F32)
    mean = jnp.sum(unit[...], axis=0, keepdims=True) * (1.0 / width)
    centred = unit[...] - mean
    inverse = lax.rsqrt(jnp.sum(centred * centred, axis=0, keepdims=True) * (1.0 / width) + EPSILON)
    unit[...] = centred * inverse
    scaled = unit[...] * gain[...] + bias[...]
    flipped[...] = scaled.astype(BF16)
    normed[...] = scaled.T.astype(BF16)
    leaving = []

    def activate(i):
        at = parts[i]
        for copy in arriving[i]:
            copy.wait()
        pre = jnp.dot(normed[...], weight_in[:, at], preferred_element_type=F32) + bias_in[:, at]
        cdf = 0.5 * (1.0 + lax.erf(pre * math.sqrt(0.5)))
        act[:, at] = (pre * cdf).astype(BF16)
        slope = cdf + pre * jnp.exp(-0.5 * pre * pre) * (1.0 / math.sqrt(2.0 * math.pi))
        grad = grad_act[:, at].astype(F32) * slope
        pre_sum[:, at] = jnp.sum(grad, axis=0, keepdims=True)
        grad_pre[:, at] = grad.astype(BF16)

    def leave(there):
        leaving.extend(started(there, left.at[pl.ds(len(leaving), len(there))]))

    activate(0)
    for i, at in enumerate(parts):
        if i + 1 < chunks:
            activate(i + 1)
        leave([(act.at[:, at], act_far.at[:, at])])
        back = lax.dot_general(grad_pre[:, at], weight_in[:, at], (((1,), (1,)), ((), ())), preferred_element_type=F32)
        total[...] = back if i == 0 else total[...] + back
        part = jnp.dot(flipped[...], grad_pre[:, at], preferred_element_type=F32)
        for c in range(chips):
            first = part[2 * c * channels : (2 * c + 1) * channels]
            second = part[(2 * c + 1) * channels : (2 * c + 2) * channels]
            keep[i, c] = retiled(jnp.where(core == 0, first, second), width).astype(BF16)
            other[i, c] = retiled(jnp.where(core == 0, second, first), width).astype(BF16)
        there = [(other.at[i, :, :, lanes], sent[i * each + p]) for p, lanes in enumerate(lane_parts(width, each))]
        leave(there + [(keep.at[i], keep_far.at[i])])
    turned = total[...].T
    lane = lax.broadcasted_iota(jnp.int32, sums.shape, 1)
    sums[...] = jnp.where(
        plan.kind(lane, 0),
        jnp.sum(turned * unit[...], axis=1, keepdims=True),
        jnp.where(plan.kind(lane, 1), jnp.sum(turned, axis=1, keepdims=True), 0.0),
    )
    grad = turned * gain[...]
    level = jnp.sum(grad, axis=0, keepdims=True) * (1.0 / width)
    tilt = jnp.sum(grad * unit[...], axis=0, keepdims=True) * (1.0 / width)
    total_low = (inverse * (grad - level - unit[...] * tilt)).astype(BF16)
    for s in range(count):
        grads[s] = total_low[s * channels : (s + 1) * channels]
    for copy in leaving:
        copy.wait()


def feed(plan, blocks, gain, bias, weight_in, bias_in, grad_act):
    rows, width, hidden, chips = plan.rows, plan.devices * plan.channels, weight_in.shape[1], plan.devices // 2
    high, each = plan.channels * hidden // CHUNKS // width, 2
    ins = [(blocks, NEAR), (gain[:, None], AUTO), (bias[:, None], AUTO), (weight_in, FAR), (bias_in[None], AUTO), (grad_act, FAR)]
    outs = [
        (blocks.shape, BF16, AUTO),
        ((rows, hidden), BF16, FAR),
        ((width, LANES), F32, AUTO),
        ((1, hidden), F32, AUTO),
        ((CHUNKS, chips, high, width), BF16, FAR),
    ] + [((chips, high, width // each), BF16, FAR)] * (CHUNKS * each)
    room = [
        pltpu.VMEM((rows, width), BF16),
        pltpu.VMEM((width, rows), BF16),
        pltpu.VMEM((width, rows), F32),
        pltpu.VMEM((rows, width), F32),
        pltpu.VMEM((width, hidden), BF16),
        pltpu.VMEM((rows, hidden), BF16),
        pltpu.VMEM((rows, hidden), BF16),
        pltpu.VMEM((rows, hidden), BF16),
        pltpu.VMEM((CHUNKS, chips, high, width), BF16),
        pltpu.VMEM((CHUNKS, chips, high, width), BF16),
        pltpu.SemaphoreType.DMA((2 * CHUNKS,)),
        pltpu.SemaphoreType.DMA((CHUNKS * (each + 2),)),
    ]
    grads, act, sums, pre_sum, keep, *sent = run(functools.partial(feed_kernel, plan), "feed_forward", ins, outs, room, micros=10, limit=LESS)
    return grads, act, sums, pre_sum, keep, sent


def out_grad_kernel(act_far, scaled_far, keep_far, *rest):
    sent, (act, scaled, keep, other, came, left) = rest[:-6], rest[-6:]
    core = own_bit(0)
    chunks, chips, high, width = keep.shape
    height, steps = chunks * high, came.shape[0] - 1
    tile, each, part = act.shape[1] // steps, chips // steps, chips // len(sent)
    parts = [pl.ds(i * tile, tile) for i in range(steps)]
    arriving, leaving = started([(scaled_far, scaled)] + [(act_far.at[:, at], act.at[:, at]) for at in parts], came), []
    arriving[0].wait()
    for i, at in enumerate(parts):
        arriving[1 + i].wait()
        low = lax.dot_general(act[:, at], scaled[...], (((0,), (0,)), ((), ())), preferred_element_type=F32).astype(BF16)
        for c in range(each):
            first = low[2 * c * height : (2 * c + 1) * height]
            second = low[(2 * c + 1) * height : (2 * c + 2) * height]
            mine, yours = jnp.where(core == 0, first, second), jnp.where(core == 0, second, first)
            for chunk in range(chunks):
                keep[chunk, i * each + c] = mine[chunk * high : (chunk + 1) * high]
                other[chunk, i * each + c] = yours[chunk * high : (chunk + 1) * high]
        some = pl.ds(i * each, each)
        there = [(other.at[:, pl.ds(p * part, part)], sent[p]) for p in range(i * each // part, (i + 1) * each // part)]
        there += [(keep.at[:, some], keep_far.at[:, some])]
        leaving += started(there, left.at[pl.ds(len(leaving), len(there))])
    for copy in leaving:
        copy.wait()


def out_grad_halves(plan, act, scaled):
    hidden, width, chips = act.shape[1], scaled.shape[1], plan.devices // 2
    high, steps, pieces = hidden // plan.devices // CHUNKS, hidden // 768, 4
    ins = [(act, FAR), (scaled, FAR)]
    outs = [((CHUNKS, chips, high, width), BF16, FAR)] + [((CHUNKS, chips // pieces, high, width), BF16, FAR)] * pieces
    room = [pltpu.VMEM(value.shape, BF16) for value in (act, scaled)] + [pltpu.VMEM(outs[0][0], BF16)] * 2
    room += [pltpu.SemaphoreType.DMA((1 + steps,)), pltpu.SemaphoreType.DMA((pieces + steps,))]
    keep, *sent = run(out_grad_kernel, "out_grad_halves", ins, outs, room)
    return keep, sent


def own_bit(bit):
    return lax.axis_index("chan") >> bit & 1


def lane_parts(width, count):
    return [pl.ds(p * (width // count), width // count) for p in range(count)]


def retiled(values, width):
    tiles = [values[r : r + SUB, c : c + LANES] for r in range(0, values.shape[0], SUB) for c in range(0, values.shape[1], LANES)]
    each = width // LANES
    return jnp.concatenate([jnp.concatenate(tiles[i : i + each], axis=1) for i in range(0, len(tiles), each)], axis=0)


def small_shares(plan, sums, pre_sum, bias_row, scale_row, rows):
    channels, count = plan.channels, plan.devices
    width = channels * count
    kinds = pre_sum.shape[1] // width
    lane = lax.broadcasted_iota(jnp.int32, sums.shape, 1)
    rows[...] = jnp.zeros_like(rows)
    for kind, row in ((2 + kinds, bias_row), (3 + kinds, scale_row)):
        for again in (0, SUB):
            rows[pl.ds(plan.extra_lane + kind + again, 1), :] = row
    total = sums + rows[...].T
    columns = jnp.broadcast_to(pre_sum, (SUB, pre_sum.shape[1])).T.reshape(count, kinds, channels, SUB)
    for kind in range(kinds):
        column = columns[:, kind].reshape(width, SUB)[:, :1]
        total = total + jnp.where(plan.kind(lane, 2 + kind), column, 0.0)
    return total


def held_back(arrays, after):
    kept = len(arrays)
    return pl.pallas_call(
        lambda *refs: None,
        out_shape=tuple(pltpu.HBM(a.shape, a.dtype) for a in arrays),
        in_specs=[whole(pltpu.HBM)] * kept + [whole(pl.ANY)] * len(after),
        out_specs=(whole(pltpu.HBM),) * kept,
        input_output_aliases={i: i for i in range(kept)},
        cost_estimate=pl.CostEstimate(flops=0, bytes_accessed=0, transcendentals=0),
        name="held_back",
    )(*map(distant, arrays), *after)


def act_grads_kernel(scaled, weight_out, *rest):
    out = rest[-1]
    tile = 768
    for c in range(0, out.shape[1], tile):
        part = lax.dot_general(scaled[...], weight_out[pl.ds(c, tile), :], (((1,), (1,)), ((), ())), preferred_element_type=F32)
        out[:, pl.ds(c, tile)] = part.astype(BF16)


def act_grads(scaled, weight_out, after):
    outs = [((scaled.shape[0], weight_out.shape[0]), BF16, AUTO)]
    return run(act_grads_kernel, "act_grads", [(scaled, AUTO), (weight_out, AUTO)], outs, [], after, micros=6)[0]


def merge_entries(at, bit, keep, got, mine, other):
    low = (1 << at) - 1
    for e in range(mine.shape[0]):
        first = (e >> at << at + 1) + (e & low)
        here, there = first + bit * (low + 1), first + (1 - bit) * (low + 1)
        other[e] = keep(here) + got(there if False else here) if False else keep(there) + got(there)
        mine[e] = keep(here) + got(here)


def first_merge_kernel(cuts, counts, *refs):
    outs, mark, scratch = refs[-12:-6], refs[-6], refs[-5:]
    mark[...] = jnp.zeros_like(mark)
    sems, groups, used, at = scratch[-1], [], 0, 0
    for which, count in enumerate(counts):
        keep, came, got = scratch[2 * which], scratch[2 * which + 1], refs[at + 1 : at + 1 + count]
        chunks, chips, high, width = keep.shape
        for i in range(chunks):
            there = [(refs[at].at[i], keep.at[i])]
            if len(got[0].shape) == 4:
                part = chips // count
                there += [(piece.at[i], came.at[i, pl.ds(p * part, part)]) for p, piece in enumerate(got)]
            else:
                each = count // chunks
                there += [(got[i * each + p], came.at[i, :, :, lanes]) for p, lanes in enumerate(lane_parts(width, each))]
            groups.append(started(there, sems.at[pl.ds(used, len(there))]))
            used += len(there)
        at += 1 + count
    for which in range(2):
        keep, came = scratch[2 * which], scratch[2 * which + 1]
        chunks, _, high, _ = keep.shape
        for i in range(chunks):
            for copy in groups[which * chunks + i]:
                copy.wait()
            pair, row = (which, i * high) if i < chunks - 1 else (2, which * high)
            cut, bit = cuts[pair]
            mine, other = (out.at[:, pl.ds(row, high)] for out in outs[2 * pair : 2 * pair + 2])
            merge_entries(cut, own_bit(bit), lambda e: keep[i, e], lambda e: came[i, e], mine, other)


def first_merge(parts, cuts, after):
    chunks, chips, high, width = parts[0][0].shape
    ins = [(value, place) for (keep, got), near_by in zip(parts, (FAR, NEAR)) for value, place in ((keep, FAR), *((piece, near_by) for piece in got))]
    outs = [((chips // 2, rows, width), BF16, NEAR) for rows in ((chunks - 1) * high, (chunks - 1) * high, 2 * high) for _ in range(2)]
    room = [pltpu.VMEM(keep.shape, BF16) for keep, _ in parts for _ in range(2)] + [pltpu.SemaphoreType.DMA((64,))]
    kernel = functools.partial(first_merge_kernel, cuts, [len(got) for _, got in parts])
    *halves, mark = run(kernel, "first_merge", ins, outs + [((SUB, LANES), F32, AUTO)], room, after, limit=LESS)
    return halves[0::2], halves[1::2], mark


def merge_kernel(jobs, *refs):
    count, pairs = sum(len(job) for job in jobs), 2 * len(jobs)
    outs, mark = refs[-1 - pairs : -1], refs[-1]
    mark[...] = jnp.zeros_like(mark)
    i = 0
    for j, job in enumerate(jobs):
        row = 0
        for at, bit in job:
            keep, got = refs[i], refs[count + i]
            rows = pl.ds(row, keep.shape[1])
            merge_entries(at, own_bit(bit), lambda e: keep[e], lambda e: got[e], outs[2 * j].at[:, rows], outs[2 * j + 1].at[:, rows])
            row += keep.shape[1]
            i += 1


def merge(keeps, gots, jobs, after=()):
    ins = [(value, NEAR) for value in keeps] + [(value, OPEN) for value in gots]
    outs, i = [], 0
    for job in jobs:
        parts = keeps[i : i + len(job)]
        i += len(job)
        outs += [((parts[0].shape[0] // 2, sum(part.shape[1] for part in parts), parts[0].shape[2]), BF16, NEAR)] * 2
    *halves, mark = run(functools.partial(merge_kernel, jobs), "merge_halves", ins, outs + [((SUB, LANES), F32, AUTO)], [], after, limit=LESS)
    return halves[0::2], halves[1::2], mark


def last_kernel(keep, got, less_keep, less_got, in_sum, out_sum):
    total = keep[0].astype(F32) + got[0].astype(F32)
    less = less_keep[0].astype(F32) + less_got[0].astype(F32)
    high = less.shape[0] // 2
    tile = in_sum.shape[1] // CHUNKS
    for i, part in enumerate((total[:high], total[high : 2 * high], less[:high])):
        in_sum[:, pl.ds(i * tile, tile)] = retiled(part, tile)
    out_sum[pl.ds(0, 2 * high), :] = total[2 * high :]
    out_sum[pl.ds(2 * high, high), :] = less[high:]


def last_sums(parts, channels, hidden, after):
    ins = [(parts[0], NEAR), (parts[1], OPEN), (parts[2], NEAR), (parts[3], OPEN)]
    high, width = parts[2].shape[1] // 2, parts[2].shape[2]
    outs = [((channels, hidden), F32, AUTO), ((CHUNKS * high, width), F32, AUTO)]

    def kernel(*refs):
        last_kernel(*refs[:4], *refs[-2:])

    return run(kernel, "last_sums", ins, outs, [], after)


def tap_places():
    reach = np.concatenate([np.arange(s) / s for s in SIDES]).astype(np.float32)
    scale = np.concatenate([np.full(s, 1.0 / math.sqrt(s)) for s in SIDES]).astype(np.float32)
    return reach, scale


def profiles(coefficient, log_rate):
    reach, scale = tap_places()
    decayed = jnp.exp(-jnp.exp(log_rate)[None] * reach[:, None, None])
    return jnp.sum(coefficient[None] * decayed, axis=2) * scale[:, None]


def profile_grads(coefficient, log_rate, grads):
    reach, scale = tap_places()
    rate = jnp.exp(log_rate)
    decayed = jnp.exp(-rate[None] * reach[:, None, None])
    weighted = (grads * scale[:, None])[:, :, None] * decayed
    return jnp.sum(weighted, axis=0), -coefficient * rate * jnp.sum(weighted * reach[:, None, None], axis=0)


def kernel_matrix(profile, part):
    side = part["side"]
    offsets = np.arange(side)[:, None] - np.arange(side)[None, :]
    picked = profile[part["tap"] + np.maximum(offsets, 0)]
    return jnp.where((offsets >= 0)[:, :, None], picked, 0.0)


def mix_plain(plan, row_pixel, channel_rows, height, width, skip):
    def one_channel(given):
        values, high, wide, weight = given
        image_order = jnp.zeros_like(values).at[row_pixel].set(values)
        pieces = []
        for part in plan.sections:
            side, count = part["side"], part["images"] * part["side"] ** 2
            block = image_order[part["pixel"] : part["pixel"] + count].reshape(-1, side, side)
            left = kernel_matrix(high[:, None], part)[:, :, 0]
            right = kernel_matrix(wide[:, None], part)[:, :, 0]
            mixed = jnp.einsum("ik,nkl,jl->nij", left, block, right, precision=lax.Precision.HIGHEST)
            pieces.append(mixed.reshape(-1))
        joined = jnp.concatenate(pieces) + weight * image_order
        return joined[row_pixel]

    return lax.map(jax.checkpoint(one_channel), (channel_rows, height.T, width.T, skip))


def exchange(blocks):
    return lax.all_to_all(blocks, "chan", 0, 0, tiled=True)


def to_blocks(rows, devices):
    return rows.T.reshape(devices, rows.shape[1] // devices, rows.shape[0])


def to_rows(blocks):
    return blocks.reshape(-1, blocks.shape[2]).T


def halve(blocks, bits):
    myself = lax.axis_index("chan")
    size = lax.axis_size("chan")
    pairs = lambda bit: [(i, i ^ 1 << bit) for i in range(size)]
    left = list(range(size.bit_length() - 1))
    for bit in bits:
        at = left.index(bit)
        viewed = blocks.reshape((-1, 2, 1 << at) + blocks.shape[1:])
        own = myself >> bit & 1
        keep = lax.dynamic_index_in_dim(viewed, own, 1, keepdims=False)
        send = lax.dynamic_index_in_dim(viewed, 1 - own, 1, keepdims=False)
        got = lax.ppermute(send, "chan", pairs(bit))
        total = keep.astype(F32) + got.astype(F32)
        left.remove(bit)
        blocks = (total if not left else total.astype(BF16)).reshape((-1,) + blocks.shape[1:])
    return blocks[0]


def swapped(x, bit):
    return lax.ppermute(x, "chan", [(i, i ^ 1 << bit) for i in range(lax.axis_size("chan"))])


def body_fast(
    tokens,
    row_pixel,
    coef_height,
    rate_height,
    coef_width,
    rate_width,
    skip_weight,
    norm_gain,
    norm_bias,
    weight_in,
    bias_in,
    weight_out,
    bias_out,
    layer_scale,
    out_grad,
):
    devices = lax.axis_size("chan")
    rows, width_all = tokens.shape
    plan = Plan(devices, rows, width_all // devices)
    token_blocks = exchange(to_blocks(tokens, devices))
    where = plan.address(row_pixel)
    spread = plan.spread()
    taps = (plan.tile_taps(profiles(coef_height, rate_height)), plan.tile_taps(profiles(coef_width, rate_width)), plan.tile_taps(skip_weight[None]))
    mixed_blocks, packed, across = mixer_forward(plan, where, token_blocks, *taps)

    scaled = out_grad.astype(F32) * layer_scale
    scaled_low = scaled.astype(BF16)
    rows_given = jnp.stack([layer_scale, bias_out, jnp.sum(scaled, axis=0)])
    grad_act = act_grads(scaled_low, weight_out, (rows_given,))
    grad_normin, act, sums, pre_sum, in_keep, in_sent = feed(plan, exchange(mixed_blocks), norm_gain, norm_bias, weight_in, bias_in, grad_act)
    grad_blocks = exchange(grad_normin)
    out_keep, out_sent = out_grad_halves(plan, act, scaled_low)
    out_got = [swapped(piece, 0) for piece in out_sent]
    in_got = [swapped(piece, 0) for piece in in_sent]

    x, y, near_z, far_z = range(1, 5)
    swap = lambda parts, bits: [swapped(part, bit) for part, bit in zip(parts, bits)]
    keeps, sends, mark = first_merge(((in_keep, in_got), (out_keep, out_got)), ((0, x), (1, y), (2, near_z)), (grad_blocks,))
    gots = swap(sends, (x, y, near_z))
    grads, block_out, shares, mark = mixer_arrive(plan, where, grad_blocks, act, weight_out, rows_given, tokens, out_grad, sums, pre_sum, (mark,))
    keeps, sends, mark = merge(keeps, gots, (((0, y),), ((0, x),), ((2, far_z),)), (mark,))
    gots = swap(sends, (y, x, far_z))
    grads, *tap_sums, mark = mixer_backward(plan, grads, *taps, packed, across, (mark,))
    both_keeps, both_sends, mark = merge(keeps[:2], gots[:2], (((0, near_z), (0, near_z)),), (mark,))
    both_gots = swap(both_sends, (near_z,))
    leaving, left = mixer_leave(plan, where, grads, shares, (mark,))
    keeps, sends, mark = merge((both_keeps[0], keeps[2]), (both_gots[0], gots[2]), (((0, far_z),), ((0, x),)), (left,))
    (moved,) = held_back((leaving,), (mark,))
    grad_tokens, *smalls = token_grads(plan, exchange(moved), out_grad, pre_sum.shape[1] // width_all)
    both_got, less_got = swap(sends, (far_z, x))
    less_keeps, less_sends, mark = merge(keeps[1:], (less_got,), (((0, y),),))
    (less_got,) = swap(less_sends, (y,))
    coef_grads = tap_grads(plan, (coef_height, rate_height, coef_width, rate_width), spread.astype(F32), tap_sums, (mark,))
    in_sum, out_sum = last_sums(
        (keeps[0], both_got, less_keeps[0], less_got), plan.channels, weight_in.shape[1], (grad_tokens, *coef_grads)
    )
    gain_grad, norm_bias_grad, bias_in_grad, bias_out_grad, scale_grad = (small[0] for small in smalls)
    return (block_out, grad_tokens, *coef_grads, gain_grad, norm_bias_grad, in_sum, bias_in_grad, out_sum, bias_out_grad, scale_grad)


def body_plain(
    tokens,
    row_pixel,
    coef_height,
    rate_height,
    coef_width,
    rate_width,
    skip_weight,
    norm_gain,
    norm_bias,
    weight_in,
    bias_in,
    weight_out,
    bias_out,
    layer_scale,
    out_grad,
):
    devices = lax.axis_size("chan")
    rows, width_all = tokens.shape
    plan = Plan(devices, rows, width_all // devices)
    token_blocks = exchange(to_blocks(tokens, devices))

    height = profiles(coef_height, rate_height)
    width = profiles(coef_width, rate_width)
    lines = lambda blocks: blocks.transpose(1, 0, 2).reshape(blocks.shape[1], -1)
    blocks_of = lambda values: values.astype(BF16).reshape(-1, devices, rows).transpose(1, 0, 2)
    mixed, mixer_back = jax.vjp(
        functools.partial(mix_plain, plan, row_pixel), lines(token_blocks).astype(F32), height, width, skip_weight
    )
    mixed_blocks = blocks_of(mixed)
    normin = to_rows(exchange(mixed_blocks)).astype(F32)

    upstream = out_grad.astype(F32)
    scaled = upstream * layer_scale
    scaled_low = scaled.astype(BF16)
    grad_act = lax.dot_general(scaled_low, weight_out, (((1,), (1,)), ((), ())), preferred_element_type=F32)

    row_mean = jnp.mean(normin, axis=1, keepdims=True)
    centred = normin - row_mean
    inv_std = lax.rsqrt(jnp.mean(centred * centred, axis=1, keepdims=True) + EPSILON)
    unit_rows = centred * inv_std
    normed = (unit_rows * norm_gain + norm_bias).astype(BF16)
    hidden_pre = jnp.dot(normed, weight_in, preferred_element_type=F32) + bias_in
    cdf = 0.5 * (1.0 + lax.erf(hidden_pre * math.sqrt(0.5)))
    act_low = (hidden_pre * cdf).astype(BF16)
    slope = cdf + hidden_pre * jnp.exp(-0.5 * hidden_pre * hidden_pre) * (1.0 / math.sqrt(2.0 * math.pi))
    grad_pre = grad_act * slope
    grad_pre_low = grad_pre.astype(BF16)
    grad_normed = lax.dot_general(grad_pre_low, weight_in, (((1,), (1,)), ((), ())), preferred_element_type=F32)
    grad_unit = grad_normed * norm_gain
    grad_normin = inv_std * (
        grad_unit
        - jnp.mean(grad_unit, axis=1, keepdims=True)
        - unit_rows * jnp.mean(grad_unit * unit_rows, axis=1, keepdims=True)
    )
    grad_blocks = exchange(to_blocks(grad_normin.astype(BF16), devices))

    branch = jnp.dot(act_low, weight_out, preferred_element_type=F32) + bias_out
    block_out = (tokens.astype(F32) + layer_scale * branch).astype(BF16)
    small = (
        jnp.sum(grad_normed * unit_rows, axis=0),
        jnp.sum(grad_normed, axis=0),
        jnp.sum(grad_pre, axis=0),
        jnp.sum(scaled, axis=0),
        jnp.sum(upstream * branch, axis=0),
    )
    weight_in_part = lax.dot_general(normed, grad_pre_low, (((0,), (0,)), ((), ())), preferred_element_type=F32)
    weight_out_part = lax.dot_general(act_low, scaled_low, (((0,), (0,)), ((), ())), preferred_element_type=F32)

    grad_mixed, grad_height, grad_width, grad_skip = mixer_back(lines(grad_blocks).astype(F32))
    grad_rows = blocks_of(grad_mixed)
    coef_height_grad, rate_height_grad = profile_grads(coef_height, rate_height, grad_height)
    coef_width_grad, rate_width_grad = profile_grads(coef_width, rate_width, grad_width)
    grad_tokens = upstream + to_rows(exchange(grad_rows)).astype(F32)

    levels = list(range(devices.bit_length() - 1))
    other = levels[:1] + levels[1:3][::-1] + levels[3:]
    in_sum = halve(weight_in_part.astype(BF16).reshape(devices, -1, weight_in.shape[1]), levels)
    out_sum = halve(weight_out_part.astype(BF16).reshape(devices, -1, weight_out.shape[1]), other)
    shares = jnp.concatenate([s.reshape(devices, -1) for s in small], axis=1)
    shares = exchange(shares).sum(axis=0)
    cuts = np.cumsum([s.shape[0] // devices for s in small])[:-1]
    gain_grad, norm_bias_grad, bias_in_grad, bias_out_grad, scale_grad = jnp.split(shares, cuts)
    return (
        block_out,
        grad_tokens,
        coef_height_grad,
        rate_height_grad,
        coef_width_grad,
        rate_width_grad,
        grad_skip,
        gain_grad,
        norm_bias_grad,
        in_sum,
        bias_in_grad,
        out_sum,
        bias_out_grad,
        scale_grad,
    )


def solution(mesh):
    split, copied = P("chan"), P()

    def body(tokens, *rest):
        devices = lax.axis_size("chan")
        fast = Plan(devices, tokens.shape[0], tokens.shape[1] // devices).fits() and devices == 32
        return (body_fast if fast else body_plain)(tokens, *rest)

    in_specs = (split, copied) + (split,) * 5 + (copied,) * 7 + (split,)
    return jax.shard_map(body, mesh=mesh, in_specs=in_specs, out_specs=(split,) * 14, check_vma=False)
```

```python
import functools
import math

import jax
import jax.numpy as jnp
import numpy as np
from jax import lax
from jax.experimental import pallas as pl
from jax.experimental.pallas import tpu as pltpu
from jax.sharding import PartitionSpec as P

SIDES = (10, 14, 18)
SHARES = (1, 1, 2)
UNIT = sum(m * s * s for s, m in zip(SIDES, SHARES))
TAPS = sum(SIDES)
EPSILON = 1e-06
LANES = 128
SUB = 8
MARGIN = 32
VMEM = 63 * 2**20
LESS = 36 * 2**20
SMALL = 20 * 2**20
CHUNKS = 3
F32 = jnp.float32
BF16 = jnp.bfloat16


class Plan:
    def __init__(self, devices, rows, channels):
        self.devices, self.rows, self.channels = devices, rows, channels
        self.pixels = devices * rows
        self.units = self.pixels // UNIT
        self.slots = LANES // channels
        self.row_pad = -(-rows // LANES) * LANES
        self.extra_row = -(-rows // SUB) * SUB
        self.sections = []
        image_row, packed_row, tap, mask_row, pixel = 0, 0, 0, 0, 0
        for side, share in zip(SIDES, SHARES):
            images = share * self.units
            pitch = -(-side // SUB) * SUB
            groups = -(-images // self.slots)
            self.sections.append(
                dict(side=side, images=images, pitch=pitch, groups=groups, image_row=image_row, packed_row=packed_row, tap=tap, mask_row=mask_row, pixel=pixel)
            )
            image_row += groups * self.slots * side * pitch
            packed_row += groups * side * pitch
            tap += side
            mask_row += side * pitch
            pixel += images * side * side
        self.image_rows = image_row
        self.packed_rows = packed_row
        self.mask_rows = mask_row

    @property
    def extra_lane(self):
        return self.extra_row - (self.row_pad - LANES)

    def kind(self, lane, which):
        return (lane == self.extra_lane + which) | (lane == self.extra_lane + SUB + which)

    def fits(self):
        room = self.row_pad - self.extra_row >= 2 * SUB
        return room and self.channels % SUB == 0 and 4 * LANES * (self.image_rows + 2 * self.row_pad + 5 * self.packed_rows) < 40 * 2**20

    def address(self, row_pixel):
        where = jnp.zeros_like(row_pixel)
        for part in self.sections:
            local = row_pixel - part["pixel"]
            line = local // part["side"]
            spot = part["image_row"] + line * part["pitch"] + local - line * part["side"]
            where = jnp.where(local >= 0, spot, where)
        return where

    def spread(self):
        lane = np.arange(LANES)
        held = (lane[None, :] % self.channels == np.arange(self.channels)[:, None]) & (lane[None, :] < self.slots * self.channels)
        return jnp.asarray(held.astype(np.float32), BF16)

    def tile_taps(self, taps):
        tiled = jnp.tile(taps, (1, self.slots))
        return jnp.pad(tiled, ((0, 0), (0, LANES - tiled.shape[1])))


def slot_masks(plan):
    lane = lax.broadcasted_iota(jnp.int32, (SUB, LANES), 1)
    return [(lane >= q * plan.channels) & (lane < (q + 1) * plan.channels) for q in range(plan.slots)]


def in_turn(plan, first, second, beside=None, steps=0, ready=None):
    first(0, 0)

    def pair(k):
        first(2 * k + 1, 1)
        second(2 * k, 0)
        first(2 * k + 2, 0)
        second(2 * k + 1, 1)

    def plain(k, carry):
        pair(k)
        return carry

    def more(k, carry):
        beside(k - begin)
        pair(k)
        return carry

    pairs = plan.devices // 2 - 1
    begin = pairs - steps
    lax.fori_loop(0, begin, plain, 0)
    if steps:
        ready()
        lax.fori_loop(begin, pairs, more, 0)
    first(plan.devices - 1, 1)
    second(plan.devices - 2, 0)
    second(plan.devices - 1, 1)


def scatter_rows(plan, where, block, buffers, image, beside=None, steps=0, ready=None):
    def turn(s, held):
        rows = block[s].astype(F32)
        full = [rows] * plan.slots
        if LANES > plan.slots * plan.channels:
            full.append(rows[: LANES - plan.slots * plan.channels])
        buffers[held][pl.ds(0, plan.rows), :] = jnp.concatenate(full, axis=0).T

    def place(s, held):
        base = s * plan.rows
        for u in range(plan.rows):
            image[pl.ds(where[base + u], 1), :] = buffers[held][pl.ds(u, 1), :]

    in_turn(plan, turn, place, beside, steps, ready)


def gather_rows(plan, where, buffers, image, out, extra=None):
    def fetch(s, held):
        base = s * plan.rows
        for u in range(plan.rows):
            buffers[held][pl.ds(u, 1), :] = image[pl.ds(where[base + u], 1), :]

    def fold(s, held):
        turned = buffers[held][...].T
        folded = turned[: plan.channels]
        for q in range(1, plan.slots):
            folded = folded + turned[q * plan.channels : (q + 1) * plan.channels]
        if extra is None:
            out[s] = folded[:, : plan.rows].astype(BF16)
            return
        last = plan.row_pad - LANES
        sums = extra[pl.ds(pl.multiple_of(s * plan.channels, SUB), plan.channels), :]
        lane = lax.broadcasted_iota(jnp.int32, sums.shape, 1) + last
        out[s, :, pl.ds(0, last)] = folded[:, :last].astype(BF16)
        out[s, :, pl.ds(last, LANES)] = jnp.where(lane < plan.extra_row, folded[:, last:], sums).astype(BF16)

    in_turn(plan, fetch, fold)


def pack_images(plan, masks, image, packed, margin):
    place = lax.broadcasted_iota(jnp.int32, (SUB, LANES), 0)
    for part in plan.sections:
        side, pitch = part["side"], part["pitch"]
        area = side * pitch
        ragged = part["images"] < part["groups"] * plan.slots

        def group(t, carry, part=part, side=side, pitch=pitch, area=area, ragged=ragged):
            start = part["image_row"] + t * (plan.slots * area)
            target = margin + part["packed_row"] + t * area
            used = masks
            if ragged:
                used = [mask & (t * plan.slots + q < part["images"]) for q, mask in enumerate(masks)]
            ends = [mask & (place < side % SUB) for mask in used]
            for i in range(side):
                for j in range(0, pitch, SUB):
                    value = jnp.zeros((SUB, LANES), F32)
                    for q in range(plan.slots):
                        row = pl.multiple_of(start + (q * area + i * pitch + j), SUB)
                        value = jnp.where((ends if j + SUB > side else used)[q], image[pl.ds(row, SUB), :], value)
                    packed[pl.ds(pl.multiple_of(target + (i * pitch + j), SUB), SUB), :] = value
            return carry

        lax.fori_loop(0, part["groups"], group, 0)


def unpack_line(plan, masks, part, t, offset, value, image):
    area = part["side"] * part["pitch"]
    for q in range(plan.slots):
        row = pl.multiple_of(part["image_row"] + (t * plan.slots + q) * area + offset, SUB)
        image[pl.ds(row, SUB), :] = jnp.where(masks[q], value, 0.0)


def wide_taps(plan, taps, table):
    for tap in range(TAPS):
        table[pl.ds(tap * SUB, SUB), :] = jnp.broadcast_to(taps[pl.ds(tap, 1), :], (SUB, LANES))


def masked_taps(plan, taps, table):
    for part in plan.sections:
        side, pitch = part["side"], part["pitch"]
        place = lax.broadcasted_iota(jnp.int32, (pitch, LANES), 0)
        for tap in range(side):
            row = taps[pl.ds(part["tap"] + tap, 1), :]
            table[pl.ds(part["mask_row"] + tap * pitch, pitch), :] = jnp.where(place >= tap, row, 0.0)


def forward_kernel(plan, where_far, block, height, width, skip, out, packed, across, first, second, image, where, px, pu, height_wide, width_masked, sems):
    masks = slot_masks(plan)
    indices = pltpu.make_async_copy(where_far, where, sems.at[0])
    indices.start()
    px[pl.ds(0, MARGIN), :] = jnp.zeros((MARGIN, LANES), F32)
    wide_taps(plan, height, height_wide)
    masked_taps(plan, width, width_masked)
    indices.wait()
    scatter_rows(plan, where, block, (first, second), image)
    pack_images(plan, masks, image, px, MARGIN)
    skips = jnp.broadcast_to(skip[...], (SUB, LANES))
    for part in plan.sections:
        side, pitch = part["side"], part["pitch"]
        area = side * pitch

        def group(t, carry, part=part, side=side, pitch=pitch, area=area):
            start = MARGIN + part["packed_row"] + t * area

            for j in range(0, pitch, SUB):
                reach = range(min(side, j + SUB))
                weights = [width_masked[pl.ds(part["mask_row"] + tap * pitch + j, SUB), :] for tap in reach]

                def line(i, inner, j=j, weights=weights):
                    base = start + i * pitch + j
                    total = weights[0] * px[pl.ds(pl.multiple_of(base, SUB), SUB), :]
                    for tap in range(1, len(weights)):
                        total = total + weights[tap] * px[pl.ds(base - tap, SUB), :]
                    pu[pl.ds(pl.multiple_of(base, SUB), SUB), :] = total
                    return inner

                lax.fori_loop(0, side, line, 0, unroll=2)

            def column(c, inner):
                first = pl.multiple_of(start + c * SUB, SUB)
                held = [pu[pl.ds(pl.multiple_of(first + k * pitch, SUB), SUB), :] for k in range(side)]
                for i in range(side):
                    total = skips * px[pl.ds(pl.multiple_of(first + i * pitch, SUB), SUB), :]
                    for k in range(i + 1):
                        total = total + height_wide[pl.ds((part["tap"] + i - k) * SUB, SUB), :] * held[k]
                    unpack_line(plan, masks, part, t, i * pitch + c * SUB, total, image)
                return inner

            lax.fori_loop(0, pitch // SUB, column, 0)
            return carry

        lax.fori_loop(0, part["groups"], group, 0)
    kept = [(px.at[pl.ds(MARGIN, plan.packed_rows)], packed), (pu.at[pl.ds(MARGIN, plan.packed_rows)], across)]
    kept = started(kept, sems.at[pl.ds(1, 2)])
    gather_rows(plan, where, (first, second), image, out)
    for copy in kept:
        copy.wait()


def arrive_kernel(plan, where_far, block_far, act_far, weight_far, given_far, tokens_far, out_grad_far, sums_far, pre_sum_far, *rest):
    grads, block_out, shares, mark, *rest = rest[-20:]
    where, block, first, second, image, act, weight_out, given, tokens, out_grad, sums, pre_sum, branch, rows, came, sems = rest
    mark[...] = jnp.zeros_like(mark)
    soon = started([(block_far, block), (where_far, where)], came.at[pl.ds(2, 2)])
    arriving = started([(act_far, act), (weight_far, weight_out)], came.at[pl.ds(0, 2)])
    there = [(given_far, given), (tokens_far, tokens), (out_grad_far, out_grad), (sums_far, sums), (pre_sum_far, pre_sum)]
    later = started(there, sems)

    def ready():
        for copy in arriving:
            copy.wait()

    def product(k):
        lanes = pl.ds(pl.multiple_of(k * LANES, LANES), LANES)
        branch[:, lanes] = jnp.dot(act[...], weight_out[:, lanes], preferred_element_type=F32)

    for copy in soon:
        copy.wait()
    scatter_rows(plan, where, block, (first, second), image, product, tokens.shape[1] // LANES, ready)
    for copy in later:
        copy.wait()
    scale, bias_out, bias_row = (given[pl.ds(i, 1), :] for i in range(3))
    total = branch[...] + bias_out
    block_out[...] = (tokens[...].astype(F32) + scale * total).astype(BF16)
    scale_row = jnp.sum(out_grad[...].astype(F32) * total, axis=0, keepdims=True)
    shares[...] = small_shares(plan, sums[...], pre_sum[...], bias_row, scale_row, rows)
    pack_images(plan, slot_masks(plan), image, grads, 0)


def leave_kernel(plan, where_far, grads, extra, *rest):
    out, mark, near, far, image, halves, where, sem = rest[-8:]
    indices = pltpu.make_async_copy(where_far, where, sem)
    indices.start()
    mark[...] = jnp.zeros_like(mark)
    masks = slot_masks(plan)
    for part in plan.sections:
        area = part["side"] * part["pitch"]

        def group(t, carry, part=part, area=area):
            for offset in range(0, area, SUB):
                row = pl.multiple_of(part["packed_row"] + t * area + offset, SUB)
                unpack_line(plan, masks, part, t, offset, grads[pl.ds(row, SUB), :], image)
            return carry

        lax.fori_loop(0, part["groups"], group, 0)
    indices.wait()
    exact = extra[...]
    high = exact.astype(BF16).astype(F32)
    lane = lax.broadcasted_iota(jnp.int32, exact.shape, 1)
    halves[...] = jnp.where(lane < plan.extra_lane + SUB, high, exact - high)
    gather_rows(plan, where, (near, far), image, out, halves)


def backward_kernel(plan, pg, height, width, skip, packed_far, across_far, *rest):
    out, height_sums, width_sums, skip_sums, mark, pd, height_wide, width_wide, packed, across, sems = rest[-11:]
    mark[...] = jnp.zeros_like(mark)
    arriving = started([(across_far, across), (packed_far, packed)], sems)
    place = lax.broadcasted_iota(jnp.int32, (SUB, LANES), 0)
    pd[pl.ds(plan.packed_rows, MARGIN), :] = jnp.zeros((MARGIN, LANES), F32)
    wide_taps(plan, height, height_wide)
    wide_taps(plan, width, width_wide)
    skips = jnp.broadcast_to(skip[...], (SUB, LANES))
    skip_sums[...] = jnp.zeros((SUB, LANES), F32)
    height_sums[...] = jnp.zeros((TAPS * SUB, LANES), F32)
    for part in plan.sections:
        side, pitch = part["side"], part["pitch"]
        area = side * pitch

        def group(t, carry, part=part, side=side, pitch=pitch, area=area):
            start = part["packed_row"] + t * area

            def column(c, inner):
                first = pl.multiple_of(start + c * SUB, SUB)
                rows = [pl.ds(pl.multiple_of(first + k * pitch, SUB), SUB) for k in range(side)]
                held = [pg[row, :] for row in rows]
                for k in range(side):
                    total = jnp.zeros((SUB, LANES), F32)
                    for i in range(k, side):
                        total = total + height_wide[pl.ds((part["tap"] + i - k) * SUB, SUB), :] * held[i]
                    pd[rows[k], :] = total
                return inner

            lax.fori_loop(0, pitch // SUB, column, 0)
            return carry

        lax.fori_loop(0, part["groups"], group, 0)
    arriving[0].wait()
    for part in plan.sections:
        side, pitch = part["side"], part["pitch"]
        area = side * pitch

        def group(t, carry, part=part, side=side, pitch=pitch, area=area):
            start = part["packed_row"] + t * area

            def column(c, inner):
                first = pl.multiple_of(start + c * SUB, SUB)
                rows = [pl.ds(pl.multiple_of(first + k * pitch, SUB), SUB) for k in range(side)]
                held = [pg[row, :] for row in rows]
                ways = [across[row, :] for row in rows]
                for tap in range(side):
                    total = held[tap] * ways[0]
                    for k in range(1, side - tap):
                        total = total + held[k + tap] * ways[k]
                    height_sums[pl.ds((part["tap"] + tap) * SUB, SUB), :] += total
                return inner

            lax.fori_loop(0, pitch // SUB, column, 0)
            return carry

        lax.fori_loop(0, part["groups"], group, 0)
    arriving[1].wait()
    for part in plan.sections:
        side, pitch = part["side"], part["pitch"]
        area = side * pitch

        def group(t, carry, part=part, side=side, pitch=pitch, area=area):
            start = part["packed_row"] + t * area

            def line(i, sums):
                sums = list(sums)
                base = start + i * pitch
                aligned = pl.multiple_of(base, SUB)
                for j in range(0, pitch, SUB):
                    here = pl.ds(pl.multiple_of(aligned + j, SUB), SUB)
                    mine, grad = packed[here, :], pg[here, :]
                    total = skips * grad
                    sums[side] = sums[side] + mine * grad
                    for tap in range(min(side, side - j)):
                        moved = pd[pl.ds(base + j + tap, SUB), :]
                        if j + SUB - 1 + tap >= pitch:
                            moved = jnp.where(place + (j + tap) < side, moved, 0.0)
                        total = total + width_wide[pl.ds((part["tap"] + tap) * SUB, SUB), :] * moved
                        sums[tap] = sums[tap] + mine * moved
                    out[here, :] = total
                return tuple(sums)

            return lax.fori_loop(0, side, line, carry)

        zero = jnp.zeros((SUB, LANES), F32)
        sums = lax.fori_loop(0, part["groups"], group, (zero,) * (side + 1))
        for tap in range(side):
            width_sums[pl.ds((part["tap"] + tap) * SUB, SUB), :] = sums[tap]
        skip_sums[...] += sums[side]


def whole(memory):
    return pl.BlockSpec(memory_space=memory)


def lanes_of(rows):
    return jax.ShapeDtypeStruct((rows, LANES), F32)


def row_buffers(plan):
    return [pltpu.VMEM((plan.row_pad, LANES), F32)] * 2 + [pltpu.VMEM((plan.image_rows, LANES), F32)]


def near(values):
    return pltpu.with_memory_space_constraint(values, pltpu.VMEM)


def distant(values):
    return pltpu.with_memory_space_constraint(values, pltpu.HBM)


def kernel_call(kernel, name, micros, memories, out_shape, scratch, args, after=(), stays=(), held=(), left=()):
    single = not isinstance(out_shape, tuple)
    shapes = (out_shape,) if single else out_shape
    shapes = tuple((pltpu.VMEM if i in stays else pltpu.HBM)(o.shape, o.dtype) for i, o in enumerate(shapes))
    outs = tuple(whole(pltpu.VMEM) for _ in shapes)
    place = lambda i, value: near(value) if i in held else value if memories[i] is pltpu.SMEM or i in left else distant(value)
    out = pl.pallas_call(
        kernel,
        out_shape=shapes,
        in_specs=[whole(m) for m in memories] + [whole(pltpu.HBM)] * len(after),
        out_specs=outs,
        scratch_shapes=scratch,
        compiler_params=pltpu.CompilerParams(vmem_limit_bytes=LESS if stays or held else VMEM),
        cost_estimate=pl.CostEstimate(flops=1_000_000, bytes_accessed=int(3_690_000 * micros), transcendentals=0),
        name=name,
    )(*[place(i, value) for i, value in enumerate(args)], *map(distant, after))
    return out[0] if single else out


def mixer_forward(plan, where, block, height, width, skip):
    rows = plan.packed_rows
    ins = [(where, FAR), (block, NEAR), (height, AUTO), (width, AUTO), (skip, AUTO)]
    outs = [(block.shape, BF16, AUTO), ((rows, LANES), F32, FAR), ((rows, LANES), F32, FAR)]
    room = row_buffers(plan) + [
        pltpu.SMEM(where.shape, jnp.int32),
        pltpu.VMEM((rows + MARGIN, LANES), F32),
        pltpu.VMEM((rows + MARGIN, LANES), F32),
        pltpu.VMEM((TAPS * SUB, LANES), F32),
        pltpu.VMEM((plan.mask_rows, LANES), F32),
        pltpu.SemaphoreType.DMA((3,)),
    ]
    return run(functools.partial(forward_kernel, plan), "mixer_forward", ins, outs, room, micros=30, limit=LESS)


def mixer_arrive(plan, where, block, act, weight_out, given, tokens, out_grad, sums, pre_sum, after):
    ins = [(value, FAR) for value in (where, block, act, weight_out, given, tokens, out_grad, sums, pre_sum)]
    width = tokens.shape[1]
    outs = [((plan.packed_rows, LANES), F32, NEAR), (tokens.shape, BF16, AUTO), ((width, LANES), F32, AUTO), ((SUB, LANES), F32, AUTO)]
    room = [pltpu.SMEM(where.shape, jnp.int32), pltpu.VMEM(block.shape, BF16)] + row_buffers(plan) + [pltpu.VMEM(value.shape, value.dtype) for value in (act, weight_out, given, tokens, out_grad, sums, pre_sum)]
    room += [pltpu.VMEM(tokens.shape, F32), pltpu.VMEM((LANES, width), F32), pltpu.SemaphoreType.DMA((4,)), pltpu.SemaphoreType.DMA((5,))]
    return run(functools.partial(arrive_kernel, plan), "mixer_arrive", ins, outs, room, after, limit=LESS)


def mixer_backward(plan, grads, height, width, skip, packed, across, after):
    rows = plan.packed_rows
    ins = [(grads, NEAR), (height, AUTO), (width, AUTO), (skip, AUTO), (packed, FAR), (across, FAR)]
    outs = [((rows, LANES), F32, NEAR)] + [((size, LANES), F32, AUTO) for size in (TAPS * SUB, TAPS * SUB, SUB, SUB)]
    room = [pltpu.VMEM((size, LANES), F32) for size in (rows + MARGIN, TAPS * SUB, TAPS * SUB, rows, rows)]
    room += [pltpu.SemaphoreType.DMA((2,))]
    return run(functools.partial(backward_kernel, plan), "mixer_backward", ins, outs, room, after, limit=LESS)


def mixer_leave(plan, where, grads, extra, after):
    ins = [(where, FAR), (grads, NEAR), (extra, AUTO)]
    outs = [((plan.devices, plan.channels, plan.row_pad), BF16, AUTO), ((SUB, LANES), F32, AUTO)]
    room = row_buffers(plan) + [pltpu.VMEM(extra.shape, F32), pltpu.SMEM(where.shape, jnp.int32), pltpu.SemaphoreType.DMA]
    return run(functools.partial(leave_kernel, plan), "mixer_leave", ins, outs, room, after, limit=LESS)


def taps_kernel(plan, coef_height, rate_height, coef_width, rate_width, spread, height_sums, width_sums, skip_sums, *rest):
    outs = rest[-5:]
    reach, scale = tap_places()
    fold = lambda sums: lax.dot_general(spread[...], sums, (((1,), (1,)), ((), ())), precision=lax.Precision.HIGHEST, preferred_element_type=F32)
    for coef, log_rate, sums, coef_out, rate_out in (
        (coef_height, rate_height, height_sums, outs[0], outs[1]),
        (coef_width, rate_width, width_sums, outs[2], outs[3]),
    ):
        grads = fold(sums[...].reshape(TAPS, SUB, LANES).sum(axis=1))
        rate = jnp.exp(log_rate[...])
        plain, moved = jnp.zeros_like(rate), jnp.zeros_like(rate)
        for tap in range(TAPS):
            weighted = (grads[:, tap : tap + 1] * float(scale[tap])) * jnp.exp(rate * float(-reach[tap]))
            plain = plain + weighted
            moved = moved + weighted * float(reach[tap])
        coef_out[...] = plain
        rate_out[...] = -coef[...] * rate * moved
    total = jnp.sum(skip_sums[...], axis=0, keepdims=True)
    outs[4][...] = lax.dot_general(total, spread[...], (((1,), (1,)), ((), ())), precision=lax.Precision.HIGHEST, preferred_element_type=F32)


def tap_grads(plan, coefs, spread, sums, after):
    shape = jax.ShapeDtypeStruct(coefs[0].shape, F32)
    outs = (shape,) * 4 + (jax.ShapeDtypeStruct((1, plan.channels), F32),)
    *grads, skips = kernel_call(functools.partial(taps_kernel, plan), "tap_grads", 0.01, [pltpu.VMEM] * 8, outs, [], (*coefs, spread, *sums), after)
    return *grads, skips[0]


def tokens_kernel(plan, blocks, out_grad, out, *rest):
    smalls, flipped = rest[:-1], rest[-1]
    total = jnp.zeros((plan.channels, LANES), F32)
    for s in range(plan.devices):
        block = blocks[s].astype(F32)
        flipped[pl.ds(s * plan.channels, plan.channels), :] = block[:, : plan.rows]
        total = total + block[:, plan.row_pad - LANES :]
    first = plan.extra_lane
    rows = total.T
    rows = rows[first : first + SUB] + rows[first + SUB : first + 2 * SUB]
    kind = 0
    for small in smalls:
        for i in range(small.shape[1] // plan.channels):
            small[:, pl.ds(i * plan.channels, plan.channels)] = rows[kind : kind + 1]
            kind += 1
    out[...] = out_grad[...].astype(F32) + flipped[...].T


def token_grads(plan, blocks, out_grad, kinds):
    outs = [(out_grad.shape, F32, AUTO)] + [((1, count * plan.channels), F32, AUTO) for count in (1, 1, kinds, 1, 1)]
    room = [pltpu.VMEM(out_grad.shape[::-1], F32)]
    return run(functools.partial(tokens_kernel, plan), "token_grads", [(blocks, NEAR), (out_grad, AUTO)], outs, room)


def started(pairs, sems):
    copies = [pltpu.make_async_copy(source, target, sems.at[i]) for i, (source, target) in enumerate(pairs)]
    for copy in copies:
        copy.start()
    return copies


NEAR, FAR, AUTO, OPEN, SCALAR = "near", "far", "auto", "open", "scalar"


def run(kernel, name, ins, outs, scratch, after=(), micros=0.01, limit=VMEM):
    same = lambda value: value
    memory = {NEAR: pltpu.VMEM, FAR: pltpu.HBM, AUTO: pltpu.VMEM, OPEN: pltpu.VMEM, SCALAR: pltpu.SMEM}
    hold = {NEAR: near, FAR: distant, AUTO: distant, OPEN: same, SCALAR: same}
    make = {NEAR: pltpu.VMEM, FAR: pltpu.HBM, AUTO: pltpu.HBM, OPEN: jax.ShapeDtypeStruct}
    return pl.pallas_call(
        kernel,
        out_shape=tuple(make[place](shape, dtype) for shape, dtype, place in outs),
        in_specs=[whole(memory[place]) for _, place in ins] + [whole(pltpu.HBM)] * len(after),
        out_specs=tuple(whole(memory[place]) for _, _, place in outs),
        scratch_shapes=scratch,
        compiler_params=pltpu.CompilerParams(vmem_limit_bytes=limit),
        cost_estimate=pl.CostEstimate(flops=1000, bytes_accessed=int(3_690_000 * micros), transcendentals=0),
        name=name,
    )(*[hold[place](value) for value, place in ins], *map(distant, after))


def feed_kernel(plan, blocks, gain, bias, weight_far, bias_in, grad_act_far, grads, act_far, sums, pre_sum, keep_far, *rest):
    sent, scratch = rest[:-12], rest[-12:]
    normed, flipped, unit, total, weight_in, grad_act, act, grad_pre, keep, other, came, left = scratch
    channels, count = plan.channels, plan.devices
    width, hidden = weight_in.shape
    chunks, chips, _, _ = keep.shape
    tile, each = hidden // chunks, len(sent) // chunks
    core = own_bit(0)
    parts = [pl.ds(i * tile, tile) for i in range(chunks)]
    arriving = []
    for i, at in enumerate(parts):
        there = [(weight_far.at[:, at], weight_in.at[:, at]), (grad_act_far.at[:, at], grad_act.at[:, at])]
        arriving.append(started(there, came.at[pl.ds(2 * i, 2)]))
    for s in range(count):
        unit[pl.ds(s * channels, channels), :] = blocks[s].astype(F32)
    mean = jnp.sum(unit[...], axis=0, keepdims=True) * (1.0 / width)
    centred = unit[...] - mean
    inverse = lax.rsqrt(jnp.sum(centred * centred, axis=0, keepdims=True) * (1.0 / width) + EPSILON)
    unit[...] = centred * inverse
    scaled = unit[...] * gain[...] + bias[...]
    flipped[...] = scaled.astype(BF16)
    normed[...] = scaled.T.astype(BF16)
    leaving = []

    def activate(i):
        at = parts[i]
        for copy in (arriving[0] if i == 0 else arriving[1] + arriving[2] if i == 1 else []):
            copy.wait()
        pre = jnp.dot(normed[...], weight_in[:, at], preferred_element_type=F32) + bias_in[:, at]
        cdf = 0.5 * (1.0 + lax.erf(pre * math.sqrt(0.5)))
        act[:, at] = (pre * cdf).astype(BF16)
        slope = cdf + pre * jnp.exp(-0.5 * pre * pre) * (1.0 / math.sqrt(2.0 * math.pi))
        grad = grad_act[:, at] * slope
        pre_sum[:, at] = jnp.sum(grad, axis=0, keepdims=True)
        grad_pre[:, at] = grad.astype(BF16)

    def leave(there):
        leaving.extend(started(there, left.at[pl.ds(len(leaving), len(there))]))

    activate(0)
    for i, at in enumerate(parts):
        if i + 1 < chunks:
            activate(i + 1)
        leave([(act.at[:, at], act_far.at[:, at])])
        part = jnp.dot(flipped[...], grad_pre[:, at], preferred_element_type=F32)
        for c in range(chips):
            first = part[2 * c * channels : (2 * c + 1) * channels]
            second = part[(2 * c + 1) * channels : (2 * c + 2) * channels]
            keep[i, c] = retiled(jnp.where(core == 0, first, second), width).astype(BF16)
            other[i, c] = retiled(jnp.where(core == 0, second, first), width).astype(BF16)
        there = [(other.at[i, :, :, lanes], sent[i * each + p]) for p, lanes in enumerate(lane_parts(width, each))]
        leave(there + [(keep.at[i], keep_far.at[i])])
        back = lax.dot_general(grad_pre[:, at], weight_in[:, at], (((1,), (1,)), ((), ())), preferred_element_type=F32)
        total[...] = back if i == 0 else total[...] + back
    turned = total[...].T
    lane = lax.broadcasted_iota(jnp.int32, sums.shape, 1)
    sums[...] = jnp.where(
        plan.kind(lane, 0),
        jnp.sum(turned * unit[...], axis=1, keepdims=True),
        jnp.where(plan.kind(lane, 1), jnp.sum(turned, axis=1, keepdims=True), 0.0),
    )
    grad = turned * gain[...]
    level = jnp.sum(grad, axis=0, keepdims=True) * (1.0 / width)
    tilt = jnp.sum(grad * unit[...], axis=0, keepdims=True) * (1.0 / width)
    total_low = (inverse * (grad - level - unit[...] * tilt)).astype(BF16)
    for s in range(count):
        grads[s] = total_low[s * channels : (s + 1) * channels]
    for copy in leaving:
        copy.wait()


def feed(plan, blocks, gain, bias, weight_in, bias_in, grad_act):
    rows, width, hidden, chips = plan.rows, plan.devices * plan.channels, weight_in.shape[1], plan.devices // 2
    high, each = plan.channels * hidden // CHUNKS // width, 2
    ins = [(blocks, NEAR), (gain[:, None], AUTO), (bias[:, None], AUTO), (weight_in, FAR), (bias_in[None], AUTO), (grad_act, FAR)]
    outs = [
        (blocks.shape, BF16, AUTO),
        ((rows, hidden), BF16, FAR),
        ((width, LANES), F32, AUTO),
        ((1, hidden), F32, AUTO),
        ((CHUNKS, chips, high, width), BF16, FAR),
    ] + [((chips, high, width // each), BF16, FAR)] * (CHUNKS * each)
    room = [
        pltpu.VMEM((rows, width), BF16),
        pltpu.VMEM((width, rows), BF16),
        pltpu.VMEM((width, rows), F32),
        pltpu.VMEM((rows, width), F32),
        pltpu.VMEM((width, hidden), BF16),
        pltpu.VMEM((rows, hidden), F32),
        pltpu.VMEM((rows, hidden), BF16),
        pltpu.VMEM((rows, hidden), BF16),
        pltpu.VMEM((CHUNKS, chips, high, width), BF16),
        pltpu.VMEM((CHUNKS, chips, high, width), BF16),
        pltpu.SemaphoreType.DMA((2 * CHUNKS,)),
        pltpu.SemaphoreType.DMA((CHUNKS * (each + 2),)),
    ]
    grads, act, sums, pre_sum, keep, *sent = run(functools.partial(feed_kernel, plan), "feed_forward", ins, outs, room, micros=10, limit=LESS)
    return grads, act, sums, pre_sum, keep, sent


def out_grad_kernel(act_far, scaled_far, keep_far, *rest):
    sent, (act, scaled, keep, other, came, left) = rest[:-6], rest[-6:]
    core = own_bit(0)
    chunks, chips, high, width = keep.shape
    height, steps = chunks * high, came.shape[0] - 1
    tile, each, part = act.shape[1] // steps, chips // steps, chips // len(sent)
    parts = [pl.ds(i * tile, tile) for i in range(steps)]
    arriving, leaving = started([(scaled_far, scaled)] + [(act_far.at[:, at], act.at[:, at]) for at in parts], came), []
    arriving[0].wait()
    for i, at in enumerate(parts):
        arriving[1 + i].wait()
        low = lax.dot_general(act[:, at], scaled[...], (((0,), (0,)), ((), ())), preferred_element_type=F32).astype(BF16)
        for c in range(each):
            first = low[2 * c * height : (2 * c + 1) * height]
            second = low[(2 * c + 1) * height : (2 * c + 2) * height]
            mine, yours = jnp.where(core == 0, first, second), jnp.where(core == 0, second, first)
            for chunk in range(chunks):
                keep[chunk, i * each + c] = mine[chunk * high : (chunk + 1) * high]
                other[chunk, i * each + c] = yours[chunk * high : (chunk + 1) * high]
        some = pl.ds(i * each, each)
        there = [(other.at[:, pl.ds(p * part, part)], sent[p]) for p in range(i * each // part, (i + 1) * each // part)]
        there += [(keep.at[:, some], keep_far.at[:, some])]
        leaving += started(there, left.at[pl.ds(len(leaving), len(there))])
    for copy in leaving:
        copy.wait()


def out_grad_halves(plan, act, scaled):
    hidden, width, chips = act.shape[1], scaled.shape[1], plan.devices // 2
    high, steps, pieces = hidden // plan.devices // CHUNKS, hidden // 768, 4
    ins = [(act, FAR), (scaled, FAR)]
    outs = [((CHUNKS, chips, high, width), BF16, FAR)] + [((CHUNKS, chips // pieces, high, width), BF16, FAR)] * pieces
    room = [pltpu.VMEM(value.shape, BF16) for value in (act, scaled)] + [pltpu.VMEM(outs[0][0], BF16)] * 2
    room += [pltpu.SemaphoreType.DMA((1 + steps,)), pltpu.SemaphoreType.DMA((pieces + steps,))]
    keep, *sent = run(out_grad_kernel, "out_grad_halves", ins, outs, room)
    return keep, sent


def own_bit(bit):
    return lax.axis_index("chan") >> bit & 1


def lane_parts(width, count):
    return [pl.ds(p * (width // count), width // count) for p in range(count)]


def retiled(values, width):
    tiles = [values[r : r + SUB, c : c + LANES] for r in range(0, values.shape[0], SUB) for c in range(0, values.shape[1], LANES)]
    each = width // LANES
    return jnp.concatenate([jnp.concatenate(tiles[i : i + each], axis=1) for i in range(0, len(tiles), each)], axis=0)


def small_shares(plan, sums, pre_sum, bias_row, scale_row, rows):
    channels, count = plan.channels, plan.devices
    width = channels * count
    kinds = pre_sum.shape[1] // width
    lane = lax.broadcasted_iota(jnp.int32, sums.shape, 1)
    rows[...] = jnp.zeros_like(rows)
    for kind, row in ((2 + kinds, bias_row), (3 + kinds, scale_row)):
        for again in (0, SUB):
            rows[pl.ds(plan.extra_lane + kind + again, 1), :] = row
    total = sums + rows[...].T
    columns = jnp.broadcast_to(pre_sum, (SUB, pre_sum.shape[1])).T.reshape(count, kinds, channels, SUB)
    for kind in range(kinds):
        column = columns[:, kind].reshape(width, SUB)[:, :1]
        total = total + jnp.where(plan.kind(lane, 2 + kind), column, 0.0)
    return total


def held_back(arrays, after):
    kept = len(arrays)
    return pl.pallas_call(
        lambda *refs: None,
        out_shape=tuple(pltpu.HBM(a.shape, a.dtype) for a in arrays),
        in_specs=[whole(pltpu.HBM)] * kept + [whole(pl.ANY)] * len(after),
        out_specs=(whole(pltpu.HBM),) * kept,
        input_output_aliases={i: i for i in range(kept)},
        cost_estimate=pl.CostEstimate(flops=0, bytes_accessed=0, transcendentals=0),
        name="held_back",
    )(*map(distant, arrays), *after)


def act_grads_kernel(scaled, weight_out, *rest):
    out = rest[-1]
    tile = 768
    for c in range(0, out.shape[1], tile):
        part = lax.dot_general(scaled[...], weight_out[pl.ds(c, tile), :], (((1,), (1,)), ((), ())), preferred_element_type=F32)
        out[:, pl.ds(c, tile)] = part


def act_grads(scaled, weight_out, after):
    outs = [((scaled.shape[0], weight_out.shape[0]), F32, AUTO)]
    return run(act_grads_kernel, "act_grads", [(scaled, AUTO), (weight_out, AUTO)], outs, [], after, micros=6)[0]


def merge_entries(at, bit, keep, got, mine, other):
    low = (1 << at) - 1
    for e in range(mine.shape[0]):
        first = (e >> at << at + 1) + (e & low)
        here, there = first + bit * (low + 1), first + (1 - bit) * (low + 1)
        other[e] = keep(here) + got(there if False else here) if False else keep(there) + got(there)
        mine[e] = keep(here) + got(here)


def first_merge_kernel(cuts, counts, *refs):
    outs, mark, scratch = refs[-12:-6], refs[-6], refs[-5:]
    mark[...] = jnp.zeros_like(mark)
    sems, groups, used, at = scratch[-1], [], 0, 0
    for which, count in enumerate(counts):
        keep, came, got = scratch[2 * which], scratch[2 * which + 1], refs[at + 1 : at + 1 + count]
        chunks, chips, high, width = keep.shape
        for i in range(chunks):
            there = [(refs[at].at[i], keep.at[i])]
            if len(got[0].shape) == 4:
                part = chips // count
                there += [(piece.at[i], came.at[i, pl.ds(p * part, part)]) for p, piece in enumerate(got)]
            else:
                each = count // chunks
                there += [(got[i * each + p], came.at[i, :, :, lanes]) for p, lanes in enumerate(lane_parts(width, each))]
            groups.append(started(there, sems.at[pl.ds(used, len(there))]))
            used += len(there)
        at += 1 + count
    for which in range(2):
        keep, came = scratch[2 * which], scratch[2 * which + 1]
        chunks, _, high, _ = keep.shape
        for i in range(chunks):
            for copy in groups[which * chunks + i]:
                copy.wait()
            pair, row = (which, i * high) if i < chunks - 1 else (2, which * high)
            cut, bit = cuts[pair]
            mine, other = (out.at[:, pl.ds(row, high)] for out in outs[2 * pair : 2 * pair + 2])
            merge_entries(cut, own_bit(bit), lambda e: keep[i, e], lambda e: came[i, e], mine, other)


def first_merge(parts, cuts, after):
    chunks, chips, high, width = parts[0][0].shape
    ins = [(value, place) for (keep, got), near_by in zip(parts, (FAR, NEAR)) for value, place in ((keep, FAR), *((piece, near_by) for piece in got))]
    outs = [((chips // 2, rows, width), BF16, NEAR) for rows in ((chunks - 1) * high, (chunks - 1) * high, 2 * high) for _ in range(2)]
    room = [pltpu.VMEM(keep.shape, BF16) for keep, _ in parts for _ in range(2)] + [pltpu.SemaphoreType.DMA((64,))]
    kernel = functools.partial(first_merge_kernel, cuts, [len(got) for _, got in parts])
    *halves, mark = run(kernel, "first_merge", ins, outs + [((SUB, LANES), F32, AUTO)], room, after, limit=LESS)
    return halves[0::2], halves[1::2], mark


def merge_kernel(jobs, *refs):
    count, pairs = sum(len(job) for job in jobs), 2 * len(jobs)
    outs, mark = refs[-1 - pairs : -1], refs[-1]
    mark[...] = jnp.zeros_like(mark)
    i = 0
    for j, job in enumerate(jobs):
        row = 0
        for at, bit in job:
            keep, got = refs[i], refs[count + i]
            rows = pl.ds(row, keep.shape[1])
            merge_entries(at, own_bit(bit), lambda e: keep[e], lambda e: got[e], outs[2 * j].at[:, rows], outs[2 * j + 1].at[:, rows])
            row += keep.shape[1]
            i += 1


def merge(keeps, gots, jobs, after=()):
    ins = [(value, NEAR) for value in keeps] + [(value, OPEN) for value in gots]
    outs, i = [], 0
    for job in jobs:
        parts = keeps[i : i + len(job)]
        i += len(job)
        outs += [((parts[0].shape[0] // 2, sum(part.shape[1] for part in parts), parts[0].shape[2]), BF16, NEAR)] * 2
    *halves, mark = run(functools.partial(merge_kernel, jobs), "merge_halves", ins, outs + [((SUB, LANES), F32, AUTO)], [], after, limit=LESS)
    return halves[0::2], halves[1::2], mark


def last_kernel(keep, got, less_keep, less_got, in_sum, out_sum):
    total = keep[0].astype(F32) + got[0].astype(F32)
    less = less_keep[0].astype(F32) + less_got[0].astype(F32)
    high = less.shape[0] // 2
    tile = in_sum.shape[1] // CHUNKS
    for i, part in enumerate((total[:high], total[high : 2 * high], less[:high])):
        in_sum[:, pl.ds(i * tile, tile)] = retiled(part, tile)
    out_sum[pl.ds(0, 2 * high), :] = total[2 * high :]
    out_sum[pl.ds(2 * high, high), :] = less[high:]


def last_sums(parts, channels, hidden, after):
    ins = [(parts[0], NEAR), (parts[1], OPEN), (parts[2], NEAR), (parts[3], OPEN)]
    high, width = parts[2].shape[1] // 2, parts[2].shape[2]
    outs = [((channels, hidden), F32, AUTO), ((CHUNKS * high, width), F32, AUTO)]

    def kernel(*refs):
        last_kernel(*refs[:4], *refs[-2:])

    return run(kernel, "last_sums", ins, outs, [], after)


def tap_places():
    reach = np.concatenate([np.arange(s) / s for s in SIDES]).astype(np.float32)
    scale = np.concatenate([np.full(s, 1.0 / math.sqrt(s)) for s in SIDES]).astype(np.float32)
    return reach, scale


def profiles(coefficient, log_rate):
    reach, scale = tap_places()
    decayed = jnp.exp(-jnp.exp(log_rate)[None] * reach[:, None, None])
    return jnp.sum(coefficient[None] * decayed, axis=2) * scale[:, None]


def profile_grads(coefficient, log_rate, grads):
    reach, scale = tap_places()
    rate = jnp.exp(log_rate)
    decayed = jnp.exp(-rate[None] * reach[:, None, None])
    weighted = (grads * scale[:, None])[:, :, None] * decayed
    return jnp.sum(weighted, axis=0), -coefficient * rate * jnp.sum(weighted * reach[:, None, None], axis=0)


def kernel_matrix(profile, part):
    side = part["side"]
    offsets = np.arange(side)[:, None] - np.arange(side)[None, :]
    picked = profile[part["tap"] + np.maximum(offsets, 0)]
    return jnp.where((offsets >= 0)[:, :, None], picked, 0.0)


def mix_plain(plan, row_pixel, channel_rows, height, width, skip):
    def one_channel(given):
        values, high, wide, weight = given
        image_order = jnp.zeros_like(values).at[row_pixel].set(values)
        pieces = []
        for part in plan.sections:
            side, count = part["side"], part["images"] * part["side"] ** 2
            block = image_order[part["pixel"] : part["pixel"] + count].reshape(-1, side, side)
            left = kernel_matrix(high[:, None], part)[:, :, 0]
            right = kernel_matrix(wide[:, None], part)[:, :, 0]
            mixed = jnp.einsum("ik,nkl,jl->nij", left, block, right, precision=lax.Precision.HIGHEST)
            pieces.append(mixed.reshape(-1))
        joined = jnp.concatenate(pieces) + weight * image_order
        return joined[row_pixel]

    return lax.map(jax.checkpoint(one_channel), (channel_rows, height.T, width.T, skip))


def exchange(blocks):
    return lax.all_to_all(blocks, "chan", 0, 0, tiled=True)


def to_blocks(rows, devices):
    return rows.T.reshape(devices, rows.shape[1] // devices, rows.shape[0])


def to_rows(blocks):
    return blocks.reshape(-1, blocks.shape[2]).T


def halve(blocks, bits):
    myself = lax.axis_index("chan")
    size = lax.axis_size("chan")
    pairs = lambda bit: [(i, i ^ 1 << bit) for i in range(size)]
    left = list(range(size.bit_length() - 1))
    for bit in bits:
        at = left.index(bit)
        viewed = blocks.reshape((-1, 2, 1 << at) + blocks.shape[1:])
        own = myself >> bit & 1
        keep = lax.dynamic_index_in_dim(viewed, own, 1, keepdims=False)
        send = lax.dynamic_index_in_dim(viewed, 1 - own, 1, keepdims=False)
        got = lax.ppermute(send, "chan", pairs(bit))
        total = keep.astype(F32) + got.astype(F32)
        left.remove(bit)
        blocks = (total if not left else total.astype(BF16)).reshape((-1,) + blocks.shape[1:])
    return blocks[0]


def swapped(x, bit):
    return lax.ppermute(x, "chan", [(i, i ^ 1 << bit) for i in range(lax.axis_size("chan"))])


def body_fast(
    tokens,
    row_pixel,
    coef_height,
    rate_height,
    coef_width,
    rate_width,
    skip_weight,
    norm_gain,
    norm_bias,
    weight_in,
    bias_in,
    weight_out,
    bias_out,
    layer_scale,
    out_grad,
):
    devices = lax.axis_size("chan")
    rows, width_all = tokens.shape
    plan = Plan(devices, rows, width_all // devices)
    token_blocks = exchange(to_blocks(tokens, devices))
    where = plan.address(row_pixel)
    spread = plan.spread()
    taps = (plan.tile_taps(profiles(coef_height, rate_height)), plan.tile_taps(profiles(coef_width, rate_width)), plan.tile_taps(skip_weight[None]))
    mixed_blocks, packed, across = mixer_forward(plan, where, token_blocks, *taps)

    scaled = out_grad.astype(F32) * layer_scale
    scaled_low = scaled.astype(BF16)
    rows_given = jnp.stack([layer_scale, bias_out, jnp.sum(scaled, axis=0)])
    grad_act = act_grads(scaled_low, weight_out, (rows_given,))
    grad_normin, act, sums, pre_sum, in_keep, in_sent = feed(plan, exchange(mixed_blocks), norm_gain, norm_bias, weight_in, bias_in, grad_act)
    grad_blocks = exchange(grad_normin)
    out_keep, out_sent = out_grad_halves(plan, act, scaled_low)
    out_got = [swapped(piece, 0) for piece in out_sent]
    in_got = [swapped(piece, 0) for piece in in_sent]

    x, y, near_z, far_z = range(1, 5)
    swap = lambda parts, bits: [swapped(part, bit) for part, bit in zip(parts, bits)]
    keeps, sends, mark = first_merge(((in_keep, in_got), (out_keep, out_got)), ((0, x), (1, y), (2, near_z)), (grad_blocks,))
    gots = swap(sends, (x, y, near_z))
    grads, block_out, shares, mark = mixer_arrive(plan, where, grad_blocks, act, weight_out, rows_given, tokens, out_grad, sums, pre_sum, (mark,))
    keeps, sends, mark = merge(keeps, gots, (((0, y),), ((0, x),), ((2, far_z),)), (mark,))
    gots = swap(sends, (y, x, far_z))
    grads, *tap_sums, mark = mixer_backward(plan, grads, *taps, packed, across, (mark,))
    both_keeps, both_sends, mark = merge(keeps[:2], gots[:2], (((0, near_z), (0, near_z)),), (mark,))
    both_gots = swap(both_sends, (near_z,))
    leaving, left = mixer_leave(plan, where, grads, shares, (mark,))
    keeps, sends, mark = merge((both_keeps[0], keeps[2]), (both_gots[0], gots[2]), (((0, far_z),), ((0, x),)), (left,))
    (moved,) = held_back((leaving,), (mark,))
    grad_tokens, *smalls = token_grads(plan, exchange(moved), out_grad, pre_sum.shape[1] // width_all)
    both_got, less_got = swap(sends, (far_z, x))
    less_keeps, less_sends, mark = merge(keeps[1:], (less_got,), (((0, y),),))
    (less_got,) = swap(less_sends, (y,))
    coef_grads = tap_grads(plan, (coef_height, rate_height, coef_width, rate_width), spread.astype(F32), tap_sums, (mark,))
    in_sum, out_sum = last_sums(
        (keeps[0], both_got, less_keeps[0], less_got), plan.channels, weight_in.shape[1], (grad_tokens, *coef_grads)
    )
    gain_grad, norm_bias_grad, bias_in_grad, bias_out_grad, scale_grad = (small[0] for small in smalls)
    return (block_out, grad_tokens, *coef_grads, gain_grad, norm_bias_grad, in_sum, bias_in_grad, out_sum, bias_out_grad, scale_grad)


def body_plain(
    tokens,
    row_pixel,
    coef_height,
    rate_height,
    coef_width,
    rate_width,
    skip_weight,
    norm_gain,
    norm_bias,
    weight_in,
    bias_in,
    weight_out,
    bias_out,
    layer_scale,
    out_grad,
):
    devices = lax.axis_size("chan")
    rows, width_all = tokens.shape
    plan = Plan(devices, rows, width_all // devices)
    token_blocks = exchange(to_blocks(tokens, devices))

    height = profiles(coef_height, rate_height)
    width = profiles(coef_width, rate_width)
    lines = lambda blocks: blocks.transpose(1, 0, 2).reshape(blocks.shape[1], -1)
    blocks_of = lambda values: values.astype(BF16).reshape(-1, devices, rows).transpose(1, 0, 2)
    mixed, mixer_back = jax.vjp(
        functools.partial(mix_plain, plan, row_pixel), lines(token_blocks).astype(F32), height, width, skip_weight
    )
    mixed_blocks = blocks_of(mixed)
    normin = to_rows(exchange(mixed_blocks)).astype(F32)

    upstream = out_grad.astype(F32)
    scaled = upstream * layer_scale
    scaled_low = scaled.astype(BF16)
    grad_act = lax.dot_general(scaled_low, weight_out, (((1,), (1,)), ((), ())), preferred_element_type=F32)

    row_mean = jnp.mean(normin, axis=1, keepdims=True)
    centred = normin - row_mean
    inv_std = lax.rsqrt(jnp.mean(centred * centred, axis=1, keepdims=True) + EPSILON)
    unit_rows = centred * inv_std
    normed = (unit_rows * norm_gain + norm_bias).astype(BF16)
    hidden_pre = jnp.dot(normed, weight_in, preferred_element_type=F32) + bias_in
    cdf = 0.5 * (1.0 + lax.erf(hidden_pre * math.sqrt(0.5)))
    act_low = (hidden_pre * cdf).astype(BF16)
    slope = cdf + hidden_pre * jnp.exp(-0.5 * hidden_pre * hidden_pre) * (1.0 / math.sqrt(2.0 * math.pi))
    grad_pre = grad_act * slope
    grad_pre_low = grad_pre.astype(BF16)
    grad_normed = lax.dot_general(grad_pre_low, weight_in, (((1,), (1,)), ((), ())), preferred_element_type=F32)
    grad_unit = grad_normed * norm_gain
    grad_normin = inv_std * (
        grad_unit
        - jnp.mean(grad_unit, axis=1, keepdims=True)
        - unit_rows * jnp.mean(grad_unit * unit_rows, axis=1, keepdims=True)
    )
    grad_blocks = exchange(to_blocks(grad_normin.astype(BF16), devices))

    branch = jnp.dot(act_low, weight_out, preferred_element_type=F32) + bias_out
    block_out = (tokens.astype(F32) + layer_scale * branch).astype(BF16)
    small = (
        jnp.sum(grad_normed * unit_rows, axis=0),
        jnp.sum(grad_normed, axis=0),
        jnp.sum(grad_pre, axis=0),
        jnp.sum(scaled, axis=0),
        jnp.sum(upstream * branch, axis=0),
    )
    weight_in_part = lax.dot_general(normed, grad_pre_low, (((0,), (0,)), ((), ())), preferred_element_type=F32)
    weight_out_part = lax.dot_general(act_low, scaled_low, (((0,), (0,)), ((), ())), preferred_element_type=F32)

    grad_mixed, grad_height, grad_width, grad_skip = mixer_back(lines(grad_blocks).astype(F32))
    grad_rows = blocks_of(grad_mixed)
    coef_height_grad, rate_height_grad = profile_grads(coef_height, rate_height, grad_height)
    coef_width_grad, rate_width_grad = profile_grads(coef_width, rate_width, grad_width)
    grad_tokens = upstream + to_rows(exchange(grad_rows)).astype(F32)

    levels = list(range(devices.bit_length() - 1))
    other = levels[:1] + levels[1:3][::-1] + levels[3:]
    in_sum = halve(weight_in_part.astype(BF16).reshape(devices, -1, weight_in.shape[1]), levels)
    out_sum = halve(weight_out_part.astype(BF16).reshape(devices, -1, weight_out.shape[1]), other)
    shares = jnp.concatenate([s.reshape(devices, -1) for s in small], axis=1)
    shares = exchange(shares).sum(axis=0)
    cuts = np.cumsum([s.shape[0] // devices for s in small])[:-1]
    gain_grad, norm_bias_grad, bias_in_grad, bias_out_grad, scale_grad = jnp.split(shares, cuts)
    return (
        block_out,
        grad_tokens,
        coef_height_grad,
        rate_height_grad,
        coef_width_grad,
        rate_width_grad,
        grad_skip,
        gain_grad,
        norm_bias_grad,
        in_sum,
        bias_in_grad,
        out_sum,
        bias_out_grad,
        scale_grad,
    )


def solution(mesh):
    split, copied = P("chan"), P()

    def body(tokens, *rest):
        devices = lax.axis_size("chan")
        fast = Plan(devices, tokens.shape[0], tokens.shape[1] // devices).fits() and devices == 32
        return (body_fast if fast else body_plain)(tokens, *rest)

    in_specs = (split, copied) + (split,) * 5 + (copied,) * 7 + (split,)
    return jax.shard_map(body, mesh=mesh, in_specs=in_specs, out_specs=(split,) * 14, check_vma=False)
```

```python
import functools
import math

import jax
import jax.numpy as jnp
import numpy as np
from jax import lax
from jax.experimental import pallas as pl
from jax.experimental.pallas import tpu as pltpu
from jax.sharding import PartitionSpec as P

SIDES = (10, 14, 18)
SHARES = (1, 1, 2)
UNIT = sum(m * s * s for s, m in zip(SIDES, SHARES))
TAPS = sum(SIDES)
EPSILON = 1e-06
LANES = 128
SUB = 8
MARGIN = 32
VMEM = 63 * 2**20
LESS = 36 * 2**20
SMALL = 20 * 2**20
CHUNKS = 3
F32 = jnp.float32
BF16 = jnp.bfloat16


class Plan:
    def __init__(self, devices, rows, channels):
        self.devices, self.rows, self.channels = devices, rows, channels
        self.pixels = devices * rows
        self.units = self.pixels // UNIT
        self.slots = LANES // channels
        self.row_pad = -(-rows // LANES) * LANES
        self.extra_row = -(-rows // SUB) * SUB
        self.sections = []
        image_row, packed_row, tap, mask_row, pixel = 0, 0, 0, 0, 0
        for side, share in zip(SIDES, SHARES):
            images = share * self.units
            pitch = -(-side // SUB) * SUB
            groups = -(-images // self.slots)
            self.sections.append(
                dict(side=side, images=images, pitch=pitch, groups=groups, image_row=image_row, packed_row=packed_row, tap=tap, mask_row=mask_row, pixel=pixel)
            )
            image_row += groups * self.slots * side * pitch
            packed_row += groups * side * pitch
            tap += side
            mask_row += side * pitch
            pixel += images * side * side
        self.image_rows = image_row
        self.packed_rows = packed_row
        self.mask_rows = mask_row

    @property
    def extra_lane(self):
        return self.extra_row - (self.row_pad - LANES)

    def kind(self, lane, which):
        return (lane == self.extra_lane + which) | (lane == self.extra_lane + SUB + which)

    def fits(self):
        room = self.row_pad - self.extra_row >= 2 * SUB
        return room and self.channels % SUB == 0 and 4 * LANES * (self.image_rows + 2 * self.row_pad + 5 * self.packed_rows) < 40 * 2**20

    def address(self, row_pixel):
        where = jnp.zeros_like(row_pixel)
        for part in self.sections:
            local = row_pixel - part["pixel"]
            line = local // part["side"]
            spot = part["image_row"] + line * part["pitch"] + local - line * part["side"]
            where = jnp.where(local >= 0, spot, where)
        return where

    def spread(self):
        lane = np.arange(LANES)
        held = (lane[None, :] % self.channels == np.arange(self.channels)[:, None]) & (lane[None, :] < self.slots * self.channels)
        return jnp.asarray(held.astype(np.float32), BF16)

    def tile_taps(self, taps):
        tiled = jnp.tile(taps, (1, self.slots))
        return jnp.pad(tiled, ((0, 0), (0, LANES - tiled.shape[1])))


def slot_masks(plan):
    lane = lax.broadcasted_iota(jnp.int32, (SUB, LANES), 1)
    return [(lane >= q * plan.channels) & (lane < (q + 1) * plan.channels) for q in range(plan.slots)]


def in_turn(plan, first, second, beside=None, steps=0, ready=None):
    first(0, 0)

    def pair(k):
        first(2 * k + 1, 1)
        second(2 * k, 0)
        first(2 * k + 2, 0)
        second(2 * k + 1, 1)

    def plain(k, carry):
        pair(k)
        return carry

    def more(k, carry):
        beside(k - begin)
        pair(k)
        return carry

    pairs = plan.devices // 2 - 1
    begin = pairs - steps
    lax.fori_loop(0, begin, plain, 0)
    if steps:
        ready()
        lax.fori_loop(begin, pairs, more, 0)
    first(plan.devices - 1, 1)
    second(plan.devices - 2, 0)
    second(plan.devices - 1, 1)


def scatter_rows(plan, where, block, buffers, image, beside=None, steps=0, ready=None):
    def turn(s, held):
        rows = block[s].astype(F32)
        full = [rows] * plan.slots
        if LANES > plan.slots * plan.channels:
            full.append(rows[: LANES - plan.slots * plan.channels])
        buffers[held][pl.ds(0, plan.rows), :] = jnp.concatenate(full, axis=0).T

    def place(s, held):
        base = s * plan.rows
        for u in range(plan.rows):
            image[pl.ds(where[base + u], 1), :] = buffers[held][pl.ds(u, 1), :]

    in_turn(plan, turn, place, beside, steps, ready)


def gather_rows(plan, where, buffers, image, out, extra=None, leave=None):
    def fetch(s, held):
        base = s * plan.rows
        for u in range(plan.rows):
            buffers[held][pl.ds(u, 1), :] = image[pl.ds(where[base + u], 1), :]

    def fold(s, held):
        turned = buffers[held][...].T
        folded = turned[: plan.channels]
        for q in range(1, plan.slots):
            folded = folded + turned[q * plan.channels : (q + 1) * plan.channels]
        if extra is None:
            out[s] = folded[:, : plan.rows].astype(BF16)
            leave(s)
            return
        last = plan.row_pad - LANES
        sums = extra[pl.ds(pl.multiple_of(s * plan.channels, SUB), plan.channels), :]
        lane = lax.broadcasted_iota(jnp.int32, sums.shape, 1) + last
        out[s, :, pl.ds(0, last)] = folded[:, :last].astype(BF16)
        out[s, :, pl.ds(last, LANES)] = jnp.where(lane < plan.extra_row, folded[:, last:], sums).astype(BF16)

    in_turn(plan, fetch, fold)


def pack_images(plan, masks, image, packed, margin):
    place = lax.broadcasted_iota(jnp.int32, (SUB, LANES), 0)
    for part in plan.sections:
        side, pitch = part["side"], part["pitch"]
        area = side * pitch
        ragged = part["images"] < part["groups"] * plan.slots

        def group(t, carry, part=part, side=side, pitch=pitch, area=area, ragged=ragged):
            start = part["image_row"] + t * (plan.slots * area)
            target = margin + part["packed_row"] + t * area
            used = masks
            if ragged:
                used = [mask & (t * plan.slots + q < part["images"]) for q, mask in enumerate(masks)]
            ends = [mask & (place < side % SUB) for mask in used]
            for i in range(side):
                for j in range(0, pitch, SUB):
                    value = jnp.zeros((SUB, LANES), F32)
                    for q in range(plan.slots):
                        row = pl.multiple_of(start + (q * area + i * pitch + j), SUB)
                        value = jnp.where((ends if j + SUB > side else used)[q], image[pl.ds(row, SUB), :], value)
                    packed[pl.ds(pl.multiple_of(target + (i * pitch + j), SUB), SUB), :] = value
            return carry

        lax.fori_loop(0, part["groups"], group, 0)


def unpack_line(plan, masks, part, t, offset, value, image):
    area = part["side"] * part["pitch"]
    for q in range(plan.slots):
        row = pl.multiple_of(part["image_row"] + (t * plan.slots + q) * area + offset, SUB)
        image[pl.ds(row, SUB), :] = jnp.where(masks[q], value, 0.0)


def wide_taps(plan, taps, table):
    for tap in range(TAPS):
        table[pl.ds(tap * SUB, SUB), :] = jnp.broadcast_to(taps[pl.ds(tap, 1), :], (SUB, LANES))


def masked_taps(plan, taps, table):
    for part in plan.sections:
        side, pitch = part["side"], part["pitch"]
        place = lax.broadcasted_iota(jnp.int32, (pitch, LANES), 0)
        for tap in range(side):
            row = taps[pl.ds(part["tap"] + tap, 1), :]
            table[pl.ds(part["mask_row"] + tap * pitch, pitch), :] = jnp.where(place >= tap, row, 0.0)


def forward_kernel(plan, where_far, block, height_far, width_far, skip_far, out_far, packed, across, first, second, image, where, px, pu, height_wide, width_masked, sems, *rest):
    height, width, skip, out, left = rest
    small = started([(height_far, height), (width_far, width), (skip_far, skip)], sems.at[pl.ds(3, 3)])
    masks = slot_masks(plan)
    indices = pltpu.make_async_copy(where_far, where, sems.at[0])
    indices.start()
    px[pl.ds(0, MARGIN), :] = jnp.zeros((MARGIN, LANES), F32)
    for copy in small:
        copy.wait()
    wide_taps(plan, height, height_wide)
    masked_taps(plan, width, width_masked)
    indices.wait()
    scatter_rows(plan, where, block, (first, second), image)
    pack_images(plan, masks, image, px, MARGIN)
    skips = jnp.broadcast_to(skip[...], (SUB, LANES))
    for part in plan.sections:
        side, pitch = part["side"], part["pitch"]
        area = side * pitch

        def group(t, carry, part=part, side=side, pitch=pitch, area=area):
            start = MARGIN + part["packed_row"] + t * area

            for j in range(0, pitch, SUB):
                reach = range(min(side, j + SUB))
                weights = [width_masked[pl.ds(part["mask_row"] + tap * pitch + j, SUB), :] for tap in reach]

                def line(i, inner, j=j, weights=weights):
                    base = start + i * pitch + j
                    total = weights[0] * px[pl.ds(pl.multiple_of(base, SUB), SUB), :]
                    for tap in range(1, len(weights)):
                        total = total + weights[tap] * px[pl.ds(base - tap, SUB), :]
                    pu[pl.ds(pl.multiple_of(base, SUB), SUB), :] = total
                    return inner

                lax.fori_loop(0, side, line, 0, unroll=2)

            def column(c, inner):
                first = pl.multiple_of(start + c * SUB, SUB)
                held = [pu[pl.ds(pl.multiple_of(first + k * pitch, SUB), SUB), :] for k in range(side)]
                for i in range(side):
                    total = skips * px[pl.ds(pl.multiple_of(first + i * pitch, SUB), SUB), :]
                    for k in range(i + 1):
                        total = total + height_wide[pl.ds((part["tap"] + i - k) * SUB, SUB), :] * held[k]
                    unpack_line(plan, masks, part, t, i * pitch + c * SUB, total, image)
                return inner

            lax.fori_loop(0, pitch // SUB, column, 0)
            return carry

        lax.fori_loop(0, part["groups"], group, 0)
    kept = [(px.at[pl.ds(MARGIN, plan.packed_rows)], packed), (pu.at[pl.ds(MARGIN, plan.packed_rows)], across)]
    kept = started(kept, sems.at[pl.ds(1, 2)])
    leaving = lambda s: pltpu.make_async_copy(out.at[s], out_far.at[s], left.at[s])
    gather_rows(plan, where, (first, second), image, out, leave=lambda s: leaving(s).start())
    for copy in kept:
        copy.wait()

    def gone(s, carry):
        leaving(s).wait()
        return carry

    lax.fori_loop(0, plan.devices, gone, 0)


def arrive_kernel(plan, where_far, block_far, act_far, weight_far, given_far, tokens_far, out_grad_far, sums_far, pre_sum_far, *rest):
    grads, block_out, shares, mark, *rest = rest[-20:]
    where, block, first, second, image, act, weight_out, given, tokens, out_grad, sums, pre_sum, branch, rows, came, sems = rest
    mark[...] = jnp.zeros_like(mark)
    soon = started([(block_far, block), (where_far, where)], came.at[pl.ds(2, 2)])
    arriving = started([(act_far, act), (weight_far, weight_out)], came.at[pl.ds(0, 2)])
    there = [(given_far, given), (tokens_far, tokens), (out_grad_far, out_grad), (sums_far, sums), (pre_sum_far, pre_sum)]
    later = started(there, sems)

    def ready():
        for copy in arriving:
            copy.wait()

    def product(k):
        lanes = pl.ds(pl.multiple_of(k * LANES, LANES), LANES)
        branch[:, lanes] = jnp.dot(act[...], weight_out[:, lanes], preferred_element_type=F32)

    for copy in soon:
        copy.wait()
    scatter_rows(plan, where, block, (first, second), image, product, tokens.shape[1] // LANES, ready)
    for copy in later:
        copy.wait()
    scale, bias_out, bias_row = (given[pl.ds(i, 1), :] for i in range(3))
    total = branch[...] + bias_out
    block_out[...] = (tokens[...].astype(F32) + scale * total).astype(BF16)
    scale_row = jnp.sum(out_grad[...].astype(F32) * total, axis=0, keepdims=True)
    shares[...] = small_shares(plan, sums[...], pre_sum[...], bias_row, scale_row, rows)
    pack_images(plan, slot_masks(plan), image, grads, 0)


def leave_kernel(plan, where_far, grads, extra, *rest):
    out, mark, near, far, image, halves, where, sem = rest[-8:]
    indices = pltpu.make_async_copy(where_far, where, sem)
    indices.start()
    mark[...] = jnp.zeros_like(mark)
    masks = slot_masks(plan)
    for part in plan.sections:
        area = part["side"] * part["pitch"]

        def group(t, carry, part=part, area=area):
            for offset in range(0, area, SUB):
                row = pl.multiple_of(part["packed_row"] + t * area + offset, SUB)
                unpack_line(plan, masks, part, t, offset, grads[pl.ds(row, SUB), :], image)
            return carry

        lax.fori_loop(0, part["groups"], group, 0)
    indices.wait()
    exact = extra[...]
    high = exact.astype(BF16).astype(F32)
    lane = lax.broadcasted_iota(jnp.int32, exact.shape, 1)
    halves[...] = jnp.where(lane < plan.extra_lane + SUB, high, exact - high)
    gather_rows(plan, where, (near, far), image, out, halves)


def backward_kernel(plan, pg, height, width, skip, packed_far, across_far, *rest):
    out, height_sums, width_sums, skip_sums, mark, pd, height_wide, width_wide, packed, across, sems = rest[-11:]
    mark[...] = jnp.zeros_like(mark)
    arriving = started([(across_far, across), (packed_far, packed)], sems)
    place = lax.broadcasted_iota(jnp.int32, (SUB, LANES), 0)
    pd[pl.ds(plan.packed_rows, MARGIN), :] = jnp.zeros((MARGIN, LANES), F32)
    wide_taps(plan, height, height_wide)
    wide_taps(plan, width, width_wide)
    skips = jnp.broadcast_to(skip[...], (SUB, LANES))
    skip_sums[...] = jnp.zeros((SUB, LANES), F32)
    height_sums[...] = jnp.zeros((TAPS * SUB, LANES), F32)
    for part in plan.sections:
        side, pitch = part["side"], part["pitch"]
        area = side * pitch

        def group(t, carry, part=part, side=side, pitch=pitch, area=area):
            start = part["packed_row"] + t * area

            def column(c, inner):
                first = pl.multiple_of(start + c * SUB, SUB)
                rows = [pl.ds(pl.multiple_of(first + k * pitch, SUB), SUB) for k in range(side)]
                held = [pg[row, :] for row in rows]
                for k in range(side):
                    total = jnp.zeros((SUB, LANES), F32)
                    for i in range(k, side):
                        total = total + height_wide[pl.ds((part["tap"] + i - k) * SUB, SUB), :] * held[i]
                    pd[rows[k], :] = total
                return inner

            lax.fori_loop(0, pitch // SUB, column, 0)
            return carry

        lax.fori_loop(0, part["groups"], group, 0)
    arriving[0].wait()
    for part in plan.sections:
        side, pitch = part["side"], part["pitch"]
        area = side * pitch

        def group(t, carry, part=part, side=side, pitch=pitch, area=area):
            start = part["packed_row"] + t * area

            def column(c, inner):
                first = pl.multiple_of(start + c * SUB, SUB)
                rows = [pl.ds(pl.multiple_of(first + k * pitch, SUB), SUB) for k in range(side)]
                held = [pg[row, :] for row in rows]
                ways = [across[row, :] for row in rows]
                for tap in range(side):
                    total = held[tap] * ways[0]
                    for k in range(1, side - tap):
                        total = total + held[k + tap] * ways[k]
                    height_sums[pl.ds((part["tap"] + tap) * SUB, SUB), :] += total
                return inner

            lax.fori_loop(0, pitch // SUB, column, 0)
            return carry

        lax.fori_loop(0, part["groups"], group, 0)
    arriving[1].wait()
    for part in plan.sections:
        side, pitch = part["side"], part["pitch"]
        area = side * pitch

        def group(t, carry, part=part, side=side, pitch=pitch, area=area):
            start = part["packed_row"] + t * area

            def line(i, sums):
                sums = list(sums)
                base = start + i * pitch
                aligned = pl.multiple_of(base, SUB)
                for j in range(0, pitch, SUB):
                    here = pl.ds(pl.multiple_of(aligned + j, SUB), SUB)
                    mine, grad = packed[here, :], pg[here, :]
                    total = skips * grad
                    sums[side] = sums[side] + mine * grad
                    for tap in range(min(side, side - j)):
                        moved = pd[pl.ds(base + j + tap, SUB), :]
                        if j + SUB - 1 + tap >= pitch:
                            moved = jnp.where(place + (j + tap) < side, moved, 0.0)
                        total = total + width_wide[pl.ds((part["tap"] + tap) * SUB, SUB), :] * moved
                        sums[tap] = sums[tap] + mine * moved
                    out[here, :] = total
                return tuple(sums)

            return lax.fori_loop(0, side, line, carry)

        zero = jnp.zeros((SUB, LANES), F32)
        sums = lax.fori_loop(0, part["groups"], group, (zero,) * (side + 1))
        for tap in range(side):
            width_sums[pl.ds((part["tap"] + tap) * SUB, SUB), :] = sums[tap]
        skip_sums[...] += sums[side]


def whole(memory):
    return pl.BlockSpec(memory_space=memory)


def lanes_of(rows):
    return jax.ShapeDtypeStruct((rows, LANES), F32)


def row_buffers(plan):
    return [pltpu.VMEM((plan.row_pad, LANES), F32)] * 2 + [pltpu.VMEM((plan.image_rows, LANES), F32)]


def near(values):
    return pltpu.with_memory_space_constraint(values, pltpu.VMEM)


def distant(values):
    return pltpu.with_memory_space_constraint(values, pltpu.HBM)


def kernel_call(kernel, name, micros, memories, out_shape, scratch, args, after=(), stays=(), held=(), left=()):
    single = not isinstance(out_shape, tuple)
    shapes = (out_shape,) if single else out_shape
    shapes = tuple((pltpu.VMEM if i in stays else pltpu.HBM)(o.shape, o.dtype) for i, o in enumerate(shapes))
    outs = tuple(whole(pltpu.VMEM) for _ in shapes)
    place = lambda i, value: near(value) if i in held else value if memories[i] is pltpu.SMEM or i in left else distant(value)
    out = pl.pallas_call(
        kernel,
        out_shape=shapes,
        in_specs=[whole(m) for m in memories] + [whole(pltpu.HBM)] * len(after),
        out_specs=outs,
        scratch_shapes=scratch,
        compiler_params=pltpu.CompilerParams(vmem_limit_bytes=LESS if stays or held else VMEM),
        cost_estimate=pl.CostEstimate(flops=1_000_000, bytes_accessed=int(3_690_000 * micros), transcendentals=0),
        name=name,
    )(*[place(i, value) for i, value in enumerate(args)], *map(distant, after))
    return out[0] if single else out


def mixer_forward(plan, where, block, height, width, skip):
    rows = plan.packed_rows
    ins = [(where, FAR), (block, NEAR), (height, FAR), (width, FAR), (skip, FAR)]
    outs = [(block.shape, BF16, FAR), ((rows, LANES), F32, FAR), ((rows, LANES), F32, FAR)]
    room = row_buffers(plan) + [
        pltpu.SMEM(where.shape, jnp.int32),
        pltpu.VMEM((rows + MARGIN, LANES), F32),
        pltpu.VMEM((rows + MARGIN, LANES), F32),
        pltpu.VMEM((TAPS * SUB, LANES), F32),
        pltpu.VMEM((plan.mask_rows, LANES), F32),
        pltpu.SemaphoreType.DMA((6,)),
        *[pltpu.VMEM(value.shape, F32) for value in (height, width, skip)],
        pltpu.VMEM(block.shape, BF16),
        pltpu.SemaphoreType.DMA((plan.devices,)),
    ]
    return run(functools.partial(forward_kernel, plan), "mixer_forward", ins, outs, room, micros=30, limit=LESS)


def mixer_arrive(plan, where, block, act, weight_out, given, tokens, out_grad, sums, pre_sum, after):
    ins = [(value, FAR) for value in (where, block, act, weight_out, given, tokens, out_grad, sums, pre_sum)]
    width = tokens.shape[1]
    outs = [((plan.packed_rows, LANES), F32, NEAR), (tokens.shape, BF16, AUTO), ((width, LANES), F32, AUTO), ((SUB, LANES), F32, AUTO)]
    room = [pltpu.SMEM(where.shape, jnp.int32), pltpu.VMEM(block.shape, BF16)] + row_buffers(plan) + [pltpu.VMEM(value.shape, value.dtype) for value in (act, weight_out, given, tokens, out_grad, sums, pre_sum)]
    room += [pltpu.VMEM(tokens.shape, F32), pltpu.VMEM((LANES, width), F32), pltpu.SemaphoreType.DMA((4,)), pltpu.SemaphoreType.DMA((5,))]
    return run(functools.partial(arrive_kernel, plan), "mixer_arrive", ins, outs, room, after, limit=LESS)


def mixer_backward(plan, grads, height, width, skip, packed, across, after):
    rows = plan.packed_rows
    ins = [(grads, NEAR), (height, AUTO), (width, AUTO), (skip, AUTO), (packed, FAR), (across, FAR)]
    outs = [((rows, LANES), F32, NEAR)] + [((size, LANES), F32, AUTO) for size in (TAPS * SUB, TAPS * SUB, SUB, SUB)]
    room = [pltpu.VMEM((size, LANES), F32) for size in (rows + MARGIN, TAPS * SUB, TAPS * SUB, rows, rows)]
    room += [pltpu.SemaphoreType.DMA((2,))]
    return run(functools.partial(backward_kernel, plan), "mixer_backward", ins, outs, room, after, limit=LESS)


def mixer_leave(plan, where, grads, extra, after):
    ins = [(where, FAR), (grads, NEAR), (extra, AUTO)]
    outs = [((plan.devices, plan.channels, plan.row_pad), BF16, AUTO), ((SUB, LANES), F32, AUTO)]
    room = row_buffers(plan) + [pltpu.VMEM(extra.shape, F32), pltpu.SMEM(where.shape, jnp.int32), pltpu.SemaphoreType.DMA]
    return run(functools.partial(leave_kernel, plan), "mixer_leave", ins, outs, room, after, limit=LESS)


def taps_kernel(plan, coef_height, rate_height, coef_width, rate_width, spread, height_sums, width_sums, skip_sums, *rest):
    outs = rest[-5:]
    reach, scale = tap_places()
    fold = lambda sums: lax.dot_general(spread[...], sums, (((1,), (1,)), ((), ())), precision=lax.Precision.HIGHEST, preferred_element_type=F32)
    for coef, log_rate, sums, coef_out, rate_out in (
        (coef_height, rate_height, height_sums, outs[0], outs[1]),
        (coef_width, rate_width, width_sums, outs[2], outs[3]),
    ):
        grads = fold(sums[...].reshape(TAPS, SUB, LANES).sum(axis=1))
        rate = jnp.exp(log_rate[...])
        plain, moved = jnp.zeros_like(rate), jnp.zeros_like(rate)
        for tap in range(TAPS):
            weighted = (grads[:, tap : tap + 1] * float(scale[tap])) * jnp.exp(rate * float(-reach[tap]))
            plain = plain + weighted
            moved = moved + weighted * float(reach[tap])
        coef_out[...] = plain
        rate_out[...] = -coef[...] * rate * moved
    total = jnp.sum(skip_sums[...], axis=0, keepdims=True)
    outs[4][...] = lax.dot_general(total, spread[...], (((1,), (1,)), ((), ())), precision=lax.Precision.HIGHEST, preferred_element_type=F32)


def tap_grads(plan, coefs, spread, sums, after):
    shape = jax.ShapeDtypeStruct(coefs[0].shape, F32)
    outs = (shape,) * 4 + (jax.ShapeDtypeStruct((1, plan.channels), F32),)
    *grads, skips = kernel_call(functools.partial(taps_kernel, plan), "tap_grads", 0.01, [pltpu.VMEM] * 8, outs, [], (*coefs, spread, *sums), after)
    return *grads, skips[0]


def tokens_kernel(plan, blocks, out_grad, out, *rest):
    smalls, flipped = rest[:-1], rest[-1]
    total = jnp.zeros((plan.channels, LANES), F32)
    for s in range(plan.devices):
        block = blocks[s].astype(F32)
        flipped[pl.ds(s * plan.channels, plan.channels), :] = block[:, : plan.rows]
        total = total + block[:, plan.row_pad - LANES :]
    first = plan.extra_lane
    rows = total.T
    rows = rows[first : first + SUB] + rows[first + SUB : first + 2 * SUB]
    kind = 0
    for small in smalls:
        for i in range(small.shape[1] // plan.channels):
            small[:, pl.ds(i * plan.channels, plan.channels)] = rows[kind : kind + 1]
            kind += 1
    out[...] = out_grad[...].astype(F32) + flipped[...].T


def token_grads(plan, blocks, out_grad, kinds):
    outs = [(out_grad.shape, F32, AUTO)] + [((1, count * plan.channels), F32, AUTO) for count in (1, 1, kinds, 1, 1)]
    room = [pltpu.VMEM(out_grad.shape[::-1], F32)]
    return run(functools.partial(tokens_kernel, plan), "token_grads", [(blocks, NEAR), (out_grad, AUTO)], outs, room)


def started(pairs, sems):
    copies = [pltpu.make_async_copy(source, target, sems.at[i]) for i, (source, target) in enumerate(pairs)]
    for copy in copies:
        copy.start()
    return copies


NEAR, FAR, AUTO, OPEN, SCALAR = "near", "far", "auto", "open", "scalar"


def run(kernel, name, ins, outs, scratch, after=(), micros=0.01, limit=VMEM):
    same = lambda value: value
    memory = {NEAR: pltpu.VMEM, FAR: pltpu.HBM, AUTO: pltpu.VMEM, OPEN: pltpu.VMEM, SCALAR: pltpu.SMEM}
    hold = {NEAR: near, FAR: distant, AUTO: distant, OPEN: same, SCALAR: same}
    make = {NEAR: pltpu.VMEM, FAR: pltpu.HBM, AUTO: pltpu.HBM, OPEN: jax.ShapeDtypeStruct}
    return pl.pallas_call(
        kernel,
        out_shape=tuple(make[place](shape, dtype) for shape, dtype, place in outs),
        in_specs=[whole(memory[place]) for _, place in ins] + [whole(pltpu.HBM)] * len(after),
        out_specs=tuple(whole(memory[place]) for _, _, place in outs),
        scratch_shapes=scratch,
        compiler_params=pltpu.CompilerParams(vmem_limit_bytes=limit),
        cost_estimate=pl.CostEstimate(flops=1000, bytes_accessed=int(3_690_000 * micros), transcendentals=0),
        name=name,
    )(*[hold[place](value) for value, place in ins], *map(distant, after))


def feed_kernel(plan, blocks, gain_far, bias_far, weight_far, bias_in_far, grad_act_far, grads_far, act_far, sums_far, pre_sum_far, keep_far, *rest):
    sent, scratch = rest[:-18], rest[-18:]
    normed, flipped, unit, total, weight_in, grad_act, act, grad_pre, keep, other, came, left = scratch[:12]
    gain, bias, bias_in, grads, sums, pre_sum = scratch[12:]
    channels, count = plan.channels, plan.devices
    width, hidden = weight_in.shape
    chunks, chips, _, _ = keep.shape
    tile, each = hidden // chunks, len(sent) // chunks
    core = own_bit(0)
    parts = [pl.ds(i * tile, tile) for i in range(chunks)]
    small = started([(gain_far, gain), (bias_far, bias), (bias_in_far, bias_in)], came.at[pl.ds(2 * chunks, 3)])
    arriving = []
    for i, at in enumerate(parts):
        there = [(weight_far.at[:, at], weight_in.at[:, at]), (grad_act_far.at[:, at], grad_act.at[:, at])]
        arriving.append(started(there, came.at[pl.ds(2 * i, 2)]))
    for s in range(count):
        unit[pl.ds(s * channels, channels), :] = blocks[s].astype(F32)
    mean = jnp.sum(unit[...], axis=0, keepdims=True) * (1.0 / width)
    centred = unit[...] - mean
    inverse = lax.rsqrt(jnp.sum(centred * centred, axis=0, keepdims=True) * (1.0 / width) + EPSILON)
    unit[...] = centred * inverse
    for copy in small:
        copy.wait()
    scaled = unit[...] * gain[...] + bias[...]
    flipped[...] = scaled.astype(BF16)
    normed[...] = scaled.T.astype(BF16)
    leaving = []

    def activate(i):
        at = parts[i]
        for copy in (arriving[0] if i == 0 else arriving[1] + arriving[2] if i == 1 else []):
            copy.wait()
        pre = jnp.dot(normed[...], weight_in[:, at], preferred_element_type=F32) + bias_in[:, at]
        cdf = 0.5 * (1.0 + lax.erf(pre * math.sqrt(0.5)))
        act[:, at] = (pre * cdf).astype(BF16)
        slope = cdf + pre * jnp.exp(-0.5 * pre * pre) * (1.0 / math.sqrt(2.0 * math.pi))
        grad = grad_act[:, at] * slope
        pre_sum[:, at] = jnp.sum(grad, axis=0, keepdims=True)
        grad_pre[:, at] = grad.astype(BF16)

    def leave(there):
        leaving.extend(started(there, left.at[pl.ds(len(leaving), len(there))]))

    activate(0)
    for i, at in enumerate(parts):
        if i + 1 < chunks:
            activate(i + 1)
        leave([(act.at[:, at], act_far.at[:, at])])
        part = jnp.dot(flipped[...], grad_pre[:, at], preferred_element_type=F32)
        for c in range(chips):
            first = part[2 * c * channels : (2 * c + 1) * channels]
            second = part[(2 * c + 1) * channels : (2 * c + 2) * channels]
            keep[i, c] = retiled(jnp.where(core == 0, first, second), width).astype(BF16)
            other[i, c] = retiled(jnp.where(core == 0, second, first), width).astype(BF16)
        there = [(other.at[i, :, :, lanes], sent[i * each + p]) for p, lanes in enumerate(lane_parts(width, each))]
        leave(there + [(keep.at[i], keep_far.at[i])])
        back = lax.dot_general(grad_pre[:, at], weight_in[:, at], (((1,), (1,)), ((), ())), preferred_element_type=F32)
        total[...] = back if i == 0 else total[...] + back
    turned = total[...].T
    grad = turned * gain[...]
    level = jnp.sum(grad, axis=0, keepdims=True) * (1.0 / width)
    tilt = jnp.sum(grad * unit[...], axis=0, keepdims=True) * (1.0 / width)
    total_low = (inverse * (grad - level - unit[...] * tilt)).astype(BF16)
    for s in range(count):
        grads[s] = total_low[s * channels : (s + 1) * channels]
    leave([(grads, grads_far)])
    lane = lax.broadcasted_iota(jnp.int32, sums.shape, 1)
    sums[...] = jnp.where(
        plan.kind(lane, 0),
        jnp.sum(turned * unit[...], axis=1, keepdims=True),
        jnp.where(plan.kind(lane, 1), jnp.sum(turned, axis=1, keepdims=True), 0.0),
    )
    leave([(sums, sums_far), (pre_sum, pre_sum_far)])
    for copy in leaving:
        copy.wait()


def feed(plan, blocks, gain, bias, weight_in, bias_in, grad_act):
    rows, width, hidden, chips = plan.rows, plan.devices * plan.channels, weight_in.shape[1], plan.devices // 2
    high, each = plan.channels * hidden // CHUNKS // width, 2
    ins = [(blocks, NEAR)] + [(value, FAR) for value in (gain[:, None], bias[:, None], weight_in, bias_in[None], grad_act)]
    outs = [
        (blocks.shape, BF16, FAR),
        ((rows, hidden), BF16, FAR),
        ((width, LANES), F32, FAR),
        ((1, hidden), F32, FAR),
        ((CHUNKS, chips, high, width), BF16, FAR),
    ] + [((chips, high, width // each), BF16, FAR)] * (CHUNKS * each)
    room = [
        pltpu.VMEM((rows, width), BF16),
        pltpu.VMEM((width, rows), BF16),
        pltpu.VMEM((width, rows), F32),
        pltpu.VMEM((rows, width), F32),
        pltpu.VMEM((width, hidden), BF16),
        pltpu.VMEM((rows, hidden), F32),
        pltpu.VMEM((rows, hidden), BF16),
        pltpu.VMEM((rows, hidden), BF16),
        pltpu.VMEM((CHUNKS, chips, high, width), BF16),
        pltpu.VMEM((CHUNKS, chips, high, width), BF16),
        pltpu.SemaphoreType.DMA((2 * CHUNKS + 3,)),
        pltpu.SemaphoreType.DMA((CHUNKS * (each + 2) + 3,)),
        pltpu.VMEM((width, 1), F32),
        pltpu.VMEM((width, 1), F32),
        pltpu.VMEM((1, hidden), F32),
        pltpu.VMEM(blocks.shape, BF16),
        pltpu.VMEM((width, LANES), F32),
        pltpu.VMEM((1, hidden), F32),
    ]
    grads, act, sums, pre_sum, keep, *sent = run(functools.partial(feed_kernel, plan), "feed_forward", ins, outs, room, micros=10, limit=LESS)
    return grads, act, sums, pre_sum, keep, sent


def out_grad_kernel(act_far, scaled_far, keep_far, *rest):
    sent, (act, scaled, keep, other, came, left) = rest[:-6], rest[-6:]
    core = own_bit(0)
    chunks, chips, high, width = keep.shape
    height, steps = chunks * high, came.shape[0] - 1
    tile, each, part = act.shape[1] // steps, chips // steps, chips // len(sent)
    parts = [pl.ds(i * tile, tile) for i in range(steps)]
    arriving, leaving = started([(scaled_far, scaled)] + [(act_far.at[:, at], act.at[:, at]) for at in parts], came), []
    arriving[0].wait()
    for i, at in enumerate(parts):
        arriving[1 + i].wait()
        low = lax.dot_general(act[:, at], scaled[...], (((0,), (0,)), ((), ())), preferred_element_type=F32).astype(BF16)
        for c in range(each):
            first = low[2 * c * height : (2 * c + 1) * height]
            second = low[(2 * c + 1) * height : (2 * c + 2) * height]
            mine, yours = jnp.where(core == 0, first, second), jnp.where(core == 0, second, first)
            for chunk in range(chunks):
                keep[chunk, i * each + c] = mine[chunk * high : (chunk + 1) * high]
                other[chunk, i * each + c] = yours[chunk * high : (chunk + 1) * high]
        some = pl.ds(i * each, each)
        there = [(other.at[:, pl.ds(p * part, part)], sent[p]) for p in range(i * each // part, (i + 1) * each // part)]
        there += [(keep.at[:, some], keep_far.at[:, some])]
        leaving += started(there, left.at[pl.ds(len(leaving), len(there))])
    for copy in leaving:
        copy.wait()


def out_grad_halves(plan, act, scaled):
    hidden, width, chips = act.shape[1], scaled.shape[1], plan.devices // 2
    high, steps, pieces = hidden // plan.devices // CHUNKS, hidden // 768, 4
    ins = [(act, FAR), (scaled, FAR)]
    outs = [((CHUNKS, chips, high, width), BF16, FAR)] + [((CHUNKS, chips // pieces, high, width), BF16, FAR)] * pieces
    room = [pltpu.VMEM(value.shape, BF16) for value in (act, scaled)] + [pltpu.VMEM(outs[0][0], BF16)] * 2
    room += [pltpu.SemaphoreType.DMA((1 + steps,)), pltpu.SemaphoreType.DMA((pieces + steps,))]
    keep, *sent = run(out_grad_kernel, "out_grad_halves", ins, outs, room)
    return keep, sent


def own_bit(bit):
    return lax.axis_index("chan") >> bit & 1


def lane_parts(width, count):
    return [pl.ds(p * (width // count), width // count) for p in range(count)]


def retiled(values, width):
    tiles = [values[r : r + SUB, c : c + LANES] for r in range(0, values.shape[0], SUB) for c in range(0, values.shape[1], LANES)]
    each = width // LANES
    return jnp.concatenate([jnp.concatenate(tiles[i : i + each], axis=1) for i in range(0, len(tiles), each)], axis=0)


def small_shares(plan, sums, pre_sum, bias_row, scale_row, rows):
    channels, count = plan.channels, plan.devices
    width = channels * count
    kinds = pre_sum.shape[1] // width
    lane = lax.broadcasted_iota(jnp.int32, sums.shape, 1)
    rows[...] = jnp.zeros_like(rows)
    for kind, row in ((2 + kinds, bias_row), (3 + kinds, scale_row)):
        for again in (0, SUB):
            rows[pl.ds(plan.extra_lane + kind + again, 1), :] = row
    total = sums + rows[...].T
    columns = jnp.broadcast_to(pre_sum, (SUB, pre_sum.shape[1])).T.reshape(count, kinds, channels, SUB)
    for kind in range(kinds):
        column = columns[:, kind].reshape(width, SUB)[:, :1]
        total = total + jnp.where(plan.kind(lane, 2 + kind), column, 0.0)
    return total


def held_back(arrays, after):
    kept = len(arrays)
    return pl.pallas_call(
        lambda *refs: None,
        out_shape=tuple(pltpu.HBM(a.shape, a.dtype) for a in arrays),
        in_specs=[whole(pltpu.HBM)] * kept + [whole(pl.ANY)] * len(after),
        out_specs=(whole(pltpu.HBM),) * kept,
        input_output_aliases={i: i for i in range(kept)},
        cost_estimate=pl.CostEstimate(flops=0, bytes_accessed=0, transcendentals=0),
        name="held_back",
    )(*map(distant, arrays), *after)


def act_grads_kernel(scaled, weight_out, *rest):
    out = rest[-1]
    tile = 768
    for c in range(0, out.shape[1], tile):
        part = lax.dot_general(scaled[...], weight_out[pl.ds(c, tile), :], (((1,), (1,)), ((), ())), preferred_element_type=F32)
        out[:, pl.ds(c, tile)] = part


def act_grads(scaled, weight_out, after):
    outs = [((scaled.shape[0], weight_out.shape[0]), F32, AUTO)]
    return run(act_grads_kernel, "act_grads", [(scaled, AUTO), (weight_out, AUTO)], outs, [], after, micros=6)[0]


def merge_entries(at, bit, keep, got, mine, other):
    low = (1 << at) - 1
    for e in range(mine.shape[0]):
        first = (e >> at << at + 1) + (e & low)
        here, there = first + bit * (low + 1), first + (1 - bit) * (low + 1)
        other[e] = keep(there) + got(there, first)
        mine[e] = keep(here) + got(here, first)


def first_merge_kernel(cuts, counts, *refs):
    outs, mark, scratch = refs[-12:-6], refs[-6], refs[-5:]
    mark[...] = jnp.zeros_like(mark)
    sems, groups, used, at, places = scratch[-1], [], 0, 0, []
    for which, count in enumerate(counts):
        keep, came, got = scratch[2 * which], scratch[2 * which + 1], refs[at + 1 : at + 1 + count]
        places.append(got)
        chunks, chips, high, width = keep.shape
        for i in range(chunks):
            there = [(refs[at].at[i], keep.at[i])]
            if len(got[0].shape) == 4:
                part = chips // count
                if i == chunks - 1:
                    there += [(piece.at[i], came.at[i, pl.ds(p * part, part)]) for p, piece in enumerate(got)]
            else:
                each = count // chunks
                there += [(got[i * each + p], came.at[i, :, :, lanes]) for p, lanes in enumerate(lane_parts(width, each))]
            groups.append(started(there, sems.at[pl.ds(used, len(there))]))
            used += len(there)
        at += 1 + count
    for which in range(2):
        keep, came = scratch[2 * which], scratch[2 * which + 1]
        chunks, _, high, _ = keep.shape
        for i in range(chunks):
            for copy in groups[which * chunks + i]:
                copy.wait()
            pair, row = (which, i * high) if i < chunks - 1 else (2, which * high)
            cut, bit = cuts[pair]
            mine, other = (out.at[:, pl.ds(row, high)] for out in outs[2 * pair : 2 * pair + 2])
            new = lambda e, first: came[i, e]
            if len(places[which][0].shape) == 4 and i < chunks - 1:
                part = places[which][0].shape[1]
                new = lambda e, first: places[which][first // part][i, e - first // part * part]
            merge_entries(cut, own_bit(bit), lambda e: keep[i, e], new, mine, other)


def first_merge(parts, cuts, after):
    chunks, chips, high, width = parts[0][0].shape
    ins = [(value, place) for (keep, got), near_by in zip(parts, (FAR, NEAR)) for value, place in ((keep, FAR), *((piece, near_by) for piece in got))]
    outs = [((chips // 2, rows, width), BF16, NEAR) for rows in ((chunks - 1) * high, (chunks - 1) * high, 2 * high) for _ in range(2)]
    room = [pltpu.VMEM(keep.shape, BF16) for keep, _ in parts for _ in range(2)] + [pltpu.SemaphoreType.DMA((64,))]
    kernel = functools.partial(first_merge_kernel, cuts, [len(got) for _, got in parts])
    *halves, mark = run(kernel, "first_merge", ins, outs + [((SUB, LANES), F32, AUTO)], room, after, limit=LESS)
    return halves[0::2], halves[1::2], mark


def merge_kernel(jobs, *refs):
    count, pairs = sum(len(job) for job in jobs), 2 * len(jobs)
    outs, mark = refs[-1 - pairs : -1], refs[-1]
    mark[...] = jnp.zeros_like(mark)
    i = 0
    for j, job in enumerate(jobs):
        row = 0
        for at, bit in job:
            keep, got = refs[i], refs[count + i]
            rows = pl.ds(row, keep.shape[1])
            merge_entries(at, own_bit(bit), lambda e: keep[e], lambda e, first: got[e], outs[2 * j].at[:, rows], outs[2 * j + 1].at[:, rows])
            row += keep.shape[1]
            i += 1


def merge(keeps, gots, jobs, after=()):
    ins = [(value, NEAR) for value in keeps] + [(value, OPEN) for value in gots]
    outs, i = [], 0
    for job in jobs:
        parts = keeps[i : i + len(job)]
        i += len(job)
        outs += [((parts[0].shape[0] // 2, sum(part.shape[1] for part in parts), parts[0].shape[2]), BF16, NEAR)] * 2
    *halves, mark = run(functools.partial(merge_kernel, jobs), "merge_halves", ins, outs + [((SUB, LANES), F32, AUTO)], [], after, limit=LESS)
    return halves[0::2], halves[1::2], mark


def last_kernel(keep, got, less_keep, less_got, in_sum, out_sum):
    total = keep[0].astype(F32) + got[0].astype(F32)
    less = less_keep[0].astype(F32) + less_got[0].astype(F32)
    high = less.shape[0] // 2
    tile = in_sum.shape[1] // CHUNKS
    for i, part in enumerate((total[:high], total[high : 2 * high], less[:high])):
        in_sum[:, pl.ds(i * tile, tile)] = retiled(part, tile)
    out_sum[pl.ds(0, 2 * high), :] = total[2 * high :]
    out_sum[pl.ds(2 * high, high), :] = less[high:]


def last_sums(parts, channels, hidden, after):
    ins = [(parts[0], NEAR), (parts[1], OPEN), (parts[2], NEAR), (parts[3], OPEN)]
    high, width = parts[2].shape[1] // 2, parts[2].shape[2]
    outs = [((channels, hidden), F32, AUTO), ((CHUNKS * high, width), F32, AUTO)]

    def kernel(*refs):
        last_kernel(*refs[:4], *refs[-2:])

    return run(kernel, "last_sums", ins, outs, [], after)


def tap_places():
    reach = np.concatenate([np.arange(s) / s for s in SIDES]).astype(np.float32)
    scale = np.concatenate([np.full(s, 1.0 / math.sqrt(s)) for s in SIDES]).astype(np.float32)
    return reach, scale


def profiles(coefficient, log_rate):
    reach, scale = tap_places()
    decayed = jnp.exp(-jnp.exp(log_rate)[None] * reach[:, None, None])
    return jnp.sum(coefficient[None] * decayed, axis=2) * scale[:, None]


def profile_grads(coefficient, log_rate, grads):
    reach, scale = tap_places()
    rate = jnp.exp(log_rate)
    decayed = jnp.exp(-rate[None] * reach[:, None, None])
    weighted = (grads * scale[:, None])[:, :, None] * decayed
    return jnp.sum(weighted, axis=0), -coefficient * rate * jnp.sum(weighted * reach[:, None, None], axis=0)


def kernel_matrix(profile, part):
    side = part["side"]
    offsets = np.arange(side)[:, None] - np.arange(side)[None, :]
    picked = profile[part["tap"] + np.maximum(offsets, 0)]
    return jnp.where((offsets >= 0)[:, :, None], picked, 0.0)


def mix_plain(plan, row_pixel, channel_rows, height, width, skip):
    def one_channel(given):
        values, high, wide, weight = given
        image_order = jnp.zeros_like(values).at[row_pixel].set(values)
        pieces = []
        for part in plan.sections:
            side, count = part["side"], part["images"] * part["side"] ** 2
            block = image_order[part["pixel"] : part["pixel"] + count].reshape(-1, side, side)
            left = kernel_matrix(high[:, None], part)[:, :, 0]
            right = kernel_matrix(wide[:, None], part)[:, :, 0]
            mixed = jnp.einsum("ik,nkl,jl->nij", left, block, right, precision=lax.Precision.HIGHEST)
            pieces.append(mixed.reshape(-1))
        joined = jnp.concatenate(pieces) + weight * image_order
        return joined[row_pixel]

    return lax.map(jax.checkpoint(one_channel), (channel_rows, height.T, width.T, skip))


def exchange(blocks):
    return lax.all_to_all(blocks, "chan", 0, 0, tiled=True)


def to_blocks(rows, devices):
    return rows.T.reshape(devices, rows.shape[1] // devices, rows.shape[0])


def to_rows(blocks):
    return blocks.reshape(-1, blocks.shape[2]).T


def halve(blocks, bits):
    myself = lax.axis_index("chan")
    size = lax.axis_size("chan")
    pairs = lambda bit: [(i, i ^ 1 << bit) for i in range(size)]
    left = list(range(size.bit_length() - 1))
    for bit in bits:
        at = left.index(bit)
        viewed = blocks.reshape((-1, 2, 1 << at) + blocks.shape[1:])
        own = myself >> bit & 1
        keep = lax.dynamic_index_in_dim(viewed, own, 1, keepdims=False)
        send = lax.dynamic_index_in_dim(viewed, 1 - own, 1, keepdims=False)
        got = lax.ppermute(send, "chan", pairs(bit))
        total = keep.astype(F32) + got.astype(F32)
        left.remove(bit)
        blocks = (total if not left else total.astype(BF16)).reshape((-1,) + blocks.shape[1:])
    return blocks[0]


def swapped(x, bit):
    return lax.ppermute(x, "chan", [(i, i ^ 1 << bit) for i in range(lax.axis_size("chan"))])


def body_fast(
    tokens,
    row_pixel,
    coef_height,
    rate_height,
    coef_width,
    rate_width,
    skip_weight,
    norm_gain,
    norm_bias,
    weight_in,
    bias_in,
    weight_out,
    bias_out,
    layer_scale,
    out_grad,
):
    devices = lax.axis_size("chan")
    rows, width_all = tokens.shape
    plan = Plan(devices, rows, width_all // devices)
    token_blocks = exchange(to_blocks(tokens, devices))
    where = plan.address(row_pixel)
    spread = plan.spread()
    taps = (plan.tile_taps(profiles(coef_height, rate_height)), plan.tile_taps(profiles(coef_width, rate_width)), plan.tile_taps(skip_weight[None]))
    mixed_blocks, packed, across = mixer_forward(plan, where, token_blocks, *taps)

    scaled = out_grad.astype(F32) * layer_scale
    scaled_low = scaled.astype(BF16)
    rows_given = jnp.stack([layer_scale, bias_out, jnp.sum(scaled, axis=0)])
    grad_act = act_grads(scaled_low, weight_out, (rows_given,))
    grad_normin, act, sums, pre_sum, in_keep, in_sent = feed(plan, exchange(mixed_blocks), norm_gain, norm_bias, weight_in, bias_in, grad_act)
    grad_blocks = exchange(grad_normin)
    out_keep, out_sent = out_grad_halves(plan, act, scaled_low)
    out_got = [swapped(piece, 0) for piece in out_sent]
    in_got = [swapped(piece, 0) for piece in in_sent]

    x, y, near_z, far_z = range(1, 5)
    swap = lambda parts, bits: [swapped(part, bit) for part, bit in zip(parts, bits)]
    keeps, sends, mark = first_merge(((in_keep, in_got), (out_keep, out_got)), ((0, x), (1, y), (2, near_z)), (grad_blocks,))
    gots = swap(sends, (x, y, near_z))
    grads, block_out, shares, mark = mixer_arrive(plan, where, grad_blocks, act, weight_out, rows_given, tokens, out_grad, sums, pre_sum, (mark,))
    keeps, sends, mark = merge(keeps, gots, (((0, y),), ((0, x),), ((2, far_z),)), (mark,))
    gots = swap(sends, (y, x, far_z))
    grads, *tap_sums, mark = mixer_backward(plan, grads, *taps, packed, across, (mark,))
    both_keeps, both_sends, mark = merge(keeps[:2], gots[:2], (((0, near_z), (0, near_z)),), (mark,))
    both_gots = swap(both_sends, (near_z,))
    leaving, left = mixer_leave(plan, where, grads, shares, (mark,))
    keeps, sends, mark = merge((both_keeps[0], keeps[2]), (both_gots[0], gots[2]), (((0, far_z),), ((0, x),)), (left,))
    (moved,) = held_back((leaving,), (mark,))
    grad_tokens, *smalls = token_grads(plan, exchange(moved), out_grad, pre_sum.shape[1] // width_all)
    both_got, less_got = swap(sends, (far_z, x))
    less_keeps, less_sends, mark = merge(keeps[1:], (less_got,), (((0, y),),))
    (less_got,) = swap(less_sends, (y,))
    coef_grads = tap_grads(plan, (coef_height, rate_height, coef_width, rate_width), spread.astype(F32), tap_sums, (mark,))
    in_sum, out_sum = last_sums(
        (keeps[0], both_got, less_keeps[0], less_got), plan.channels, weight_in.shape[1], (grad_tokens, *coef_grads)
    )
    gain_grad, norm_bias_grad, bias_in_grad, bias_out_grad, scale_grad = (small[0] for small in smalls)
    return (block_out, grad_tokens, *coef_grads, gain_grad, norm_bias_grad, in_sum, bias_in_grad, out_sum, bias_out_grad, scale_grad)


def body_plain(
    tokens,
    row_pixel,
    coef_height,
    rate_height,
    coef_width,
    rate_width,
    skip_weight,
    norm_gain,
    norm_bias,
    weight_in,
    bias_in,
    weight_out,
    bias_out,
    layer_scale,
    out_grad,
):
    devices = lax.axis_size("chan")
    rows, width_all = tokens.shape
    plan = Plan(devices, rows, width_all // devices)
    token_blocks = exchange(to_blocks(tokens, devices))

    height = profiles(coef_height, rate_height)
    width = profiles(coef_width, rate_width)
    lines = lambda blocks: blocks.transpose(1, 0, 2).reshape(blocks.shape[1], -1)
    blocks_of = lambda values: values.astype(BF16).reshape(-1, devices, rows).transpose(1, 0, 2)
    mixed, mixer_back = jax.vjp(
        functools.partial(mix_plain, plan, row_pixel), lines(token_blocks).astype(F32), height, width, skip_weight
    )
    mixed_blocks = blocks_of(mixed)
    normin = to_rows(exchange(mixed_blocks)).astype(F32)

    upstream = out_grad.astype(F32)
    scaled = upstream * layer_scale
    scaled_low = scaled.astype(BF16)
    grad_act = lax.dot_general(scaled_low, weight_out, (((1,), (1,)), ((), ())), preferred_element_type=F32)

    row_mean = jnp.mean(normin, axis=1, keepdims=True)
    centred = normin - row_mean
    inv_std = lax.rsqrt(jnp.mean(centred * centred, axis=1, keepdims=True) + EPSILON)
    unit_rows = centred * inv_std
    normed = (unit_rows * norm_gain + norm_bias).astype(BF16)
    hidden_pre = jnp.dot(normed, weight_in, preferred_element_type=F32) + bias_in
    cdf = 0.5 * (1.0 + lax.erf(hidden_pre * math.sqrt(0.5)))
    act_low = (hidden_pre * cdf).astype(BF16)
    slope = cdf + hidden_pre * jnp.exp(-0.5 * hidden_pre * hidden_pre) * (1.0 / math.sqrt(2.0 * math.pi))
    grad_pre = grad_act * slope
    grad_pre_low = grad_pre.astype(BF16)
    grad_normed = lax.dot_general(grad_pre_low, weight_in, (((1,), (1,)), ((), ())), preferred_element_type=F32)
    grad_unit = grad_normed * norm_gain
    grad_normin = inv_std * (
        grad_unit
        - jnp.mean(grad_unit, axis=1, keepdims=True)
        - unit_rows * jnp.mean(grad_unit * unit_rows, axis=1, keepdims=True)
    )
    grad_blocks = exchange(to_blocks(grad_normin.astype(BF16), devices))

    branch = jnp.dot(act_low, weight_out, preferred_element_type=F32) + bias_out
    block_out = (tokens.astype(F32) + layer_scale * branch).astype(BF16)
    small = (
        jnp.sum(grad_normed * unit_rows, axis=0),
        jnp.sum(grad_normed, axis=0),
        jnp.sum(grad_pre, axis=0),
        jnp.sum(scaled, axis=0),
        jnp.sum(upstream * branch, axis=0),
    )
    weight_in_part = lax.dot_general(normed, grad_pre_low, (((0,), (0,)), ((), ())), preferred_element_type=F32)
    weight_out_part = lax.dot_general(act_low, scaled_low, (((0,), (0,)), ((), ())), preferred_element_type=F32)

    grad_mixed, grad_height, grad_width, grad_skip = mixer_back(lines(grad_blocks).astype(F32))
    grad_rows = blocks_of(grad_mixed)
    coef_height_grad, rate_height_grad = profile_grads(coef_height, rate_height, grad_height)
    coef_width_grad, rate_width_grad = profile_grads(coef_width, rate_width, grad_width)
    grad_tokens = upstream + to_rows(exchange(grad_rows)).astype(F32)

    levels = list(range(devices.bit_length() - 1))
    other = levels[:1] + levels[1:3][::-1] + levels[3:]
    in_sum = halve(weight_in_part.astype(BF16).reshape(devices, -1, weight_in.shape[1]), levels)
    out_sum = halve(weight_out_part.astype(BF16).reshape(devices, -1, weight_out.shape[1]), other)
    shares = jnp.concatenate([s.reshape(devices, -1) for s in small], axis=1)
    shares = exchange(shares).sum(axis=0)
    cuts = np.cumsum([s.shape[0] // devices for s in small])[:-1]
    gain_grad, norm_bias_grad, bias_in_grad, bias_out_grad, scale_grad = jnp.split(shares, cuts)
    return (
        block_out,
        grad_tokens,
        coef_height_grad,
        rate_height_grad,
        coef_width_grad,
        rate_width_grad,
        grad_skip,
        gain_grad,
        norm_bias_grad,
        in_sum,
        bias_in_grad,
        out_sum,
        bias_out_grad,
        scale_grad,
    )


def solution(mesh):
    split, copied = P("chan"), P()

    def body(tokens, *rest):
        devices = lax.axis_size("chan")
        fast = Plan(devices, tokens.shape[0], tokens.shape[1] // devices).fits() and devices == 32
        return (body_fast if fast else body_plain)(tokens, *rest)

    in_specs = (split, copied) + (split,) * 5 + (copied,) * 7 + (split,)
    return jax.shard_map(body, mesh=mesh, in_specs=in_specs, out_specs=(split,) * 14, check_vma=False)
```

```python
import functools
import math

import jax
import jax.numpy as jnp
import numpy as np
from jax import lax
from jax.experimental import pallas as pl
from jax.experimental.pallas import tpu as pltpu
from jax.sharding import PartitionSpec as P

SIDES = (10, 14, 18)
SHARES = (1, 1, 2)
UNIT = sum(m * s * s for s, m in zip(SIDES, SHARES))
TAPS = sum(SIDES)
EPSILON = 1e-06
LANES = 128
SUB = 8
MARGIN = 32
VMEM = 63 * 2**20
LESS = 36 * 2**20
SMALL = 20 * 2**20
CHUNKS = 3
F32 = jnp.float32
BF16 = jnp.bfloat16


class Plan:
    def __init__(self, devices, rows, channels):
        self.devices, self.rows, self.channels = devices, rows, channels
        self.pixels = devices * rows
        self.units = self.pixels // UNIT
        self.slots = LANES // channels
        self.row_pad = -(-rows // LANES) * LANES
        self.extra_row = -(-rows // SUB) * SUB
        self.sections = []
        image_row, packed_row, tap, mask_row, pixel = 0, 0, 0, 0, 0
        for side, share in zip(SIDES, SHARES):
            images = share * self.units
            pitch = -(-side // SUB) * SUB
            groups = -(-images // self.slots)
            self.sections.append(
                dict(side=side, images=images, pitch=pitch, groups=groups, image_row=image_row, packed_row=packed_row, tap=tap, mask_row=mask_row, pixel=pixel)
            )
            image_row += groups * self.slots * side * pitch
            packed_row += groups * side * pitch
            tap += side
            mask_row += side * pitch
            pixel += images * side * side
        self.image_rows = image_row
        self.packed_rows = packed_row
        self.mask_rows = mask_row

    @property
    def extra_lane(self):
        return self.extra_row - (self.row_pad - LANES)

    def kind(self, lane, which):
        return (lane == self.extra_lane + which) | (lane == self.extra_lane + SUB + which)

    def fits(self):
        room = self.row_pad - self.extra_row >= 2 * SUB
        return room and self.channels % SUB == 0 and 4 * LANES * (self.image_rows + 2 * self.row_pad + 5 * self.packed_rows) < 40 * 2**20

    def address(self, row_pixel):
        where = jnp.zeros_like(row_pixel)
        for part in self.sections:
            local = row_pixel - part["pixel"]
            line = local // part["side"]
            spot = part["image_row"] + line * part["pitch"] + local - line * part["side"]
            where = jnp.where(local >= 0, spot, where)
        return where

    def spread(self):
        lane = np.arange(LANES)
        held = (lane[None, :] % self.channels == np.arange(self.channels)[:, None]) & (lane[None, :] < self.slots * self.channels)
        return jnp.asarray(held.astype(np.float32), BF16)

    def tile_taps(self, taps):
        tiled = jnp.tile(taps, (1, self.slots))
        return jnp.pad(tiled, ((0, 0), (0, LANES - tiled.shape[1])))


def slot_masks(plan):
    lane = lax.broadcasted_iota(jnp.int32, (SUB, LANES), 1)
    return [(lane >= q * plan.channels) & (lane < (q + 1) * plan.channels) for q in range(plan.slots)]


def in_turn(plan, first, second, beside=None, steps=0, ready=None):
    first(0, 0)

    def pair(k):
        first(2 * k + 1, 1)
        second(2 * k, 0)
        first(2 * k + 2, 0)
        second(2 * k + 1, 1)

    def plain(k, carry):
        pair(k)
        return carry

    def more(k, carry):
        beside(k - begin)
        pair(k)
        return carry

    pairs = plan.devices // 2 - 1
    begin = pairs - steps
    lax.fori_loop(0, begin, plain, 0)
    if steps:
        ready()
        lax.fori_loop(begin, pairs, more, 0)
    first(plan.devices - 1, 1)
    second(plan.devices - 2, 0)
    second(plan.devices - 1, 1)


def scatter_rows(plan, where, block, buffers, image, beside=None, steps=0, ready=None):
    def turn(s, held):
        rows = block[s].astype(F32)
        full = [rows] * plan.slots
        if LANES > plan.slots * plan.channels:
            full.append(rows[: LANES - plan.slots * plan.channels])
        buffers[held][pl.ds(0, plan.rows), :] = jnp.concatenate(full, axis=0).T

    def place(s, held):
        base = s * plan.rows
        for u in range(plan.rows):
            image[pl.ds(where[base + u], 1), :] = buffers[held][pl.ds(u, 1), :]

    in_turn(plan, turn, place, beside, steps, ready)


def gather_rows(plan, where, buffers, image, out, extra=None, leave=None):
    def fetch(s, held):
        base = s * plan.rows
        for u in range(plan.rows):
            buffers[held][pl.ds(u, 1), :] = image[pl.ds(where[base + u], 1), :]

    def fold(s, held):
        turned = buffers[held][...].T
        folded = turned[: plan.channels]
        for q in range(1, plan.slots):
            folded = folded + turned[q * plan.channels : (q + 1) * plan.channels]
        if extra is None:
            out[s] = folded[:, : plan.rows].astype(BF16)
            leave(s)
            return
        last = plan.row_pad - LANES
        sums = extra[pl.ds(pl.multiple_of(s * plan.channels, SUB), plan.channels), :]
        lane = lax.broadcasted_iota(jnp.int32, sums.shape, 1) + last
        out[s, :, pl.ds(0, last)] = folded[:, :last].astype(BF16)
        out[s, :, pl.ds(last, LANES)] = jnp.where(lane < plan.extra_row, folded[:, last:], sums).astype(BF16)

    in_turn(plan, fetch, fold)


def pack_images(plan, masks, image, packed, margin):
    place = lax.broadcasted_iota(jnp.int32, (SUB, LANES), 0)
    for part in plan.sections:
        side, pitch = part["side"], part["pitch"]
        area = side * pitch
        ragged = part["images"] < part["groups"] * plan.slots

        def group(t, carry, part=part, side=side, pitch=pitch, area=area, ragged=ragged):
            start = part["image_row"] + t * (plan.slots * area)
            target = margin + part["packed_row"] + t * area
            used = masks
            if ragged:
                used = [mask & (t * plan.slots + q < part["images"]) for q, mask in enumerate(masks)]
            ends = [mask & (place < side % SUB) for mask in used]
            for i in range(side):
                for j in range(0, pitch, SUB):
                    value = jnp.zeros((SUB, LANES), F32)
                    for q in range(plan.slots):
                        row = pl.multiple_of(start + (q * area + i * pitch + j), SUB)
                        value = jnp.where((ends if j + SUB > side else used)[q], image[pl.ds(row, SUB), :], value)
                    packed[pl.ds(pl.multiple_of(target + (i * pitch + j), SUB), SUB), :] = value
            return carry

        lax.fori_loop(0, part["groups"], group, 0)


def unpack_line(plan, masks, part, t, offset, value, image):
    area = part["side"] * part["pitch"]
    for q in range(plan.slots):
        row = pl.multiple_of(part["image_row"] + (t * plan.slots + q) * area + offset, SUB)
        image[pl.ds(row, SUB), :] = jnp.where(masks[q], value, 0.0)


def wide_taps(plan, taps, table):
    for tap in range(TAPS):
        table[pl.ds(tap * SUB, SUB), :] = jnp.broadcast_to(taps[pl.ds(tap, 1), :], (SUB, LANES))


def masked_taps(plan, taps, table):
    for part in plan.sections:
        side, pitch = part["side"], part["pitch"]
        place = lax.broadcasted_iota(jnp.int32, (pitch, LANES), 0)
        for tap in range(side):
            row = taps[pl.ds(part["tap"] + tap, 1), :]
            table[pl.ds(part["mask_row"] + tap * pitch, pitch), :] = jnp.where(place >= tap, row, 0.0)


def forward_kernel(plan, where_far, block, height_far, width_far, skip_far, out_far, packed, across, first, second, image, where, px, pu, height_wide, width_masked, sems, *rest):
    height, width, skip, out, left = rest
    small = started([(height_far, height), (width_far, width), (skip_far, skip)], sems.at[pl.ds(3, 3)])
    masks = slot_masks(plan)
    indices = pltpu.make_async_copy(where_far, where, sems.at[0])
    indices.start()
    px[pl.ds(0, MARGIN), :] = jnp.zeros((MARGIN, LANES), F32)
    for copy in small:
        copy.wait()
    wide_taps(plan, height, height_wide)
    masked_taps(plan, width, width_masked)
    indices.wait()
    scatter_rows(plan, where, block, (first, second), image)
    pack_images(plan, masks, image, px, MARGIN)
    skips = jnp.broadcast_to(skip[...], (SUB, LANES))
    for part in plan.sections:
        side, pitch = part["side"], part["pitch"]
        area = side * pitch

        def group(t, carry, part=part, side=side, pitch=pitch, area=area):
            start = MARGIN + part["packed_row"] + t * area

            for j in range(0, pitch, SUB):
                reach = range(min(side, j + SUB))
                weights = [width_masked[pl.ds(part["mask_row"] + tap * pitch + j, SUB), :] for tap in reach]

                def line(i, inner, j=j, weights=weights):
                    base = start + i * pitch + j
                    total = weights[0] * px[pl.ds(pl.multiple_of(base, SUB), SUB), :]
                    for tap in range(1, len(weights)):
                        total = total + weights[tap] * px[pl.ds(base - tap, SUB), :]
                    pu[pl.ds(pl.multiple_of(base, SUB), SUB), :] = total
                    return inner

                lax.fori_loop(0, side, line, 0, unroll=2)

            def column(c, inner):
                first = pl.multiple_of(start + c * SUB, SUB)
                held = [pu[pl.ds(pl.multiple_of(first + k * pitch, SUB), SUB), :] for k in range(side)]
                for i in range(side):
                    total = skips * px[pl.ds(pl.multiple_of(first + i * pitch, SUB), SUB), :]
                    for k in range(i + 1):
                        total = total + height_wide[pl.ds((part["tap"] + i - k) * SUB, SUB), :] * held[k]
                    unpack_line(plan, masks, part, t, i * pitch + c * SUB, total, image)
                return inner

            lax.fori_loop(0, pitch // SUB, column, 0)
            return carry

        lax.fori_loop(0, part["groups"], group, 0)
    kept = [(px.at[pl.ds(MARGIN, plan.packed_rows)], packed), (pu.at[pl.ds(MARGIN, plan.packed_rows)], across)]
    kept = started(kept, sems.at[pl.ds(1, 2)])
    leaving = lambda s: pltpu.make_async_copy(out.at[s], out_far.at[s], left.at[s])
    gather_rows(plan, where, (first, second), image, out, leave=lambda s: leaving(s).start())
    for copy in kept:
        copy.wait()

    def gone(s, carry):
        leaving(s).wait()
        return carry

    lax.fori_loop(0, plan.devices, gone, 0)


def arrive_kernel(plan, where_far, block_far, act_far, weight_far, given_far, tokens_far, out_grad_far, sums_far, pre_sum_far, *rest):
    grads, block_out, shares, mark, *rest = rest[-20:]
    where, block, first, second, image, act, weight_out, given, tokens, out_grad, sums, pre_sum, branch, rows, came, sems = rest
    mark[...] = jnp.zeros_like(mark)
    soon = started([(block_far, block), (where_far, where)], came.at[pl.ds(2, 2)])
    arriving = started([(act_far, act), (weight_far, weight_out)], came.at[pl.ds(0, 2)])
    there = [(given_far, given), (tokens_far, tokens), (out_grad_far, out_grad), (sums_far, sums), (pre_sum_far, pre_sum)]
    later = started(there, sems)

    def ready():
        for copy in arriving:
            copy.wait()

    def product(k):
        lanes = pl.ds(pl.multiple_of(k * LANES, LANES), LANES)
        branch[:, lanes] = jnp.dot(act[...], weight_out[:, lanes], preferred_element_type=F32)

    for copy in soon:
        copy.wait()
    scatter_rows(plan, where, block, (first, second), image, product, tokens.shape[1] // LANES, ready)
    for copy in later:
        copy.wait()
    scale, bias_out, bias_row = (given[pl.ds(i, 1), :] for i in range(3))
    total = branch[...] + bias_out
    block_out[...] = (tokens[...].astype(F32) + scale * total).astype(BF16)
    scale_row = jnp.sum(out_grad[...].astype(F32) * total, axis=0, keepdims=True)
    shares[...] = small_shares(plan, sums[...], pre_sum[...], bias_row, scale_row, rows)
    pack_images(plan, slot_masks(plan), image, grads, 0)


def leave_kernel(plan, where_far, grads, extra, *rest):
    out, mark, near, far, image, halves, where, sem = rest[-8:]
    indices = pltpu.make_async_copy(where_far, where, sem)
    indices.start()
    mark[...] = jnp.zeros_like(mark)
    masks = slot_masks(plan)
    for part in plan.sections:
        area = part["side"] * part["pitch"]

        def group(t, carry, part=part, area=area):
            for offset in range(0, area, SUB):
                row = pl.multiple_of(part["packed_row"] + t * area + offset, SUB)
                unpack_line(plan, masks, part, t, offset, grads[pl.ds(row, SUB), :], image)
            return carry

        lax.fori_loop(0, part["groups"], group, 0)
    indices.wait()
    exact = extra[...]
    high = exact.astype(BF16).astype(F32)
    lane = lax.broadcasted_iota(jnp.int32, exact.shape, 1)
    halves[...] = jnp.where(lane < plan.extra_lane + SUB, high, exact - high)
    gather_rows(plan, where, (near, far), image, out, halves)


def backward_kernel(plan, pg, height_far, width_far, skip_far, packed_far, across_far, *rest):
    out, height_sums, width_sums, skip_sums, mark, pd, height_wide, width_wide, packed, across, sems, height, width, skip = rest[-14:]
    small = started([(height_far, height), (width_far, width), (skip_far, skip)], sems.at[pl.ds(2, 3)])
    mark[...] = jnp.zeros_like(mark)
    arriving = started([(across_far, across), (packed_far, packed)], sems.at[pl.ds(0, 2)])
    place = lax.broadcasted_iota(jnp.int32, (SUB, LANES), 0)
    pd[pl.ds(plan.packed_rows, MARGIN), :] = jnp.zeros((MARGIN, LANES), F32)
    for copy in small:
        copy.wait()
    wide_taps(plan, height, height_wide)
    wide_taps(plan, width, width_wide)
    skips = jnp.broadcast_to(skip[...], (SUB, LANES))
    skip_sums[...] = jnp.zeros((SUB, LANES), F32)
    height_sums[...] = jnp.zeros((TAPS * SUB, LANES), F32)
    for part in plan.sections:
        side, pitch = part["side"], part["pitch"]
        area = side * pitch

        def group(t, carry, part=part, side=side, pitch=pitch, area=area):
            start = part["packed_row"] + t * area

            def column(c, inner):
                first = pl.multiple_of(start + c * SUB, SUB)
                rows = [pl.ds(pl.multiple_of(first + k * pitch, SUB), SUB) for k in range(side)]
                held = [pg[row, :] for row in rows]
                for k in range(side):
                    total = jnp.zeros((SUB, LANES), F32)
                    for i in range(k, side):
                        total = total + height_wide[pl.ds((part["tap"] + i - k) * SUB, SUB), :] * held[i]
                    pd[rows[k], :] = total
                return inner

            lax.fori_loop(0, pitch // SUB, column, 0)
            return carry

        lax.fori_loop(0, part["groups"], group, 0)
    arriving[0].wait()
    for part in plan.sections:
        side, pitch = part["side"], part["pitch"]
        area = side * pitch

        def group(t, carry, part=part, side=side, pitch=pitch, area=area):
            start = part["packed_row"] + t * area

            def column(c, inner):
                first = pl.multiple_of(start + c * SUB, SUB)
                rows = [pl.ds(pl.multiple_of(first + k * pitch, SUB), SUB) for k in range(side)]
                held = [pg[row, :] for row in rows]
                ways = [across[row, :] for row in rows]
                for tap in range(side):
                    total = held[tap] * ways[0]
                    for k in range(1, side - tap):
                        total = total + held[k + tap] * ways[k]
                    height_sums[pl.ds((part["tap"] + tap) * SUB, SUB), :] += total
                return inner

            lax.fori_loop(0, pitch // SUB, column, 0)
            return carry

        lax.fori_loop(0, part["groups"], group, 0)
    arriving[1].wait()
    for part in plan.sections:
        side, pitch = part["side"], part["pitch"]
        area = side * pitch

        def group(t, carry, part=part, side=side, pitch=pitch, area=area):
            start = part["packed_row"] + t * area

            def line(i, sums):
                sums = list(sums)
                base = start + i * pitch
                aligned = pl.multiple_of(base, SUB)
                for j in range(0, pitch, SUB):
                    here = pl.ds(pl.multiple_of(aligned + j, SUB), SUB)
                    mine, grad = packed[here, :], pg[here, :]
                    total = skips * grad
                    sums[side] = sums[side] + mine * grad
                    for tap in range(min(side, side - j)):
                        moved = pd[pl.ds(base + j + tap, SUB), :]
                        if j + SUB - 1 + tap >= pitch:
                            moved = jnp.where(place + (j + tap) < side, moved, 0.0)
                        total = total + width_wide[pl.ds((part["tap"] + tap) * SUB, SUB), :] * moved
                        sums[tap] = sums[tap] + mine * moved
                    out[here, :] = total
                return tuple(sums)

            return lax.fori_loop(0, side, line, carry)

        zero = jnp.zeros((SUB, LANES), F32)
        sums = lax.fori_loop(0, part["groups"], group, (zero,) * (side + 1))
        for tap in range(side):
            width_sums[pl.ds((part["tap"] + tap) * SUB, SUB), :] = sums[tap]
        skip_sums[...] += sums[side]


def whole(memory):
    return pl.BlockSpec(memory_space=memory)


def lanes_of(rows):
    return jax.ShapeDtypeStruct((rows, LANES), F32)


def row_buffers(plan):
    return [pltpu.VMEM((plan.row_pad, LANES), F32)] * 2 + [pltpu.VMEM((plan.image_rows, LANES), F32)]


def near(values):
    return pltpu.with_memory_space_constraint(values, pltpu.VMEM)


def distant(values):
    return pltpu.with_memory_space_constraint(values, pltpu.HBM)


def kernel_call(kernel, name, micros, memories, out_shape, scratch, args, after=(), stays=(), held=(), left=()):
    single = not isinstance(out_shape, tuple)
    shapes = (out_shape,) if single else out_shape
    shapes = tuple((pltpu.VMEM if i in stays else pltpu.HBM)(o.shape, o.dtype) for i, o in enumerate(shapes))
    outs = tuple(whole(pltpu.VMEM) for _ in shapes)
    place = lambda i, value: near(value) if i in held else value if memories[i] is pltpu.SMEM or i in left else distant(value)
    out = pl.pallas_call(
        kernel,
        out_shape=shapes,
        in_specs=[whole(m) for m in memories] + [whole(pltpu.HBM)] * len(after),
        out_specs=outs,
        scratch_shapes=scratch,
        compiler_params=pltpu.CompilerParams(vmem_limit_bytes=LESS if stays or held else VMEM),
        cost_estimate=pl.CostEstimate(flops=1_000_000, bytes_accessed=int(3_690_000 * micros), transcendentals=0),
        name=name,
    )(*[place(i, value) for i, value in enumerate(args)], *map(distant, after))
    return out[0] if single else out


def mixer_forward(plan, where, block, height, width, skip):
    rows = plan.packed_rows
    ins = [(where, FAR), (block, NEAR), (height, FAR), (width, FAR), (skip, FAR)]
    outs = [(block.shape, BF16, FAR), ((rows, LANES), F32, FAR), ((rows, LANES), F32, FAR)]
    room = row_buffers(plan) + [
        pltpu.SMEM(where.shape, jnp.int32),
        pltpu.VMEM((rows + MARGIN, LANES), F32),
        pltpu.VMEM((rows + MARGIN, LANES), F32),
        pltpu.VMEM((TAPS * SUB, LANES), F32),
        pltpu.VMEM((plan.mask_rows, LANES), F32),
        pltpu.SemaphoreType.DMA((6,)),
        *[pltpu.VMEM(value.shape, F32) for value in (height, width, skip)],
        pltpu.VMEM(block.shape, BF16),
        pltpu.SemaphoreType.DMA((plan.devices,)),
    ]
    return run(functools.partial(forward_kernel, plan), "mixer_forward", ins, outs, room, micros=30, limit=LESS)


def mixer_arrive(plan, where, block, act, weight_out, given, tokens, out_grad, sums, pre_sum, after):
    ins = [(value, FAR) for value in (where, block, act, weight_out, given, tokens, out_grad, sums, pre_sum)]
    width = tokens.shape[1]
    outs = [((plan.packed_rows, LANES), F32, NEAR), (tokens.shape, BF16, AUTO), ((width, LANES), F32, AUTO), ((SUB, LANES), F32, AUTO)]
    room = [pltpu.SMEM(where.shape, jnp.int32), pltpu.VMEM(block.shape, BF16)] + row_buffers(plan) + [pltpu.VMEM(value.shape, value.dtype) for value in (act, weight_out, given, tokens, out_grad, sums, pre_sum)]
    room += [pltpu.VMEM(tokens.shape, F32), pltpu.VMEM((LANES, width), F32), pltpu.SemaphoreType.DMA((4,)), pltpu.SemaphoreType.DMA((5,))]
    return run(functools.partial(arrive_kernel, plan), "mixer_arrive", ins, outs, room, after, limit=LESS)


def mixer_backward(plan, grads, height, width, skip, packed, across, after):
    rows = plan.packed_rows
    ins = [(grads, NEAR)] + [(value, FAR) for value in (height, width, skip, packed, across)]
    outs = [((rows, LANES), F32, NEAR)] + [((size, LANES), F32, AUTO) for size in (TAPS * SUB, TAPS * SUB, SUB, SUB)]
    room = [pltpu.VMEM((size, LANES), F32) for size in (rows + MARGIN, TAPS * SUB, TAPS * SUB, rows, rows)]
    room += [pltpu.SemaphoreType.DMA((5,))] + [pltpu.VMEM(value.shape, F32) for value in (height, width, skip)]
    return run(functools.partial(backward_kernel, plan), "mixer_backward", ins, outs, room, after, limit=LESS)


def mixer_leave(plan, where, grads, extra, after):
    ins = [(where, FAR), (grads, NEAR), (extra, AUTO)]
    outs = [((plan.devices, plan.channels, plan.row_pad), BF16, AUTO), ((SUB, LANES), F32, AUTO)]
    room = row_buffers(plan) + [pltpu.VMEM(extra.shape, F32), pltpu.SMEM(where.shape, jnp.int32), pltpu.SemaphoreType.DMA]
    return run(functools.partial(leave_kernel, plan), "mixer_leave", ins, outs, room, after, limit=LESS)


def taps_kernel(plan, coef_height, rate_height, coef_width, rate_width, spread, height_sums, width_sums, skip_sums, *rest):
    outs = rest[-5:]
    reach, scale = tap_places()
    fold = lambda sums: lax.dot_general(spread[...], sums, (((1,), (1,)), ((), ())), precision=lax.Precision.HIGHEST, preferred_element_type=F32)
    for coef, log_rate, sums, coef_out, rate_out in (
        (coef_height, rate_height, height_sums, outs[0], outs[1]),
        (coef_width, rate_width, width_sums, outs[2], outs[3]),
    ):
        grads = fold(sums[...].reshape(TAPS, SUB, LANES).sum(axis=1))
        rate = jnp.exp(log_rate[...])
        plain, moved = jnp.zeros_like(rate), jnp.zeros_like(rate)
        for tap in range(TAPS):
            weighted = (grads[:, tap : tap + 1] * float(scale[tap])) * jnp.exp(rate * float(-reach[tap]))
            plain = plain + weighted
            moved = moved + weighted * float(reach[tap])
        coef_out[...] = plain
        rate_out[...] = -coef[...] * rate * moved
    total = jnp.sum(skip_sums[...], axis=0, keepdims=True)
    outs[4][...] = lax.dot_general(total, spread[...], (((1,), (1,)), ((), ())), precision=lax.Precision.HIGHEST, preferred_element_type=F32)


def tap_grads(plan, coefs, spread, sums, after):
    shape = jax.ShapeDtypeStruct(coefs[0].shape, F32)
    outs = (shape,) * 4 + (jax.ShapeDtypeStruct((1, plan.channels), F32),)
    *grads, skips = kernel_call(functools.partial(taps_kernel, plan), "tap_grads", 0.01, [pltpu.VMEM] * 8, outs, [], (*coefs, spread, *sums), after)
    return *grads, skips[0]


def tokens_kernel(plan, blocks, out_grad, out, *rest):
    smalls, flipped = rest[:-1], rest[-1]
    total = jnp.zeros((plan.channels, LANES), F32)
    for s in range(plan.devices):
        block = blocks[s].astype(F32)
        flipped[pl.ds(s * plan.channels, plan.channels), :] = block[:, : plan.rows]
        total = total + block[:, plan.row_pad - LANES :]
    first = plan.extra_lane
    rows = total.T
    rows = rows[first : first + SUB] + rows[first + SUB : first + 2 * SUB]
    kind = 0
    for small in smalls:
        for i in range(small.shape[1] // plan.channels):
            small[:, pl.ds(i * plan.channels, plan.channels)] = rows[kind : kind + 1]
            kind += 1
    out[...] = out_grad[...].astype(F32) + flipped[...].T


def token_grads(plan, blocks, out_grad, kinds):
    outs = [(out_grad.shape, F32, AUTO)] + [((1, count * plan.channels), F32, AUTO) for count in (1, 1, kinds, 1, 1)]
    room = [pltpu.VMEM(out_grad.shape[::-1], F32)]
    return run(functools.partial(tokens_kernel, plan), "token_grads", [(blocks, NEAR), (out_grad, AUTO)], outs, room)


def started(pairs, sems):
    copies = [pltpu.make_async_copy(source, target, sems.at[i]) for i, (source, target) in enumerate(pairs)]
    for copy in copies:
        copy.start()
    return copies


NEAR, FAR, AUTO, OPEN, SCALAR = "near", "far", "auto", "open", "scalar"


def run(kernel, name, ins, outs, scratch, after=(), micros=0.01, limit=VMEM):
    same = lambda value: value
    memory = {NEAR: pltpu.VMEM, FAR: pltpu.HBM, AUTO: pltpu.VMEM, OPEN: pltpu.VMEM, SCALAR: pltpu.SMEM}
    hold = {NEAR: near, FAR: distant, AUTO: distant, OPEN: same, SCALAR: same}
    make = {NEAR: pltpu.VMEM, FAR: pltpu.HBM, AUTO: pltpu.HBM, OPEN: jax.ShapeDtypeStruct}
    return pl.pallas_call(
        kernel,
        out_shape=tuple(make[place](shape, dtype) for shape, dtype, place in outs),
        in_specs=[whole(memory[place]) for _, place in ins] + [whole(pltpu.HBM)] * len(after),
        out_specs=tuple(whole(memory[place]) for _, _, place in outs),
        scratch_shapes=scratch,
        compiler_params=pltpu.CompilerParams(vmem_limit_bytes=limit),
        cost_estimate=pl.CostEstimate(flops=1000, bytes_accessed=int(3_690_000 * micros), transcendentals=0),
        name=name,
    )(*[hold[place](value) for value, place in ins], *map(distant, after))


def feed_kernel(plan, blocks, gain_far, bias_far, weight_far, bias_in_far, grad_act_far, grads_far, act_far, sums_far, pre_sum_far, keep_far, *rest):
    sent, scratch = rest[:-18], rest[-18:]
    normed, flipped, unit, total, weight_in, grad_act, act, grad_pre, keep, other, came, left = scratch[:12]
    gain, bias, bias_in, grads, sums, pre_sum = scratch[12:]
    channels, count = plan.channels, plan.devices
    width, hidden = weight_in.shape
    chunks, chips, _, _ = keep.shape
    tile, each = hidden // chunks, len(sent) // chunks
    core = own_bit(0)
    parts = [pl.ds(i * tile, tile) for i in range(chunks)]
    small = started([(gain_far, gain), (bias_far, bias), (bias_in_far, bias_in)], came.at[pl.ds(2 * chunks, 3)])
    arriving = []
    for i, at in enumerate(parts):
        there = [(weight_far.at[:, at], weight_in.at[:, at]), (grad_act_far.at[:, at], grad_act.at[:, at])]
        arriving.append(started(there, came.at[pl.ds(2 * i, 2)]))
    for s in range(count):
        unit[pl.ds(s * channels, channels), :] = blocks[s].astype(F32)
    mean = jnp.sum(unit[...], axis=0, keepdims=True) * (1.0 / width)
    centred = unit[...] - mean
    inverse = lax.rsqrt(jnp.sum(centred * centred, axis=0, keepdims=True) * (1.0 / width) + EPSILON)
    unit[...] = centred * inverse
    for copy in small:
        copy.wait()
    scaled = unit[...] * gain[...] + bias[...]
    flipped[...] = scaled.astype(BF16)
    normed[...] = scaled.T.astype(BF16)
    leaving = []

    def activate(i):
        at = parts[i]
        for copy in (arriving[0] if i == 0 else arriving[1] + arriving[2] if i == 1 else []):
            copy.wait()
        pre = jnp.dot(normed[...], weight_in[:, at], preferred_element_type=F32) + bias_in[:, at]
        cdf = 0.5 * (1.0 + lax.erf(pre * math.sqrt(0.5)))
        act[:, at] = (pre * cdf).astype(BF16)
        slope = cdf + pre * jnp.exp(-0.5 * pre * pre) * (1.0 / math.sqrt(2.0 * math.pi))
        grad = grad_act[:, at] * slope
        pre_sum[:, at] = jnp.sum(grad, axis=0, keepdims=True)
        grad_pre[:, at] = grad.astype(BF16)

    def leave(there):
        leaving.extend(started(there, left.at[pl.ds(len(leaving), len(there))]))

    activate(0)
    for i, at in enumerate(parts):
        if i + 1 < chunks:
            activate(i + 1)
        leave([(act.at[:, at], act_far.at[:, at])])
        part = jnp.dot(flipped[...], grad_pre[:, at], preferred_element_type=F32)
        for c in range(chips):
            first = part[2 * c * channels : (2 * c + 1) * channels]
            second = part[(2 * c + 1) * channels : (2 * c + 2) * channels]
            keep[i, c] = retiled(jnp.where(core == 0, first, second), width).astype(BF16)
            other[i, c] = retiled(jnp.where(core == 0, second, first), width).astype(BF16)
        there = [(other.at[i, :, :, lanes], sent[i * each + p]) for p, lanes in enumerate(lane_parts(width, each))]
        leave(there + [(keep.at[i], keep_far.at[i])])
        back = lax.dot_general(grad_pre[:, at], weight_in[:, at], (((1,), (1,)), ((), ())), preferred_element_type=F32)
        total[...] = back if i == 0 else total[...] + back
    turned = total[...].T
    grad = turned * gain[...]
    level = jnp.sum(grad, axis=0, keepdims=True) * (1.0 / width)
    tilt = jnp.sum(grad * unit[...], axis=0, keepdims=True) * (1.0 / width)
    total_low = (inverse * (grad - level - unit[...] * tilt)).astype(BF16)
    for s in range(count):
        grads[s] = total_low[s * channels : (s + 1) * channels]
    leave([(grads, grads_far)])
    lane = lax.broadcasted_iota(jnp.int32, sums.shape, 1)
    sums[...] = jnp.where(
        plan.kind(lane, 0),
        jnp.sum(turned * unit[...], axis=1, keepdims=True),
        jnp.where(plan.kind(lane, 1), jnp.sum(turned, axis=1, keepdims=True), 0.0),
    )
    leave([(sums, sums_far), (pre_sum, pre_sum_far)])
    for copy in leaving:
        copy.wait()


def feed(plan, blocks, gain, bias, weight_in, bias_in, grad_act):
    rows, width, hidden, chips = plan.rows, plan.devices * plan.channels, weight_in.shape[1], plan.devices // 2
    high, each = plan.channels * hidden // CHUNKS // width, 2
    ins = [(blocks, NEAR)] + [(value, FAR) for value in (gain[:, None], bias[:, None], weight_in, bias_in[None], grad_act)]
    outs = [
        (blocks.shape, BF16, FAR),
        ((rows, hidden), BF16, FAR),
        ((width, LANES), F32, FAR),
        ((1, hidden), F32, FAR),
        ((CHUNKS, chips, high, width), BF16, FAR),
    ] + [((chips, high, width // each), BF16, FAR)] * (CHUNKS * each)
    room = [
        pltpu.VMEM((rows, width), BF16),
        pltpu.VMEM((width, rows), BF16),
        pltpu.VMEM((width, rows), F32),
        pltpu.VMEM((rows, width), F32),
        pltpu.VMEM((width, hidden), BF16),
        pltpu.VMEM((rows, hidden), F32),
        pltpu.VMEM((rows, hidden), BF16),
        pltpu.VMEM((rows, hidden), BF16),
        pltpu.VMEM((CHUNKS, chips, high, width), BF16),
        pltpu.VMEM((CHUNKS, chips, high, width), BF16),
        pltpu.SemaphoreType.DMA((2 * CHUNKS + 3,)),
        pltpu.SemaphoreType.DMA((CHUNKS * (each + 2) + 3,)),
        pltpu.VMEM((width, 1), F32),
        pltpu.VMEM((width, 1), F32),
        pltpu.VMEM((1, hidden), F32),
        pltpu.VMEM(blocks.shape, BF16),
        pltpu.VMEM((width, LANES), F32),
        pltpu.VMEM((1, hidden), F32),
    ]
    grads, act, sums, pre_sum, keep, *sent = run(functools.partial(feed_kernel, plan), "feed_forward", ins, outs, room, micros=10, limit=LESS)
    return grads, act, sums, pre_sum, keep, sent


def out_grad_kernel(act_far, scaled_far, keep_far, *rest):
    sent, (act, scaled, keep, other, came, left) = rest[:-6], rest[-6:]
    core = own_bit(0)
    chunks, chips, high, width = keep.shape
    height, steps = chunks * high, came.shape[0] - 1
    tile, each, part = act.shape[1] // steps, chips // steps, chips // len(sent)
    parts = [pl.ds(i * tile, tile) for i in range(steps)]
    arriving, leaving = started([(scaled_far, scaled)] + [(act_far.at[:, at], act.at[:, at]) for at in parts], came), []
    arriving[0].wait()
    for i, at in enumerate(parts):
        arriving[1 + i].wait()
        low = lax.dot_general(act[:, at], scaled[...], (((0,), (0,)), ((), ())), preferred_element_type=F32).astype(BF16)
        for c in range(each):
            first = low[2 * c * height : (2 * c + 1) * height]
            second = low[(2 * c + 1) * height : (2 * c + 2) * height]
            mine, yours = jnp.where(core == 0, first, second), jnp.where(core == 0, second, first)
            for chunk in range(chunks):
                keep[chunk, i * each + c] = mine[chunk * high : (chunk + 1) * high]
                other[chunk, i * each + c] = yours[chunk * high : (chunk + 1) * high]
        some = pl.ds(i * each, each)
        there = [(other.at[:, pl.ds(p * part, part)], sent[p]) for p in range(i * each // part, (i + 1) * each // part)]
        there += [(keep.at[:, some], keep_far.at[:, some])]
        leaving += started(there, left.at[pl.ds(len(leaving), len(there))])
    for copy in leaving:
        copy.wait()


def out_grad_halves(plan, act, scaled):
    hidden, width, chips = act.shape[1], scaled.shape[1], plan.devices // 2
    high, steps, pieces = hidden // plan.devices // CHUNKS, hidden // 768, 4
    ins = [(act, FAR), (scaled, FAR)]
    outs = [((CHUNKS, chips, high, width), BF16, FAR)] + [((CHUNKS, chips // pieces, high, width), BF16, FAR)] * pieces
    room = [pltpu.VMEM(value.shape, BF16) for value in (act, scaled)] + [pltpu.VMEM(outs[0][0], BF16)] * 2
    room += [pltpu.SemaphoreType.DMA((1 + steps,)), pltpu.SemaphoreType.DMA((pieces + steps,))]
    keep, *sent = run(out_grad_kernel, "out_grad_halves", ins, outs, room)
    return keep, sent


def own_bit(bit):
    return lax.axis_index("chan") >> bit & 1


def lane_parts(width, count):
    return [pl.ds(p * (width // count), width // count) for p in range(count)]


def retiled(values, width):
    tiles = [values[r : r + SUB, c : c + LANES] for r in range(0, values.shape[0], SUB) for c in range(0, values.shape[1], LANES)]
    each = width // LANES
    return jnp.concatenate([jnp.concatenate(tiles[i : i + each], axis=1) for i in range(0, len(tiles), each)], axis=0)


def small_shares(plan, sums, pre_sum, bias_row, scale_row, rows):
    channels, count = plan.channels, plan.devices
    width = channels * count
    kinds = pre_sum.shape[1] // width
    lane = lax.broadcasted_iota(jnp.int32, sums.shape, 1)
    rows[...] = jnp.zeros_like(rows)
    for kind, row in ((2 + kinds, bias_row), (3 + kinds, scale_row)):
        for again in (0, SUB):
            rows[pl.ds(plan.extra_lane + kind + again, 1), :] = row
    total = sums + rows[...].T
    columns = jnp.broadcast_to(pre_sum, (SUB, pre_sum.shape[1])).T.reshape(count, kinds, channels, SUB)
    for kind in range(kinds):
        column = columns[:, kind].reshape(width, SUB)[:, :1]
        total = total + jnp.where(plan.kind(lane, 2 + kind), column, 0.0)
    return total


def held_back(arrays, after):
    kept = len(arrays)
    return pl.pallas_call(
        lambda *refs: None,
        out_shape=tuple(pltpu.HBM(a.shape, a.dtype) for a in arrays),
        in_specs=[whole(pltpu.HBM)] * kept + [whole(pl.ANY)] * len(after),
        out_specs=(whole(pltpu.HBM),) * kept,
        input_output_aliases={i: i for i in range(kept)},
        cost_estimate=pl.CostEstimate(flops=0, bytes_accessed=0, transcendentals=0),
        name="held_back",
    )(*map(distant, arrays), *after)


def act_grads_kernel(scaled, weight_out, *rest):
    out = rest[-1]
    tile = 768
    for c in range(0, out.shape[1], tile):
        part = lax.dot_general(scaled[...], weight_out[pl.ds(c, tile), :], (((1,), (1,)), ((), ())), preferred_element_type=F32)
        out[:, pl.ds(c, tile)] = part


def act_grads(scaled, weight_out, after):
    outs = [((scaled.shape[0], weight_out.shape[0]), F32, AUTO)]
    return run(act_grads_kernel, "act_grads", [(scaled, AUTO), (weight_out, AUTO)], outs, [], after, micros=6)[0]


def merge_entries(at, bit, keep, got, mine, other):
    low = (1 << at) - 1
    for e in range(mine.shape[0]):
        first = (e >> at << at + 1) + (e & low)
        here, there = first + bit * (low + 1), first + (1 - bit) * (low + 1)
        other[e] = keep(there) + got(there, first)
        mine[e] = keep(here) + got(here, first)


def first_merge_kernel(cuts, counts, *refs):
    outs, mark, scratch = refs[-12:-6], refs[-6], refs[-5:]
    mark[...] = jnp.zeros_like(mark)
    sems, groups, used, at, places = scratch[-1], [], 0, 0, []
    for which, count in enumerate(counts):
        keep, came, got = scratch[2 * which], scratch[2 * which + 1], refs[at + 1 : at + 1 + count]
        places.append(got)
        chunks, chips, high, width = keep.shape
        for i in range(chunks):
            there = [(refs[at].at[i], keep.at[i])]
            if len(got[0].shape) == 4:
                part = chips // count
                if i == chunks - 1:
                    there += [(piece.at[i], came.at[i, pl.ds(p * part, part)]) for p, piece in enumerate(got)]
            else:
                each = count // chunks
                there += [(got[i * each + p], came.at[i, :, :, lanes]) for p, lanes in enumerate(lane_parts(width, each))]
            groups.append(started(there, sems.at[pl.ds(used, len(there))]))
            used += len(there)
        at += 1 + count
    for which in range(2):
        keep, came = scratch[2 * which], scratch[2 * which + 1]
        chunks, _, high, _ = keep.shape
        for i in range(chunks):
            for copy in groups[which * chunks + i]:
                copy.wait()
            pair, row = (which, i * high) if i < chunks - 1 else (2, which * high)
            cut, bit = cuts[pair]
            mine, other = (out.at[:, pl.ds(row, high)] for out in outs[2 * pair : 2 * pair + 2])
            new = lambda e, first: came[i, e]
            if len(places[which][0].shape) == 4 and i < chunks - 1:
                part = places[which][0].shape[1]
                new = lambda e, first: places[which][first // part][i, e - first // part * part]
            merge_entries(cut, own_bit(bit), lambda e: keep[i, e], new, mine, other)


def first_merge(parts, cuts, after):
    chunks, chips, high, width = parts[0][0].shape
    ins = [(value, place) for (keep, got), near_by in zip(parts, (FAR, NEAR)) for value, place in ((keep, FAR), *((piece, near_by) for piece in got))]
    outs = [((chips // 2, rows, width), BF16, NEAR) for rows in ((chunks - 1) * high, (chunks - 1) * high, 2 * high) for _ in range(2)]
    room = [pltpu.VMEM(keep.shape, BF16) for keep, _ in parts for _ in range(2)] + [pltpu.SemaphoreType.DMA((64,))]
    kernel = functools.partial(first_merge_kernel, cuts, [len(got) for _, got in parts])
    *halves, mark = run(kernel, "first_merge", ins, outs + [((SUB, LANES), F32, AUTO)], room, after, limit=LESS)
    return halves[0::2], halves[1::2], mark


def merge_kernel(jobs, *refs):
    count, pairs = sum(len(job) for job in jobs), 2 * len(jobs)
    outs, mark = refs[-1 - pairs : -1], refs[-1]
    mark[...] = jnp.zeros_like(mark)
    i = 0
    for j, job in enumerate(jobs):
        row = 0
        for at, bit in job:
            keep, got = refs[i], refs[count + i]
            rows = pl.ds(row, keep.shape[1])
            merge_entries(at, own_bit(bit), lambda e: keep[e], lambda e, first: got[e], outs[2 * j].at[:, rows], outs[2 * j + 1].at[:, rows])
            row += keep.shape[1]
            i += 1


def merge(keeps, gots, jobs, after=()):
    ins = [(value, NEAR) for value in keeps] + [(value, OPEN) for value in gots]
    outs, i = [], 0
    for job in jobs:
        parts = keeps[i : i + len(job)]
        i += len(job)
        outs += [((parts[0].shape[0] // 2, sum(part.shape[1] for part in parts), parts[0].shape[2]), BF16, NEAR)] * 2
    *halves, mark = run(functools.partial(merge_kernel, jobs), "merge_halves", ins, outs + [((SUB, LANES), F32, AUTO)], [], after, limit=LESS)
    return halves[0::2], halves[1::2], mark


def last_kernel(keep, got, less_keep, less_got, in_sum, out_sum):
    total = keep[0].astype(F32) + got[0].astype(F32)
    less = less_keep[0].astype(F32) + less_got[0].astype(F32)
    high = less.shape[0] // 2
    tile = in_sum.shape[1] // CHUNKS
    for i, part in enumerate((total[:high], total[high : 2 * high], less[:high])):
        in_sum[:, pl.ds(i * tile, tile)] = retiled(part, tile)
    out_sum[pl.ds(0, 2 * high), :] = total[2 * high :]
    out_sum[pl.ds(2 * high, high), :] = less[high:]


def last_sums(parts, channels, hidden, after):
    ins = [(parts[0], NEAR), (parts[1], OPEN), (parts[2], NEAR), (parts[3], OPEN)]
    high, width = parts[2].shape[1] // 2, parts[2].shape[2]
    outs = [((channels, hidden), F32, AUTO), ((CHUNKS * high, width), F32, AUTO)]

    def kernel(*refs):
        last_kernel(*refs[:4], *refs[-2:])

    return run(kernel, "last_sums", ins, outs, [], after)


def tap_places():
    reach = np.concatenate([np.arange(s) / s for s in SIDES]).astype(np.float32)
    scale = np.concatenate([np.full(s, 1.0 / math.sqrt(s)) for s in SIDES]).astype(np.float32)
    return reach, scale


def profiles(coefficient, log_rate):
    reach, scale = tap_places()
    decayed = jnp.exp(-jnp.exp(log_rate)[None] * reach[:, None, None])
    return jnp.sum(coefficient[None] * decayed, axis=2) * scale[:, None]


def profile_grads(coefficient, log_rate, grads):
    reach, scale = tap_places()
    rate = jnp.exp(log_rate)
    decayed = jnp.exp(-rate[None] * reach[:, None, None])
    weighted = (grads * scale[:, None])[:, :, None] * decayed
    return jnp.sum(weighted, axis=0), -coefficient * rate * jnp.sum(weighted * reach[:, None, None], axis=0)


def kernel_matrix(profile, part):
    side = part["side"]
    offsets = np.arange(side)[:, None] - np.arange(side)[None, :]
    picked = profile[part["tap"] + np.maximum(offsets, 0)]
    return jnp.where((offsets >= 0)[:, :, None], picked, 0.0)


def mix_plain(plan, row_pixel, channel_rows, height, width, skip):
    def one_channel(given):
        values, high, wide, weight = given
        image_order = jnp.zeros_like(values).at[row_pixel].set(values)
        pieces = []
        for part in plan.sections:
            side, count = part["side"], part["images"] * part["side"] ** 2
            block = image_order[part["pixel"] : part["pixel"] + count].reshape(-1, side, side)
            left = kernel_matrix(high[:, None], part)[:, :, 0]
            right = kernel_matrix(wide[:, None], part)[:, :, 0]
            mixed = jnp.einsum("ik,nkl,jl->nij", left, block, right, precision=lax.Precision.HIGHEST)
            pieces.append(mixed.reshape(-1))
        joined = jnp.concatenate(pieces) + weight * image_order
        return joined[row_pixel]

    return lax.map(jax.checkpoint(one_channel), (channel_rows, height.T, width.T, skip))


def exchange(blocks):
    return lax.all_to_all(blocks, "chan", 0, 0, tiled=True)


def to_blocks(rows, devices):
    return rows.T.reshape(devices, rows.shape[1] // devices, rows.shape[0])


def to_rows(blocks):
    return blocks.reshape(-1, blocks.shape[2]).T


def halve(blocks, bits):
    myself = lax.axis_index("chan")
    size = lax.axis_size("chan")
    pairs = lambda bit: [(i, i ^ 1 << bit) for i in range(size)]
    left = list(range(size.bit_length() - 1))
    for bit in bits:
        at = left.index(bit)
        viewed = blocks.reshape((-1, 2, 1 << at) + blocks.shape[1:])
        own = myself >> bit & 1
        keep = lax.dynamic_index_in_dim(viewed, own, 1, keepdims=False)
        send = lax.dynamic_index_in_dim(viewed, 1 - own, 1, keepdims=False)
        got = lax.ppermute(send, "chan", pairs(bit))
        total = keep.astype(F32) + got.astype(F32)
        left.remove(bit)
        blocks = (total if not left else total.astype(BF16)).reshape((-1,) + blocks.shape[1:])
    return blocks[0]


def swapped(x, bit):
    return lax.ppermute(x, "chan", [(i, i ^ 1 << bit) for i in range(lax.axis_size("chan"))])


def body_fast(
    tokens,
    row_pixel,
    coef_height,
    rate_height,
    coef_width,
    rate_width,
    skip_weight,
    norm_gain,
    norm_bias,
    weight_in,
    bias_in,
    weight_out,
    bias_out,
    layer_scale,
    out_grad,
):
    devices = lax.axis_size("chan")
    rows, width_all = tokens.shape
    plan = Plan(devices, rows, width_all // devices)
    token_blocks = exchange(to_blocks(tokens, devices))
    where = plan.address(row_pixel)
    spread = plan.spread()
    taps = (plan.tile_taps(profiles(coef_height, rate_height)), plan.tile_taps(profiles(coef_width, rate_width)), plan.tile_taps(skip_weight[None]))
    mixed_blocks, packed, across = mixer_forward(plan, where, token_blocks, *taps)

    scaled = out_grad.astype(F32) * layer_scale
    scaled_low = scaled.astype(BF16)
    rows_given = jnp.stack([layer_scale, bias_out, jnp.sum(scaled, axis=0)])
    grad_act = act_grads(scaled_low, weight_out, (rows_given,))
    grad_normin, act, sums, pre_sum, in_keep, in_sent = feed(plan, exchange(mixed_blocks), norm_gain, norm_bias, weight_in, bias_in, grad_act)
    grad_blocks = exchange(grad_normin)
    out_keep, out_sent = out_grad_halves(plan, act, scaled_low)
    out_got = [swapped(piece, 0) for piece in out_sent]
    in_got = [swapped(piece, 0) for piece in in_sent]

    x, y, near_z, far_z = range(1, 5)
    swap = lambda parts, bits: [swapped(part, bit) for part, bit in zip(parts, bits)]
    keeps, sends, mark = first_merge(((in_keep, in_got), (out_keep, out_got)), ((0, x), (1, y), (2, near_z)), (grad_blocks,))
    gots = swap(sends, (x, y, near_z))
    grads, block_out, shares, mark = mixer_arrive(plan, where, grad_blocks, act, weight_out, rows_given, tokens, out_grad, sums, pre_sum, (mark,))
    keeps, sends, mark = merge(keeps, gots, (((0, y),), ((0, x),), ((2, far_z),)), (mark,))
    gots = swap(sends, (y, x, far_z))
    grads, *tap_sums, mark = mixer_backward(plan, grads, *taps, packed, across, (mark,))
    both_keeps, both_sends, mark = merge(keeps[:2], gots[:2], (((0, near_z), (0, near_z)),), (mark,))
    both_gots = swap(both_sends, (near_z,))
    leaving, left = mixer_leave(plan, where, grads, shares, (mark,))
    keeps, sends, mark = merge((both_keeps[0], keeps[2]), (both_gots[0], gots[2]), (((0, far_z),), ((0, x),)), (left,))
    (moved,) = held_back((leaving,), (mark,))
    grad_tokens, *smalls = token_grads(plan, exchange(moved), out_grad, pre_sum.shape[1] // width_all)
    both_got, less_got = swap(sends, (far_z, x))
    less_keeps, less_sends, mark = merge(keeps[1:], (less_got,), (((0, y),),))
    (less_got,) = swap(less_sends, (y,))
    coef_grads = tap_grads(plan, (coef_height, rate_height, coef_width, rate_width), spread.astype(F32), tap_sums, (mark,))
    in_sum, out_sum = last_sums(
        (keeps[0], both_got, less_keeps[0], less_got), plan.channels, weight_in.shape[1], (grad_tokens, *coef_grads)
    )
    gain_grad, norm_bias_grad, bias_in_grad, bias_out_grad, scale_grad = (small[0] for small in smalls)
    return (block_out, grad_tokens, *coef_grads, gain_grad, norm_bias_grad, in_sum, bias_in_grad, out_sum, bias_out_grad, scale_grad)


def body_plain(
    tokens,
    row_pixel,
    coef_height,
    rate_height,
    coef_width,
    rate_width,
    skip_weight,
    norm_gain,
    norm_bias,
    weight_in,
    bias_in,
    weight_out,
    bias_out,
    layer_scale,
    out_grad,
):
    devices = lax.axis_size("chan")
    rows, width_all = tokens.shape
    plan = Plan(devices, rows, width_all // devices)
    token_blocks = exchange(to_blocks(tokens, devices))

    height = profiles(coef_height, rate_height)
    width = profiles(coef_width, rate_width)
    lines = lambda blocks: blocks.transpose(1, 0, 2).reshape(blocks.shape[1], -1)
    blocks_of = lambda values: values.astype(BF16).reshape(-1, devices, rows).transpose(1, 0, 2)
    mixed, mixer_back = jax.vjp(
        functools.partial(mix_plain, plan, row_pixel), lines(token_blocks).astype(F32), height, width, skip_weight
    )
    mixed_blocks = blocks_of(mixed)
    normin = to_rows(exchange(mixed_blocks)).astype(F32)

    upstream = out_grad.astype(F32)
    scaled = upstream * layer_scale
    scaled_low = scaled.astype(BF16)
    grad_act = lax.dot_general(scaled_low, weight_out, (((1,), (1,)), ((), ())), preferred_element_type=F32)

    row_mean = jnp.mean(normin, axis=1, keepdims=True)
    centred = normin - row_mean
    inv_std = lax.rsqrt(jnp.mean(centred * centred, axis=1, keepdims=True) + EPSILON)
    unit_rows = centred * inv_std
    normed = (unit_rows * norm_gain + norm_bias).astype(BF16)
    hidden_pre = jnp.dot(normed, weight_in, preferred_element_type=F32) + bias_in
    cdf = 0.5 * (1.0 + lax.erf(hidden_pre * math.sqrt(0.5)))
    act_low = (hidden_pre * cdf).astype(BF16)
    slope = cdf + hidden_pre * jnp.exp(-0.5 * hidden_pre * hidden_pre) * (1.0 / math.sqrt(2.0 * math.pi))
    grad_pre = grad_act * slope
    grad_pre_low = grad_pre.astype(BF16)
    grad_normed = lax.dot_general(grad_pre_low, weight_in, (((1,), (1,)), ((), ())), preferred_element_type=F32)
    grad_unit = grad_normed * norm_gain
    grad_normin = inv_std * (
        grad_unit
        - jnp.mean(grad_unit, axis=1, keepdims=True)
        - unit_rows * jnp.mean(grad_unit * unit_rows, axis=1, keepdims=True)
    )
    grad_blocks = exchange(to_blocks(grad_normin.astype(BF16), devices))

    branch = jnp.dot(act_low, weight_out, preferred_element_type=F32) + bias_out
    block_out = (tokens.astype(F32) + layer_scale * branch).astype(BF16)
    small = (
        jnp.sum(grad_normed * unit_rows, axis=0),
        jnp.sum(grad_normed, axis=0),
        jnp.sum(grad_pre, axis=0),
        jnp.sum(scaled, axis=0),
        jnp.sum(upstream * branch, axis=0),
    )
    weight_in_part = lax.dot_general(normed, grad_pre_low, (((0,), (0,)), ((), ())), preferred_element_type=F32)
    weight_out_part = lax.dot_general(act_low, scaled_low, (((0,), (0,)), ((), ())), preferred_element_type=F32)

    grad_mixed, grad_height, grad_width, grad_skip = mixer_back(lines(grad_blocks).astype(F32))
    grad_rows = blocks_of(grad_mixed)
    coef_height_grad, rate_height_grad = profile_grads(coef_height, rate_height, grad_height)
    coef_width_grad, rate_width_grad = profile_grads(coef_width, rate_width, grad_width)
    grad_tokens = upstream + to_rows(exchange(grad_rows)).astype(F32)

    levels = list(range(devices.bit_length() - 1))
    other = levels[:1] + levels[1:3][::-1] + levels[3:]
    in_sum = halve(weight_in_part.astype(BF16).reshape(devices, -1, weight_in.shape[1]), levels)
    out_sum = halve(weight_out_part.astype(BF16).reshape(devices, -1, weight_out.shape[1]), other)
    shares = jnp.concatenate([s.reshape(devices, -1) for s in small], axis=1)
    shares = exchange(shares).sum(axis=0)
    cuts = np.cumsum([s.shape[0] // devices for s in small])[:-1]
    gain_grad, norm_bias_grad, bias_in_grad, bias_out_grad, scale_grad = jnp.split(shares, cuts)
    return (
        block_out,
        grad_tokens,
        coef_height_grad,
        rate_height_grad,
        coef_width_grad,
        rate_width_grad,
        grad_skip,
        gain_grad,
        norm_bias_grad,
        in_sum,
        bias_in_grad,
        out_sum,
        bias_out_grad,
        scale_grad,
    )


def solution(mesh):
    split, copied = P("chan"), P()

    def body(tokens, *rest):
        devices = lax.axis_size("chan")
        fast = Plan(devices, tokens.shape[0], tokens.shape[1] // devices).fits() and devices == 32
        return (body_fast if fast else body_plain)(tokens, *rest)

    in_specs = (split, copied) + (split,) * 5 + (copied,) * 7 + (split,)
    return jax.shard_map(body, mesh=mesh, in_specs=in_specs, out_specs=(split,) * 14, check_vma=False)
```
